32 devices in a mesh: parts: 2 (over y), pool: 4 (over z), tp: 2 (over x), sub: 2 (over core).
Axes of the slice: x: 2, y: 2, z: 4, core: 2. Of those that a mesh axis runs over, the one named last changes fastest.
Arguments:
- deltas: bfloat16 [32, 2, 512, 1024], P(('parts', 'pool'), None, 'sub', 'tp'), parts along dimension 0, may hold values from -6 to 6
- anchors: bfloat16 [32, 2, 32, 1024], P(('parts', 'pool'), None, 'sub', 'tp'), parts along dimension 0, may hold values from -6 to 6
- chan_scale: bfloat16 [32, 2, 1024], P(('parts', 'pool'), None, 'tp'), parts along dimension 0, may hold values from 0.049804688 to 0.5
- lengths: int32 [32], P(('parts', 'pool')), parts along dimension 0, may hold values from 128 to 512, as said below
- route: int32 [32], P(('parts', 'pool')), parts along dimension 0, may hold values from 0 to 3, as said below
- new_query: bfloat16 [32, 4, 8192], P(('parts', 'pool'), None, ('tp', 'sub')), parts along dimension 0, may hold values from -32 to 32
- new_kv: bfloat16 [32, 2, 4, 1024], P(('parts', 'pool'), None, None, 'tp'), parts along dimension 0, may hold values from -8 to 8
Outputs:
- cache: bfloat16 [32, 2, 512, 1024], P(('parts', 'pool'), None, 'sub', 'tp'), parts along dimension 0
- attended: bfloat16 [32, 4, 8192], P(('parts', 'pool'), None, ('tp', 'sub')), parts along dimension 0
The draws below stay inside these ranges and needn't reach their ends.
There are 2 independent parts, one for each index of `parts`. The reference program is written for one: setup_inputs(seed, part) draws one part's arguments, and reference() takes and returns one part's arrays. A program takes and returns all parts, laid end to end along the dimension named above; each array names one. Nothing has to cross between parts.
Inputs may be any that keep to these rules, and one draw needn't show every extreme that they name: `lengths`: multiples of 128; every draw holds a request of length 512. `route`: each prefill index sends exactly 1 of its requests to every decode group.
All inputs are finite; a program needn't handle non-finite values.
Results may differ from the reference program's by a relative error of at most 0.003.
Values may be sent and summed in bfloat16 or wider, within the bound.
No kernel may reach another device: no remote copies, remote signals or barrier semaphores. Data moves between devices by JAX's collectives and lax.ppermute only.
A program may use at most 64 MiB of HBM per device.

```python
import math
import jax
import jax.numpy as jnp
from jax import lax

KV_HEADS = 8
HEAD_DIM = 128
Q_PER_KV = 8
STEPS = 4
ANCHOR = 16
PAGE = 128
SLOTS = 1
MAXLEN = 512
REQ_DEV = 4
REQUESTS = 16
N_POOL = 4


def draw_new_query(key, part):
    key = jax.random.fold_in(key, 21)
    value = jnp.clip(jax.random.normal(key, (REQUESTS, STEPS, KV_HEADS * Q_PER_KV * HEAD_DIM), jnp.float32), -6.0, 6.0)
    return value.astype(jnp.bfloat16)


def draw_new_kv(key, part):
    key = jax.random.fold_in(key, 22)
    value = jnp.clip(jax.random.normal(key, (REQUESTS, 2, STEPS, KV_HEADS * HEAD_DIM), jnp.float32), -6.0, 6.0)
    return value.astype(jnp.bfloat16)


def draw_route(key, part):
    key = jax.random.fold_in(key, 31)
    groups = jnp.arange(REQ_DEV, dtype=jnp.int32) // SLOTS
    sources = jax.random.split(key, N_POOL)
    shuffled = jax.vmap(lambda sub_key: jax.random.permutation(sub_key, groups))(sources)
    return shuffled.reshape(REQUESTS).astype(jnp.int32)


def draw_lengths(key, part):
    key = jax.random.fold_in(key, 41)
    pages = jax.random.randint(key, (REQUESTS,), 1, MAXLEN // PAGE + 1)
    longest = jax.random.randint(jax.random.fold_in(key, 42), (), 0, REQUESTS)
    lengths = (pages * PAGE).astype(jnp.int32)
    return lengths.at[longest].set(MAXLEN).astype(jnp.int32)


def block_levels(stream_key, dims, pieces, smallest, largest):
    level = 1.0
    for dim, parts in pieces:
        draws = jax.random.uniform(jax.random.fold_in(jax.random.fold_in(stream_key, 6), dim), (parts,), jnp.float32, smallest / len(pieces), largest / len(pieces))
        level = level * jnp.repeat(jnp.exp(draws), dims[dim] // parts).reshape((-1,) + (1,) * (len(dims) - 1 - dim))
    return level


def centred(own_key, shape, width, limit, pieces=(), kind=jnp.bfloat16):
    values = width * jax.random.normal(own_key, shape, jnp.float32)
    if pieces:
        values = values * block_levels(own_key, shape, pieces, -0.22, 0.18)
    return jnp.clip(values, -limit, limit).astype(kind)


def setup_inputs(seed: int = 0, part: int = 0) -> dict:
    streams_of = jax.random.split(jax.random.key(seed), 8)
    own_keys = jax.random.split(jax.random.fold_in(streams_of[7], part), 8)
    deltas = centred(own_keys[0], (REQUESTS, 2, MAXLEN, KV_HEADS * HEAD_DIM), 1.0, 6.0, ((0, 4), (2, 2), (3, 2)))
    anchors = centred(own_keys[1], (REQUESTS, 2, MAXLEN // ANCHOR, KV_HEADS * HEAD_DIM), 1.0, 6.0, ((0, 4), (2, 2), (3, 2)))
    chan_scale = jnp.clip(jnp.exp(math.log(0.5) - 2.306499 * jax.random.uniform(own_keys[2], (REQUESTS, 2, KV_HEADS * HEAD_DIM), jnp.float32) ** block_levels(own_keys[2], (REQUESTS, 2, KV_HEADS * HEAD_DIM), ((0, 4), (2, 2)), -0.2, 0.2)), 0.049804688, 0.5).astype(jnp.bfloat16)
    lengths = draw_lengths(jax.random.fold_in(jax.random.fold_in(streams_of[7], part), 71), part)
    route = draw_route(jax.random.fold_in(jax.random.fold_in(streams_of[7], part), 71), part)
    new_query = draw_new_query(jax.random.fold_in(jax.random.fold_in(streams_of[7], part), 71), part)
    new_kv = draw_new_kv(jax.random.fold_in(jax.random.fold_in(streams_of[7], part), 71), part)
    return {"deltas": deltas, "anchors": anchors, "chan_scale": chan_scale, "lengths": lengths, "route": route, "new_query": new_query, "new_kv": new_kv}


def rebuild_one(delta, anchor, scale, length):
    full = jnp.repeat(anchor.astype(jnp.float32), ANCHOR, axis=1)
    value = full + scale.astype(jnp.float32)[:, None, :] * delta.astype(jnp.float32)
    position = jnp.arange(MAXLEN, dtype=jnp.int32)
    value = jnp.where((position < length)[None, :, None], value, jnp.float32(0.0))
    return value.astype(jnp.bfloat16)

def attend_one(cached, length, query, fresh):
    factor = 1.0 / math.sqrt(HEAD_DIM)
    q_heads = query.reshape(STEPS, KV_HEADS, Q_PER_KV, HEAD_DIM).astype(jnp.float32)
    keys = cached[0].reshape(MAXLEN, KV_HEADS, HEAD_DIM).astype(jnp.float32)
    values = cached[1].reshape(MAXLEN, KV_HEADS, HEAD_DIM).astype(jnp.float32)
    new_keys = fresh[0].reshape(STEPS, KV_HEADS, HEAD_DIM).astype(jnp.float32)
    new_values = fresh[1].reshape(STEPS, KV_HEADS, HEAD_DIM).astype(jnp.float32)
    old_scores = jnp.einsum('tjgd,sjd->jtgs', q_heads, keys) * factor
    new_scores = jnp.einsum('tjgd,ujd->jtgu', q_heads, new_keys) * factor
    live = (jnp.arange(MAXLEN, dtype=jnp.int32) < length)[None, None, None, :]
    steps_idx = jnp.arange(STEPS, dtype=jnp.int32)
    causal = (steps_idx[None, :] <= steps_idx[:, None])[None, :, None, :]
    old_scores = jnp.where(live, old_scores, jnp.float32(-1e+30))
    new_scores = jnp.where(causal, new_scores, jnp.float32(-1e+30))
    top = jnp.maximum(lax.optimization_barrier(jnp.max(old_scores, axis=-1)), lax.optimization_barrier(jnp.max(new_scores, axis=-1)))
    old_weights = jnp.where(live, jnp.exp(old_scores - top[..., None]), jnp.float32(0.0))
    new_weights = jnp.where(causal, jnp.exp(new_scores - top[..., None]), jnp.float32(0.0))
    total = lax.optimization_barrier(jnp.sum(old_weights, axis=-1)) + lax.optimization_barrier(jnp.sum(new_weights, axis=-1))
    old_round = old_weights.astype(jnp.bfloat16)
    new_round = new_weights.astype(jnp.bfloat16)
    old_round, new_round = lax.optimization_barrier((old_round, new_round))
    summed = jnp.einsum('jtgs,sjd->jtgd', old_round.astype(jnp.float32), values)
    summed = summed + jnp.einsum('jtgu,ujd->jtgd', new_round.astype(jnp.float32), new_values)
    result = summed / total[..., None]
    result = jnp.transpose(result, (1, 0, 2, 3)).reshape(STEPS, KV_HEADS * Q_PER_KV * HEAD_DIM)
    return result.astype(jnp.bfloat16)

def reference(deltas, anchors, chan_scale, lengths, route, new_query, new_kv):
    sort_key = route.astype(jnp.int32) * REQUESTS + jnp.arange(REQUESTS, dtype=jnp.int32)
    order = jnp.argsort(sort_key, stable=True).astype(jnp.int32)

    def one_row(index):
        source = order[index]
        cached = rebuild_one(deltas[source], anchors[source], chan_scale[source], lengths[source])
        result = attend_one(cached, lengths[source], new_query[index], new_kv[index])
        return (cached, result)
    cache, attended = lax.map(one_row, jnp.arange(REQUESTS, dtype=jnp.int32))
    return (cache, attended)
```

```python
import functools
import math

import jax
import jax.numpy as jnp
from jax import lax
from jax.experimental import pallas as pl
from jax.experimental.pallas import tpu as pltpu
from jax.sharding import PartitionSpec as P

HEAD_DIM = 128
Q_PER_KV = 8
TILE = 16
PAD_STEPS = 8
BF = jnp.bfloat16
F32 = jnp.float32


def partner_to(z, k, n):
    return z ^ k if n & (n - 1) == 0 else (z + k) % n


def partner_from(z, k, n):
    return z ^ k if n & (n - 1) == 0 else (z + n - k) % n


def side_block(scale, length):
    shape = (TILE, scale.shape[-1])
    row = lax.broadcasted_iota(jnp.int32, shape, 0)
    scale = scale.astype(F32)
    out = jnp.where(row == 0, scale[0:1, :], jnp.float32(0.0))
    out = jnp.where(row == 1, scale[1:2, :], out)
    out = jnp.where(row == 2, length.astype(F32), out)
    return out.astype(BF)


def pack_kernel(n, route, lengths, place, deltas, anchors, scale, *rest):
    outs, (side, sems) = rest[: 2 * n], rest[2 * n:]
    count = route.shape[0]
    span, rows = deltas.shape[2], anchors.shape[2]
    z = place[0]
    copies = []
    for k in list(range(1, n)) + [0]:
        key_msg, value_msg = outs[2 * k], outs[2 * k + 1]
        dest = partner_to(z, k, n)
        index = jnp.int32(0)
        for j in range(count):
            index = jnp.where(route[j] == dest, jnp.int32(j), index)
        side[k] = side_block(scale[index], lengths[index])
        moves = [
            (deltas.at[index, 0], key_msg.at[pl.ds(0, span)]),
            (anchors.at[index, 0], key_msg.at[pl.ds(span, rows)]),
            (anchors.at[index, 1], key_msg.at[pl.ds(span + rows, rows)]),
            (side.at[k], key_msg.at[pl.ds(span + 2 * rows, TILE)]),
            (deltas.at[index, 1], value_msg),
        ]
        for i, (src, dst) in enumerate(moves):
            copy = pltpu.make_async_copy(src, dst, sems.at[k, i])
            copy.start()
            copies.append(copy)
    for copy in copies:
        copy.wait()


def pack(route, lengths, place, deltas, anchors, scale, n):
    span, channels = deltas.shape[2:]
    rows = anchors.shape[2]
    tall = span + 2 * rows + TILE
    smem = pl.BlockSpec(memory_space=pltpu.SMEM)
    anywhere = pl.BlockSpec(memory_space=pl.ANY)
    shapes = []
    for _ in range(n):
        shapes.append(jax.ShapeDtypeStruct((tall, channels), BF))
        shapes.append(jax.ShapeDtypeStruct((span, channels), BF))
    return pl.pallas_call(
        functools.partial(pack_kernel, n),
        out_shape=shapes,
        in_specs=[smem, smem, smem, anywhere, anywhere, pl.BlockSpec(memory_space=pltpu.VMEM)],
        out_specs=[anywhere] * (2 * n),
        scratch_shapes=[
            pltpu.VMEM((n, TILE, channels), BF),
            pltpu.SemaphoreType.DMA((n, 5)),
        ],
        cost_estimate=pl.CostEstimate(flops=0, bytes_accessed=4 * n * span * channels * 2, transcendentals=0),
    )(route, lengths, place, deltas, anchors, scale)


def rebuild_kernel(which, width, place, *refs):
    delta, anchor, side, cache, mine, theirs = refs[-6:]
    span = delta.shape[0]
    rows = anchor.shape[0]
    repeat = span // rows
    scale = side[which:which + 1, :].astype(F32)
    length = side[2:3, :].astype(F32)
    base = place[2] * span
    mine_at, theirs_at = place[3], place[4]
    blocks = delta.shape[1] // width
    for i in range(rows):
        part = pl.ds(i * repeat, repeat)
        value = anchor[i:i + 1, :].astype(F32) + scale * delta[part, :].astype(F32)
        keep = (base + i * repeat).astype(F32) < length
        value = jnp.where(keep, value, jnp.float32(0.0)).astype(BF)
        cache[0, 0, part, :] = value
        for out, at in ((mine, mine_at), (theirs, theirs_at)):
            piece = value[:, :width]
            for b in range(1, blocks):
                piece = jnp.where(at == b, value[:, b * width:(b + 1) * width], piece)
            out[part, :] = piece


def rebuild(which, k, place, delta, anchor_msg, cache, count, width, span, rows):
    channels = delta.shape[1]
    n_prefetch = 1
    grid = (1,)
    in_specs = [
        pl.BlockSpec((span, channels), lambda i, p: (0, 0)),
        pl.BlockSpec((rows, channels), lambda i, p: (span // rows + which, 0)),
        pl.BlockSpec((TILE, channels), lambda i, p: ((span + 2 * rows) // TILE, 0)),
    ]
    args = [place, delta, anchor_msg, anchor_msg]
    aliases = {}
    if cache is not None:
        in_specs = [pl.BlockSpec(memory_space=pl.ANY)] + in_specs
        args = [place, cache, delta, anchor_msg, anchor_msg]
        aliases = {1: 0}
    return pl.pallas_call(
        functools.partial(rebuild_kernel, which, width),
        grid_spec=pltpu.PrefetchScalarGridSpec(
            num_scalar_prefetch=n_prefetch,
            grid=grid,
            in_specs=in_specs,
            out_specs=[
                pl.BlockSpec((1, 1, span, channels), lambda i, p: (p[5 + k], which, 0, 0)),
                pl.BlockSpec((span, width), lambda i, p: (0, 0)),
                pl.BlockSpec((span, width), lambda i, p: (0, 0)),
            ],
        ),
        out_shape=[
            jax.ShapeDtypeStruct((count, 2, span, channels), BF),
            jax.ShapeDtypeStruct((span, width), BF),
            jax.ShapeDtypeStruct((span, width), BF),
        ],
        input_output_aliases=aliases,
        cost_estimate=pl.CostEstimate(
            flops=4 * span * channels, bytes_accessed=6 * span * channels, transcendentals=0
        ),
    )(*args)


def attend_kernel(steps, place, *refs):
    query, new_kv, side, key_mine, key_other, value_mine, value_other, out = refs[-8:]
    heads, wide = query.shape[1], query.shape[2]
    group = wide // PAD_STEPS
    span = key_mine.shape[0]
    fresh = new_kv.shape[2]
    factor = 1.0 / math.sqrt(HEAD_DIM)
    length = side[2:3, :span].astype(F32) if side.shape[1] >= span else None
    if length is None:
        length = jnp.broadcast_to(side[2:3, 0:1].astype(F32), (1, span))
    spot = lax.broadcasted_iota(jnp.int32, (1, span), 1)
    live_mine = (spot + place[2] * span).astype(F32) < length
    live_other = (spot + (1 - place[2]) * span).astype(F32) < length
    step = lax.broadcasted_iota(jnp.int32, (wide, fresh), 0) % PAD_STEPS
    token = lax.broadcasted_iota(jnp.int32, (wide, fresh), 1)
    causal = (token <= step) & (token < steps)
    nt = (((1,), (1,)), ((), ()))
    low = jnp.float32(-1e30)
    for j in range(heads):
        lanes = slice(j * HEAD_DIM, (j + 1) * HEAD_DIM)
        q = query[0, j]
        s0 = lax.dot_general(q, key_mine[:, lanes], nt, preferred_element_type=F32) * factor
        s1 = lax.dot_general(q, key_other[:, lanes], nt, preferred_element_type=F32) * factor
        s2 = lax.dot_general(q, new_kv[0, 0, :, lanes], nt, preferred_element_type=F32) * factor
        s0 = jnp.where(live_mine, s0, low)
        s1 = jnp.where(live_other, s1, low)
        s2 = jnp.where(causal, s2, low)
        top = jnp.maximum(
            jnp.max(jnp.maximum(s0, s1), axis=1, keepdims=True), jnp.max(s2, axis=1, keepdims=True)
        )
        w0 = jnp.where(live_mine, jnp.exp(s0 - top), jnp.float32(0.0))
        w1 = jnp.where(live_other, jnp.exp(s1 - top), jnp.float32(0.0))
        w2 = jnp.where(causal, jnp.exp(s2 - top), jnp.float32(0.0))
        total = jnp.sum(w0 + w1, axis=1, keepdims=True) + jnp.sum(w2, axis=1, keepdims=True)
        acc = jnp.dot(w0.astype(BF), value_mine[:, lanes], preferred_element_type=F32)
        acc = acc + jnp.dot(w1.astype(BF), value_other[:, lanes], preferred_element_type=F32)
        acc = acc + jnp.dot(w2.astype(BF), new_kv[0, 1, :, lanes], preferred_element_type=F32)
        acc = (acc / total).astype(BF)
        for g in range(group):
            at = (j * group + g) * HEAD_DIM
            out[0, :, at:at + HEAD_DIM] = acc[g * PAD_STEPS:g * PAD_STEPS + steps, :]


def attend(k, place, query, new_kv, msg, keys, values, attended, count, steps, span, rows, width):
    heads, wide = query.shape[1:3]
    fresh = new_kv.shape[2]
    channels = msg.shape[1]
    full = pl.BlockSpec((span, width), lambda i, p: (0, 0))
    in_specs = [
        pl.BlockSpec((1, heads, wide, HEAD_DIM), lambda i, p: (p[5 + k], 0, 0, 0)),
        pl.BlockSpec((1, 2, fresh, width), lambda i, p: (p[5 + k], 0, 0, p[3])),
        pl.BlockSpec((TILE, channels), lambda i, p: ((span + 2 * rows) // TILE, 0)),
        full, full, full, full,
    ]
    args = [query, new_kv, msg, *keys, *values]
    aliases = {}
    if attended is not None:
        in_specs = [pl.BlockSpec(memory_space=pl.ANY)] + in_specs
        args = [attended] + args
        aliases = {1: 0}
    outer = heads * (wide // PAD_STEPS) * HEAD_DIM
    return pl.pallas_call(
        functools.partial(attend_kernel, steps),
        grid_spec=pltpu.PrefetchScalarGridSpec(
            num_scalar_prefetch=1,
            grid=(1,),
            in_specs=in_specs,
            out_specs=pl.BlockSpec((1, steps, outer), lambda i, p: (p[5 + k], 0, 0)),
        ),
        out_shape=jax.ShapeDtypeStruct((count, steps, outer), BF),
        input_output_aliases=aliases,
        cost_estimate=pl.CostEstimate(
            flops=8 * heads * wide * span * HEAD_DIM,
            bytes_accessed=8 * span * width,
            transcendentals=2 * heads * wide * span,
        ),
    )(place, *args)


def body(deltas, anchors, chan_scale, lengths, route, new_query, new_kv):
    n = lax.axis_size("pool")
    count, _, span, channels = deltas.shape
    rows = anchors.shape[2]
    steps = new_query.shape[1]
    q_local = new_query.shape[2] // HEAD_DIM
    heads = max(1, q_local // Q_PER_KV)
    group = q_local // heads
    width = heads * HEAD_DIM
    z = lax.axis_index("pool")
    sub = lax.axis_index("sub")
    mine_at = (sub * q_local) // Q_PER_KV // heads
    theirs_at = ((1 - sub) * q_local) // Q_PER_KV // heads
    place = jnp.stack(
        [z, z, sub, mine_at, theirs_at] + [partner_from(z, k, n) for k in range(n)]
    ).astype(jnp.int32)

    query = new_query.reshape(count, steps, heads, group, HEAD_DIM).transpose(0, 2, 3, 1, 4)
    query = jnp.pad(query, ((0, 0),) * 3 + ((0, PAD_STEPS - steps), (0, 0)))
    query = query.reshape(count, heads, group * PAD_STEPS, HEAD_DIM)
    fresh = jnp.pad(new_kv, ((0, 0), (0, 0), (0, TILE - steps), (0, 0)))

    packed = pack(route, lengths, place, deltas, anchors, chan_scale, n)
    order = sorted(range(1, n), key=lambda k: (k == 1, k))
    key_msg, value_msg = [packed[0]] + [None] * (n - 1), [packed[1]] + [None] * (n - 1)
    for msgs, at in ((key_msg, 0), (value_msg, 1)):
        for k in order:
            perm = [(i, partner_to(i, k, n)) for i in range(n)]
            msgs[k] = lax.ppermute(packed[2 * k + at], "pool", perm)

    swap = [(0, 1), (1, 0)]
    cache = None
    keys, values = [None] * n, [None] * n
    use = [0, 1] + [k for k in order if k != 1] if n > 1 else [0]
    for which, msgs, made in ((0, key_msg, keys), (1, value_msg, values)):
        for k in use:
            cache, mine, theirs = rebuild(
                which, k, place, msgs[k], key_msg[k], cache, count, width, span, rows
            )
            made[k] = (mine, lax.ppermute(theirs, "sub", swap))
    attended = None
    for k in use:
        attended = attend(
            k, place, query, fresh, key_msg[k], keys[k], values[k], attended,
            count, steps, span, rows, width,
        )
    return cache, attended


def solution(mesh):
    placed = (
        P(("parts", "pool"), None, "sub", "tp"),
        P(("parts", "pool"), None, "sub", "tp"),
        P(("parts", "pool"), None, "tp"),
        P(("parts", "pool")),
        P(("parts", "pool")),
        P(("parts", "pool"), None, ("tp", "sub")),
        P(("parts", "pool"), None, None, "tp"),
    )
    return jax.shard_map(
        body,
        mesh=mesh,
        in_specs=placed,
        out_specs=(
            P(("parts", "pool"), None, "sub", "tp"),
            P(("parts", "pool"), None, ("tp", "sub")),
        ),
        check_vma=False,
    )
```

```python
import functools
import math

import jax
import jax.numpy as jnp
from jax import lax
from jax.experimental import pallas as pl
from jax.experimental.pallas import tpu as pltpu
from jax.sharding import PartitionSpec as P

HEAD_DIM = 128
Q_PER_KV = 8
TILE = 16
PAD_STEPS = 8
BF = jnp.bfloat16
F32 = jnp.float32


def ring_of(n):
    return (0, 2, 3, 1) if n == 4 else tuple(range(n))


def shifts_of(n):
    return sorted(range(1, n), key=lambda k: (min(k, n - k), k))


def pick(values, at):
    out = jnp.int32(values[0])
    for i, value in enumerate(values[1:], 1):
        out = jnp.where(at == i, jnp.int32(value), out)
    return out


def far(n, k):
    ring = ring_of(n)
    return tuple(ring[(ring.index(z) + k) % n] for z in range(n))


def vmem(x):
    return pltpu.with_memory_space_constraint(x, pltpu.VMEM)


IN_VMEM = pl.BlockSpec(memory_space=pltpu.VMEM)
IN_SMEM = pl.BlockSpec(memory_space=pltpu.SMEM)
IN_HBM = pl.BlockSpec(memory_space=pltpu.HBM)
LIMIT = pltpu.CompilerParams(vmem_limit_bytes=16 * 1024 * 1024)


def side_block(scale, length):
    shape = (TILE, scale.shape[-1])
    row = lax.broadcasted_iota(jnp.int32, shape, 0)
    scale = scale.astype(F32)
    out = jnp.where(row == 0, scale[0:1, :], jnp.float32(0.0))
    out = jnp.where(row == 1, scale[1:2, :], out)
    out = jnp.where(row == 2, length.astype(F32), out)
    return out.astype(BF)


def pack_kernel(n, order, route, lengths, deltas, anchors, scale, *rest):
    outs, sems = rest[:-1], rest[-1]
    count = route.shape[0]
    span, rows = deltas.shape[2], anchors.shape[2]
    z = lax.axis_index("pool")
    copies = []
    for at, k in enumerate(order):
        key_msg, value_msg = outs[2 * at], outs[2 * at + 1]
        dest = pick(far(n, k), z)
        index = jnp.int32(0)
        for j in range(count):
            index = jnp.where(route[j] == dest, jnp.int32(j), index)
        moves = [
            (deltas.at[index, 0], key_msg.at[pl.ds(0, span)]),
            (anchors.at[index, 0], key_msg.at[pl.ds(span, rows)]),
            (anchors.at[index, 1], key_msg.at[pl.ds(span + rows, rows)]),
            (deltas.at[index, 1], value_msg),
        ]
        for i, (src, dst) in enumerate(moves):
            copy = pltpu.make_async_copy(src, dst, sems.at[at, i])
            copy.start()
            copies.append(copy)
        key_msg[pl.ds(span + 2 * rows, TILE), :] = side_block(scale[index], lengths[index])
    for copy in copies:
        copy.wait()


def pack(route, lengths, deltas, anchors, scale, n, order):
    span, channels = deltas.shape[2:]
    tall = span + 2 * anchors.shape[2] + TILE
    shapes = []
    for _ in order:
        shapes += [pltpu.VMEM((tall, channels), BF), pltpu.VMEM((span, channels), BF)]
    return pl.pallas_call(
        functools.partial(pack_kernel, n, order),
        out_shape=shapes,
        in_specs=[IN_SMEM, IN_SMEM, IN_HBM, IN_HBM, IN_VMEM],
        out_specs=[IN_VMEM] * len(shapes),
        scratch_shapes=[pltpu.SemaphoreType.DMA((len(order), 4))],
        compiler_params=LIMIT,
        cost_estimate=pl.CostEstimate(
            flops=0, bytes_accessed=4 * len(order) * span * channels * 2, transcendentals=0
        ),
    )(route, lengths, deltas, anchors, scale)


def rebuild_kernel(n, k, which, rows, delta, key_msg, *refs):
    cache, mine, theirs, made, sem = refs[-5:]
    span, channels = delta.shape[0] if which else key_msg.shape[0] - 2 * rows - TILE, key_msg.shape[1]
    width = mine.shape[1]
    repeat = span // rows
    sub = lax.axis_index("sub")
    row = pick(far(n, n - k), lax.axis_index("pool"))
    side = span + 2 * rows
    scale = key_msg[side + which:side + which + 1, :].astype(F32)
    length = key_msg[side + 2:side + 3, :].astype(F32)
    base = sub * span
    for i in range(rows):
        part = pl.ds(i * repeat, repeat)
        at = span + which * rows + i
        anchor = key_msg[at:at + 1, :].astype(F32)
        value = anchor + scale * delta[part, :].astype(F32)
        keep = (base + i * repeat).astype(F32) < length
        made[part, :] = jnp.where(keep, value, jnp.float32(0.0)).astype(BF)
    copy = pltpu.make_async_copy(made, cache.at[row, which], sem)
    copy.start()
    if width == channels:
        mine[...] = made[...]
        theirs[...] = made[...]
    else:
        @pl.when(sub == 0)
        def _():
            mine[...] = made[:, :width]
            theirs[...] = made[:, width:]

        @pl.when(sub != 0)
        def _():
            mine[...] = made[:, width:]
            theirs[...] = made[:, :width]
    copy.wait()


def rebuild(which, k, n, delta, key_msg, cache, count, width, span, rows):
    channels = delta.shape[1]
    args = [vmem(delta), vmem(key_msg)]
    in_specs = [IN_VMEM, IN_VMEM]
    aliases = {}
    if cache is not None:
        args.append(cache)
        in_specs.append(IN_HBM)
        aliases = {2: 0}
    return pl.pallas_call(
        functools.partial(rebuild_kernel, n, k, which, rows),
        in_specs=in_specs,
        out_specs=[IN_HBM, IN_VMEM, IN_VMEM],
        out_shape=[
            pltpu.HBM((count, 2, span, channels), BF),
            pltpu.VMEM((span, width), BF),
            pltpu.VMEM((span, width), BF),
        ],
        scratch_shapes=[pltpu.VMEM((span, channels), BF), pltpu.SemaphoreType.DMA],
        input_output_aliases=aliases,
        compiler_params=LIMIT,
        cost_estimate=pl.CostEstimate(
            flops=4 * span * channels, bytes_accessed=6 * span * channels, transcendentals=0
        ),
    )(*args)


def attend_kernel(n, k, steps, rows, query, new_kv, key_msg, key_mine, key_other, value_mine, value_other, *refs):
    out, made, sem = refs[-3:]
    heads, wide = query.shape[1], query.shape[2]
    group = wide // PAD_STEPS
    span, width = key_mine.shape
    fresh = new_kv.shape[2]
    factor = 1.0 / math.sqrt(HEAD_DIM)
    sub = lax.axis_index("sub")
    row = pick(far(n, n - k), lax.axis_index("pool"))
    side = span + 2 * rows
    length = key_msg[side + 2:side + 3, 0:1].astype(F32)
    spot = lax.broadcasted_iota(jnp.int32, (1, span), 1)
    live_mine = (spot + sub * span).astype(F32) < length
    live_other = (spot + (1 - sub) * span).astype(F32) < length
    step = lax.broadcasted_iota(jnp.int32, (wide, fresh), 0) % PAD_STEPS
    token = lax.broadcasted_iota(jnp.int32, (wide, fresh), 1)
    causal = (token <= step) & (token < steps)
    nt = (((1,), (1,)), ((), ()))
    low = jnp.float32(-1e30)
    for j in range(heads):
        lanes = slice(j * HEAD_DIM, (j + 1) * HEAD_DIM)
        q = query[row, j]
        new_key, new_value = new_kv[row, 0, :, lanes], new_kv[row, 1, :, lanes]
        s0 = lax.dot_general(q, key_mine[:, lanes], nt, preferred_element_type=F32) * factor
        s1 = lax.dot_general(q, key_other[:, lanes], nt, preferred_element_type=F32) * factor
        s2 = lax.dot_general(q, new_key, nt, preferred_element_type=F32) * factor
        s0 = jnp.where(live_mine, s0, low)
        s1 = jnp.where(live_other, s1, low)
        s2 = jnp.where(causal, s2, low)
        top = jnp.maximum(
            jnp.max(jnp.maximum(s0, s1), axis=1, keepdims=True), jnp.max(s2, axis=1, keepdims=True)
        )
        w0 = jnp.where(live_mine, jnp.exp(s0 - top), jnp.float32(0.0))
        w1 = jnp.where(live_other, jnp.exp(s1 - top), jnp.float32(0.0))
        w2 = jnp.where(causal, jnp.exp(s2 - top), jnp.float32(0.0))
        total = jnp.sum(w0 + w1, axis=1, keepdims=True) + jnp.sum(w2, axis=1, keepdims=True)
        acc = jnp.dot(w0.astype(BF), value_mine[:, lanes], preferred_element_type=F32)
        acc = acc + jnp.dot(w1.astype(BF), value_other[:, lanes], preferred_element_type=F32)
        acc = acc + jnp.dot(w2.astype(BF), new_value, preferred_element_type=F32)
        acc = (acc / total).astype(BF)
        for g in range(group):
            at = (j * group + g) * HEAD_DIM
            made[:, at:at + HEAD_DIM] = acc[g * PAD_STEPS:g * PAD_STEPS + steps, :]
    copy = pltpu.make_async_copy(made, out.at[row], sem)
    copy.start()
    copy.wait()


def attend(k, n, query, new_kv, msg, keys, values, attended, count, steps, span, rows):
    heads, wide = query.shape[1:3]
    args = [vmem(x) for x in (query, new_kv, msg, *keys, *values)]
    in_specs = [IN_VMEM] * len(args)
    aliases = {}
    if attended is not None:
        aliases = {len(args): 0}
        args.append(attended)
        in_specs.append(IN_HBM)
    outer = heads * (wide // PAD_STEPS) * HEAD_DIM
    return pl.pallas_call(
        functools.partial(attend_kernel, n, k, steps, rows),
        in_specs=in_specs,
        out_specs=IN_HBM,
        out_shape=pltpu.HBM((count, steps, outer), BF),
        scratch_shapes=[pltpu.VMEM((steps, outer), BF), pltpu.SemaphoreType.DMA],
        input_output_aliases=aliases,
        compiler_params=LIMIT,
        cost_estimate=pl.CostEstimate(
            flops=8 * heads * wide * span * HEAD_DIM,
            bytes_accessed=8 * span * keys[0].shape[1],
            transcendentals=2 * heads * wide * span,
        ),
    )(*args)


def body(deltas, anchors, chan_scale, lengths, route, new_query, new_kv):
    n = lax.axis_size("pool")
    count, _, span, channels = deltas.shape
    rows = anchors.shape[2]
    steps = new_query.shape[1]
    q_local = new_query.shape[2] // HEAD_DIM
    heads = max(1, q_local // Q_PER_KV)
    group = q_local // heads
    width = heads * HEAD_DIM
    sub = lax.axis_index("sub")

    query = new_query.reshape(count, steps, heads, group, HEAD_DIM).transpose(0, 2, 3, 1, 4)
    query = jnp.pad(query, ((0, 0),) * 3 + ((0, PAD_STEPS - steps), (0, 0)))
    query = query.reshape(count, heads, group * PAD_STEPS, HEAD_DIM)
    fresh = new_kv if width == channels else jnp.where(
        sub == 0, new_kv[..., :width], new_kv[..., channels - width:]
    )
    fresh = jnp.pad(fresh, ((0, 0), (0, 0), (0, TILE - steps), (0, 0)))

    order = shifts_of(n)
    packed = pack(route, lengths, deltas, anchors, chan_scale, n, order + [0])
    key_msg, value_msg = {0: packed[-2]}, {0: packed[-1]}
    for at, k in enumerate(order):
        perm = list(enumerate(far(n, k)))
        key_msg[k] = lax.ppermute(packed[2 * at], "pool", perm)
        value_msg[k] = lax.ppermute(packed[2 * at + 1], "pool", perm)

    swap = [(0, 1), (1, 0)]
    cache = attended = None
    for k in [0] + order:
        parts = []
        for which, msg in ((0, key_msg[k]), (1, value_msg[k])):
            cache, mine, theirs = rebuild(
                which, k, n, msg, key_msg[k], cache, count, width, span, rows
            )
            parts.append((mine, lax.ppermute(theirs, "sub", swap)))
        attended = attend(
            k, n, query, fresh, key_msg[k], *parts, attended, count, steps, span, rows
        )
    return cache, attended


def solution(mesh):
    placed = (
        P(("parts", "pool"), None, "sub", "tp"),
        P(("parts", "pool"), None, "sub", "tp"),
        P(("parts", "pool"), None, "tp"),
        P(("parts", "pool")),
        P(("parts", "pool")),
        P(("parts", "pool"), None, ("tp", "sub")),
        P(("parts", "pool"), None, None, "tp"),
    )
    return jax.shard_map(
        body,
        mesh=mesh,
        in_specs=placed,
        out_specs=(
            P(("parts", "pool"), None, "sub", "tp"),
            P(("parts", "pool"), None, ("tp", "sub")),
        ),
        check_vma=False,
    )
```

```python
import functools
import math

import jax
import jax.numpy as jnp
from jax import lax
from jax.experimental import pallas as pl
from jax.experimental.pallas import tpu as pltpu
from jax.sharding import PartitionSpec as P

HEAD_DIM = 128
Q_PER_KV = 8
TILE = 16
PAD_STEPS = 8
BF = jnp.bfloat16
F32 = jnp.float32
LOW = -1e30
NT = (((1,), (1,)), ((), ()))

IN_VMEM = pl.BlockSpec(memory_space=pltpu.VMEM)
IN_SMEM = pl.BlockSpec(memory_space=pltpu.SMEM)
IN_HBM = pl.BlockSpec(memory_space=pltpu.HBM)
LIMIT = pltpu.CompilerParams(vmem_limit_bytes=16 * 1024 * 1024)


def vmem(x):
    return pltpu.with_memory_space_constraint(x, pltpu.VMEM)


def hbm(x):
    return pltpu.with_memory_space_constraint(x, pltpu.HBM)


def far(n, k):
    ring = (0, 2, 3, 1) if n == 4 else tuple(range(n))
    return tuple(ring[(ring.index(z) + k) % n] for z in range(n))


def pick(values, at):
    out = jnp.int32(values[0])
    for i, value in enumerate(values[1:], 1):
        out = jnp.where(at == i, jnp.int32(value), out)
    return out


class Sizes:
    def __init__(self, deltas, anchors, new_query, n):
        self.n = n
        self.count, _, self.span, self.channels = deltas.shape
        self.rows = anchors.shape[2]
        self.repeat = self.span // self.rows
        self.steps = new_query.shape[1]
        self.heads = self.channels // HEAD_DIM
        self.q_local = new_query.shape[2] // HEAD_DIM
        self.mine = max(1, self.q_local // Q_PER_KV)
        self.group = self.q_local // self.mine
        self.wide = self.group * PAD_STEPS

    def anchor_at(self, which, parts):
        return len(parts) * self.heads * self.span + which * self.heads * self.rows

    def side_at(self, parts):
        return len(parts) * self.heads * self.span + 2 * self.heads * self.rows

    def message_rows(self, parts):
        if 0 in parts:
            return self.side_at(parts) + TILE
        return len(parts) * self.heads * self.span

    def source_row(self, k):
        return pick(far(self.n, self.n - k), lax.axis_index("pool"))


def side_block(size, scale, length):
    row = lax.broadcasted_iota(jnp.int32, (TILE, HEAD_DIM), 0)
    scale = scale.astype(F32)
    out = jnp.where(row == 2 * size.heads, length.astype(F32), jnp.float32(0.0))
    for which in range(2):
        for h in range(size.heads):
            piece = scale[which:which + 1, h * HEAD_DIM:(h + 1) * HEAD_DIM]
            out = jnp.where(row == which * size.heads + h, piece, out)
    return out.astype(BF)


def pack_kernel(size, plan, route, lengths, deltas, anchors, scale, *rest):
    outs, sems = rest[:-1], rest[-1]
    z = lax.axis_index("pool")
    copies = []
    for m, (k, parts) in enumerate(plan):
        msg = outs[m]
        dest = pick(far(size.n, k), z)
        index = jnp.int32(0)
        for j in range(size.count):
            index = jnp.where(route[j] == dest, jnp.int32(j), index)
        moves = []
        for p, which in enumerate(parts):
            for h in range(size.heads):
                lanes = pl.ds(h * HEAD_DIM, HEAD_DIM)
                at = (p * size.heads + h) * size.span
                moves.append((deltas.at[index, which, :, lanes], msg.at[pl.ds(at, size.span)]))
        if 0 in parts:
            for which in range(2):
                for h in range(size.heads):
                    lanes = pl.ds(h * HEAD_DIM, HEAD_DIM)
                    at = size.anchor_at(which, parts) + h * size.rows
                    moves.append((anchors.at[index, which, :, lanes], msg.at[pl.ds(at, size.rows)]))
        for i, (src, dst) in enumerate(moves):
            copy = pltpu.make_async_copy(src, dst, sems.at[m, i])
            copy.start()
            copies.append(copy)
        if 0 in parts:
            msg[pl.ds(size.side_at(parts), TILE), :] = side_block(size, scale[index], lengths[index])
    for copy in copies:
        copy.wait()


def pack(size, plan, route, lengths, deltas, anchors, scale):
    shapes = [pltpu.VMEM((size.message_rows(parts), HEAD_DIM), BF) for _, parts in plan]
    return pl.pallas_call(
        functools.partial(pack_kernel, size, plan),
        out_shape=shapes,
        in_specs=[IN_SMEM, IN_SMEM, IN_HBM, IN_HBM, IN_VMEM],
        out_specs=[IN_VMEM] * len(shapes),
        scratch_shapes=[pltpu.SemaphoreType.DMA((len(plan), 4 * size.heads))],
        compiler_params=LIMIT,
        cost_estimate=pl.CostEstimate(
            flops=0, bytes_accessed=2 * len(plan) * size.span * size.channels * 2, transcendentals=0
        ),
    )(hbm(route), hbm(lengths), hbm(deltas), hbm(anchors), hbm(scale))


def row_copies(size, k, parts, cache, mine, theirs, sems):
    sub = lax.axis_index("sub")
    row = size.source_row(k)
    rest = size.heads - size.mine
    copies = []
    for o, (out, first) in enumerate(((mine, sub * rest), (theirs, (1 - sub) * rest))):
        if o and not rest:
            break
        for p, which in enumerate(parts):
            for j in range(size.mine):
                lanes = pl.ds(pl.multiple_of((first + j) * HEAD_DIM, HEAD_DIM), HEAD_DIM)
                at = (p * size.mine + j) * size.span
                copies.append(pltpu.make_async_copy(
                    out.at[pl.ds(at, size.span)],
                    cache.at[row, which, :, lanes],
                    sems.at[o, p * size.mine + j],
                ))
    return copies


def rebuild_kernel(size, k, parts, all_parts, store, chained, *refs):
    if parts == all_parts:
        message = tables = refs[0]
        refs = refs[1:]
    else:
        message, tables = refs[0], refs[1]
        refs = refs[2:]
    refs = refs[2 * chained:]
    cache, _, mine, theirs = refs[:4]
    sub = lax.axis_index("sub")
    rest = size.heads - size.mine
    side_at = size.side_at(all_parts)
    side = tables[side_at:side_at + TILE, :].astype(F32)
    length = side[2 * size.heads:2 * size.heads + 1, :]
    base = sub * size.span
    copies = row_copies(size, k, parts, cache, mine, theirs, refs[4]) if store else []
    at_copy = 0
    for o, out in enumerate((theirs, mine)):
        first = (1 - sub) * rest if o == 0 else sub * rest
        other = sub == 0 if o == 0 else sub != 0
        for p, which in enumerate(parts):
            for j in range(size.mine):
                h = which * size.heads + j
                scale = jnp.where(other, side[h + rest:h + rest + 1, :], side[h:h + 1, :])
                table = pl.multiple_of(
                    size.anchor_at(which, all_parts) + (first + j) * size.rows, TILE
                )
                anchor = tables[pl.ds(table, size.rows), :].astype(F32)
                source = (p * size.heads + first + j) * size.span
                to = (p * size.mine + j) * size.span
                for i in range(size.rows):
                    at = pl.multiple_of(source + i * size.repeat, TILE)
                    value = anchor[i:i + 1, :] + scale * message[pl.ds(at, size.repeat), :].astype(F32)
                    keep = (base + i * size.repeat).astype(F32) < length
                    value = jnp.where(keep, value, jnp.float32(0.0)).astype(BF)
                    out[to + i * size.repeat:to + (i + 1) * size.repeat, :] = value
    for copy in copies:
        copy.start()
    for copy in copies:
        copy.wait()


def rebuild(size, k, parts, all_parts, message, tables, state, store=True):
    args = [vmem(message)] + ([vmem(tables)] if tables is not None else [])
    in_specs = [IN_VMEM] * len(args)
    aliases = {}
    if state is not None:
        aliases = {len(args): 0, len(args) + 1: 1}
        args += list(state)
        in_specs += [IN_HBM, IN_HBM]
    given = (len(parts) * size.mine * size.span, HEAD_DIM)
    scratch = [pltpu.SemaphoreType.DMA((2, len(parts) * size.mine))] if store else []
    out = pl.pallas_call(
        functools.partial(rebuild_kernel, size, k, parts, all_parts, store, state is not None),
        in_specs=in_specs,
        out_specs=[IN_HBM, IN_HBM, IN_VMEM, IN_VMEM],
        out_shape=[
            pltpu.HBM((size.count, 2, size.span, size.channels), BF),
            pltpu.HBM((size.count, size.steps, size.q_local * HEAD_DIM), BF),
            pltpu.VMEM(given, BF),
            pltpu.VMEM(given, BF),
        ],
        scratch_shapes=scratch,
        input_output_aliases=aliases,
        compiler_params=LIMIT,
        cost_estimate=pl.CostEstimate(
            flops=4 * len(parts) * size.span * size.channels,
            bytes_accessed=6 * len(parts) * size.span * size.channels,
            transcendentals=0,
        ),
    )(*args)
    return tuple(out[:2]), out[2], out[3]


def weigh(size, j, q, new_key, key_mine, key_other, live_mine, live_other, causal):
    factor = 1.0 / math.sqrt(HEAD_DIM)
    s0 = lax.dot_general(q, key_mine, NT, preferred_element_type=F32) * factor
    s1 = lax.dot_general(q, key_other, NT, preferred_element_type=F32) * factor
    s2 = lax.dot_general(q, new_key, NT, preferred_element_type=F32) * factor
    s0 = jnp.where(live_mine, s0, jnp.float32(LOW))
    s1 = jnp.where(live_other, s1, jnp.float32(LOW))
    s2 = jnp.where(causal, s2, jnp.float32(LOW))
    top = jnp.maximum(
        jnp.max(jnp.maximum(s0, s1), axis=1, keepdims=True), jnp.max(s2, axis=1, keepdims=True)
    )
    w0 = jnp.where(live_mine, jnp.exp(s0 - top), jnp.float32(0.0))
    w1 = jnp.where(live_other, jnp.exp(s1 - top), jnp.float32(0.0))
    w2 = jnp.where(causal, jnp.exp(s2 - top), jnp.float32(0.0))
    total = jnp.sum(w0 + w1, axis=1, keepdims=True) + jnp.sum(w2, axis=1, keepdims=True)
    return w0.astype(BF), w1.astype(BF), w2.astype(BF), total


def masks(size, tables, parts, fresh):
    sub = lax.axis_index("sub")
    at = size.side_at(parts)
    side = tables[at:at + TILE, :].astype(F32)
    length = side[2 * size.heads:2 * size.heads + 1, 0:1]
    spot = lax.broadcasted_iota(jnp.int32, (1, size.span), 1)
    live_mine = (spot + sub * size.span).astype(F32) < length
    live_other = (spot + (1 - sub) * size.span).astype(F32) < length
    step = lax.broadcasted_iota(jnp.int32, (size.wide, fresh), 0) % PAD_STEPS
    token = lax.broadcasted_iota(jnp.int32, (size.wide, fresh), 1)
    return live_mine, live_other, (token <= step) & (token < size.steps)


def place_heads(size, made, j, result):
    for g in range(size.group):
        at = (j * size.group + g) * HEAD_DIM
        made[:, at:at + HEAD_DIM] = result[g * PAD_STEPS:g * PAD_STEPS + size.steps, :]


def attend_kernel(size, k, parts, query, new_kv, tables, mine, other, *refs):
    _, attended, made, sem = refs[2:]
    row = size.source_row(k)
    live_mine, live_other, causal = masks(size, tables, parts, new_kv.shape[2])
    for j in range(size.mine):
        lanes = slice(j * HEAD_DIM, (j + 1) * HEAD_DIM)
        keys = slice(j * size.span, (j + 1) * size.span)
        values = slice((size.mine + j) * size.span, (size.mine + j + 1) * size.span)
        w0, w1, w2, total = weigh(
            size, j, query[row, j], new_kv[row, 0, :, lanes], mine[keys, :], other[keys, :],
            live_mine, live_other, causal,
        )
        acc = jnp.dot(w0, mine[values, :], preferred_element_type=F32)
        acc = acc + jnp.dot(w1, other[values, :], preferred_element_type=F32)
        acc = acc + jnp.dot(w2, new_kv[row, 1, :, lanes], preferred_element_type=F32)
        place_heads(size, made, j, (acc / total).astype(BF))
    copy = pltpu.make_async_copy(made, attended.at[row], sem)
    copy.start()
    copy.wait()


def weights_kernel(size, k, parts, query, new_kv, tables, mine, other, *refs):
    weights, share, totals = refs[4:]
    row = size.source_row(k)
    live_mine, live_other, causal = masks(size, tables, parts, new_kv.shape[2])
    for j in range(size.mine):
        lanes = slice(j * HEAD_DIM, (j + 1) * HEAD_DIM)
        keys = slice(j * size.span, (j + 1) * size.span)
        w0, w1, w2, total = weigh(
            size, j, query[row, j], new_kv[row, 0, :, lanes], mine[keys, :], other[keys, :],
            live_mine, live_other, causal,
        )
        weights[j, :, :size.span] = w0
        weights[j, :, size.span:] = w1
        share[j] = jnp.dot(w2, new_kv[row, 1, :, lanes], preferred_element_type=F32)
        totals[j] = jnp.broadcast_to(total, totals.shape[1:])


def finish_kernel(size, k, parts, weights, share, totals, mine, other, theirs, *refs):
    cache, attended, made, sem, sems = refs[2:]
    row = size.source_row(k)
    copies = row_copies(size, k, parts, cache, mine, theirs, sems)
    for copy in copies:
        copy.start()
    for j in range(size.mine):
        values = slice(j * size.span, (j + 1) * size.span)
        acc = jnp.dot(weights[j, :, :size.span], mine[values, :], preferred_element_type=F32)
        acc = acc + jnp.dot(weights[j, :, size.span:], other[values, :], preferred_element_type=F32)
        place_heads(size, made, j, ((acc + share[j]) / totals[j]).astype(BF))
    copy = pltpu.make_async_copy(made, attended.at[row], sem)
    copy.start()
    for each in copies:
        each.wait()
    copy.wait()


def chained_call(size, kernel, args, state, shapes, scratch, flops):
    args = [vmem(x) for x in args]
    many = len(args)
    out = pl.pallas_call(
        kernel,
        in_specs=[IN_VMEM] * many + [IN_HBM, IN_HBM],
        out_specs=[IN_HBM, IN_HBM] + [IN_VMEM] * len(shapes),
        out_shape=[pltpu.HBM(x.shape, x.dtype) for x in state] + shapes,
        scratch_shapes=scratch,
        input_output_aliases={many: 0, many + 1: 1},
        compiler_params=LIMIT,
        cost_estimate=pl.CostEstimate(
            flops=flops,
            bytes_accessed=8 * size.span * size.channels,
            transcendentals=2 * size.mine * size.wide * size.span,
        ),
    )(*args, *state)
    return tuple(out[:2]), out[2:]


def body(deltas, anchors, chan_scale, lengths, route, new_query, new_kv):
    n = lax.axis_size("pool")
    size = Sizes(deltas, anchors, new_query, n)
    sub = lax.axis_index("sub")
    both, last = (0, 1), n - 1
    plan = [(k, both) for k in range(1, last)] + [(last, (0,)), (last, (1,)), (0, both)]

    query = new_query.reshape(size.count, size.steps, size.mine, size.group, HEAD_DIM)
    query = jnp.pad(query.transpose(0, 2, 3, 1, 4), ((0, 0),) * 3 + ((0, PAD_STEPS - size.steps), (0, 0)))
    query = query.reshape(size.count, size.mine, size.wide, HEAD_DIM)
    width = size.mine * HEAD_DIM
    fresh = new_kv if width == size.channels else jnp.where(
        sub == 0, new_kv[..., :width], new_kv[..., size.channels - width:]
    )
    fresh = jnp.pad(fresh, ((0, 0), (0, 0), (0, TILE - size.steps), (0, 0)))

    packed = dict(zip(plan, pack(size, plan, route, lengths, deltas, anchors, chan_scale)))
    message = {}
    for k, parts in plan:
        message[k, parts] = packed[k, parts]
        if k:
            message[k, parts] = lax.ppermute(packed[k, parts], "pool", list(enumerate(far(n, k))))

    def swapped(x):
        return lax.ppermute(x, "sub", [(0, 1), (1, 0)])

    flops = 8 * size.mine * size.wide * size.span * HEAD_DIM
    result = pltpu.VMEM((size.steps, size.q_local * HEAD_DIM), BF)
    one = pltpu.SemaphoreType.DMA

    def attend(k, mine, other, state):
        state, _ = chained_call(
            size, functools.partial(attend_kernel, size, k, both),
            (query, fresh, message[k, both], mine, other), state, [], [result, one], flops,
        )
        return state

    state, mine, theirs = rebuild(size, 0, both, both, message[0, both], None, None)
    held = (0, mine, swapped(theirs))
    for k in range(1, last):
        state, mine, theirs = rebuild(size, k, both, both, message[k, both], None, state)
        state = attend(*held, state)
        held = (k, mine, swapped(theirs))
    state = attend(*held, state)

    tables = message[last, (0,)]
    state, mine, theirs = rebuild(size, last, (0,), (0,), tables, None, state)
    state, (weights, share, totals) = chained_call(
        size, functools.partial(weights_kernel, size, last, (0,)),
        (query, fresh, tables, mine, swapped(theirs)), state,
        [
            pltpu.VMEM((size.mine, size.wide, 2 * size.span), BF),
            pltpu.VMEM((size.mine, size.wide, HEAD_DIM), F32),
            pltpu.VMEM((size.mine, size.wide, HEAD_DIM), F32),
        ],
        [], flops // 2,
    )
    state, mine, theirs = rebuild(size, last, (1,), (0,), message[last, (1,)], tables, state, store=False)
    state, _ = chained_call(
        size, functools.partial(finish_kernel, size, last, (1,)),
        (weights, share, totals, mine, swapped(theirs), theirs), state, [],
        [result, one, pltpu.SemaphoreType.DMA((2, size.mine))], flops // 2,
    )
    return state


def solution(mesh):
    placed = (
        P(("parts", "pool"), None, "sub", "tp"),
        P(("parts", "pool"), None, "sub", "tp"),
        P(("parts", "pool"), None, "tp"),
        P(("parts", "pool")),
        P(("parts", "pool")),
        P(("parts", "pool"), None, ("tp", "sub")),
        P(("parts", "pool"), None, None, "tp"),
    )
    return jax.shard_map(
        body,
        mesh=mesh,
        in_specs=placed,
        out_specs=(
            P(("parts", "pool"), None, "sub", "tp"),
            P(("parts", "pool"), None, ("tp", "sub")),
        ),
        check_vma=False,
    )
```

```python
import functools
import math

import jax
import jax.numpy as jnp
from jax import lax
from jax.experimental import pallas as pl
from jax.experimental.pallas import tpu as pltpu
from jax.sharding import PartitionSpec as P

HEAD_DIM = 128
Q_PER_KV = 8
TILE = 16
PAD_STEPS = 8
BF = jnp.bfloat16
F32 = jnp.float32
LOW = -1e30
NT = (((1,), (1,)), ((), ()))

IN_VMEM = pl.BlockSpec(memory_space=pltpu.VMEM)
IN_SMEM = pl.BlockSpec(memory_space=pltpu.SMEM)
IN_HBM = pl.BlockSpec(memory_space=pltpu.HBM)
LIMIT = pltpu.CompilerParams(vmem_limit_bytes=16 * 1024 * 1024)


def vmem(x):
    return pltpu.with_memory_space_constraint(x, pltpu.VMEM)


def hbm(x):
    return pltpu.with_memory_space_constraint(x, pltpu.HBM)


def far(n, k):
    ring = (0, 2, 3, 1) if n == 4 else tuple(range(n))
    return tuple(ring[(ring.index(z) + k) % n] for z in range(n))


def pick(values, at):
    out = jnp.int32(values[0])
    for i, value in enumerate(values[1:], 1):
        out = jnp.where(at == i, jnp.int32(value), out)
    return out


class Sizes:
    def __init__(self, deltas, anchors, new_query, n):
        self.n = n
        self.count, _, self.span, self.channels = deltas.shape
        self.rows = anchors.shape[2]
        self.repeat = self.span // self.rows
        self.steps = new_query.shape[1]
        self.heads = self.channels // HEAD_DIM
        self.q_local = new_query.shape[2] // HEAD_DIM
        self.mine = max(1, self.q_local // Q_PER_KV)
        self.group = self.q_local // self.mine
        self.wide = self.group * PAD_STEPS

    def anchor_at(self, which, parts):
        return (len(parts) * self.span + parts.index(which) * self.rows) * self.heads

    def side_at(self, parts):
        return len(parts) * self.heads * (self.span + self.rows)

    def message_rows(self, parts):
        return self.side_at(parts) + (TILE if 0 in parts else 0)

    def source_row(self, k):
        return pick(far(self.n, self.n - k), lax.axis_index("pool"))


def side_block(size, scale, length):
    row = lax.broadcasted_iota(jnp.int32, (TILE, HEAD_DIM), 0)
    scale = scale.astype(F32)
    out = jnp.where(row == 2 * size.heads, length.astype(F32), jnp.float32(0.0))
    for which in range(2):
        for h in range(size.heads):
            piece = scale[which:which + 1, h * HEAD_DIM:(h + 1) * HEAD_DIM]
            out = jnp.where(row == which * size.heads + h, piece, out)
    return out.astype(BF)


def pack_kernel(size, plan, route, lengths, deltas, anchors, scale, *rest):
    outs, (held, tables, sems) = rest[:-3], rest[-3:]
    z = lax.axis_index("pool")
    work = []
    for m, (k, parts) in enumerate(plan):
        dest = pick(far(size.n, k), z)
        index = jnp.int32(0)
        for j in range(size.count):
            index = jnp.where(route[j] == dest, jnp.int32(j), index)
        for which in parts:
            slot = len(work)
            copies = (
                pltpu.make_async_copy(deltas.at[index, which], held.at[slot], sems.at[0, slot]),
                pltpu.make_async_copy(anchors.at[index, which], tables.at[slot], sems.at[1, slot]),
            )
            for copy in copies:
                copy.start()
            work.append((outs[m], parts, which, slot, copies))
        if 0 in parts:
            outs[m][pl.ds(size.side_at(parts), TILE), :] = side_block(size, scale[index], lengths[index])
    for msg, parts, which, slot, copies in work:
        for copy in copies:
            copy.wait()
        for h in range(size.heads):
            lanes = slice(h * HEAD_DIM, (h + 1) * HEAD_DIM)
            at = (parts.index(which) * size.heads + h) * size.span
            msg[at:at + size.span, :] = held[slot, :, lanes]
            at = size.anchor_at(which, parts) + h * size.rows
            msg[at:at + size.rows, :] = tables[slot, :, lanes]


def pack(size, plan, route, lengths, deltas, anchors, scale):
    shapes = [pltpu.VMEM((size.message_rows(parts), HEAD_DIM), BF) for _, parts in plan]
    slots = sum(len(parts) for _, parts in plan)
    return pl.pallas_call(
        functools.partial(pack_kernel, size, plan),
        out_shape=shapes,
        in_specs=[IN_SMEM, IN_SMEM, IN_HBM, IN_HBM, IN_VMEM],
        out_specs=[IN_VMEM] * len(shapes),
        scratch_shapes=[
            pltpu.VMEM((slots, size.span, size.channels), BF),
            pltpu.VMEM((slots, size.rows, size.channels), BF),
            pltpu.SemaphoreType.DMA((2, slots)),
        ],
        compiler_params=LIMIT,
        cost_estimate=pl.CostEstimate(
            flops=0, bytes_accessed=2 * slots * size.span * size.channels, transcendentals=0
        ),
    )(hbm(route), hbm(lengths), hbm(deltas), hbm(anchors), hbm(scale))


def arrange_kernel(size, new_query, new_kv, query, fresh, wide, tall):
    sub = lax.axis_index("sub")
    rest = size.heads - size.mine
    wide[...] = jnp.zeros_like(wide)
    tall[...] = jnp.zeros_like(tall)
    for r in range(size.count):
        for j in range(size.mine):
            for g in range(size.group):
                at = (j * size.group + g) * HEAD_DIM
                piece = new_query[r, :, at:at + HEAD_DIM].astype(F32)
                wide[g * PAD_STEPS:g * PAD_STEPS + size.steps, :] = piece
            query[r, j] = wide[...].astype(BF)
            for which in range(2):
                own, other = (
                    new_kv[r, which, :, h * HEAD_DIM:(h + 1) * HEAD_DIM].astype(F32) for h in (j, j + rest)
                )
                tall[:size.steps, :] = jnp.where(sub == 0, own, other)
                fresh[r, which, j] = tall[...].astype(BF)


def arrange(size, new_query, new_kv):
    return pl.pallas_call(
        functools.partial(arrange_kernel, size),
        in_specs=[IN_VMEM, IN_VMEM],
        out_specs=[IN_VMEM, IN_VMEM],
        out_shape=[
            pltpu.VMEM((size.count, size.mine, size.wide, HEAD_DIM), BF),
            pltpu.VMEM((size.count, 2, size.mine, TILE, HEAD_DIM), BF),
        ],
        scratch_shapes=[pltpu.VMEM((size.wide, HEAD_DIM), F32), pltpu.VMEM((TILE, HEAD_DIM), F32)],
        compiler_params=LIMIT,
    )(hbm(new_query), hbm(new_kv))


def row_copies(size, k, parts, cache, mine, theirs, sems):
    sub = lax.axis_index("sub")
    row = size.source_row(k)
    rest = size.heads - size.mine
    copies = []
    for o, (out, first) in enumerate(((mine, sub * rest), (theirs, (1 - sub) * rest))):
        if o and not rest:
            break
        for p, which in enumerate(parts):
            for j in range(size.mine):
                lanes = pl.ds(pl.multiple_of((first + j) * HEAD_DIM, HEAD_DIM), HEAD_DIM)
                at = (p * size.mine + j) * size.span
                copies.append(pltpu.make_async_copy(
                    out.at[pl.ds(at, size.span)],
                    cache.at[row, which, :, lanes],
                    sems.at[o, p * size.mine + j],
                ))
    return copies


def rebuild_kernel(size, k, parts, store, chained, *refs):
    message, tables = refs[0], refs[0 if 0 in parts else 1]
    refs = refs[1 if 0 in parts else 2:]
    refs = refs[2 * chained:]
    cache, _, mine, theirs = refs[:4]
    sub = lax.axis_index("sub")
    rest = size.heads - size.mine
    side_at = size.side_at(parts if 0 in parts else (0,))
    side = tables[side_at:side_at + TILE, :].astype(F32)
    length = side[2 * size.heads:2 * size.heads + 1, :]
    base = sub * size.span
    copies = row_copies(size, k, parts, cache, mine, theirs, refs[4]) if store else []
    at_copy = 0
    for o, out in enumerate((theirs, mine)):
        first = (1 - sub) * rest if o == 0 else sub * rest
        other = sub == 0 if o == 0 else sub != 0
        for p, which in enumerate(parts):
            for j in range(size.mine):
                h = which * size.heads + j
                scale = jnp.where(other, side[h + rest:h + rest + 1, :], side[h:h + 1, :])
                table = pl.multiple_of(
                    size.anchor_at(which, parts) + (first + j) * size.rows, TILE
                )
                anchor = message[pl.ds(table, size.rows), :].astype(F32)
                source = (p * size.heads + first + j) * size.span
                to = (p * size.mine + j) * size.span
                for i in range(size.rows):
                    at = pl.multiple_of(source + i * size.repeat, TILE)
                    value = anchor[i:i + 1, :] + scale * message[pl.ds(at, size.repeat), :].astype(F32)
                    keep = (base + i * size.repeat).astype(F32) < length
                    value = jnp.where(keep, value, jnp.float32(0.0)).astype(BF)
                    out[to + i * size.repeat:to + (i + 1) * size.repeat, :] = value
    for copy in copies:
        copy.start()
    for copy in copies:
        copy.wait()


def rebuild(size, k, parts, message, tables, state, store=True):
    args = [vmem(message)] + ([vmem(tables)] if tables is not None else [])
    in_specs = [IN_VMEM] * len(args)
    aliases = {}
    if state is not None:
        aliases = {len(args): 0, len(args) + 1: 1}
        args += list(state)
        in_specs += [IN_HBM, IN_HBM]
    given = (len(parts) * size.mine * size.span, HEAD_DIM)
    scratch = [pltpu.SemaphoreType.DMA((2, len(parts) * size.mine))] if store else []
    out = pl.pallas_call(
        functools.partial(rebuild_kernel, size, k, parts, store, state is not None),
        in_specs=in_specs,
        out_specs=[IN_HBM, IN_HBM, IN_VMEM, IN_VMEM],
        out_shape=[
            pltpu.HBM((size.count, 2, size.span, size.channels), BF),
            pltpu.HBM((size.count, size.steps, size.q_local * HEAD_DIM), BF),
            pltpu.VMEM(given, BF),
            pltpu.VMEM(given, BF),
        ],
        scratch_shapes=scratch,
        input_output_aliases=aliases,
        compiler_params=LIMIT,
        cost_estimate=pl.CostEstimate(
            flops=4 * len(parts) * size.span * size.channels,
            bytes_accessed=6 * len(parts) * size.span * size.channels,
            transcendentals=0,
        ),
    )(*args)
    return tuple(out[:2]), out[2], out[3]


def weigh(size, j, q, new_key, key_mine, key_other, live_mine, live_other, causal):
    factor = 1.0 / math.sqrt(HEAD_DIM)
    s0 = lax.dot_general(q, key_mine, NT, preferred_element_type=F32) * factor
    s1 = lax.dot_general(q, key_other, NT, preferred_element_type=F32) * factor
    s2 = lax.dot_general(q, new_key, NT, preferred_element_type=F32) * factor
    s0 = jnp.where(live_mine, s0, jnp.float32(LOW))
    s1 = jnp.where(live_other, s1, jnp.float32(LOW))
    s2 = jnp.where(causal, s2, jnp.float32(LOW))
    top = jnp.maximum(
        jnp.max(jnp.maximum(s0, s1), axis=1, keepdims=True), jnp.max(s2, axis=1, keepdims=True)
    )
    w0 = jnp.where(live_mine, jnp.exp(s0 - top), jnp.float32(0.0))
    w1 = jnp.where(live_other, jnp.exp(s1 - top), jnp.float32(0.0))
    w2 = jnp.where(causal, jnp.exp(s2 - top), jnp.float32(0.0))
    total = jnp.sum(w0 + w1, axis=1, keepdims=True) + jnp.sum(w2, axis=1, keepdims=True)
    return w0.astype(BF), w1.astype(BF), w2.astype(BF), total


def masks(size, tables, parts, fresh):
    sub = lax.axis_index("sub")
    at = size.side_at(parts)
    side = tables[at:at + TILE, :].astype(F32)
    length = side[2 * size.heads:2 * size.heads + 1, 0:1]
    spot = lax.broadcasted_iota(jnp.int32, (1, size.span), 1)
    live_mine = (spot + sub * size.span).astype(F32) < length
    live_other = (spot + (1 - sub) * size.span).astype(F32) < length
    step = lax.broadcasted_iota(jnp.int32, (size.wide, fresh), 0) % PAD_STEPS
    token = lax.broadcasted_iota(jnp.int32, (size.wide, fresh), 1)
    return live_mine, live_other, (token <= step) & (token < size.steps)


def place_heads(size, made, j, result):
    for g in range(size.group):
        at = (j * size.group + g) * HEAD_DIM
        made[:, at:at + HEAD_DIM] = result[g * PAD_STEPS:g * PAD_STEPS + size.steps, :]


def attend_kernel(size, k, parts, query, new_kv, tables, mine, other, *refs):
    _, attended, made, sem = refs[2:]
    row = size.source_row(k)
    live_mine, live_other, causal = masks(size, tables, parts, new_kv.shape[3])
    for j in range(size.mine):
        keys = slice(j * size.span, (j + 1) * size.span)
        values = slice((size.mine + j) * size.span, (size.mine + j + 1) * size.span)
        w0, w1, w2, total = weigh(
            size, j, query[row, j], new_kv[row, 0, j], mine[keys, :], other[keys, :],
            live_mine, live_other, causal,
        )
        acc = jnp.dot(w0, mine[values, :], preferred_element_type=F32)
        acc = acc + jnp.dot(w1, other[values, :], preferred_element_type=F32)
        acc = acc + jnp.dot(w2, new_kv[row, 1, j], preferred_element_type=F32)
        place_heads(size, made, j, (acc / total).astype(BF))
    copy = pltpu.make_async_copy(made, attended.at[row], sem)
    copy.start()
    copy.wait()


def weights_kernel(size, k, parts, query, new_kv, tables, mine, other, *refs):
    weights, share, totals = refs[4:]
    row = size.source_row(k)
    live_mine, live_other, causal = masks(size, tables, parts, new_kv.shape[3])
    for j in range(size.mine):
        keys = slice(j * size.span, (j + 1) * size.span)
        w0, w1, w2, total = weigh(
            size, j, query[row, j], new_kv[row, 0, j], mine[keys, :], other[keys, :],
            live_mine, live_other, causal,
        )
        weights[j, :, :size.span] = w0
        weights[j, :, size.span:] = w1
        share[j] = jnp.dot(w2, new_kv[row, 1, j], preferred_element_type=F32)
        totals[j] = jnp.broadcast_to(total, totals.shape[1:])


def finish_kernel(size, k, parts, weights, share, totals, mine, other, theirs, *refs):
    cache, attended, made, sem, sems = refs[2:]
    row = size.source_row(k)
    copies = row_copies(size, k, parts, cache, mine, theirs, sems)
    for copy in copies:
        copy.start()
    for j in range(size.mine):
        values = slice(j * size.span, (j + 1) * size.span)
        acc = jnp.dot(weights[j, :, :size.span], mine[values, :], preferred_element_type=F32)
        acc = acc + jnp.dot(weights[j, :, size.span:], other[values, :], preferred_element_type=F32)
        place_heads(size, made, j, ((acc + share[j]) / totals[j]).astype(BF))
    copy = pltpu.make_async_copy(made, attended.at[row], sem)
    copy.start()
    for each in copies:
        each.wait()
    copy.wait()


def chained_call(size, kernel, args, state, shapes, scratch, flops):
    args = [vmem(x) for x in args]
    many = len(args)
    out = pl.pallas_call(
        kernel,
        in_specs=[IN_VMEM] * many + [IN_HBM, IN_HBM],
        out_specs=[IN_HBM, IN_HBM] + [IN_VMEM] * len(shapes),
        out_shape=[pltpu.HBM(x.shape, x.dtype) for x in state] + shapes,
        scratch_shapes=scratch,
        input_output_aliases={many: 0, many + 1: 1},
        compiler_params=LIMIT,
        cost_estimate=pl.CostEstimate(
            flops=flops,
            bytes_accessed=8 * size.span * size.channels,
            transcendentals=2 * size.mine * size.wide * size.span,
        ),
    )(*args, *state)
    return tuple(out[:2]), out[2:]


def body(deltas, anchors, chan_scale, lengths, route, new_query, new_kv):
    n = lax.axis_size("pool")
    size = Sizes(deltas, anchors, new_query, n)
    both, last = (0, 1), n - 1
    plan = [(k, both) for k in range(1, last)] + [(last, (0,)), (last, (1,)), (0, both)]
    query, fresh = arrange(size, new_query, new_kv)
    message = {}
    for part in (plan[:1], plan[1:]):
        for (k, parts), msg in zip(part, pack(size, part, route, lengths, deltas, anchors, chan_scale)):
            if k:
                msg = lax.ppermute(msg, "pool", list(enumerate(far(n, k))))
            message[k, parts] = msg

    def swapped(x):
        return lax.ppermute(x, "sub", [(0, 1), (1, 0)])

    flops = 8 * size.mine * size.wide * size.span * HEAD_DIM
    result = pltpu.VMEM((size.steps, size.q_local * HEAD_DIM), BF)
    one = pltpu.SemaphoreType.DMA

    def attend(k, mine, other, state):
        state, _ = chained_call(
            size, functools.partial(attend_kernel, size, k, both),
            (query, fresh, message[k, both], mine, other), state, [], [result, one], flops,
        )
        return state

    def take(k, parts, state, store=True):
        tables = None if 0 in parts else message[last, (0,)]
        state, mine, theirs = rebuild(size, k, parts, message[k, parts], tables, state, store)
        return state, mine, theirs, swapped(theirs)

    state, held = None, []
    for k in range(last):
        state, mine, _, other = take(k, both, state)
        held.append((k, mine, other))
        if 0 < k < last - 1:
            state = attend(*held.pop(0), state)
    state, mine, _, other = take(last, (0,), state)
    for each in held:
        state = attend(*each, state)
    state, (weights, share, totals) = chained_call(
        size, functools.partial(weights_kernel, size, last, (0,)),
        (query, fresh, message[last, (0,)], mine, other), state,
        [
            pltpu.VMEM((size.mine, size.wide, 2 * size.span), BF),
            pltpu.VMEM((size.mine, size.wide, HEAD_DIM), F32),
            pltpu.VMEM((size.mine, size.wide, HEAD_DIM), F32),
        ],
        [], flops // 2,
    )
    state, mine, theirs, other = take(last, (1,), state, store=False)
    state, _ = chained_call(
        size, functools.partial(finish_kernel, size, last, (1,)),
        (weights, share, totals, mine, other, theirs), state, [],
        [result, one, pltpu.SemaphoreType.DMA((2, size.mine))], flops // 2,
    )
    return state


def solution(mesh):
    placed = (
        P(("parts", "pool"), None, "sub", "tp"),
        P(("parts", "pool"), None, "sub", "tp"),
        P(("parts", "pool"), None, "tp"),
        P(("parts", "pool")),
        P(("parts", "pool")),
        P(("parts", "pool"), None, ("tp", "sub")),
        P(("parts", "pool"), None, None, "tp"),
    )
    return jax.shard_map(
        body,
        mesh=mesh,
        in_specs=placed,
        out_specs=(
            P(("parts", "pool"), None, "sub", "tp"),
            P(("parts", "pool"), None, ("tp", "sub")),
        ),
        check_vma=False,
    )
```

```python
import functools
import math

import jax
import jax.numpy as jnp
from jax import lax
from jax.experimental import pallas as pl
from jax.experimental.pallas import tpu as pltpu
from jax.sharding import PartitionSpec as P

HEAD_DIM = 128
Q_PER_KV = 8
TILE = 16
PAGE = 128
PAD_STEPS = 8
BF = jnp.bfloat16
F32 = jnp.float32
LOW = -1e30
NT = (((1,), (1,)), ((), ()))

IN_VMEM = pl.BlockSpec(memory_space=pltpu.VMEM)
IN_SMEM = pl.BlockSpec(memory_space=pltpu.SMEM)
IN_HBM = pl.BlockSpec(memory_space=pltpu.HBM)
LIMIT = pltpu.CompilerParams(vmem_limit_bytes=16 * 1024 * 1024)


def vmem(x):
    return pltpu.with_memory_space_constraint(x, pltpu.VMEM)


def hbm(x):
    return pltpu.with_memory_space_constraint(x, pltpu.HBM)


def pick(values, at):
    out = jnp.int32(values[0])
    for i, value in enumerate(values[1:], 1):
        out = jnp.where(at == i, jnp.int32(value), out)
    return out


class Sizes:
    def __init__(self, deltas, anchors, new_query, n):
        self.n = n
        self.count, _, self.span, self.channels = deltas.shape
        self.rows = anchors.shape[2]
        self.repeat = self.span // self.rows
        self.steps = new_query.shape[1]
        self.heads = self.channels // HEAD_DIM
        self.q_local = new_query.shape[2] // HEAD_DIM
        self.mine = max(1, self.q_local // Q_PER_KV)
        self.rest = self.heads - self.mine
        self.group = self.q_local // self.mine
        self.wide = self.group * PAD_STEPS
        self.pages = self.span // PAGE
        self.page_rows = PAGE // self.repeat

    def anchor_at(self, which, parts):
        return (len(parts) * self.span + parts.index(which) * self.rows) * self.heads

    def side_at(self, parts):
        return len(parts) * self.heads * (self.span + self.rows)

    def message_rows(self, parts):
        return self.side_at(parts) + (TILE if 0 in parts else 0)

    def page_anchor_at(self):
        return 2 * self.heads * PAGE

    def page_side_at(self):
        return 2 * self.heads * (PAGE + self.page_rows)

    def page_message_rows(self):
        return self.page_side_at() + TILE

    def partner(self, k):
        return lax.axis_index("pool") ^ k


def request_for(size, k, route):
    index = jnp.int32(0)
    for j in range(size.count):
        index = jnp.where(route[j] == size.partner(k), jnp.int32(j), index)
    return index


def levels_kernel(size, *refs):
    many = size.n - 1
    sub = lax.axis_index("sub")
    for sent, got, out in zip(refs[:many], refs[many:2 * many], refs[2 * many:]):
        longer = jnp.max(jnp.maximum(sent[...], got[...]))
        pages = (longer + (PAGE - 1)) // PAGE - size.pages
        out[0] = jnp.where(sub == 0, 0, jnp.clip(pages, 0, size.pages))


def levels_of(size, sent, got):
    many = size.n - 1
    out = pl.pallas_call(
        functools.partial(levels_kernel, size),
        in_specs=[IN_VMEM] * (2 * many),
        out_specs=[IN_SMEM] * many,
        out_shape=[jax.ShapeDtypeStruct((1,), jnp.int32)] * many,
        compiler_params=LIMIT,
    )(*[vmem(x) for x in (*sent, *got)])
    return [x.reshape(()) for x in out]


def side_block(size, scale):
    row = lax.broadcasted_iota(jnp.int32, (TILE, HEAD_DIM), 0)
    scale = scale.astype(F32)
    out = jnp.zeros((TILE, HEAD_DIM), F32)
    for which in range(2):
        for h in range(size.heads):
            piece = scale[which:which + 1, h * HEAD_DIM:(h + 1) * HEAD_DIM]
            out = jnp.where(row == which * size.heads + h, piece, out)
    return out.astype(BF)


def pack_kernel(size, plan, first, route, lengths, deltas, anchors, scale, *rest):
    outs, (held, tables, block, sems) = rest[:-4], rest[-4:]
    sub = lax.axis_index("sub")
    work, slot = [], 0
    for k, layout in plan:
        index = request_for(size, k, route)
        copies = []
        for which in range(2):
            for source, target, s in ((deltas, held, 0), (anchors, tables, 1)):
                copy = pltpu.make_async_copy(
                    source.at[index, which], target.at[slot + which], sems.at[s, slot + which]
                )
                copy.start()
                copies.append(copy)
        whole, outs = outs[:len(layout)], outs[len(layout):]
        pages, outs = (outs[:size.pages], outs[size.pages:]) if k else ((), outs)
        work.append((k, layout, slot, index, copies, whole, pages))
        slot += 2
    if first:
        for k, out in enumerate(outs):
            out[...] = jnp.full(out.shape, lengths[request_for(size, k, route)], jnp.int32)
    for k, layout, slot, index, copies, whole, pages in work:
        side = side_block(size, scale[index])
        for copy in copies:
            copy.wait()

        def fill_whole(layout=layout, slot=slot, side=side, whole=whole):
            for parts, msg in zip(layout, whole):
                for which in parts:
                    for h in range(size.heads):
                        lanes = slice(h * HEAD_DIM, (h + 1) * HEAD_DIM)
                        at = (parts.index(which) * size.heads + h) * size.span
                        msg[at:at + size.span, :] = held[slot + which, :, lanes]
                        at = size.anchor_at(which, parts) + h * size.rows
                        msg[at:at + size.rows, :] = tables[slot + which, :, lanes]
                if 0 in parts:
                    msg[size.side_at(parts):size.side_at(parts) + TILE, :] = side

        def fill_pages(slot=slot, side=side, pages=pages):
            for page, msg in enumerate(pages):
                for which in range(2):
                    table = tables[slot + which].astype(F32)
                    for h in range(size.heads):
                        lanes = slice(h * HEAD_DIM, (h + 1) * HEAD_DIM)
                        at = (which * size.heads + h) * PAGE
                        msg[at:at + PAGE, :] = held[slot + which, page * PAGE:(page + 1) * PAGE, lanes]
                        at = (which * size.heads + h) * size.page_rows
                        first = page * size.page_rows
                        block[at:at + size.page_rows, :] = table[first:first + size.page_rows, lanes]
                msg[size.page_anchor_at():size.page_side_at(), :] = block[...].astype(BF)
                msg[size.page_side_at():size.page_side_at() + TILE, :] = side

        if k:
            pl.when(sub == 0)(fill_whole)
            pl.when(sub != 0)(fill_pages)
        else:
            fill_whole()


def pack(size, plan, first, route, lengths, deltas, anchors, scale):
    shapes = []
    for k, layout in plan:
        shapes += [pltpu.VMEM((size.message_rows(parts), HEAD_DIM), BF) for parts in layout]
        if k:
            shapes += [pltpu.VMEM((size.page_message_rows(), HEAD_DIM), BF)] * size.pages
    if first:
        shapes += [pltpu.VMEM((8, HEAD_DIM), jnp.int32)] * size.n
    slots = 2 * len(plan)
    outs = pl.pallas_call(
        functools.partial(pack_kernel, size, plan, first),
        out_shape=shapes,
        in_specs=[IN_SMEM, IN_SMEM, IN_HBM, IN_HBM, IN_VMEM],
        out_specs=[IN_VMEM] * len(shapes),
        scratch_shapes=[
            pltpu.VMEM((slots, size.span, size.channels), BF),
            pltpu.VMEM((slots, size.rows, size.channels), BF),
            pltpu.VMEM((2 * size.heads * size.page_rows, HEAD_DIM), F32),
            pltpu.SemaphoreType.DMA((2, slots)),
        ],
        compiler_params=LIMIT,
        cost_estimate=pl.CostEstimate(
            flops=0, bytes_accessed=2 * slots * size.span * size.channels, transcendentals=0
        ),
    )(hbm(route), hbm(lengths), hbm(deltas), hbm(anchors), hbm(scale))
    whole, paged = {}, {}
    for k, layout in plan:
        whole[k], outs = dict(zip(layout, outs[:len(layout)])), outs[len(layout):]
        if k:
            paged[k], outs = outs[:size.pages], outs[size.pages:]
    return whole, paged, outs


def arrange_kernel(size, new_query, new_kv, query, fresh, wide, tall):
    sub = lax.axis_index("sub")
    rest = size.heads - size.mine
    wide[...] = jnp.zeros_like(wide)
    tall[...] = jnp.zeros_like(tall)
    for r in range(size.count):
        for j in range(size.mine):
            for g in range(size.group):
                at = (j * size.group + g) * HEAD_DIM
                piece = new_query[r, :, at:at + HEAD_DIM].astype(F32)
                wide[g * PAD_STEPS:g * PAD_STEPS + size.steps, :] = piece
            query[r, j] = wide[...].astype(BF)
            for which in range(2):
                own, other = (
                    new_kv[r, which, :, h * HEAD_DIM:(h + 1) * HEAD_DIM].astype(F32) for h in (j, j + rest)
                )
                tall[:size.steps, :] = jnp.where(sub == 0, own, other)
                fresh[r, which, j] = tall[...].astype(BF)


def arrange(size, new_query, new_kv):
    return pl.pallas_call(
        functools.partial(arrange_kernel, size),
        in_specs=[IN_VMEM, IN_VMEM],
        out_specs=[IN_VMEM, IN_VMEM],
        out_shape=[
            pltpu.VMEM((size.count, size.mine, size.wide, HEAD_DIM), BF),
            pltpu.VMEM((size.count, 2, size.mine, TILE, HEAD_DIM), BF),
        ],
        scratch_shapes=[pltpu.VMEM((size.wide, HEAD_DIM), F32), pltpu.VMEM((TILE, HEAD_DIM), F32)],
        compiler_params=LIMIT,
    )(hbm(new_query), hbm(new_kv))


def row_copies(size, k, parts, cache, mine, theirs, sems):
    sub = lax.axis_index("sub")
    row = size.partner(k)
    copies = []
    for o, (out, first) in enumerate(((mine, sub * size.rest), (theirs, (1 - sub) * size.rest))):
        if o and not size.rest:
            break
        for p, which in enumerate(parts):
            for j in range(size.mine):
                lanes = pl.ds(pl.multiple_of((first + j) * HEAD_DIM, HEAD_DIM), HEAD_DIM)
                at = (p * size.mine + j) * size.span
                copies.append(pltpu.make_async_copy(
                    out.at[pl.ds(at, size.span)],
                    cache.at[row, which, :, lanes],
                    sems.at[o, p * size.mine + j],
                ))
    return copies


def rebuild_kernel(size, k, parts, store, chained, extra, length, *refs):
    message, tables = refs[0], refs[0 if 0 in parts else 1]
    refs = refs[1 if 0 in parts else 2:]
    pages, refs = (refs[:size.pages], refs[size.pages:]) if k else ((), refs)
    refs = refs[extra + 2 * chained:]
    cache, _, mine, theirs = refs[:4]
    sub = lax.axis_index("sub")
    copies = row_copies(size, k, parts, cache, mine, theirs, refs[4]) if store else []
    limit = length[0:1, :]

    def fill(upper, paged):
        if paged:
            at = size.page_side_at()
            side = pages[0][at:at + TILE, :].astype(F32)
            blocks = [x[size.page_anchor_at():at, :].astype(F32) for x in pages]
        else:
            at = size.side_at(parts if 0 in parts else (0,))
            side = tables[at:at + TILE, :].astype(F32)
        for o, out in enumerate((theirs, mine)):
            first = size.rest if (o == 0) != upper else 0
            for p, which in enumerate(parts):
                for j in range(size.mine):
                    h = first + j
                    scale = side[which * size.heads + h:which * size.heads + h + 1, :]
                    to = (p * size.mine + j) * size.span
                    if not paged:
                        at = size.anchor_at(which, parts) + h * size.rows
                        table = message[at:at + size.rows, :].astype(F32)
                    for i in range(size.rows):
                        if paged:
                            page, r = divmod(i, size.page_rows)
                            at = (which * size.heads + h) * size.page_rows + r
                            anchor = blocks[page][at:at + 1, :]
                            at = (which * size.heads + h) * PAGE + r * size.repeat
                            delta = pages[page][at:at + size.repeat, :]
                        else:
                            anchor = table[i:i + 1, :]
                            at = (p * size.heads + h) * size.span + i * size.repeat
                            delta = message[at:at + size.repeat, :]
                        value = anchor + scale * delta.astype(F32)
                        keep = (int(upper) * size.span + i * size.repeat) < limit
                        value = jnp.where(keep, value, jnp.float32(0.0)).astype(BF)
                        out[to + i * size.repeat:to + (i + 1) * size.repeat, :] = value

    pl.when(sub == 0)(functools.partial(fill, False, False))
    pl.when(sub != 0)(functools.partial(fill, True, k != 0))
    for copy in copies:
        copy.start()
    for copy in copies:
        copy.wait()


def rebuild(size, k, parts, length, message, tables, pages, after, state, store=True):
    args = [vmem(x) for x in (length, message, *([] if tables is None else [tables]), *pages)]
    in_specs = [IN_VMEM] * len(args) + [pl.BlockSpec(memory_space=pl.ANY)] * len(after)
    args += list(after)
    aliases = {}
    if state is not None:
        aliases = {len(args): 0, len(args) + 1: 1}
        args += list(state)
        in_specs += [IN_HBM, IN_HBM]
    given = (len(parts) * size.mine * size.span, HEAD_DIM)
    scratch = [pltpu.SemaphoreType.DMA((2, len(parts) * size.mine))] if store else []
    out = pl.pallas_call(
        functools.partial(rebuild_kernel, size, k, parts, store, state is not None, len(after)),
        in_specs=in_specs,
        out_specs=[IN_HBM, IN_HBM, IN_VMEM, IN_VMEM],
        out_shape=[
            pltpu.HBM((size.count, 2, size.span, size.channels), BF),
            pltpu.HBM((size.count, size.steps, size.q_local * HEAD_DIM), BF),
            pltpu.VMEM(given, BF),
            pltpu.VMEM(given, BF),
        ],
        scratch_shapes=scratch,
        input_output_aliases=aliases,
        compiler_params=LIMIT,
        cost_estimate=pl.CostEstimate(
            flops=4 * len(parts) * size.span * size.channels,
            bytes_accessed=6 * len(parts) * size.span * size.channels,
            transcendentals=0,
        ),
    )(*args)
    return tuple(out[:2]), out[2], out[3]


def weigh(size, j, q, new_key, key_mine, key_other, live_mine, live_other, causal):
    factor = 1.0 / math.sqrt(HEAD_DIM)
    s0 = lax.dot_general(q, key_mine, NT, preferred_element_type=F32) * factor
    s1 = lax.dot_general(q, key_other, NT, preferred_element_type=F32) * factor
    s2 = lax.dot_general(q, new_key, NT, preferred_element_type=F32) * factor
    s0 = jnp.where(live_mine, s0, jnp.float32(LOW))
    s1 = jnp.where(live_other, s1, jnp.float32(LOW))
    s2 = jnp.where(causal, s2, jnp.float32(LOW))
    top = jnp.maximum(
        jnp.max(jnp.maximum(s0, s1), axis=1, keepdims=True), jnp.max(s2, axis=1, keepdims=True)
    )
    w0 = jnp.where(live_mine, jnp.exp(s0 - top), jnp.float32(0.0))
    w1 = jnp.where(live_other, jnp.exp(s1 - top), jnp.float32(0.0))
    w2 = jnp.where(causal, jnp.exp(s2 - top), jnp.float32(0.0))
    total = jnp.sum(w0 + w1, axis=1, keepdims=True) + jnp.sum(w2, axis=1, keepdims=True)
    return w0.astype(BF), w1.astype(BF), w2.astype(BF), total


def masks(size, length, fresh):
    sub = lax.axis_index("sub")
    limit = length[0:1, 0:1]
    spot = lax.broadcasted_iota(jnp.int32, (1, size.span), 1)
    live_mine = spot + sub * size.span < limit
    live_other = spot + (1 - sub) * size.span < limit
    step = lax.broadcasted_iota(jnp.int32, (size.wide, fresh), 0) % PAD_STEPS
    token = lax.broadcasted_iota(jnp.int32, (size.wide, fresh), 1)
    return live_mine, live_other, (token <= step) & (token < size.steps)


def place_heads(size, made, j, result):
    for g in range(size.group):
        at = (j * size.group + g) * HEAD_DIM
        made[:, at:at + HEAD_DIM] = result[g * PAD_STEPS:g * PAD_STEPS + size.steps, :]


def attend_kernel(size, k, query, new_kv, length, mine, other, *refs):
    _, attended, made, sem = refs[2:]
    row = size.partner(k)
    live_mine, live_other, causal = masks(size, length, new_kv.shape[3])
    for j in range(size.mine):
        keys = slice(j * size.span, (j + 1) * size.span)
        values = slice((size.mine + j) * size.span, (size.mine + j + 1) * size.span)
        w0, w1, w2, total = weigh(
            size, j, query[row, j], new_kv[row, 0, j], mine[keys, :], other[keys, :],
            live_mine, live_other, causal,
        )
        acc = jnp.dot(w0, mine[values, :], preferred_element_type=F32)
        acc = acc + jnp.dot(w1, other[values, :], preferred_element_type=F32)
        acc = acc + jnp.dot(w2, new_kv[row, 1, j], preferred_element_type=F32)
        place_heads(size, made, j, (acc / total).astype(BF))
    copy = pltpu.make_async_copy(made, attended.at[row], sem)
    copy.start()
    copy.wait()


def weights_kernel(size, k, query, new_kv, length, mine, other, *refs):
    weights, share, totals = refs[4:]
    row = size.partner(k)
    live_mine, live_other, causal = masks(size, length, new_kv.shape[3])
    for j in range(size.mine):
        keys = slice(j * size.span, (j + 1) * size.span)
        w0, w1, w2, total = weigh(
            size, j, query[row, j], new_kv[row, 0, j], mine[keys, :], other[keys, :],
            live_mine, live_other, causal,
        )
        weights[j, :, :size.span] = w0
        weights[j, :, size.span:] = w1
        share[j] = jnp.dot(w2, new_kv[row, 1, j], preferred_element_type=F32)
        totals[j] = jnp.broadcast_to(total, totals.shape[1:])


def finish_kernel(size, k, parts, weights, share, totals, mine, other, theirs, *refs):
    cache, attended, made, sem, sems = refs[2:]
    row = size.partner(k)
    copies = row_copies(size, k, parts, cache, mine, theirs, sems)
    for copy in copies:
        copy.start()
    for j in range(size.mine):
        values = slice(j * size.span, (j + 1) * size.span)
        acc = jnp.dot(weights[j, :, :size.span], mine[values, :], preferred_element_type=F32)
        acc = acc + jnp.dot(weights[j, :, size.span:], other[values, :], preferred_element_type=F32)
        place_heads(size, made, j, ((acc + share[j]) / totals[j]).astype(BF))
    copy = pltpu.make_async_copy(made, attended.at[row], sem)
    copy.start()
    for each in copies:
        each.wait()
    copy.wait()


def chained_call(size, kernel, args, state, shapes, scratch, flops):
    args = [vmem(x) for x in args]
    many = len(args)
    out = pl.pallas_call(
        kernel,
        in_specs=[IN_VMEM] * many + [IN_HBM, IN_HBM],
        out_specs=[IN_HBM, IN_HBM] + [IN_VMEM] * len(shapes),
        out_shape=[pltpu.HBM(x.shape, x.dtype) for x in state] + shapes,
        scratch_shapes=scratch,
        input_output_aliases={many: 0, many + 1: 1},
        compiler_params=LIMIT,
        cost_estimate=pl.CostEstimate(
            flops=flops,
            bytes_accessed=8 * size.span * size.channels,
            transcendentals=2 * size.mine * size.wide * size.span,
        ),
    )(*args, *state)
    return tuple(out[:2]), out[2:]


def body(deltas, anchors, chan_scale, lengths, route, new_query, new_kv):
    n = lax.axis_size("pool")
    size = Sizes(deltas, anchors, new_query, n)
    both = (0, 1)
    order = list(range(n - 2, 0, -1)) + [n - 1]
    last = order[-1]

    def across(x, k):
        return lax.ppermute(x, "pool", [(z, z ^ k) for z in range(n)])

    def lower(x, k):
        return lax.ppermute(x, ("pool", "sub"), [(2 * z, 2 * (z ^ k)) for z in range(n)])

    def upper(level, pages, k):
        def branch(many):
            return lambda *xs: tuple(across(x, k) if i < many else x for i, x in enumerate(xs))
        return lax.switch(level, [branch(many) for many in range(size.pages + 1)], *pages)

    plan = [(k, (both,)) for k in order + [0]]
    message, paged = {}, {}
    for first, part in ((True, plan[:1]), (False, plan[1:])):
        whole, pages, extra = pack(size, part, first, route, lengths, deltas, anchors, chan_scale)
        if first:
            sent, length = extra, [extra[0]] + [across(extra[k], k) for k in range(1, n)]
        paged.update(pages)
        for k, layout in part:
            for parts in layout:
                message[k, parts] = lower(whole[k][parts], k) if k else whole[k][parts]
    query, fresh = arrange(size, new_query, new_kv)
    levels = levels_of(size, sent[1:], length[1:])
    pages = {0: ()}
    for k in sorted(order, reverse=True):
        pages[k] = upper(levels[k - 1], paged[k], k)

    def swapped(x):
        return lax.ppermute(x, "sub", [(0, 1), (1, 0)])

    flops = 8 * size.mine * size.wide * size.span * HEAD_DIM
    result = pltpu.VMEM((size.steps, size.q_local * HEAD_DIM), BF)
    one = pltpu.SemaphoreType.DMA

    def attend(k, mine, other, state):
        state, _ = chained_call(
            size, functools.partial(attend_kernel, size, k),
            (query, fresh, length[k], mine, other), state, [], [result, one], flops,
        )
        return state

    def take(k, parts, state, after=(), store=True):
        tables = None if 0 in parts else message[k, (0,)]
        state, mine, theirs = rebuild(
            size, k, parts, length[k], message[k, parts], tables, pages[k], after, state, store
        )
        return state, mine, theirs, swapped(theirs)

    state, held = None, []
    for k in [0] + order:
        after = [x for j in order if j != k for x in pages[j][:1]] if k == order[0] else ()
        state, mine, _, other = take(k, both, state, after)
        held.append((k, mine, other))
        if k and k != last:
            state = attend(*held.pop(0), state)
    for each in held:
        state = attend(*each, state)
    return state


def solution(mesh):
    placed = (
        P(("parts", "pool"), None, "sub", "tp"),
        P(("parts", "pool"), None, "sub", "tp"),
        P(("parts", "pool"), None, "tp"),
        P(("parts", "pool")),
        P(("parts", "pool")),
        P(("parts", "pool"), None, ("tp", "sub")),
        P(("parts", "pool"), None, None, "tp"),
    )
    return jax.shard_map(
        body,
        mesh=mesh,
        in_specs=placed,
        out_specs=(
            P(("parts", "pool"), None, "sub", "tp"),
            P(("parts", "pool"), None, ("tp", "sub")),
        ),
        check_vma=False,
    )
```

```python
import functools
import math

import jax
import jax.numpy as jnp
from jax import lax
from jax.experimental import pallas as pl
from jax.experimental.pallas import tpu as pltpu
from jax.sharding import PartitionSpec as P

HEAD_DIM = 128
Q_PER_KV = 8
TILE = 16
PAGE = 128
BF = jnp.bfloat16
F32 = jnp.float32
LOW = -1e30
NT = (((1,), (1,)), ((), ()))

IN_VMEM = pl.BlockSpec(memory_space=pltpu.VMEM)
IN_SMEM = pl.BlockSpec(memory_space=pltpu.SMEM)
IN_HBM = pl.BlockSpec(memory_space=pltpu.HBM)
LIMIT = pltpu.CompilerParams(vmem_limit_bytes=16 * 1024 * 1024)


def vmem(x):
    return pltpu.with_memory_space_constraint(x, pltpu.VMEM)


def hbm(x):
    return pltpu.with_memory_space_constraint(x, pltpu.HBM)


def pick(values, at):
    out = jnp.int32(values[0])
    for i, value in enumerate(values[1:], 1):
        out = jnp.where(at == i, jnp.int32(value), out)
    return out


class Sizes:
    def __init__(self, deltas, anchors, new_query, n):
        self.n = n
        self.count, _, self.span, self.channels = deltas.shape
        self.rows = anchors.shape[2]
        self.repeat = self.span // self.rows
        self.steps = new_query.shape[1]
        self.heads = self.channels // HEAD_DIM
        self.q_local = new_query.shape[2] // HEAD_DIM
        self.mine = max(1, self.q_local // Q_PER_KV)
        self.rest = self.heads - self.mine
        self.group = self.q_local // self.mine
        self.wide = self.group * self.steps
        self.pages = self.span // PAGE
        self.page_rows = PAGE // self.repeat

    def anchor_at(self, which, parts):
        return (len(parts) * self.span + parts.index(which) * self.rows) * self.heads

    def side_at(self, parts):
        return len(parts) * self.heads * (self.span + self.rows)

    def message_rows(self, parts):
        return self.side_at(parts) + (TILE if 0 in parts else 0)

    def page_anchor_at(self):
        return 2 * self.heads * PAGE

    def page_side_at(self):
        return 2 * self.heads * (PAGE + self.page_rows)

    def page_message_rows(self):
        return self.page_side_at() + TILE

    def partner(self, k):
        return lax.axis_index("pool") ^ k


def request_for(size, k, route):
    index = jnp.int32(0)
    for j in range(size.count):
        index = jnp.where(route[j] == size.partner(k), jnp.int32(j), index)
    return index


def lengths_kernel(size, route, lengths, *outs):
    for k, out in enumerate(outs):
        out[...] = jnp.full(out.shape, lengths[request_for(size, k, route)], jnp.int32)


def outgoing_lengths(size, route, lengths):
    return pl.pallas_call(
        functools.partial(lengths_kernel, size),
        in_specs=[IN_SMEM, IN_SMEM],
        out_specs=[IN_VMEM] * size.n,
        out_shape=[pltpu.VMEM((8, HEAD_DIM), jnp.int32)] * size.n,
        compiler_params=LIMIT,
    )(hbm(route), hbm(lengths))


def levels_kernel(size, *refs):
    many = size.n - 1
    sub = lax.axis_index("sub")
    for sent, got, out in zip(refs[:many], refs[many:2 * many], refs[2 * many + 1:3 * many + 1]):
        longer = jnp.max(jnp.maximum(sent[...], got[...]))
        pages = (longer + (PAGE - 1)) // PAGE - size.pages
        out[0] = jnp.where(sub == 0, 0, jnp.clip(pages, 0, size.pages))


def levels_of(size, sent, got, message):
    many = size.n - 1
    args = [vmem(x) for x in (*sent, *got, message)]
    out = pl.pallas_call(
        functools.partial(levels_kernel, size),
        in_specs=[IN_VMEM] * len(args),
        out_specs=[IN_SMEM] * many + [IN_VMEM],
        out_shape=[jax.ShapeDtypeStruct((1,), jnp.int32)] * many + [pltpu.VMEM(message.shape, BF)],
        input_output_aliases={2 * many: many},
        compiler_params=LIMIT,
    )(*args)
    return out[:many], out[many]


def side_block(size, scale):
    row = lax.broadcasted_iota(jnp.int32, (TILE, HEAD_DIM), 0)
    scale = scale.astype(F32)
    out = jnp.zeros((TILE, HEAD_DIM), F32)
    for which in range(2):
        for h in range(size.heads):
            piece = scale[which:which + 1, h * HEAD_DIM:(h + 1) * HEAD_DIM]
            out = jnp.where(row == which * size.heads + h, piece, out)
    return out.astype(BF)


def pack_kernel(size, plan, after, route, deltas, anchors, scale, *rest):
    outs, (held, tables, block, sems) = rest[after:-4], rest[-4:]
    sub = lax.axis_index("sub")
    work, slot = [], 0
    for k, layout in plan:
        index = request_for(size, k, route)
        copies = []
        for which in range(2):
            for source, target, s in ((deltas, held, 0), (anchors, tables, 1)):
                copy = pltpu.make_async_copy(
                    source.at[index, which], target.at[slot + which], sems.at[s, slot + which]
                )
                copy.start()
                copies.append(copy)
        whole, outs = outs[:len(layout)], outs[len(layout):]
        pages, outs = (outs[:size.pages], outs[size.pages:]) if k else ((), outs)
        work.append((k, layout, slot, index, copies, whole, pages))
        slot += 2
    for k, layout, slot, index, copies, whole, pages in work:
        side = side_block(size, scale[index])
        for copy in copies:
            copy.wait()

        def fill_whole(layout=layout, slot=slot, side=side, whole=whole):
            for parts, msg in zip(layout, whole):
                for which in parts:
                    for h in range(size.heads):
                        lanes = slice(h * HEAD_DIM, (h + 1) * HEAD_DIM)
                        at = (parts.index(which) * size.heads + h) * size.span
                        msg[at:at + size.span, :] = held[slot + which, :, lanes]
                        at = size.anchor_at(which, parts) + h * size.rows
                        msg[at:at + size.rows, :] = tables[slot + which, :, lanes]
                if 0 in parts:
                    msg[size.side_at(parts):size.side_at(parts) + TILE, :] = side

        def fill_pages(slot=slot, side=side, pages=pages):
            for page, msg in enumerate(pages):
                for which in range(2):
                    table = tables[slot + which].astype(F32)
                    for h in range(size.heads):
                        lanes = slice(h * HEAD_DIM, (h + 1) * HEAD_DIM)
                        at = (which * size.heads + h) * PAGE
                        msg[at:at + PAGE, :] = held[slot + which, page * PAGE:(page + 1) * PAGE, lanes]
                        at = (which * size.heads + h) * size.page_rows
                        first = page * size.page_rows
                        block[at:at + size.page_rows, :] = table[first:first + size.page_rows, lanes]
                msg[size.page_anchor_at():size.page_side_at(), :] = block[...].astype(BF)
                msg[size.page_side_at():size.page_side_at() + TILE, :] = side

        if k:
            pl.when(sub == 0)(fill_whole)
            pl.when(sub != 0)(fill_pages)
        else:
            fill_whole()


def pack(size, plan, after, route, deltas, anchors, scale):
    shapes = []
    for k, layout in plan:
        shapes += [pltpu.VMEM((size.message_rows(parts), HEAD_DIM), BF) for parts in layout]
        if k:
            shapes += [pltpu.VMEM((size.page_message_rows(), HEAD_DIM), BF)] * size.pages
    slots = 2 * len(plan)
    outs = pl.pallas_call(
        functools.partial(pack_kernel, size, plan, len(after)),
        out_shape=shapes,
        in_specs=[IN_SMEM, IN_HBM, IN_HBM, IN_VMEM] + [pl.BlockSpec(memory_space=pl.ANY)] * len(after),
        out_specs=[IN_VMEM] * len(shapes),
        scratch_shapes=[
            pltpu.VMEM((slots, size.span, size.channels), BF),
            pltpu.VMEM((slots, size.rows, size.channels), BF),
            pltpu.VMEM((2 * size.heads * size.page_rows, HEAD_DIM), F32),
            pltpu.SemaphoreType.DMA((2, slots)),
        ],
        compiler_params=LIMIT,
        cost_estimate=pl.CostEstimate(
            flops=0, bytes_accessed=2 * slots * size.span * size.channels, transcendentals=0
        ),
    )(hbm(route), hbm(deltas), hbm(anchors), hbm(scale), *after)
    whole, paged = {}, {}
    for k, layout in plan:
        whole[k], outs = dict(zip(layout, outs[:len(layout)])), outs[len(layout):]
        if k:
            paged[k], outs = outs[:size.pages], outs[size.pages:]
    return whole, paged


def arrange_kernel(size, new_query, new_kv, query, fresh, wide, tall):
    sub = lax.axis_index("sub")
    rest = size.heads - size.mine
    tall[...] = jnp.zeros_like(tall)
    for r in range(size.count):
        for j in range(size.mine):
            for g in range(size.group):
                at = (j * size.group + g) * HEAD_DIM
                piece = new_query[r, :, at:at + HEAD_DIM].astype(F32)
                wide[g * size.steps:(g + 1) * size.steps, :] = piece
            query[r, j] = wide[...].astype(BF)
            for which in range(2):
                own, other = (
                    new_kv[r, which, :, h * HEAD_DIM:(h + 1) * HEAD_DIM].astype(F32) for h in (j, j + rest)
                )
                tall[:size.steps, :] = jnp.where(sub == 0, own, other)
                fresh[r, which, j] = tall[...].astype(BF)


def arrange(size, new_query, new_kv):
    return pl.pallas_call(
        functools.partial(arrange_kernel, size),
        in_specs=[IN_VMEM, IN_VMEM],
        out_specs=[IN_VMEM, IN_VMEM],
        out_shape=[
            pltpu.VMEM((size.count, size.mine, size.wide, HEAD_DIM), BF),
            pltpu.VMEM((size.count, 2, size.mine, TILE, HEAD_DIM), BF),
        ],
        scratch_shapes=[pltpu.VMEM((size.wide, HEAD_DIM), F32), pltpu.VMEM((TILE, HEAD_DIM), F32)],
        compiler_params=LIMIT,
    )(hbm(new_query), hbm(new_kv))


def row_copies(size, k, parts, cache, mine, theirs, sems):
    sub = lax.axis_index("sub")
    row = size.partner(k)
    copies = []
    for o, (out, first) in enumerate(((mine, sub * size.rest), (theirs, (1 - sub) * size.rest))):
        if o and not size.rest:
            break
        for p, which in enumerate(parts):
            for j in range(size.mine):
                lanes = pl.ds(pl.multiple_of((first + j) * HEAD_DIM, HEAD_DIM), HEAD_DIM)
                at = (p * size.mine + j) * size.span
                copies.append(pltpu.make_async_copy(
                    out.at[pl.ds(at, size.span)],
                    cache.at[row, which, :, lanes],
                    sems.at[o, p * size.mine + j],
                ))
    return copies


def rebuild_kernel(size, k, parts, chained, extra, gated, length, *refs):
    message, tables = refs[0], refs[0 if 0 in parts else 1]
    refs = refs[1 if 0 in parts else 2:]
    pages, refs = (refs[:size.pages], refs[size.pages:]) if k else ((), refs)
    if gated:
        refs[-1][0] = refs[extra][0]
    refs = refs[extra + gated + 2 * chained:]
    _, _, mine, theirs = refs[:4]
    sub = lax.axis_index("sub")
    limit = length[0:1, :]

    def fill(upper, paged):
        if paged:
            at = size.page_side_at()
            side = pages[0][at:at + TILE, :].astype(F32)
            blocks = [x[size.page_anchor_at():at, :].astype(F32) for x in pages]
        else:
            at = size.side_at(parts if 0 in parts else (0,))
            side = tables[at:at + TILE, :].astype(F32)
        for o, out in enumerate((theirs, mine)):
            first = size.rest if (o == 0) != upper else 0
            for p, which in enumerate(parts):
                for j in range(size.mine):
                    h = first + j
                    scale = side[which * size.heads + h:which * size.heads + h + 1, :]
                    to = (p * size.mine + j) * size.span
                    if not paged:
                        at = size.anchor_at(which, parts) + h * size.rows
                        table = message[at:at + size.rows, :].astype(F32)
                    for i in range(size.rows):
                        if paged:
                            page, r = divmod(i, size.page_rows)
                            at = (which * size.heads + h) * size.page_rows + r
                            anchor = blocks[page][at:at + 1, :]
                            at = (which * size.heads + h) * PAGE + r * size.repeat
                            delta = pages[page][at:at + size.repeat, :]
                        else:
                            anchor = table[i:i + 1, :]
                            at = (p * size.heads + h) * size.span + i * size.repeat
                            delta = message[at:at + size.repeat, :]
                        value = anchor + scale * delta.astype(F32)
                        keep = (int(upper) * size.span + i * size.repeat) < limit
                        value = jnp.where(keep, value, jnp.float32(0.0)).astype(BF)
                        out[to + i * size.repeat:to + (i + 1) * size.repeat, :] = value

    pl.when(sub == 0)(functools.partial(fill, False, False))
    pl.when(sub != 0)(functools.partial(fill, True, k != 0))


def rebuild(size, k, parts, length, message, tables, pages, after, gate, state):
    args = [vmem(x) for x in (length, message, *([] if tables is None else [tables]), *pages)]
    in_specs = [IN_VMEM] * len(args) + [pl.BlockSpec(memory_space=pl.ANY)] * len(after)
    args += list(after) + list(gate)
    in_specs += [IN_SMEM] * len(gate)
    aliases = {}
    if state is not None:
        aliases = {len(args): 0, len(args) + 1: 1}
        args += list(state)
        in_specs += [IN_HBM, IN_HBM]
    given = (len(parts) * size.mine * size.span, HEAD_DIM)
    out = pl.pallas_call(
        functools.partial(rebuild_kernel, size, k, parts, state is not None, len(after), len(gate)),
        in_specs=in_specs,
        out_specs=[IN_HBM, IN_HBM, IN_VMEM, IN_VMEM] + [IN_SMEM] * len(gate),
        out_shape=[
            pltpu.HBM((size.count, 2, size.span, size.channels), BF),
            pltpu.HBM((size.count, size.steps, size.q_local * HEAD_DIM), BF),
            pltpu.VMEM(given, BF),
            pltpu.VMEM(given, BF),
        ] + [jax.ShapeDtypeStruct((1,), jnp.int32)] * len(gate),
        input_output_aliases=aliases,
        compiler_params=LIMIT,
        cost_estimate=pl.CostEstimate(
            flops=4 * len(parts) * size.span * size.channels,
            bytes_accessed=6 * len(parts) * size.span * size.channels,
            transcendentals=0,
        ),
    )(*args)
    return tuple(out[:2]), out[2], out[3], out[4:]


def weigh(size, j, q, new_key, key_mine, key_other, live_mine, live_other, causal):
    factor = 1.0 / math.sqrt(HEAD_DIM)
    s0 = lax.dot_general(q, key_mine, NT, preferred_element_type=F32) * factor
    s1 = lax.dot_general(q, key_other, NT, preferred_element_type=F32) * factor
    s2 = lax.dot_general(q, new_key, NT, preferred_element_type=F32) * factor
    s0 = jnp.where(live_mine, s0, jnp.float32(LOW))
    s1 = jnp.where(live_other, s1, jnp.float32(LOW))
    s2 = jnp.where(causal, s2, jnp.float32(LOW))
    top = jnp.maximum(
        jnp.max(jnp.maximum(s0, s1), axis=1, keepdims=True), jnp.max(s2, axis=1, keepdims=True)
    )
    w0 = jnp.where(live_mine, jnp.exp(s0 - top), jnp.float32(0.0))
    w1 = jnp.where(live_other, jnp.exp(s1 - top), jnp.float32(0.0))
    w2 = jnp.where(causal, jnp.exp(s2 - top), jnp.float32(0.0))
    total = jnp.sum(w0 + w1, axis=1, keepdims=True) + jnp.sum(w2, axis=1, keepdims=True)
    return w0.astype(BF), w1.astype(BF), w2.astype(BF), total


def masks(size, length, fresh):
    sub = lax.axis_index("sub")
    limit = length[0:1, 0:1]
    spot = lax.broadcasted_iota(jnp.int32, (1, size.span), 1)
    live_mine = spot + sub * size.span < limit
    live_other = spot + (1 - sub) * size.span < limit
    step = lax.broadcasted_iota(jnp.int32, (size.wide, fresh), 0) % size.steps
    token = lax.broadcasted_iota(jnp.int32, (size.wide, fresh), 1)
    return live_mine, live_other, (token <= step) & (token < size.steps)


def attend_kernel(size, k, query, new_kv, length, mine, other, theirs, *refs):
    cache, attended, made, flat, sem, sems = refs[2:]
    row = size.partner(k)
    copies = row_copies(size, k, (0, 1), cache, mine, theirs, sems)
    for copy in copies:
        copy.start()
    live_mine, live_other, causal = masks(size, length, new_kv.shape[3])
    for j in range(size.mine):
        keys = slice(j * size.span, (j + 1) * size.span)
        values = slice((size.mine + j) * size.span, (size.mine + j + 1) * size.span)
        w0, w1, w2, total = weigh(
            size, j, query[row, j], new_kv[row, 0, j], mine[keys, :], other[keys, :],
            live_mine, live_other, causal,
        )
        acc = jnp.dot(w0, mine[values, :], preferred_element_type=F32)
        acc = acc + jnp.dot(w1, other[values, :], preferred_element_type=F32)
        acc = acc + jnp.dot(w2, new_kv[row, 1, j], preferred_element_type=F32)
        flat[j] = acc / total
    for j in range(size.mine):
        for g in range(size.group):
            at = (j * size.group + g) * HEAD_DIM
            made[:, at:at + HEAD_DIM] = flat[j, g * size.steps:(g + 1) * size.steps, :].astype(BF)
    copy = pltpu.make_async_copy(made, attended.at[row], sem)
    copy.start()
    for each in copies:
        each.wait()
    copy.wait()


def chained_call(size, kernel, args, state, shapes, scratch, flops):
    args = [vmem(x) for x in args]
    many = len(args)
    out = pl.pallas_call(
        kernel,
        in_specs=[IN_VMEM] * many + [IN_HBM, IN_HBM],
        out_specs=[IN_HBM, IN_HBM] + [IN_VMEM] * len(shapes),
        out_shape=[pltpu.HBM(x.shape, x.dtype) for x in state] + shapes,
        scratch_shapes=scratch,
        input_output_aliases={many: 0, many + 1: 1},
        compiler_params=LIMIT,
        cost_estimate=pl.CostEstimate(
            flops=flops,
            bytes_accessed=8 * size.span * size.channels,
            transcendentals=2 * size.mine * size.wide * size.span,
        ),
    )(*args, *state)
    return tuple(out[:2]), out[2:]


def body(deltas, anchors, chan_scale, lengths, route, new_query, new_kv):
    n = lax.axis_size("pool")
    size = Sizes(deltas, anchors, new_query, n)
    both = (0, 1)
    order = list(range(n - 2, 0, -1)) + [n - 1]
    last = order[-1]

    def across(x, k):
        return lax.ppermute(x, "pool", [(z, z ^ k) for z in range(n)])

    def lower(x, k):
        return lax.ppermute(x, ("pool", "sub"), [(2 * z, 2 * (z ^ k)) for z in range(n)])

    def upper(level, pages, k):
        def branch(many):
            return lambda *xs: tuple(across(x, k) if i < many else x for i, x in enumerate(xs))
        return lax.switch(level.reshape(()), [branch(many) for many in range(size.pages + 1)], *pages)

    def swapped(x):
        return lax.ppermute(x, "sub", [(0, 1), (1, 0)])

    sent = outgoing_lengths(size, route, lengths)
    length = [sent[0]] + [across(sent[k], k) for k in range(1, n)]
    plan = [(k, (both,)) for k in order + [0]]
    whole, paged = pack(size, plan[:1], sent[:1], route, deltas, anchors, chan_scale)
    levels, whole[order[0]][both] = levels_of(size, sent[1:], length[1:], whole[order[0]][both])
    more, pages = pack(size, plan[1:], levels[:1], route, deltas, anchors, chan_scale)
    whole.update(more)
    paged.update(pages)
    message = {k: lower(whole[k][both], k) if k else whole[k][both] for k in order + [0]}
    query, fresh = arrange(size, new_query, new_kv)
    pages = {0: ()}

    flops = 8 * size.mine * size.wide * size.span * HEAD_DIM
    scratch = [
        pltpu.VMEM((size.steps, size.q_local * HEAD_DIM), BF),
        pltpu.VMEM((size.mine, size.wide, HEAD_DIM), F32),
        pltpu.SemaphoreType.DMA,
        pltpu.SemaphoreType.DMA((2, 2 * size.mine)),
    ]

    def take(k, state, after=(), gate=()):
        state, mine, theirs, gate = rebuild(
            size, k, both, length[k], message[k], None, pages[k], after, gate, state
        )
        return state, (k, mine, swapped(theirs), theirs), gate

    def attend(k, mine, other, theirs, state):
        state, _ = chained_call(
            size, functools.partial(attend_kernel, size, k),
            (query, fresh, length[k], mine, other, theirs), state, [], scratch, flops,
        )
        return state

    waiting = [k for k in order if k != 1]
    pages[1] = upper(levels[0], paged[1], 1)
    state, each, gate = take(0, None, pages[1][:1], [levels[waiting[0] - 1]])
    held = [each]
    for k in order:
        after = ()
        if waiting:
            j = waiting.pop(0)
            pages[j] = upper(gate[0], paged[j], j)
            after = pages[j][:1] if j != k else ()
        state = attend(*held.pop(0), state)
        state, each, gate = take(k, state, after, [levels[j - 1] for j in waiting[:1]])
        held.append(each)
    state = attend(*held.pop(0), state)
    return state


def solution(mesh):
    placed = (
        P(("parts", "pool"), None, "sub", "tp"),
        P(("parts", "pool"), None, "sub", "tp"),
        P(("parts", "pool"), None, "tp"),
        P(("parts", "pool")),
        P(("parts", "pool")),
        P(("parts", "pool"), None, ("tp", "sub")),
        P(("parts", "pool"), None, None, "tp"),
    )
    return jax.shard_map(
        body,
        mesh=mesh,
        in_specs=placed,
        out_specs=(
            P(("parts", "pool"), None, "sub", "tp"),
            P(("parts", "pool"), None, ("tp", "sub")),
        ),
        check_vma=False,
    )
```

```python
import functools
import math

import jax
import jax.numpy as jnp
from jax import lax
from jax.experimental import pallas as pl
from jax.experimental.pallas import tpu as pltpu
from jax.sharding import PartitionSpec as P

HEAD_DIM = 128
Q_PER_KV = 8
TILE = 16
BF = jnp.bfloat16
F32 = jnp.float32
LOW = -1e30
NT = (((1,), (1,)), ((), ()))

IN_VMEM = pl.BlockSpec(memory_space=pltpu.VMEM)
IN_SMEM = pl.BlockSpec(memory_space=pltpu.SMEM)
IN_HBM = pl.BlockSpec(memory_space=pltpu.HBM)
LIMIT = pltpu.CompilerParams(vmem_limit_bytes=16 * 1024 * 1024)


def vmem(x):
    return pltpu.with_memory_space_constraint(x, pltpu.VMEM)


def hbm(x):
    return pltpu.with_memory_space_constraint(x, pltpu.HBM)


def far(n, k):
    ring = (0, 2, 3, 1) if n == 4 else tuple(range(n))
    return tuple(ring[(ring.index(z) + k) % n] for z in range(n))


def pick(values, at):
    out = jnp.int32(values[0])
    for i, value in enumerate(values[1:], 1):
        out = jnp.where(at == i, jnp.int32(value), out)
    return out


class Sizes:
    def __init__(self, deltas, anchors, new_query, n):
        self.n = n
        self.count, _, self.span, self.channels = deltas.shape
        self.rows = anchors.shape[2]
        self.repeat = self.span // self.rows
        self.steps = new_query.shape[1]
        self.heads = self.channels // HEAD_DIM
        self.q_local = new_query.shape[2] // HEAD_DIM
        self.mine = max(1, self.q_local // Q_PER_KV)
        self.group = self.q_local // self.mine
        self.wide = self.group * self.steps

    def anchor_at(self, which, parts):
        return (len(parts) * self.span + parts.index(which) * self.rows) * self.heads

    def side_at(self, parts):
        return len(parts) * self.heads * (self.span + self.rows)

    def message_rows(self, parts):
        return self.side_at(parts) + (TILE if 0 in parts else 0)

    def source_row(self, k):
        return pick(far(self.n, self.n - k), lax.axis_index("pool"))


def side_block(size, scale, length):
    row = lax.broadcasted_iota(jnp.int32, (TILE, HEAD_DIM), 0)
    scale = scale.astype(F32)
    out = jnp.where(row == 2 * size.heads, length.astype(F32), jnp.float32(0.0))
    for which in range(2):
        for h in range(size.heads):
            piece = scale[which:which + 1, h * HEAD_DIM:(h + 1) * HEAD_DIM]
            out = jnp.where(row == which * size.heads + h, piece, out)
    return out.astype(BF)


def pack_kernel(size, plan, route, lengths, deltas, anchors, scale, *rest):
    outs, (held, tables, sems) = rest[:-3], rest[-3:]
    z = lax.axis_index("pool")
    work = []
    for m, (k, parts) in enumerate(plan):
        dest = pick(far(size.n, k), z)
        index = jnp.int32(0)
        for j in range(size.count):
            index = jnp.where(route[j] == dest, jnp.int32(j), index)
        for which in parts:
            slot = len(work)
            copies = (
                pltpu.make_async_copy(deltas.at[index, which], held.at[slot], sems.at[0, slot]),
                pltpu.make_async_copy(anchors.at[index, which], tables.at[slot], sems.at[1, slot]),
            )
            for copy in copies:
                copy.start()
            work.append((outs[m], parts, which, slot, copies))
        if 0 in parts:
            outs[m][pl.ds(size.side_at(parts), TILE), :] = side_block(size, scale[index], lengths[index])
    for msg, parts, which, slot, copies in work:
        for copy in copies:
            copy.wait()
        for h in range(size.heads):
            lanes = slice(h * HEAD_DIM, (h + 1) * HEAD_DIM)
            at = (parts.index(which) * size.heads + h) * size.span
            msg[at:at + size.span, :] = held[slot, :, lanes]
            at = size.anchor_at(which, parts) + h * size.rows
            msg[at:at + size.rows, :] = tables[slot, :, lanes]


def pack(size, plan, route, lengths, deltas, anchors, scale):
    shapes = [pltpu.VMEM((size.message_rows(parts), HEAD_DIM), BF) for _, parts in plan]
    slots = sum(len(parts) for _, parts in plan)
    return pl.pallas_call(
        functools.partial(pack_kernel, size, plan),
        out_shape=shapes,
        in_specs=[IN_SMEM, IN_SMEM, IN_HBM, IN_HBM, IN_VMEM],
        out_specs=[IN_VMEM] * len(shapes),
        scratch_shapes=[
            pltpu.VMEM((slots, size.span, size.channels), BF),
            pltpu.VMEM((slots, size.rows, size.channels), BF),
            pltpu.SemaphoreType.DMA((2, slots)),
        ],
        compiler_params=LIMIT,
        cost_estimate=pl.CostEstimate(
            flops=0, bytes_accessed=2 * slots * size.span * size.channels, transcendentals=0
        ),
    )(hbm(route), hbm(lengths), hbm(deltas), hbm(anchors), hbm(scale))


def arrange_kernel(size, new_query, new_kv, query, fresh, wide, tall):
    sub = lax.axis_index("sub")
    rest = size.heads - size.mine
    tall[...] = jnp.zeros_like(tall)
    for r in range(size.count):
        for j in range(size.mine):
            for g in range(size.group):
                at = (j * size.group + g) * HEAD_DIM
                piece = new_query[r, :, at:at + HEAD_DIM].astype(F32)
                wide[g * size.steps:(g + 1) * size.steps, :] = piece
            query[r, j] = wide[...].astype(BF)
            for which in range(2):
                own, other = (
                    new_kv[r, which, :, h * HEAD_DIM:(h + 1) * HEAD_DIM].astype(F32) for h in (j, j + rest)
                )
                tall[:size.steps, :] = jnp.where(sub == 0, own, other)
                fresh[r, which, j] = tall[...].astype(BF)


def arrange(size, new_query, new_kv):
    return pl.pallas_call(
        functools.partial(arrange_kernel, size),
        in_specs=[IN_VMEM, IN_VMEM],
        out_specs=[IN_VMEM, IN_VMEM],
        out_shape=[
            pltpu.VMEM((size.count, size.mine, size.wide, HEAD_DIM), BF),
            pltpu.VMEM((size.count, 2, size.mine, TILE, HEAD_DIM), BF),
        ],
        scratch_shapes=[pltpu.VMEM((size.wide, HEAD_DIM), F32), pltpu.VMEM((TILE, HEAD_DIM), F32)],
        compiler_params=LIMIT,
    )(hbm(new_query), hbm(new_kv))


def row_copies(size, k, parts, cache, mine, theirs, sems):
    sub = lax.axis_index("sub")
    row = size.source_row(k)
    rest = size.heads - size.mine
    copies = []
    for o, (out, first) in enumerate(((mine, sub * rest), (theirs, (1 - sub) * rest))):
        if o and not rest:
            break
        for p, which in enumerate(parts):
            for j in range(size.mine):
                lanes = pl.ds(pl.multiple_of((first + j) * HEAD_DIM, HEAD_DIM), HEAD_DIM)
                at = (p * size.mine + j) * size.span
                copies.append(pltpu.make_async_copy(
                    out.at[pl.ds(at, size.span)],
                    cache.at[row, which, :, lanes],
                    sems.at[o, p * size.mine + j],
                ))
    return copies


def rebuild_kernel(size, parts, chained, *refs):
    message, tables = refs[0], refs[0 if 0 in parts else 1]
    refs = refs[1 if 0 in parts else 2:]
    refs = refs[2 * chained:]
    _, _, mine, theirs = refs
    sub = lax.axis_index("sub")
    rest = size.heads - size.mine
    side_at = size.side_at(parts if 0 in parts else (0,))
    side = tables[side_at:side_at + TILE, :].astype(F32)
    length = side[2 * size.heads:2 * size.heads + 1, :]
    base = sub * size.span
    for o, out in enumerate((theirs, mine)):
        first = (1 - sub) * rest if o == 0 else sub * rest
        other = sub == 0 if o == 0 else sub != 0
        for p, which in enumerate(parts):
            for j in range(size.mine):
                h = which * size.heads + j
                scale = jnp.where(other, side[h + rest:h + rest + 1, :], side[h:h + 1, :])
                table = pl.multiple_of(
                    size.anchor_at(which, parts) + (first + j) * size.rows, TILE
                )
                anchor = message[pl.ds(table, size.rows), :].astype(F32)
                source = (p * size.heads + first + j) * size.span
                to = (p * size.mine + j) * size.span
                for i in range(size.rows):
                    at = pl.multiple_of(source + i * size.repeat, TILE)
                    value = anchor[i:i + 1, :] + scale * message[pl.ds(at, size.repeat), :].astype(F32)
                    keep = (base + i * size.repeat).astype(F32) < length
                    value = jnp.where(keep, value, jnp.float32(0.0)).astype(BF)
                    out[to + i * size.repeat:to + (i + 1) * size.repeat, :] = value


def rebuild(size, parts, message, tables, state):
    args = [vmem(message)] + ([vmem(tables)] if tables is not None else [])
    in_specs = [IN_VMEM] * len(args)
    aliases = {}
    if state is not None:
        aliases = {len(args): 0, len(args) + 1: 1}
        args += list(state)
        in_specs += [IN_HBM, IN_HBM]
    given = (len(parts) * size.mine * size.span, HEAD_DIM)
    out = pl.pallas_call(
        functools.partial(rebuild_kernel, size, parts, state is not None),
        in_specs=in_specs,
        out_specs=[IN_HBM, IN_HBM, IN_VMEM, IN_VMEM],
        out_shape=[
            pltpu.HBM((size.count, 2, size.span, size.channels), BF),
            pltpu.HBM((size.count, size.steps, size.q_local * HEAD_DIM), BF),
            pltpu.VMEM(given, BF),
            pltpu.VMEM(given, BF),
        ],
        input_output_aliases=aliases,
        compiler_params=LIMIT,
        cost_estimate=pl.CostEstimate(
            flops=4 * len(parts) * size.span * size.channels,
            bytes_accessed=6 * len(parts) * size.span * size.channels,
            transcendentals=0,
        ),
    )(*args)
    return tuple(out[:2]), out[2], out[3]


def weigh(size, j, q, new_key, key_mine, key_other, live_mine, live_other, causal):
    factor = 1.0 / math.sqrt(HEAD_DIM)
    s0 = lax.dot_general(q, key_mine, NT, preferred_element_type=F32) * factor
    s1 = lax.dot_general(q, key_other, NT, preferred_element_type=F32) * factor
    s2 = lax.dot_general(q, new_key, NT, preferred_element_type=F32) * factor
    s0 = jnp.where(live_mine, s0, jnp.float32(LOW))
    s1 = jnp.where(live_other, s1, jnp.float32(LOW))
    s2 = jnp.where(causal, s2, jnp.float32(LOW))
    top = jnp.maximum(
        jnp.max(jnp.maximum(s0, s1), axis=1, keepdims=True), jnp.max(s2, axis=1, keepdims=True)
    )
    w0 = jnp.where(live_mine, jnp.exp(s0 - top), jnp.float32(0.0))
    w1 = jnp.where(live_other, jnp.exp(s1 - top), jnp.float32(0.0))
    w2 = jnp.where(causal, jnp.exp(s2 - top), jnp.float32(0.0))
    total = jnp.sum(w0 + w1, axis=1, keepdims=True) + jnp.sum(w2, axis=1, keepdims=True)
    return w0.astype(BF), w1.astype(BF), w2.astype(BF), total


def masks(size, tables, parts, fresh):
    sub = lax.axis_index("sub")
    at = size.side_at(parts)
    side = tables[at:at + TILE, :].astype(F32)
    length = side[2 * size.heads:2 * size.heads + 1, 0:1]
    spot = lax.broadcasted_iota(jnp.int32, (1, size.span), 1)
    live_mine = (spot + sub * size.span).astype(F32) < length
    live_other = (spot + (1 - sub) * size.span).astype(F32) < length
    step = lax.broadcasted_iota(jnp.int32, (size.wide, fresh), 0) % size.steps
    token = lax.broadcasted_iota(jnp.int32, (size.wide, fresh), 1)
    return live_mine, live_other, (token <= step) & (token < size.steps)


def start_store(size, k, parts, cache, mine, theirs, sems):
    copies = row_copies(size, k, parts, cache, mine, theirs, sems)
    for copy in copies:
        copy.start()
    return copies


def store_heads(size, k, flat, made, attended, sem, copies):
    for j in range(size.mine):
        for g in range(size.group):
            at = (j * size.group + g) * HEAD_DIM
            made[:, at:at + HEAD_DIM] = flat[j, g * size.steps:(g + 1) * size.steps, :].astype(BF)
    copy = pltpu.make_async_copy(made, attended.at[size.source_row(k)], sem)
    copy.start()
    for each in copies:
        each.wait()
    copy.wait()


def attend_kernel(size, k, query, new_kv, tables, mine, other, theirs, *refs):
    cache, attended, made, flat, sem, sems = refs[2:]
    row = size.source_row(k)
    copies = start_store(size, k, (0, 1), cache, mine, theirs, sems)
    live_mine, live_other, causal = masks(size, tables, (0, 1), new_kv.shape[3])
    for j in range(size.mine):
        keys = slice(j * size.span, (j + 1) * size.span)
        values = slice((size.mine + j) * size.span, (size.mine + j + 1) * size.span)
        w0, w1, w2, total = weigh(
            size, j, query[row, j], new_kv[row, 0, j], mine[keys, :], other[keys, :],
            live_mine, live_other, causal,
        )
        acc = jnp.dot(w0, mine[values, :], preferred_element_type=F32)
        acc = acc + jnp.dot(w1, other[values, :], preferred_element_type=F32)
        acc = acc + jnp.dot(w2, new_kv[row, 1, j], preferred_element_type=F32)
        flat[j] = acc / total
    store_heads(size, k, flat, made, attended, sem, copies)


def weights_kernel(size, k, query, new_kv, tables, mine, other, theirs, *refs):
    cache, _, weights, share, totals, sems = refs[2:]
    row = size.source_row(k)
    copies = start_store(size, k, (0,), cache, mine, theirs, sems)
    live_mine, live_other, causal = masks(size, tables, (0,), new_kv.shape[3])
    for j in range(size.mine):
        keys = slice(j * size.span, (j + 1) * size.span)
        w0, w1, w2, total = weigh(
            size, j, query[row, j], new_kv[row, 0, j], mine[keys, :], other[keys, :],
            live_mine, live_other, causal,
        )
        weights[j, :, :size.span] = w0
        weights[j, :, size.span:] = w1
        share[j] = jnp.dot(w2, new_kv[row, 1, j], preferred_element_type=F32)
        totals[j] = jnp.broadcast_to(total, totals.shape[1:])
    for copy in copies:
        copy.wait()


def half_kernel(size, k, weights, share, mine, theirs, *refs):
    cache, _, half, sems = refs[2:]
    copies = start_store(size, k, (1,), cache, mine, theirs, sems)
    for j in range(size.mine):
        values = slice(j * size.span, (j + 1) * size.span)
        half[j] = share[j] + jnp.dot(
            weights[j, :, :size.span], mine[values, :], preferred_element_type=F32
        )
    for copy in copies:
        copy.wait()


def finish_kernel(size, k, weights, half, totals, other, *refs):
    _, attended, made, flat, sem = refs[2:]
    for j in range(size.mine):
        values = slice(j * size.span, (j + 1) * size.span)
        acc = half[j] + jnp.dot(
            weights[j, :, size.span:], other[values, :], preferred_element_type=F32
        )
        flat[j] = acc / totals[j]
    store_heads(size, k, flat, made, attended, sem, ())


def chained_call(size, kernel, args, state, shapes, scratch, flops):
    args = [vmem(x) for x in args]
    many = len(args)
    out = pl.pallas_call(
        kernel,
        in_specs=[IN_VMEM] * many + [IN_HBM, IN_HBM],
        out_specs=[IN_HBM, IN_HBM] + [IN_VMEM] * len(shapes),
        out_shape=[pltpu.HBM(x.shape, x.dtype) for x in state] + shapes,
        scratch_shapes=scratch,
        input_output_aliases={many: 0, many + 1: 1},
        compiler_params=LIMIT,
        cost_estimate=pl.CostEstimate(
            flops=flops,
            bytes_accessed=8 * size.span * size.channels,
            transcendentals=2 * size.mine * size.wide * size.span,
        ),
    )(*args, *state)
    return tuple(out[:2]), out[2:]


def body(deltas, anchors, chan_scale, lengths, route, new_query, new_kv):
    n = lax.axis_size("pool")
    size = Sizes(deltas, anchors, new_query, n)
    both, last = (0, 1), n - 1
    plan = [(k, both) for k in range(1, last)] + [(last, (0,)), (last, (1,)), (0, both)]
    query, fresh = arrange(size, new_query, new_kv)
    message = {}
    for part in (plan[:1], plan[1:]):
        for (k, parts), msg in zip(part, pack(size, part, route, lengths, deltas, anchors, chan_scale)):
            if k:
                msg = lax.ppermute(msg, "pool", list(enumerate(far(n, k))))
            message[k, parts] = msg

    def swapped(x):
        return lax.ppermute(x, "sub", [(0, 1), (1, 0)])

    flops = 8 * size.mine * size.wide * size.span * HEAD_DIM
    rows = [
        pltpu.VMEM((size.steps, size.q_local * HEAD_DIM), BF),
        pltpu.VMEM((size.mine, size.wide, HEAD_DIM), F32),
        pltpu.SemaphoreType.DMA,
    ]
    sems = pltpu.SemaphoreType.DMA((2, 2 * size.mine))
    wide = pltpu.VMEM((size.mine, size.wide, HEAD_DIM), F32)

    def attend(k, mine, other, theirs, state):
        state, _ = chained_call(
            size, functools.partial(attend_kernel, size, k),
            (query, fresh, message[k, both], mine, other, theirs), state, [], rows + [sems], flops,
        )
        return state

    def take(k, parts, state):
        tables = None if 0 in parts else message[last, (0,)]
        state, mine, theirs = rebuild(size, parts, message[k, parts], tables, state)
        return state, mine, swapped(theirs), theirs

    state, held = None, []
    for k in range(last):
        state, *each = take(k, both, state)
        held.append((k, *each))
        if 0 < k < last - 1:
            state = attend(*held.pop(0), state)
    state, *keys = take(last, (0,), state)
    for each in held:
        state = attend(*each, state)
    state, (weights, share, totals) = chained_call(
        size, functools.partial(weights_kernel, size, last),
        (query, fresh, message[last, (0,)], *keys), state,
        [pltpu.VMEM((size.mine, size.wide, 2 * size.span), BF), wide, wide], [sems], flops // 2,
    )
    state, mine, other, theirs = take(last, (1,), state)
    state, (half,) = chained_call(
        size, functools.partial(half_kernel, size, last),
        (weights, share, mine, theirs), state, [wide], [sems], flops // 4,
    )
    state, _ = chained_call(
        size, functools.partial(finish_kernel, size, last),
        (weights, half, totals, other), state, [], rows, flops // 4,
    )
    return state


def solution(mesh):
    placed = (
        P(("parts", "pool"), None, "sub", "tp"),
        P(("parts", "pool"), None, "sub", "tp"),
        P(("parts", "pool"), None, "tp"),
        P(("parts", "pool")),
        P(("parts", "pool")),
        P(("parts", "pool"), None, ("tp", "sub")),
        P(("parts", "pool"), None, None, "tp"),
    )
    return jax.shard_map(
        body,
        mesh=mesh,
        in_specs=placed,
        out_specs=(
            P(("parts", "pool"), None, "sub", "tp"),
            P(("parts", "pool"), None, ("tp", "sub")),
        ),
        check_vma=False,
    )
```

```python
import functools
import math

import jax
import jax.numpy as jnp
from jax import lax
from jax.experimental import pallas as pl
from jax.experimental.pallas import tpu as pltpu
from jax.sharding import PartitionSpec as P

HEAD_DIM = 128
Q_PER_KV = 8
TILE = 16
BF = jnp.bfloat16
F32 = jnp.float32
LOW = -1e30
NT = (((1,), (1,)), ((), ()))

IN_VMEM = pl.BlockSpec(memory_space=pltpu.VMEM)
IN_SMEM = pl.BlockSpec(memory_space=pltpu.SMEM)
IN_HBM = pl.BlockSpec(memory_space=pltpu.HBM)
LIMIT = pltpu.CompilerParams(vmem_limit_bytes=16 * 1024 * 1024)


def vmem(x):
    return pltpu.with_memory_space_constraint(x, pltpu.VMEM)


def hbm(x):
    return pltpu.with_memory_space_constraint(x, pltpu.HBM)


def far(n, k):
    ring = (0, 2, 3, 1) if n == 4 else tuple(range(n))
    return tuple(ring[(ring.index(z) + k) % n] for z in range(n))


def pick(values, at):
    out = jnp.int32(values[0])
    for i, value in enumerate(values[1:], 1):
        out = jnp.where(at == i, jnp.int32(value), out)
    return out


class Sizes:
    def __init__(self, deltas, anchors, new_query, n):
        self.n = n
        self.count, _, self.span, self.channels = deltas.shape
        self.rows = anchors.shape[2]
        self.repeat = self.span // self.rows
        self.steps = new_query.shape[1]
        self.heads = self.channels // HEAD_DIM
        self.q_local = new_query.shape[2] // HEAD_DIM
        self.mine = max(1, self.q_local // Q_PER_KV)
        self.group = self.q_local // self.mine
        self.wide = self.group * self.steps

    def anchor_at(self, which, parts):
        return (len(parts) * self.span + parts.index(which) * self.rows) * self.heads

    def side_at(self, parts):
        return len(parts) * self.heads * (self.span + self.rows)

    def message_rows(self, parts):
        return self.side_at(parts) + (TILE if 0 in parts else 0)

    def source_row(self, k):
        return pick(far(self.n, self.n - k), lax.axis_index("pool"))


def side_block(size, scale, length):
    row = lax.broadcasted_iota(jnp.int32, (TILE, HEAD_DIM), 0)
    scale = scale.astype(F32)
    out = jnp.where(row == 2 * size.heads, length.astype(F32), jnp.float32(0.0))
    for which in range(2):
        for h in range(size.heads):
            piece = scale[which:which + 1, h * HEAD_DIM:(h + 1) * HEAD_DIM]
            out = jnp.where(row == which * size.heads + h, piece, out)
    return out.astype(BF)


def pack_kernel(size, plan, route, lengths, deltas, anchors, scale, *rest):
    outs, (held, tables, sems) = rest[:-3], rest[-3:]
    z = lax.axis_index("pool")
    work = []
    for m, (k, parts) in enumerate(plan):
        dest = pick(far(size.n, k), z)
        index = jnp.int32(0)
        for j in range(size.count):
            index = jnp.where(route[j] == dest, jnp.int32(j), index)
        for which in parts:
            slot = len(work)
            copies = (
                pltpu.make_async_copy(deltas.at[index, which], held.at[slot], sems.at[0, slot]),
                pltpu.make_async_copy(anchors.at[index, which], tables.at[slot], sems.at[1, slot]),
            )
            for copy in copies:
                copy.start()
            work.append((outs[m], parts, which, slot, copies))
        if 0 in parts:
            outs[m][pl.ds(size.side_at(parts), TILE), :] = side_block(size, scale[index], lengths[index])
    for msg, parts, which, slot, copies in work:
        for copy in copies:
            copy.wait()
        for h in range(size.heads):
            lanes = slice(h * HEAD_DIM, (h + 1) * HEAD_DIM)
            at = (parts.index(which) * size.heads + h) * size.span
            msg[at:at + size.span, :] = held[slot, :, lanes]
            at = size.anchor_at(which, parts) + h * size.rows
            msg[at:at + size.rows, :] = tables[slot, :, lanes]


def pack(size, plan, route, lengths, deltas, anchors, scale):
    shapes = [pltpu.VMEM((size.message_rows(parts), HEAD_DIM), BF) for _, parts in plan]
    slots = sum(len(parts) for _, parts in plan)
    return pl.pallas_call(
        functools.partial(pack_kernel, size, plan),
        out_shape=shapes,
        in_specs=[IN_SMEM, IN_SMEM, IN_HBM, IN_HBM, IN_VMEM],
        out_specs=[IN_VMEM] * len(shapes),
        scratch_shapes=[
            pltpu.VMEM((slots, size.span, size.channels), BF),
            pltpu.VMEM((slots, size.rows, size.channels), BF),
            pltpu.SemaphoreType.DMA((2, slots)),
        ],
        compiler_params=LIMIT,
        cost_estimate=pl.CostEstimate(
            flops=0, bytes_accessed=2 * slots * size.span * size.channels, transcendentals=0
        ),
    )(hbm(route), hbm(lengths), hbm(deltas), hbm(anchors), hbm(scale))


def arrange_kernel(size, new_query, new_kv, query, fresh, wide, tall):
    sub = lax.axis_index("sub")
    rest = size.heads - size.mine
    tall[...] = jnp.zeros_like(tall)
    for r in range(size.count):
        for j in range(size.mine):
            for g in range(size.group):
                at = (j * size.group + g) * HEAD_DIM
                piece = new_query[r, :, at:at + HEAD_DIM].astype(F32)
                wide[g * size.steps:(g + 1) * size.steps, :] = piece
            query[r, j] = wide[...].astype(BF)
            for which in range(2):
                own, other = (
                    new_kv[r, which, :, h * HEAD_DIM:(h + 1) * HEAD_DIM].astype(F32) for h in (j, j + rest)
                )
                tall[:size.steps, :] = jnp.where(sub == 0, own, other)
                fresh[r, which, j] = tall[...].astype(BF)


def arrange(size, new_query, new_kv):
    return pl.pallas_call(
        functools.partial(arrange_kernel, size),
        in_specs=[IN_VMEM, IN_VMEM],
        out_specs=[IN_VMEM, IN_VMEM],
        out_shape=[
            pltpu.VMEM((size.count, size.mine, size.wide, HEAD_DIM), BF),
            pltpu.VMEM((size.count, 2, size.mine, TILE, HEAD_DIM), BF),
        ],
        scratch_shapes=[pltpu.VMEM((size.wide, HEAD_DIM), F32), pltpu.VMEM((TILE, HEAD_DIM), F32)],
        compiler_params=LIMIT,
    )(hbm(new_query), hbm(new_kv))


def row_copies(size, k, parts, cache, mine, theirs, sems):
    sub = lax.axis_index("sub")
    row = size.source_row(k)
    rest = size.heads - size.mine
    copies = []
    for o, (out, first) in enumerate(((mine, sub * rest), (theirs, (1 - sub) * rest))):
        if o and not rest:
            break
        for p, which in enumerate(parts):
            for j in range(size.mine):
                lanes = pl.ds(pl.multiple_of((first + j) * HEAD_DIM, HEAD_DIM), HEAD_DIM)
                at = (p * size.mine + j) * size.span
                copies.append(pltpu.make_async_copy(
                    out.at[pl.ds(at, size.span)],
                    cache.at[row, which, :, lanes],
                    sems.at[o, p * size.mine + j],
                ))
    return copies


def rebuild_kernel(size, parts, chained, *refs):
    message, tables = refs[0], refs[0 if 0 in parts else 1]
    refs = refs[1 if 0 in parts else 2:]
    refs = refs[2 * chained:]
    _, _, mine, theirs = refs
    sub = lax.axis_index("sub")
    rest = size.heads - size.mine
    side_at = size.side_at(parts if 0 in parts else (0,))
    side = tables[side_at:side_at + TILE, :].astype(F32)
    length = side[2 * size.heads:2 * size.heads + 1, :]
    base = sub * size.span
    for o, out in enumerate((theirs, mine)):
        first = (1 - sub) * rest if o == 0 else sub * rest
        other = sub == 0 if o == 0 else sub != 0
        for p, which in enumerate(parts):
            for j in range(size.mine):
                h = which * size.heads + j
                scale = jnp.where(other, side[h + rest:h + rest + 1, :], side[h:h + 1, :])
                table = pl.multiple_of(
                    size.anchor_at(which, parts) + (first + j) * size.rows, TILE
                )
                anchor = message[pl.ds(table, size.rows), :].astype(F32)
                source = (p * size.heads + first + j) * size.span
                to = (p * size.mine + j) * size.span
                for i in range(size.rows):
                    at = pl.multiple_of(source + i * size.repeat, TILE)
                    value = anchor[i:i + 1, :] + scale * message[pl.ds(at, size.repeat), :].astype(F32)
                    keep = (base + i * size.repeat).astype(F32) < length
                    value = jnp.where(keep, value, jnp.float32(0.0)).astype(BF)
                    out[to + i * size.repeat:to + (i + 1) * size.repeat, :] = value


def rebuild(size, parts, message, tables, state):
    args = [vmem(message)] + ([vmem(tables)] if tables is not None else [])
    in_specs = [IN_VMEM] * len(args)
    aliases = {}
    if state is not None:
        aliases = {len(args): 0, len(args) + 1: 1}
        args += list(state)
        in_specs += [IN_HBM, IN_HBM]
    given = (len(parts) * size.mine * size.span, HEAD_DIM)
    out = pl.pallas_call(
        functools.partial(rebuild_kernel, size, parts, state is not None),
        in_specs=in_specs,
        out_specs=[IN_HBM, IN_HBM, IN_VMEM, IN_VMEM],
        out_shape=[
            pltpu.HBM((size.count, 2, size.span, size.channels), BF),
            pltpu.HBM((size.count, size.steps, size.q_local * HEAD_DIM), BF),
            pltpu.VMEM(given, BF),
            pltpu.VMEM(given, BF),
        ],
        input_output_aliases=aliases,
        compiler_params=LIMIT,
        cost_estimate=pl.CostEstimate(
            flops=4 * len(parts) * size.span * size.channels,
            bytes_accessed=6 * len(parts) * size.span * size.channels,
            transcendentals=0,
        ),
    )(*args)
    return tuple(out[:2]), out[2], out[3]


def weigh(size, j, q, new_key, key_mine, key_other, live_mine, live_other, causal):
    factor = 1.0 / math.sqrt(HEAD_DIM)
    s0 = lax.dot_general(q, key_mine, NT, preferred_element_type=F32) * factor
    s1 = lax.dot_general(q, key_other, NT, preferred_element_type=F32) * factor
    s2 = lax.dot_general(q, new_key, NT, preferred_element_type=F32) * factor
    s0 = jnp.where(live_mine, s0, jnp.float32(LOW))
    s1 = jnp.where(live_other, s1, jnp.float32(LOW))
    s2 = jnp.where(causal, s2, jnp.float32(LOW))
    top = jnp.maximum(
        jnp.max(jnp.maximum(s0, s1), axis=1, keepdims=True), jnp.max(s2, axis=1, keepdims=True)
    )
    w0 = jnp.where(live_mine, jnp.exp(s0 - top), jnp.float32(0.0))
    w1 = jnp.where(live_other, jnp.exp(s1 - top), jnp.float32(0.0))
    w2 = jnp.where(causal, jnp.exp(s2 - top), jnp.float32(0.0))
    total = jnp.sum(w0 + w1, axis=1, keepdims=True) + jnp.sum(w2, axis=1, keepdims=True)
    return w0.astype(BF), w1.astype(BF), w2.astype(BF), total


def masks(size, tables, parts, fresh):
    sub = lax.axis_index("sub")
    at = size.side_at(parts)
    side = tables[at:at + TILE, :].astype(F32)
    length = side[2 * size.heads:2 * size.heads + 1, 0:1]
    spot = lax.broadcasted_iota(jnp.int32, (1, size.span), 1)
    live_mine = (spot + sub * size.span).astype(F32) < length
    live_other = (spot + (1 - sub) * size.span).astype(F32) < length
    step = lax.broadcasted_iota(jnp.int32, (size.wide, fresh), 0) % size.steps
    token = lax.broadcasted_iota(jnp.int32, (size.wide, fresh), 1)
    return live_mine, live_other, (token <= step) & (token < size.steps)


def start_store(size, k, parts, cache, mine, theirs, sems):
    copies = row_copies(size, k, parts, cache, mine, theirs, sems)
    for copy in copies:
        copy.start()
    return copies


def store_heads(size, k, flat, made, attended, sem, copies):
    for j in range(size.mine):
        for g in range(size.group):
            at = (j * size.group + g) * HEAD_DIM
            made[:, at:at + HEAD_DIM] = flat[j, g * size.steps:(g + 1) * size.steps, :].astype(BF)
    copy = pltpu.make_async_copy(made, attended.at[size.source_row(k)], sem)
    copy.start()
    for each in copies:
        each.wait()
    copy.wait()


def attend_kernel(size, k, query, new_kv, tables, mine, other, theirs, *refs):
    cache, attended, made, flat, sem, sems = refs[2:]
    row = size.source_row(k)
    copies = start_store(size, k, (0, 1), cache, mine, theirs, sems)
    live_mine, live_other, causal = masks(size, tables, (0, 1), new_kv.shape[3])
    for j in range(size.mine):
        keys = slice(j * size.span, (j + 1) * size.span)
        values = slice((size.mine + j) * size.span, (size.mine + j + 1) * size.span)
        w0, w1, w2, total = weigh(
            size, j, query[row, j], new_kv[row, 0, j], mine[keys, :], other[keys, :],
            live_mine, live_other, causal,
        )
        acc = jnp.dot(w0, mine[values, :], preferred_element_type=F32)
        acc = acc + jnp.dot(w1, other[values, :], preferred_element_type=F32)
        acc = acc + jnp.dot(w2, new_kv[row, 1, j], preferred_element_type=F32)
        flat[j] = acc / total
    store_heads(size, k, flat, made, attended, sem, copies)


def weights_kernel(size, k, query, new_kv, tables, mine, other, theirs, *refs):
    cache, _, weights, share, totals, sems = refs[2:]
    row = size.source_row(k)
    copies = start_store(size, k, (0,), cache, mine, theirs, sems)
    live_mine, live_other, causal = masks(size, tables, (0,), new_kv.shape[3])
    for j in range(size.mine):
        keys = slice(j * size.span, (j + 1) * size.span)
        w0, w1, w2, total = weigh(
            size, j, query[row, j], new_kv[row, 0, j], mine[keys, :], other[keys, :],
            live_mine, live_other, causal,
        )
        weights[j, :, :size.span] = w0
        weights[j, :, size.span:] = w1
        share[j] = jnp.dot(w2, new_kv[row, 1, j], preferred_element_type=F32)
        totals[j] = jnp.broadcast_to(total, totals.shape[1:])
    for copy in copies:
        copy.wait()


def half_kernel(size, k, weights, share, mine, theirs, *refs):
    cache, _, half, sems = refs[2:]
    copies = start_store(size, k, (1,), cache, mine, theirs, sems)
    for j in range(size.mine):
        values = slice(j * size.span, (j + 1) * size.span)
        half[j] = share[j] + jnp.dot(
            weights[j, :, :size.span], mine[values, :], preferred_element_type=F32
        )
    for copy in copies:
        copy.wait()


def finish_kernel(size, k, weights, half, totals, other, *refs):
    _, attended, made, flat, sem = refs[2:]
    for j in range(size.mine):
        values = slice(j * size.span, (j + 1) * size.span)
        acc = half[j] + jnp.dot(
            weights[j, :, size.span:], other[values, :], preferred_element_type=F32
        )
        flat[j] = acc / totals[j]
    store_heads(size, k, flat, made, attended, sem, ())


def chained_call(size, kernel, args, state, shapes, scratch, flops):
    args = [vmem(x) for x in args]
    many = len(args)
    out = pl.pallas_call(
        kernel,
        in_specs=[IN_VMEM] * many + [IN_HBM, IN_HBM],
        out_specs=[IN_HBM, IN_HBM] + [IN_VMEM] * len(shapes),
        out_shape=[pltpu.HBM(x.shape, x.dtype) for x in state] + shapes,
        scratch_shapes=scratch,
        input_output_aliases={many: 0, many + 1: 1},
        compiler_params=LIMIT,
        cost_estimate=pl.CostEstimate(
            flops=flops,
            bytes_accessed=8 * size.span * size.channels,
            transcendentals=2 * size.mine * size.wide * size.span,
        ),
    )(*args, *state)
    return tuple(out[:2]), out[2:]


def body(deltas, anchors, chan_scale, lengths, route, new_query, new_kv):
    n = lax.axis_size("pool")
    size = Sizes(deltas, anchors, new_query, n)
    both, last = (0, 1), n - 1
    plan = [(k, both) for k in range(1, last)] + [(last, (0,)), (last, (1,)), (0, both)]
    query, fresh = arrange(size, new_query, new_kv)
    message = {}
    for (k, parts), msg in zip(plan, pack(size, plan, route, lengths, deltas, anchors, chan_scale)):
        message[k, parts] = lax.ppermute(msg, "pool", list(enumerate(far(n, k)))) if k else msg

    def swapped(x):
        return lax.ppermute(x, "sub", [(0, 1), (1, 0)])

    flops = 8 * size.mine * size.wide * size.span * HEAD_DIM
    rows = [
        pltpu.VMEM((size.steps, size.q_local * HEAD_DIM), BF),
        pltpu.VMEM((size.mine, size.wide, HEAD_DIM), F32),
        pltpu.SemaphoreType.DMA,
    ]
    sems = pltpu.SemaphoreType.DMA((2, 2 * size.mine))
    wide = pltpu.VMEM((size.mine, size.wide, HEAD_DIM), F32)

    def attend(k, mine, other, theirs, state):
        state, _ = chained_call(
            size, functools.partial(attend_kernel, size, k),
            (query, fresh, message[k, both], mine, other, theirs), state, [], rows + [sems], flops,
        )
        return state

    def take(k, parts, state):
        tables = None if 0 in parts else message[last, (0,)]
        state, mine, theirs = rebuild(size, parts, message[k, parts], tables, state)
        return state, mine, swapped(theirs), theirs

    state, held = None, []
    for k in range(last):
        state, *each = take(k, both, state)
        held.append((k, *each))
        if 0 < k < last - 1:
            state = attend(*held.pop(0), state)
    state, *keys = take(last, (0,), state)
    for each in held:
        state = attend(*each, state)
    state, (weights, share, totals) = chained_call(
        size, functools.partial(weights_kernel, size, last),
        (query, fresh, message[last, (0,)], *keys), state,
        [pltpu.VMEM((size.mine, size.wide, 2 * size.span), BF), wide, wide], [sems], flops // 2,
    )
    state, mine, other, theirs = take(last, (1,), state)
    state, (half,) = chained_call(
        size, functools.partial(half_kernel, size, last),
        (weights, share, mine, theirs), state, [wide], [sems], flops // 4,
    )
    state, _ = chained_call(
        size, functools.partial(finish_kernel, size, last),
        (weights, half, totals, other), state, [], rows, flops // 4,
    )
    return state


def solution(mesh):
    placed = (
        P(("parts", "pool"), None, "sub", "tp"),
        P(("parts", "pool"), None, "sub", "tp"),
        P(("parts", "pool"), None, "tp"),
        P(("parts", "pool")),
        P(("parts", "pool")),
        P(("parts", "pool"), None, ("tp", "sub")),
        P(("parts", "pool"), None, None, "tp"),
    )
    return jax.shard_map(
        body,
        mesh=mesh,
        in_specs=placed,
        out_specs=(
            P(("parts", "pool"), None, "sub", "tp"),
            P(("parts", "pool"), None, ("tp", "sub")),
        ),
        check_vma=False,
    )
```

```python
import functools
import math

import jax
import jax.numpy as jnp
from jax import lax
from jax.experimental import pallas as pl
from jax.experimental.pallas import tpu as pltpu
from jax.sharding import PartitionSpec as P

HEAD_DIM = 128
Q_PER_KV = 8
TILE = 16
BF = jnp.bfloat16
F32 = jnp.float32
LOW = -1e30
NT = (((1,), (1,)), ((), ()))

IN_VMEM = pl.BlockSpec(memory_space=pltpu.VMEM)
IN_SMEM = pl.BlockSpec(memory_space=pltpu.SMEM)
IN_HBM = pl.BlockSpec(memory_space=pltpu.HBM)
LIMIT = pltpu.CompilerParams(vmem_limit_bytes=16 * 1024 * 1024)


def vmem(x):
    return pltpu.with_memory_space_constraint(x, pltpu.VMEM)


def hbm(x):
    return pltpu.with_memory_space_constraint(x, pltpu.HBM)


def far(n, k):
    ring = (0, 2, 3, 1) if n == 4 else tuple(range(n))
    return tuple(ring[(ring.index(z) + k) % n] for z in range(n))


def pick(values, at):
    out = jnp.int32(values[0])
    for i, value in enumerate(values[1:], 1):
        out = jnp.where(at == i, jnp.int32(value), out)
    return out


class Sizes:
    def __init__(self, deltas, anchors, new_query, n):
        self.n = n
        self.count, _, self.span, self.channels = deltas.shape
        self.rows = anchors.shape[2]
        self.repeat = self.span // self.rows
        self.steps = new_query.shape[1]
        self.heads = self.channels // HEAD_DIM
        self.q_local = new_query.shape[2] // HEAD_DIM
        self.mine = max(1, self.q_local // Q_PER_KV)
        self.group = self.q_local // self.mine
        self.wide = self.group * self.steps

    def anchor_at(self, which, parts):
        return (len(parts) * self.span + parts.index(which) * self.rows) * self.heads

    def side_at(self, parts):
        return len(parts) * self.heads * (self.span + self.rows)

    def message_rows(self, parts):
        return self.side_at(parts) + (TILE if 0 in parts else 0)

    def source_row(self, k):
        return pick(far(self.n, self.n - k), lax.axis_index("pool"))


def side_block(size, scale, length):
    row = lax.broadcasted_iota(jnp.int32, (TILE, HEAD_DIM), 0)
    scale = scale.astype(F32)
    out = jnp.where(row == 2 * size.heads, length.astype(F32), jnp.float32(0.0))
    for which in range(2):
        for h in range(size.heads):
            piece = scale[which:which + 1, h * HEAD_DIM:(h + 1) * HEAD_DIM]
            out = jnp.where(row == which * size.heads + h, piece, out)
    return out.astype(BF)


def pack_kernel(size, plan, route, lengths, deltas, anchors, scale, *rest):
    outs, (held, tables, sems) = rest[:-3], rest[-3:]
    z = lax.axis_index("pool")
    work = []
    for m, (k, parts) in enumerate(plan):
        dest = pick(far(size.n, k), z)
        index = jnp.int32(0)
        for j in range(size.count):
            index = jnp.where(route[j] == dest, jnp.int32(j), index)
        for which in parts:
            slot = len(work)
            copies = (
                pltpu.make_async_copy(deltas.at[index, which], held.at[slot], sems.at[0, slot]),
                pltpu.make_async_copy(anchors.at[index, which], tables.at[slot], sems.at[1, slot]),
            )
            for copy in copies:
                copy.start()
            work.append((outs[m], parts, which, slot, copies))
        if 0 in parts:
            outs[m][pl.ds(size.side_at(parts), TILE), :] = side_block(size, scale[index], lengths[index])
    for msg, parts, which, slot, copies in work:
        for copy in copies:
            copy.wait()
        for h in range(size.heads):
            lanes = slice(h * HEAD_DIM, (h + 1) * HEAD_DIM)
            at = (parts.index(which) * size.heads + h) * size.span
            msg[at:at + size.span, :] = held[slot, :, lanes]
            at = size.anchor_at(which, parts) + h * size.rows
            msg[at:at + size.rows, :] = tables[slot, :, lanes]


def pack(size, plan, route, lengths, deltas, anchors, scale):
    shapes = [pltpu.VMEM((size.message_rows(parts), HEAD_DIM), BF) for _, parts in plan]
    slots = sum(len(parts) for _, parts in plan)
    return pl.pallas_call(
        functools.partial(pack_kernel, size, plan),
        out_shape=shapes,
        in_specs=[IN_SMEM, IN_SMEM, IN_HBM, IN_HBM, IN_VMEM],
        out_specs=[IN_VMEM] * len(shapes),
        scratch_shapes=[
            pltpu.VMEM((slots, size.span, size.channels), BF),
            pltpu.VMEM((slots, size.rows, size.channels), BF),
            pltpu.SemaphoreType.DMA((2, slots)),
        ],
        compiler_params=LIMIT,
        cost_estimate=pl.CostEstimate(
            flops=0, bytes_accessed=2 * slots * size.span * size.channels, transcendentals=0
        ),
    )(hbm(route), hbm(lengths), hbm(deltas), hbm(anchors), hbm(scale))


def arrange_kernel(size, new_query, new_kv, query, fresh, wide, tall):
    sub = lax.axis_index("sub")
    rest = size.heads - size.mine
    tall[...] = jnp.zeros_like(tall)
    for r in range(size.count):
        for j in range(size.mine):
            for g in range(size.group):
                at = (j * size.group + g) * HEAD_DIM
                piece = new_query[r, :, at:at + HEAD_DIM].astype(F32)
                wide[g * size.steps:(g + 1) * size.steps, :] = piece
            query[r, j] = wide[...].astype(BF)
            for which in range(2):
                own, other = (
                    new_kv[r, which, :, h * HEAD_DIM:(h + 1) * HEAD_DIM].astype(F32) for h in (j, j + rest)
                )
                tall[:size.steps, :] = jnp.where(sub == 0, own, other)
                fresh[r, which, j] = tall[...].astype(BF)


def arrange(size, new_query, new_kv):
    return pl.pallas_call(
        functools.partial(arrange_kernel, size),
        in_specs=[IN_VMEM, IN_VMEM],
        out_specs=[IN_VMEM, IN_VMEM],
        out_shape=[
            pltpu.VMEM((size.count, size.mine, size.wide, HEAD_DIM), BF),
            pltpu.VMEM((size.count, 2, size.mine, TILE, HEAD_DIM), BF),
        ],
        scratch_shapes=[pltpu.VMEM((size.wide, HEAD_DIM), F32), pltpu.VMEM((TILE, HEAD_DIM), F32)],
        compiler_params=LIMIT,
    )(hbm(new_query), hbm(new_kv))


def row_copies(size, k, parts, cache, mine, theirs, sems):
    sub = lax.axis_index("sub")
    row = size.source_row(k)
    rest = size.heads - size.mine
    copies = []
    for o, (out, first) in enumerate(((mine, sub * rest), (theirs, (1 - sub) * rest))):
        if o and not rest:
            break
        for p, which in enumerate(parts):
            for j in range(size.mine):
                lanes = pl.ds(pl.multiple_of((first + j) * HEAD_DIM, HEAD_DIM), HEAD_DIM)
                at = (p * size.mine + j) * size.span
                copies.append(pltpu.make_async_copy(
                    out.at[pl.ds(at, size.span)],
                    cache.at[row, which, :, lanes],
                    sems.at[o, p * size.mine + j],
                ))
    return copies


def rebuild_kernel(size, parts, chained, *refs):
    message, tables = refs[0], refs[0 if 0 in parts else 1]
    refs = refs[1 if 0 in parts else 2:]
    refs = refs[2 * chained:]
    _, _, mine, theirs = refs
    sub = lax.axis_index("sub")
    rest = size.heads - size.mine
    side_at = size.side_at(parts if 0 in parts else (0,))
    side = tables[side_at:side_at + TILE, :].astype(F32)
    length = side[2 * size.heads:2 * size.heads + 1, :]
    base = sub * size.span
    for o, out in enumerate((theirs, mine)):
        first = (1 - sub) * rest if o == 0 else sub * rest
        other = sub == 0 if o == 0 else sub != 0
        for p, which in enumerate(parts):
            for j in range(size.mine):
                h = which * size.heads + j
                scale = jnp.where(other, side[h + rest:h + rest + 1, :], side[h:h + 1, :])
                table = pl.multiple_of(
                    size.anchor_at(which, parts) + (first + j) * size.rows, TILE
                )
                anchor = message[pl.ds(table, size.rows), :].astype(F32)
                source = (p * size.heads + first + j) * size.span
                to = (p * size.mine + j) * size.span
                for i in range(size.rows):
                    at = pl.multiple_of(source + i * size.repeat, TILE)
                    value = anchor[i:i + 1, :] + scale * message[pl.ds(at, size.repeat), :].astype(F32)
                    keep = (base + i * size.repeat).astype(F32) < length
                    value = jnp.where(keep, value, jnp.float32(0.0)).astype(BF)
                    out[to + i * size.repeat:to + (i + 1) * size.repeat, :] = value


def rebuild(size, parts, message, tables, state):
    args = [vmem(message)] + ([vmem(tables)] if tables is not None else [])
    in_specs = [IN_VMEM] * len(args)
    aliases = {}
    if state is not None:
        aliases = {len(args): 0, len(args) + 1: 1}
        args += list(state)
        in_specs += [IN_HBM, IN_HBM]
    given = (len(parts) * size.mine * size.span, HEAD_DIM)
    out = pl.pallas_call(
        functools.partial(rebuild_kernel, size, parts, state is not None),
        in_specs=in_specs,
        out_specs=[IN_HBM, IN_HBM, IN_VMEM, IN_VMEM],
        out_shape=[
            pltpu.HBM((size.count, 2, size.span, size.channels), BF),
            pltpu.HBM((size.count, size.steps, size.q_local * HEAD_DIM), BF),
            pltpu.VMEM(given, BF),
            pltpu.VMEM(given, BF),
        ],
        input_output_aliases=aliases,
        compiler_params=LIMIT,
        cost_estimate=pl.CostEstimate(
            flops=4 * len(parts) * size.span * size.channels,
            bytes_accessed=6 * len(parts) * size.span * size.channels,
            transcendentals=0,
        ),
    )(*args)
    return tuple(out[:2]), out[2], out[3]


def weigh(size, j, q, new_key, key_mine, key_other, live_mine, live_other, causal):
    factor = 1.0 / math.sqrt(HEAD_DIM)
    s0 = lax.dot_general(q, key_mine, NT, preferred_element_type=F32) * factor
    s1 = lax.dot_general(q, key_other, NT, preferred_element_type=F32) * factor
    s2 = lax.dot_general(q, new_key, NT, preferred_element_type=F32) * factor
    s0 = jnp.where(live_mine, s0, jnp.float32(LOW))
    s1 = jnp.where(live_other, s1, jnp.float32(LOW))
    s2 = jnp.where(causal, s2, jnp.float32(LOW))
    top = jnp.maximum(
        jnp.max(jnp.maximum(s0, s1), axis=1, keepdims=True), jnp.max(s2, axis=1, keepdims=True)
    )
    w0 = jnp.where(live_mine, jnp.exp(s0 - top), jnp.float32(0.0))
    w1 = jnp.where(live_other, jnp.exp(s1 - top), jnp.float32(0.0))
    w2 = jnp.where(causal, jnp.exp(s2 - top), jnp.float32(0.0))
    total = jnp.sum(w0 + w1, axis=1, keepdims=True) + jnp.sum(w2, axis=1, keepdims=True)
    return w0.astype(BF), w1.astype(BF), w2.astype(BF), total


def masks(size, tables, parts, fresh):
    sub = lax.axis_index("sub")
    at = size.side_at(parts)
    side = tables[at:at + TILE, :].astype(F32)
    length = side[2 * size.heads:2 * size.heads + 1, 0:1]
    spot = lax.broadcasted_iota(jnp.int32, (1, size.span), 1)
    live_mine = (spot + sub * size.span).astype(F32) < length
    live_other = (spot + (1 - sub) * size.span).astype(F32) < length
    step = lax.broadcasted_iota(jnp.int32, (size.wide, fresh), 0) % size.steps
    token = lax.broadcasted_iota(jnp.int32, (size.wide, fresh), 1)
    return live_mine, live_other, (token <= step) & (token < size.steps)


def start_store(size, k, parts, cache, mine, theirs, sems):
    copies = row_copies(size, k, parts, cache, mine, theirs, sems)
    for copy in copies:
        copy.start()
    return copies


def store_heads(size, k, flat, made, attended, sem, copies):
    for j in range(size.mine):
        for g in range(size.group):
            at = (j * size.group + g) * HEAD_DIM
            made[:, at:at + HEAD_DIM] = flat[j, g * size.steps:(g + 1) * size.steps, :].astype(BF)
    copy = pltpu.make_async_copy(made, attended.at[size.source_row(k)], sem)
    copy.start()
    for each in copies:
        each.wait()
    copy.wait()


def attend_kernel(size, k, query, new_kv, tables, mine, other, theirs, *refs):
    cache, attended, made, flat, sem, sems = refs[2:]
    row = size.source_row(k)
    copies = start_store(size, k, (0, 1), cache, mine, theirs, sems)
    live_mine, live_other, causal = masks(size, tables, (0, 1), new_kv.shape[3])
    for j in range(size.mine):
        keys = slice(j * size.span, (j + 1) * size.span)
        values = slice((size.mine + j) * size.span, (size.mine + j + 1) * size.span)
        w0, w1, w2, total = weigh(
            size, j, query[row, j], new_kv[row, 0, j], mine[keys, :], other[keys, :],
            live_mine, live_other, causal,
        )
        acc = jnp.dot(w0, mine[values, :], preferred_element_type=F32)
        acc = acc + jnp.dot(w1, other[values, :], preferred_element_type=F32)
        acc = acc + jnp.dot(w2, new_kv[row, 1, j], preferred_element_type=F32)
        flat[j] = acc / total
    store_heads(size, k, flat, made, attended, sem, copies)


def weights_kernel(size, k, query, new_kv, tables, mine, other, theirs, *refs):
    cache, _, weights, share, totals, sems = refs[2:]
    row = size.source_row(k)
    copies = start_store(size, k, (0,), cache, mine, theirs, sems)
    live_mine, live_other, causal = masks(size, tables, (0,), new_kv.shape[3])
    for j in range(size.mine):
        keys = slice(j * size.span, (j + 1) * size.span)
        w0, w1, w2, total = weigh(
            size, j, query[row, j], new_kv[row, 0, j], mine[keys, :], other[keys, :],
            live_mine, live_other, causal,
        )
        weights[j, :, :size.span] = w0
        weights[j, :, size.span:] = w1
        share[j] = jnp.dot(w2, new_kv[row, 1, j], preferred_element_type=F32)
        totals[j] = jnp.broadcast_to(total, totals.shape[1:])
    for copy in copies:
        copy.wait()


def half_kernel(size, k, weights, share, mine, theirs, *refs):
    cache, _, half, sems = refs[2:]
    copies = start_store(size, k, (1,), cache, mine, theirs, sems)
    for j in range(size.mine):
        values = slice(j * size.span, (j + 1) * size.span)
        half[j] = share[j] + jnp.dot(
            weights[j, :, :size.span], mine[values, :], preferred_element_type=F32
        )
    for copy in copies:
        copy.wait()


def finish_kernel(size, k, weights, half, totals, other, *refs):
    _, attended, made, flat, sem = refs[2:]
    for j in range(size.mine):
        values = slice(j * size.span, (j + 1) * size.span)
        acc = half[j] + jnp.dot(
            weights[j, :, size.span:], other[values, :], preferred_element_type=F32
        )
        flat[j] = acc / totals[j]
    store_heads(size, k, flat, made, attended, sem, ())


def chained_call(size, kernel, args, state, shapes, scratch, flops):
    args = [vmem(x) for x in args]
    many = len(args)
    out = pl.pallas_call(
        kernel,
        in_specs=[IN_VMEM] * many + [IN_HBM, IN_HBM],
        out_specs=[IN_HBM, IN_HBM] + [IN_VMEM] * len(shapes),
        out_shape=[pltpu.HBM(x.shape, x.dtype) for x in state] + shapes,
        scratch_shapes=scratch,
        input_output_aliases={many: 0, many + 1: 1},
        compiler_params=LIMIT,
        cost_estimate=pl.CostEstimate(
            flops=flops,
            bytes_accessed=8 * size.span * size.channels,
            transcendentals=2 * size.mine * size.wide * size.span,
        ),
    )(*args, *state)
    return tuple(out[:2]), out[2:]


def body(deltas, anchors, chan_scale, lengths, route, new_query, new_kv):
    n = lax.axis_size("pool")
    size = Sizes(deltas, anchors, new_query, n)
    both = (0, 1)
    order = sorted(range(1, n), key=lambda k: (min(k, n - k), k))
    last = order[-1]
    plan = [(k, both) for k in order[:-1]] + [(last, (0,)), (last, (1,)), (0, both)]
    query, fresh = arrange(size, new_query, new_kv)
    message = {}
    for part in (plan[:1], plan[1:]):
        for (k, parts), msg in zip(part, pack(size, part, route, lengths, deltas, anchors, chan_scale)):
            if k:
                msg = lax.ppermute(msg, "pool", list(enumerate(far(n, k))))
            message[k, parts] = msg

    def swapped(x):
        return lax.ppermute(x, "sub", [(0, 1), (1, 0)])

    flops = 8 * size.mine * size.wide * size.span * HEAD_DIM
    rows = [
        pltpu.VMEM((size.steps, size.q_local * HEAD_DIM), BF),
        pltpu.VMEM((size.mine, size.wide, HEAD_DIM), F32),
        pltpu.SemaphoreType.DMA,
    ]
    sems = pltpu.SemaphoreType.DMA((2, 2 * size.mine))
    wide = pltpu.VMEM((size.mine, size.wide, HEAD_DIM), F32)

    def attend(k, mine, other, theirs, state):
        state, _ = chained_call(
            size, functools.partial(attend_kernel, size, k),
            (query, fresh, message[k, both], mine, other, theirs), state, [], rows + [sems], flops,
        )
        return state

    def take(k, parts, state):
        tables = None if 0 in parts else message[last, (0,)]
        state, mine, theirs = rebuild(size, parts, message[k, parts], tables, state)
        return state, mine, swapped(theirs), theirs

    state, held = None, []
    for k in [0] + order[:-1]:
        state, *each = take(k, both, state)
        held.append((k, *each))
        if k and k != order[-2]:
            state = attend(*held.pop(0), state)
    state, *keys = take(last, (0,), state)
    for each in held:
        state = attend(*each, state)
    state, (weights, share, totals) = chained_call(
        size, functools.partial(weights_kernel, size, last),
        (query, fresh, message[last, (0,)], *keys), state,
        [pltpu.VMEM((size.mine, size.wide, 2 * size.span), BF), wide, wide], [sems], flops // 2,
    )
    state, mine, other, theirs = take(last, (1,), state)
    state, (half,) = chained_call(
        size, functools.partial(half_kernel, size, last),
        (weights, share, mine, theirs), state, [wide], [sems], flops // 4,
    )
    state, _ = chained_call(
        size, functools.partial(finish_kernel, size, last),
        (weights, half, totals, other), state, [], rows, flops // 4,
    )
    return state


def solution(mesh):
    placed = (
        P(("parts", "pool"), None, "sub", "tp"),
        P(("parts", "pool"), None, "sub", "tp"),
        P(("parts", "pool"), None, "tp"),
        P(("parts", "pool")),
        P(("parts", "pool")),
        P(("parts", "pool"), None, ("tp", "sub")),
        P(("parts", "pool"), None, None, "tp"),
    )
    return jax.shard_map(
        body,
        mesh=mesh,
        in_specs=placed,
        out_specs=(
            P(("parts", "pool"), None, "sub", "tp"),
            P(("parts", "pool"), None, ("tp", "sub")),
        ),
        check_vma=False,
    )
```

```python
import functools
import math

import jax
import jax.numpy as jnp
from jax import lax
from jax.experimental import pallas as pl
from jax.experimental.pallas import tpu as pltpu
from jax.sharding import PartitionSpec as P

HEAD_DIM = 128
Q_PER_KV = 8
TILE = 16
CHUNKS = 4
BF = jnp.bfloat16
F32 = jnp.float32
LOW = -1e30
NT = (((1,), (1,)), ((), ()))

IN_VMEM = pl.BlockSpec(memory_space=pltpu.VMEM)
IN_SMEM = pl.BlockSpec(memory_space=pltpu.SMEM)
IN_HBM = pl.BlockSpec(memory_space=pltpu.HBM)
LIMIT = pltpu.CompilerParams(vmem_limit_bytes=16 * 1024 * 1024)


def vmem(x):
    return pltpu.with_memory_space_constraint(x, pltpu.VMEM)


def hbm(x):
    return pltpu.with_memory_space_constraint(x, pltpu.HBM)


def far(n, k):
    ring = (0, 2, 3, 1) if n == 4 else tuple(range(n))
    return tuple(ring[(ring.index(z) + k) % n] for z in range(n))


def pick(values, at):
    out = jnp.int32(values[0])
    for i, value in enumerate(values[1:], 1):
        out = jnp.where(at == i, jnp.int32(value), out)
    return out


class Sizes:
    def __init__(self, deltas, anchors, new_query, n):
        self.n = n
        self.count, _, self.span, self.channels = deltas.shape
        self.rows = anchors.shape[2]
        self.repeat = self.span // self.rows
        self.steps = new_query.shape[1]
        self.heads = self.channels // HEAD_DIM
        self.q_local = new_query.shape[2] // HEAD_DIM
        self.mine = max(1, self.q_local // Q_PER_KV)
        self.group = self.q_local // self.mine
        self.wide = self.group * self.steps

    def anchor_at(self, which, parts):
        return (len(parts) * self.span + parts.index(which) * self.rows) * self.heads

    def side_at(self, parts):
        return len(parts) * self.heads * (self.span + self.rows)

    def message_rows(self, parts):
        return self.side_at(parts) + (TILE if 0 in parts else 0)

    def source_row(self, k):
        return pick(far(self.n, self.n - k), lax.axis_index("pool"))


def side_block(size, scale, length):
    row = lax.broadcasted_iota(jnp.int32, (TILE, HEAD_DIM), 0)
    scale = scale.astype(F32)
    out = jnp.where(row == 2 * size.heads, length.astype(F32), jnp.float32(0.0))
    for which in range(2):
        for h in range(size.heads):
            piece = scale[which:which + 1, h * HEAD_DIM:(h + 1) * HEAD_DIM]
            out = jnp.where(row == which * size.heads + h, piece, out)
    return out.astype(BF)


def pack_kernel(size, plan, route, lengths, deltas, anchors, scale, *rest):
    outs, (to, long, scales, held, tables, sems, few) = rest[:-7], rest[-7:]
    first = [
        pltpu.make_async_copy(source, target, few.at[i])
        for i, (source, target) in enumerate(((route, to), (lengths, long), (scale, scales)))
    ]
    for copy in first:
        copy.start()
    z = lax.axis_index("pool")
    step = size.span // CHUNKS
    first[0].wait()
    work, indices = [], []
    for m, (k, parts) in enumerate(plan):
        dest = pick(far(size.n, k), z)
        index = jnp.int32(0)
        for j in range(size.count):
            index = jnp.where(to[j] == dest, jnp.int32(j), index)
        indices.append(index)
        for which in parts:
            slot = len(work)
            copies = [
                pltpu.make_async_copy(
                    deltas.at[index, which, pl.ds(c * step, step)],
                    held.at[slot, pl.ds(c * step, step)],
                    sems.at[slot, c],
                )
                for c in range(CHUNKS)
            ]
            copies.append(
                pltpu.make_async_copy(anchors.at[index, which], tables.at[slot], sems.at[slot, CHUNKS])
            )
            for copy in copies:
                copy.start()
            work.append((outs[m], parts, which, slot, copies))
    for copy in first[1:]:
        copy.wait()
    for m, (k, parts) in enumerate(plan):
        if 0 in parts:
            side = side_block(size, scales[indices[m]], long[indices[m]])
            outs[m][pl.ds(size.side_at(parts), TILE), :] = side
    for msg, parts, which, slot, copies in work:
        for c, copy in enumerate(copies):
            copy.wait()
            for h in range(size.heads):
                lanes = slice(h * HEAD_DIM, (h + 1) * HEAD_DIM)
                if c < CHUNKS:
                    at = (parts.index(which) * size.heads + h) * size.span + c * step
                    msg[at:at + step, :] = held[slot, c * step:(c + 1) * step, lanes]
                else:
                    at = size.anchor_at(which, parts) + h * size.rows
                    msg[at:at + size.rows, :] = tables[slot, :, lanes]


def pack(size, plan, route, lengths, deltas, anchors, scale):
    shapes = [pltpu.VMEM((size.message_rows(parts), HEAD_DIM), BF) for _, parts in plan]
    slots = sum(len(parts) for _, parts in plan)
    return pl.pallas_call(
        functools.partial(pack_kernel, size, plan),
        out_shape=shapes,
        in_specs=[IN_HBM] * 5,
        out_specs=[IN_VMEM] * len(shapes),
        scratch_shapes=[
            pltpu.SMEM(route.shape, jnp.int32),
            pltpu.SMEM(lengths.shape, jnp.int32),
            pltpu.VMEM(scale.shape, BF),
            pltpu.VMEM((slots, size.span, size.channels), BF),
            pltpu.VMEM((slots, size.rows, size.channels), BF),
            pltpu.SemaphoreType.DMA((slots, CHUNKS + 1)),
            pltpu.SemaphoreType.DMA((3,)),
        ],
        compiler_params=LIMIT,
        cost_estimate=pl.CostEstimate(
            flops=0, bytes_accessed=2 * slots * size.span * size.channels, transcendentals=0
        ),
    )(hbm(route), hbm(lengths), hbm(deltas), hbm(anchors), hbm(scale))


def arrange_kernel(size, new_query, new_kv, query, fresh, wide, tall):
    sub = lax.axis_index("sub")
    rest = size.heads - size.mine
    tall[...] = jnp.zeros_like(tall)
    for r in range(size.count):
        for j in range(size.mine):
            for g in range(size.group):
                at = (j * size.group + g) * HEAD_DIM
                piece = new_query[r, :, at:at + HEAD_DIM].astype(F32)
                wide[g * size.steps:(g + 1) * size.steps, :] = piece
            query[r, j] = wide[...].astype(BF)
            for which in range(2):
                own, other = (
                    new_kv[r, which, :, h * HEAD_DIM:(h + 1) * HEAD_DIM].astype(F32) for h in (j, j + rest)
                )
                tall[:size.steps, :] = jnp.where(sub == 0, own, other)
                fresh[r, which, j] = tall[...].astype(BF)


def arrange(size, new_query, new_kv):
    return pl.pallas_call(
        functools.partial(arrange_kernel, size),
        in_specs=[IN_VMEM, IN_VMEM],
        out_specs=[IN_VMEM, IN_VMEM],
        out_shape=[
            pltpu.VMEM((size.count, size.mine, size.wide, HEAD_DIM), BF),
            pltpu.VMEM((size.count, 2, size.mine, TILE, HEAD_DIM), BF),
        ],
        scratch_shapes=[pltpu.VMEM((size.wide, HEAD_DIM), F32), pltpu.VMEM((TILE, HEAD_DIM), F32)],
        compiler_params=LIMIT,
    )(hbm(new_query), hbm(new_kv))


def row_copies(size, k, parts, cache, mine, theirs, sems):
    sub = lax.axis_index("sub")
    row = size.source_row(k)
    rest = size.heads - size.mine
    copies = []
    for o, (out, first) in enumerate(((mine, sub * rest), (theirs, (1 - sub) * rest))):
        if o and not rest:
            break
        for p, which in enumerate(parts):
            for j in range(size.mine):
                lanes = pl.ds(pl.multiple_of((first + j) * HEAD_DIM, HEAD_DIM), HEAD_DIM)
                at = (p * size.mine + j) * size.span
                copies.append(pltpu.make_async_copy(
                    out.at[pl.ds(at, size.span)],
                    cache.at[row, which, :, lanes],
                    sems.at[o, p * size.mine + j],
                ))
    return copies


def rebuild_kernel(size, parts, chained, *refs):
    message, tables = refs[0], refs[0 if 0 in parts else 1]
    refs = refs[1 if 0 in parts else 2:]
    refs = refs[2 * chained:]
    _, _, mine, theirs = refs
    sub = lax.axis_index("sub")
    rest = size.heads - size.mine
    side_at = size.side_at(parts if 0 in parts else (0,))
    side = tables[side_at:side_at + TILE, :].astype(F32)
    length = side[2 * size.heads:2 * size.heads + 1, :]
    base = sub * size.span
    for o, out in enumerate((theirs, mine)):
        first = (1 - sub) * rest if o == 0 else sub * rest
        other = sub == 0 if o == 0 else sub != 0
        for p, which in enumerate(parts):
            for j in range(size.mine):
                h = which * size.heads + j
                scale = jnp.where(other, side[h + rest:h + rest + 1, :], side[h:h + 1, :])
                table = pl.multiple_of(
                    size.anchor_at(which, parts) + (first + j) * size.rows, TILE
                )
                anchor = message[pl.ds(table, size.rows), :].astype(F32)
                source = (p * size.heads + first + j) * size.span
                to = (p * size.mine + j) * size.span
                for i in range(size.rows):
                    at = pl.multiple_of(source + i * size.repeat, TILE)
                    value = anchor[i:i + 1, :] + scale * message[pl.ds(at, size.repeat), :].astype(F32)
                    keep = (base + i * size.repeat).astype(F32) < length
                    value = jnp.where(keep, value, jnp.float32(0.0)).astype(BF)
                    out[to + i * size.repeat:to + (i + 1) * size.repeat, :] = value


def rebuild(size, parts, message, tables, state):
    args = [vmem(message)] + ([vmem(tables)] if tables is not None else [])
    in_specs = [IN_VMEM] * len(args)
    aliases = {}
    if state is not None:
        aliases = {len(args): 0, len(args) + 1: 1}
        args += list(state)
        in_specs += [IN_HBM, IN_HBM]
    given = (len(parts) * size.mine * size.span, HEAD_DIM)
    out = pl.pallas_call(
        functools.partial(rebuild_kernel, size, parts, state is not None),
        in_specs=in_specs,
        out_specs=[IN_HBM, IN_HBM, IN_VMEM, IN_VMEM],
        out_shape=[
            pltpu.HBM((size.count, 2, size.span, size.channels), BF),
            pltpu.HBM((size.count, size.steps, size.q_local * HEAD_DIM), BF),
            pltpu.VMEM(given, BF),
            pltpu.VMEM(given, BF),
        ],
        input_output_aliases=aliases,
        compiler_params=LIMIT,
        cost_estimate=pl.CostEstimate(
            flops=4 * len(parts) * size.span * size.channels,
            bytes_accessed=6 * len(parts) * size.span * size.channels,
            transcendentals=0,
        ),
    )(*args)
    return tuple(out[:2]), out[2], out[3]


def weigh(size, j, q, new_key, key_mine, key_other, live_mine, live_other, causal):
    factor = 1.0 / math.sqrt(HEAD_DIM)
    s0 = lax.dot_general(q, key_mine, NT, preferred_element_type=F32) * factor
    s1 = lax.dot_general(q, key_other, NT, preferred_element_type=F32) * factor
    s2 = lax.dot_general(q, new_key, NT, preferred_element_type=F32) * factor
    s0 = jnp.where(live_mine, s0, jnp.float32(LOW))
    s1 = jnp.where(live_other, s1, jnp.float32(LOW))
    s2 = jnp.where(causal, s2, jnp.float32(LOW))
    top = jnp.maximum(
        jnp.max(jnp.maximum(s0, s1), axis=1, keepdims=True), jnp.max(s2, axis=1, keepdims=True)
    )
    w0 = jnp.where(live_mine, jnp.exp(s0 - top), jnp.float32(0.0))
    w1 = jnp.where(live_other, jnp.exp(s1 - top), jnp.float32(0.0))
    w2 = jnp.where(causal, jnp.exp(s2 - top), jnp.float32(0.0))
    total = jnp.sum(w0 + w1, axis=1, keepdims=True) + jnp.sum(w2, axis=1, keepdims=True)
    return w0.astype(BF), w1.astype(BF), w2.astype(BF), total


def masks(size, tables, parts, fresh):
    sub = lax.axis_index("sub")
    at = size.side_at(parts)
    side = tables[at:at + TILE, :].astype(F32)
    length = side[2 * size.heads:2 * size.heads + 1, 0:1]
    spot = lax.broadcasted_iota(jnp.int32, (1, size.span), 1)
    live_mine = (spot + sub * size.span).astype(F32) < length
    live_other = (spot + (1 - sub) * size.span).astype(F32) < length
    step = lax.broadcasted_iota(jnp.int32, (size.wide, fresh), 0) % size.steps
    token = lax.broadcasted_iota(jnp.int32, (size.wide, fresh), 1)
    return live_mine, live_other, (token <= step) & (token < size.steps)


def start_store(size, k, parts, cache, mine, theirs, sems):
    copies = row_copies(size, k, parts, cache, mine, theirs, sems)
    for copy in copies:
        copy.start()
    return copies


def store_heads(size, k, flat, made, attended, sem, copies):
    for j in range(size.mine):
        for g in range(size.group):
            at = (j * size.group + g) * HEAD_DIM
            made[:, at:at + HEAD_DIM] = flat[j, g * size.steps:(g + 1) * size.steps, :].astype(BF)
    copy = pltpu.make_async_copy(made, attended.at[size.source_row(k)], sem)
    copy.start()
    for each in copies:
        each.wait()
    copy.wait()


def attend_kernel(size, k, query, new_kv, tables, mine, other, theirs, *refs):
    cache, attended, made, flat, sem, sems = refs[2:]
    row = size.source_row(k)
    copies = start_store(size, k, (0, 1), cache, mine, theirs, sems)
    live_mine, live_other, causal = masks(size, tables, (0, 1), new_kv.shape[3])
    for j in range(size.mine):
        keys = slice(j * size.span, (j + 1) * size.span)
        values = slice((size.mine + j) * size.span, (size.mine + j + 1) * size.span)
        w0, w1, w2, total = weigh(
            size, j, query[row, j], new_kv[row, 0, j], mine[keys, :], other[keys, :],
            live_mine, live_other, causal,
        )
        acc = jnp.dot(w0, mine[values, :], preferred_element_type=F32)
        acc = acc + jnp.dot(w1, other[values, :], preferred_element_type=F32)
        acc = acc + jnp.dot(w2, new_kv[row, 1, j], preferred_element_type=F32)
        flat[j] = acc / total
    store_heads(size, k, flat, made, attended, sem, copies)


def weights_kernel(size, k, query, new_kv, tables, mine, other, theirs, *refs):
    cache, _, weights, share, totals, sems = refs[2:]
    row = size.source_row(k)
    copies = start_store(size, k, (0,), cache, mine, theirs, sems)
    live_mine, live_other, causal = masks(size, tables, (0,), new_kv.shape[3])
    for j in range(size.mine):
        keys = slice(j * size.span, (j + 1) * size.span)
        w0, w1, w2, total = weigh(
            size, j, query[row, j], new_kv[row, 0, j], mine[keys, :], other[keys, :],
            live_mine, live_other, causal,
        )
        weights[j, :, :size.span] = w0
        weights[j, :, size.span:] = w1
        share[j] = jnp.dot(w2, new_kv[row, 1, j], preferred_element_type=F32)
        totals[j] = jnp.broadcast_to(total, totals.shape[1:])
    for copy in copies:
        copy.wait()


def half_kernel(size, k, weights, share, mine, theirs, *refs):
    cache, _, half, sems = refs[2:]
    copies = start_store(size, k, (1,), cache, mine, theirs, sems)
    for j in range(size.mine):
        values = slice(j * size.span, (j + 1) * size.span)
        half[j] = share[j] + jnp.dot(
            weights[j, :, :size.span], mine[values, :], preferred_element_type=F32
        )
    for copy in copies:
        copy.wait()


def finish_kernel(size, k, weights, half, totals, other, *refs):
    _, attended, made, flat, sem = refs[2:]
    for j in range(size.mine):
        values = slice(j * size.span, (j + 1) * size.span)
        acc = half[j] + jnp.dot(
            weights[j, :, size.span:], other[values, :], preferred_element_type=F32
        )
        flat[j] = acc / totals[j]
    store_heads(size, k, flat, made, attended, sem, ())


def chained_call(size, kernel, args, state, shapes, scratch, flops):
    args = [vmem(x) for x in args]
    many = len(args)
    out = pl.pallas_call(
        kernel,
        in_specs=[IN_VMEM] * many + [IN_HBM, IN_HBM],
        out_specs=[IN_HBM, IN_HBM] + [IN_VMEM] * len(shapes),
        out_shape=[pltpu.HBM(x.shape, x.dtype) for x in state] + shapes,
        scratch_shapes=scratch,
        input_output_aliases={many: 0, many + 1: 1},
        compiler_params=LIMIT,
        cost_estimate=pl.CostEstimate(
            flops=flops,
            bytes_accessed=8 * size.span * size.channels,
            transcendentals=2 * size.mine * size.wide * size.span,
        ),
    )(*args, *state)
    return tuple(out[:2]), out[2:]


def body(deltas, anchors, chan_scale, lengths, route, new_query, new_kv):
    n = lax.axis_size("pool")
    size = Sizes(deltas, anchors, new_query, n)
    both = (0, 1)
    order = sorted(range(1, n), key=lambda k: (min(k, n - k), k))
    last = order[-1]
    plan = [(k, both) for k in order[:-1]] + [(last, (0,)), (last, (1,)), (0, both)]
    query, fresh = arrange(size, new_query, new_kv)
    message = {}
    for part in (plan[:1], plan[1:]):
        for (k, parts), msg in zip(part, pack(size, part, route, lengths, deltas, anchors, chan_scale)):
            if k:
                msg = lax.ppermute(msg, "pool", list(enumerate(far(n, k))))
            message[k, parts] = msg

    def swapped(x):
        return lax.ppermute(x, "sub", [(0, 1), (1, 0)])

    flops = 8 * size.mine * size.wide * size.span * HEAD_DIM
    rows = [
        pltpu.VMEM((size.steps, size.q_local * HEAD_DIM), BF),
        pltpu.VMEM((size.mine, size.wide, HEAD_DIM), F32),
        pltpu.SemaphoreType.DMA,
    ]
    sems = pltpu.SemaphoreType.DMA((2, 2 * size.mine))
    wide = pltpu.VMEM((size.mine, size.wide, HEAD_DIM), F32)

    def attend(k, mine, other, theirs, state):
        state, _ = chained_call(
            size, functools.partial(attend_kernel, size, k),
            (query, fresh, message[k, both], mine, other, theirs), state, [], rows + [sems], flops,
        )
        return state

    def take(k, parts, state):
        tables = None if 0 in parts else message[last, (0,)]
        state, mine, theirs = rebuild(size, parts, message[k, parts], tables, state)
        return state, mine, swapped(theirs), theirs

    state, held = None, []
    for k in [0] + order[:-1]:
        state, *each = take(k, both, state)
        held.append((k, *each))
        if k and k != order[-2]:
            state = attend(*held.pop(0), state)
    state, *keys = take(last, (0,), state)
    for each in held:
        state = attend(*each, state)
    state, (weights, share, totals) = chained_call(
        size, functools.partial(weights_kernel, size, last),
        (query, fresh, message[last, (0,)], *keys), state,
        [pltpu.VMEM((size.mine, size.wide, 2 * size.span), BF), wide, wide], [sems], flops // 2,
    )
    state, mine, other, theirs = take(last, (1,), state)
    state, (half,) = chained_call(
        size, functools.partial(half_kernel, size, last),
        (weights, share, mine, theirs), state, [wide], [sems], flops // 4,
    )
    state, _ = chained_call(
        size, functools.partial(finish_kernel, size, last),
        (weights, half, totals, other), state, [], rows, flops // 4,
    )
    return state


def solution(mesh):
    placed = (
        P(("parts", "pool"), None, "sub", "tp"),
        P(("parts", "pool"), None, "sub", "tp"),
        P(("parts", "pool"), None, "tp"),
        P(("parts", "pool")),
        P(("parts", "pool")),
        P(("parts", "pool"), None, ("tp", "sub")),
        P(("parts", "pool"), None, None, "tp"),
    )
    return jax.shard_map(
        body,
        mesh=mesh,
        in_specs=placed,
        out_specs=(
            P(("parts", "pool"), None, "sub", "tp"),
            P(("parts", "pool"), None, ("tp", "sub")),
        ),
        check_vma=False,
    )
```

```python
import functools
import math

import jax
import jax.numpy as jnp
from jax import lax
from jax.experimental import pallas as pl
from jax.experimental.pallas import tpu as pltpu
from jax.sharding import PartitionSpec as P

HEAD_DIM = 128
Q_PER_KV = 8
TILE = 16
BF = jnp.bfloat16
F32 = jnp.float32
LOW = -1e30
NT = (((1,), (1,)), ((), ()))

IN_VMEM = pl.BlockSpec(memory_space=pltpu.VMEM)
IN_SMEM = pl.BlockSpec(memory_space=pltpu.SMEM)
IN_HBM = pl.BlockSpec(memory_space=pltpu.HBM)
LIMIT = pltpu.CompilerParams(vmem_limit_bytes=16 * 1024 * 1024)


def vmem(x):
    return pltpu.with_memory_space_constraint(x, pltpu.VMEM)


def hbm(x):
    return pltpu.with_memory_space_constraint(x, pltpu.HBM)


def far(n, k):
    ring = (0, 2, 3, 1) if n == 4 else tuple(range(n))
    return tuple(ring[(ring.index(z) + k) % n] for z in range(n))


def pick(values, at):
    out = jnp.int32(values[0])
    for i, value in enumerate(values[1:], 1):
        out = jnp.where(at == i, jnp.int32(value), out)
    return out


class Sizes:
    def __init__(self, deltas, anchors, new_query, n):
        self.n = n
        self.count, _, self.span, self.channels = deltas.shape
        self.rows = anchors.shape[2]
        self.repeat = self.span // self.rows
        self.steps = new_query.shape[1]
        self.heads = self.channels // HEAD_DIM
        self.q_local = new_query.shape[2] // HEAD_DIM
        self.mine = max(1, self.q_local // Q_PER_KV)
        self.group = self.q_local // self.mine
        self.wide = self.group * self.steps

    def anchor_at(self, which, parts):
        return (len(parts) * self.span + parts.index(which) * self.rows) * self.heads

    def side_at(self, parts):
        return len(parts) * self.heads * (self.span + self.rows)

    def message_rows(self, parts):
        return self.side_at(parts) + (TILE if 0 in parts else 0)

    def source_row(self, k):
        return pick(far(self.n, self.n - k), lax.axis_index("pool"))


def side_block(size, scale, length):
    row = lax.broadcasted_iota(jnp.int32, (TILE, HEAD_DIM), 0)
    scale = scale.astype(F32)
    out = jnp.where(row == 2 * size.heads, length.astype(F32), jnp.float32(0.0))
    for which in range(2):
        for h in range(size.heads):
            piece = scale[which:which + 1, h * HEAD_DIM:(h + 1) * HEAD_DIM]
            out = jnp.where(row == which * size.heads + h, piece, out)
    return out.astype(BF)


def pack_kernel(size, plan, route, lengths, deltas, anchors, scale, *rest):
    outs, (held, tables, sems) = rest[:-3], rest[-3:]
    z = lax.axis_index("pool")
    work = []
    for m, (k, parts) in enumerate(plan):
        dest = pick(far(size.n, k), z)
        index = jnp.int32(0)
        for j in range(size.count):
            index = jnp.where(route[j] == dest, jnp.int32(j), index)
        for which in parts:
            slot = len(work)
            copies = (
                pltpu.make_async_copy(deltas.at[index, which], held.at[slot], sems.at[0, slot]),
                pltpu.make_async_copy(anchors.at[index, which], tables.at[slot], sems.at[1, slot]),
            )
            for copy in copies:
                copy.start()
            work.append((outs[m], parts, which, slot, copies))
        if 0 in parts:
            outs[m][pl.ds(size.side_at(parts), TILE), :] = side_block(size, scale[index], lengths[index])
    for msg, parts, which, slot, copies in work:
        for copy in copies:
            copy.wait()
        for h in range(size.heads):
            lanes = slice(h * HEAD_DIM, (h + 1) * HEAD_DIM)
            at = (parts.index(which) * size.heads + h) * size.span
            msg[at:at + size.span, :] = held[slot, :, lanes]
            at = size.anchor_at(which, parts) + h * size.rows
            msg[at:at + size.rows, :] = tables[slot, :, lanes]


def pack(size, plan, route, lengths, deltas, anchors, scale):
    shapes = [pltpu.VMEM((size.message_rows(parts), HEAD_DIM), BF) for _, parts in plan]
    slots = sum(len(parts) for _, parts in plan)
    return pl.pallas_call(
        functools.partial(pack_kernel, size, plan),
        out_shape=shapes,
        in_specs=[IN_SMEM, IN_SMEM, IN_HBM, IN_HBM, IN_VMEM],
        out_specs=[IN_VMEM] * len(shapes),
        scratch_shapes=[
            pltpu.VMEM((slots, size.span, size.channels), BF),
            pltpu.VMEM((slots, size.rows, size.channels), BF),
            pltpu.SemaphoreType.DMA((2, slots)),
        ],
        compiler_params=LIMIT,
        cost_estimate=pl.CostEstimate(
            flops=0, bytes_accessed=2 * slots * size.span * size.channels, transcendentals=0
        ),
    )(hbm(route), hbm(lengths), hbm(deltas), hbm(anchors), hbm(scale))


def arrange_kernel(size, new_query, new_kv, query, fresh, wide, tall):
    sub = lax.axis_index("sub")
    rest = size.heads - size.mine
    tall[...] = jnp.zeros_like(tall)
    for r in range(size.count):
        for j in range(size.mine):
            for g in range(size.group):
                at = (j * size.group + g) * HEAD_DIM
                piece = new_query[r, :, at:at + HEAD_DIM].astype(F32)
                wide[g * size.steps:(g + 1) * size.steps, :] = piece
            query[r, j] = wide[...].astype(BF)
            for which in range(2):
                own, other = (
                    new_kv[r, which, :, h * HEAD_DIM:(h + 1) * HEAD_DIM].astype(F32) for h in (j, j + rest)
                )
                tall[:size.steps, :] = jnp.where(sub == 0, own, other)
                fresh[r, which, j] = tall[...].astype(BF)


def arrange(size, new_query, new_kv):
    return pl.pallas_call(
        functools.partial(arrange_kernel, size),
        in_specs=[IN_VMEM, IN_VMEM],
        out_specs=[IN_VMEM, IN_VMEM],
        out_shape=[
            pltpu.VMEM((size.count, size.mine, size.wide, HEAD_DIM), BF),
            pltpu.VMEM((size.count, 2, size.mine, TILE, HEAD_DIM), BF),
        ],
        scratch_shapes=[pltpu.VMEM((size.wide, HEAD_DIM), F32), pltpu.VMEM((TILE, HEAD_DIM), F32)],
        compiler_params=LIMIT,
    )(hbm(new_query), hbm(new_kv))


def row_copies(size, k, parts, cache, mine, theirs, sems):
    sub = lax.axis_index("sub")
    row = size.source_row(k)
    rest = size.heads - size.mine
    copies = []
    for o, (out, first) in enumerate(((mine, sub * rest), (theirs, (1 - sub) * rest))):
        if o and not rest:
            break
        for p, which in enumerate(parts):
            for j in range(size.mine):
                lanes = pl.ds(pl.multiple_of((first + j) * HEAD_DIM, HEAD_DIM), HEAD_DIM)
                at = (p * size.mine + j) * size.span
                copies.append(pltpu.make_async_copy(
                    out.at[pl.ds(at, size.span)],
                    cache.at[row, which, :, lanes],
                    sems.at[o, p * size.mine + j],
                ))
    return copies


def rebuild_heads(size, parts, message, tables, mine, theirs):
    sub = lax.axis_index("sub")
    rest = size.heads - size.mine
    side_at = size.side_at(parts if 0 in parts else (0,))
    side = tables[side_at:side_at + TILE, :].astype(F32)
    length = side[2 * size.heads:2 * size.heads + 1, :]
    base = sub * size.span
    for o, out in enumerate((theirs, mine)):
        first = (1 - sub) * rest if o == 0 else sub * rest
        other = sub == 0 if o == 0 else sub != 0
        for p, which in enumerate(parts):
            for j in range(size.mine):
                h = which * size.heads + j
                scale = jnp.where(other, side[h + rest:h + rest + 1, :], side[h:h + 1, :])
                table = pl.multiple_of(
                    size.anchor_at(which, parts) + (first + j) * size.rows, TILE
                )
                anchor = message[pl.ds(table, size.rows), :].astype(F32)
                source = (p * size.heads + first + j) * size.span
                to = (p * size.mine + j) * size.span
                for i in range(size.rows):
                    at = pl.multiple_of(source + i * size.repeat, TILE)
                    value = anchor[i:i + 1, :] + scale * message[pl.ds(at, size.repeat), :].astype(F32)
                    keep = (base + i * size.repeat).astype(F32) < length
                    value = jnp.where(keep, value, jnp.float32(0.0)).astype(BF)
                    out[to + i * size.repeat:to + (i + 1) * size.repeat, :] = value


def rebuild_kernel(size, parts, chained, message, *refs):
    _, _, mine, theirs = refs[2 * chained:]
    rebuild_heads(size, parts, message, message, mine, theirs)


def rebuild(size, parts, message, state):
    args = [vmem(message)]
    in_specs = [IN_VMEM] * len(args)
    aliases = {}
    if state is not None:
        aliases = {len(args): 0, len(args) + 1: 1}
        args += list(state)
        in_specs += [IN_HBM, IN_HBM]
    given = (len(parts) * size.mine * size.span, HEAD_DIM)
    out = pl.pallas_call(
        functools.partial(rebuild_kernel, size, parts, state is not None),
        in_specs=in_specs,
        out_specs=[IN_HBM, IN_HBM, IN_VMEM, IN_VMEM],
        out_shape=[
            pltpu.HBM((size.count, 2, size.span, size.channels), BF),
            pltpu.HBM((size.count, size.steps, size.q_local * HEAD_DIM), BF),
            pltpu.VMEM(given, BF),
            pltpu.VMEM(given, BF),
        ],
        input_output_aliases=aliases,
        compiler_params=LIMIT,
        cost_estimate=pl.CostEstimate(
            flops=4 * len(parts) * size.span * size.channels,
            bytes_accessed=6 * len(parts) * size.span * size.channels,
            transcendentals=0,
        ),
    )(*args)
    return tuple(out[:2]), out[2], out[3]


def weigh(size, j, q, new_key, key_mine, key_other, live_mine, live_other, causal):
    factor = 1.0 / math.sqrt(HEAD_DIM)
    s0 = lax.dot_general(q, key_mine, NT, preferred_element_type=F32) * factor
    s1 = lax.dot_general(q, key_other, NT, preferred_element_type=F32) * factor
    s2 = lax.dot_general(q, new_key, NT, preferred_element_type=F32) * factor
    s0 = jnp.where(live_mine, s0, jnp.float32(LOW))
    s1 = jnp.where(live_other, s1, jnp.float32(LOW))
    s2 = jnp.where(causal, s2, jnp.float32(LOW))
    top = jnp.maximum(
        jnp.max(jnp.maximum(s0, s1), axis=1, keepdims=True), jnp.max(s2, axis=1, keepdims=True)
    )
    w0 = jnp.where(live_mine, jnp.exp(s0 - top), jnp.float32(0.0))
    w1 = jnp.where(live_other, jnp.exp(s1 - top), jnp.float32(0.0))
    w2 = jnp.where(causal, jnp.exp(s2 - top), jnp.float32(0.0))
    total = jnp.sum(w0 + w1, axis=1, keepdims=True) + jnp.sum(w2, axis=1, keepdims=True)
    return w0.astype(BF), w1.astype(BF), w2.astype(BF), total


def masks(size, tables, parts, fresh):
    sub = lax.axis_index("sub")
    at = size.side_at(parts)
    side = tables[at:at + TILE, :].astype(F32)
    length = side[2 * size.heads:2 * size.heads + 1, 0:1]
    spot = lax.broadcasted_iota(jnp.int32, (1, size.span), 1)
    live_mine = (spot + sub * size.span).astype(F32) < length
    live_other = (spot + (1 - sub) * size.span).astype(F32) < length
    step = lax.broadcasted_iota(jnp.int32, (size.wide, fresh), 0) % size.steps
    token = lax.broadcasted_iota(jnp.int32, (size.wide, fresh), 1)
    return live_mine, live_other, (token <= step) & (token < size.steps)


def start_store(size, k, parts, cache, mine, theirs, sems):
    copies = row_copies(size, k, parts, cache, mine, theirs, sems)
    for copy in copies:
        copy.start()
    return copies


def store_heads(size, k, flat, made, attended, sem, copies):
    for j in range(size.mine):
        for g in range(size.group):
            at = (j * size.group + g) * HEAD_DIM
            made[:, at:at + HEAD_DIM] = flat[j, g * size.steps:(g + 1) * size.steps, :].astype(BF)
    copy = pltpu.make_async_copy(made, attended.at[size.source_row(k)], sem)
    copy.start()
    for each in copies:
        each.wait()
    copy.wait()


def attend_kernel(size, k, query, new_kv, tables, mine, other, theirs, *refs):
    cache, attended, made, flat, sem, sems = refs[2:]
    row = size.source_row(k)
    copies = start_store(size, k, (0, 1), cache, mine, theirs, sems)
    live_mine, live_other, causal = masks(size, tables, (0, 1), new_kv.shape[3])
    for j in range(size.mine):
        keys = slice(j * size.span, (j + 1) * size.span)
        values = slice((size.mine + j) * size.span, (size.mine + j + 1) * size.span)
        w0, w1, w2, total = weigh(
            size, j, query[row, j], new_kv[row, 0, j], mine[keys, :], other[keys, :],
            live_mine, live_other, causal,
        )
        acc = jnp.dot(w0, mine[values, :], preferred_element_type=F32)
        acc = acc + jnp.dot(w1, other[values, :], preferred_element_type=F32)
        acc = acc + jnp.dot(w2, new_kv[row, 1, j], preferred_element_type=F32)
        flat[j] = acc / total
    store_heads(size, k, flat, made, attended, sem, copies)


def weights_kernel(size, k, query, new_kv, tables, mine, other, theirs, *refs):
    cache, _, weights, lent, share, totals, sems = refs[2:]
    row = size.source_row(k)
    copies = start_store(size, k, (0,), cache, mine, theirs, sems)
    live_mine, live_other, causal = masks(size, tables, (0,), new_kv.shape[3])
    for j in range(size.mine):
        keys = slice(j * size.span, (j + 1) * size.span)
        w0, w1, w2, total = weigh(
            size, j, query[row, j], new_kv[row, 0, j], mine[keys, :], other[keys, :],
            live_mine, live_other, causal,
        )
        weights[j] = w0
        lent[j] = w1
        share[j] = jnp.dot(w2, new_kv[row, 1, j], preferred_element_type=F32)
        totals[j] = jnp.broadcast_to(total, totals.shape[1:])
    for copy in copies:
        copy.wait()


def values_kernel(size, weights, share, lent, message, tables, *refs):
    _, _, mine, theirs, kept, given = refs[2:]
    rebuild_heads(size, (1,), message, tables, mine, theirs)
    for j in range(size.mine):
        values = slice(j * size.span, (j + 1) * size.span)
        kept[j] = share[j] + jnp.dot(weights[j], mine[values, :], preferred_element_type=F32)
        given[j] = jnp.dot(lent[j], theirs[values, :], preferred_element_type=F32)


def store_kernel(size, k, mine, theirs, *refs):
    cache, _, sems = refs[2:]
    for copy in start_store(size, k, (1,), cache, mine, theirs, sems):
        copy.wait()


def finish_kernel(size, k, kept, got, totals, *refs):
    _, attended, made, flat, sem = refs[2:]
    for j in range(size.mine):
        flat[j] = (kept[j] + got[j]) / totals[j]
    store_heads(size, k, flat, made, attended, sem, ())


def chained_call(size, kernel, args, state, shapes, scratch, flops):
    args = [vmem(x) for x in args]
    many = len(args)
    out = pl.pallas_call(
        kernel,
        in_specs=[IN_VMEM] * many + [IN_HBM, IN_HBM],
        out_specs=[IN_HBM, IN_HBM] + [IN_VMEM] * len(shapes),
        out_shape=[pltpu.HBM(x.shape, x.dtype) for x in state] + shapes,
        scratch_shapes=scratch,
        input_output_aliases={many: 0, many + 1: 1},
        compiler_params=LIMIT,
        cost_estimate=pl.CostEstimate(
            flops=flops,
            bytes_accessed=8 * size.span * size.channels,
            transcendentals=2 * size.mine * size.wide * size.span,
        ),
    )(*args, *state)
    return tuple(out[:2]), out[2:]


def body(deltas, anchors, chan_scale, lengths, route, new_query, new_kv):
    n = lax.axis_size("pool")
    size = Sizes(deltas, anchors, new_query, n)
    both = (0, 1)
    order = sorted(range(1, n), key=lambda k: (min(k, n - k), k))
    last = order[-1]
    plan = [(k, both) for k in order[:-1]] + [(last, (0,)), (last, (1,)), (0, both)]
    query, fresh = arrange(size, new_query, new_kv)
    message = {}
    for part in (plan[:1], plan[1:]):
        for (k, parts), msg in zip(part, pack(size, part, route, lengths, deltas, anchors, chan_scale)):
            if k:
                msg = lax.ppermute(msg, "pool", list(enumerate(far(n, k))))
            message[k, parts] = msg

    def swapped(x):
        return lax.ppermute(x, "sub", [(0, 1), (1, 0)])

    flops = 8 * size.mine * size.wide * size.span * HEAD_DIM
    rows = [
        pltpu.VMEM((size.steps, size.q_local * HEAD_DIM), BF),
        pltpu.VMEM((size.mine, size.wide, HEAD_DIM), F32),
        pltpu.SemaphoreType.DMA,
    ]
    sems = pltpu.SemaphoreType.DMA((2, 2 * size.mine))
    wide = pltpu.VMEM((size.mine, size.wide, HEAD_DIM), F32)

    def attend(k, mine, other, theirs, state):
        state, _ = chained_call(
            size, functools.partial(attend_kernel, size, k),
            (query, fresh, message[k, both], mine, other, theirs), state, [], rows + [sems], flops,
        )
        return state

    def take(k, parts, state):
        state, mine, theirs = rebuild(size, parts, message[k, parts], state)
        return state, mine, swapped(theirs), theirs

    state, held = None, []
    for k in [0] + order[:-1]:
        state, *each = take(k, both, state)
        held.append((k, *each))
        if k:
            state = attend(*held.pop(0), state)
    state = attend(*held.pop(0), state)
    state, *keys = take(last, (0,), state)
    half = pltpu.VMEM((size.mine, size.wide, size.span), BF)
    state, (weights, lent, share, totals) = chained_call(
        size, functools.partial(weights_kernel, size, last),
        (query, fresh, message[last, (0,)], *keys), state, [half, half, wide, wide], [sems], flops // 2,
    )
    given = pltpu.VMEM((size.mine * size.span, HEAD_DIM), BF)
    state, (mine, theirs, kept, given) = chained_call(
        size, functools.partial(values_kernel, size),
        (weights, share, swapped(lent), message[last, (1,)], message[last, (0,)]), state,
        [given, given, wide, wide], [], flops // 2,
    )
    got = swapped(given)
    state, _ = chained_call(
        size, functools.partial(store_kernel, size, last), (mine, theirs), state, [], [sems], 0
    )
    state, _ = chained_call(
        size, functools.partial(finish_kernel, size, last), (kept, got, totals), state, [], rows, 0
    )
    return state


def solution(mesh):
    placed = (
        P(("parts", "pool"), None, "sub", "tp"),
        P(("parts", "pool"), None, "sub", "tp"),
        P(("parts", "pool"), None, "tp"),
        P(("parts", "pool")),
        P(("parts", "pool")),
        P(("parts", "pool"), None, ("tp", "sub")),
        P(("parts", "pool"), None, None, "tp"),
    )
    return jax.shard_map(
        body,
        mesh=mesh,
        in_specs=placed,
        out_specs=(
            P(("parts", "pool"), None, "sub", "tp"),
            P(("parts", "pool"), None, ("tp", "sub")),
        ),
        check_vma=False,
    )
```

```python
import functools
import math

import jax
import jax.numpy as jnp
from jax import lax
from jax.experimental import pallas as pl
from jax.experimental.pallas import tpu as pltpu
from jax.sharding import PartitionSpec as P

HEAD_DIM = 128
Q_PER_KV = 8
TILE = 16
PAGE = 128
BF = jnp.bfloat16
F32 = jnp.float32
LOW = -1e30
NT = (((1,), (1,)), ((), ()))

IN_VMEM = pl.BlockSpec(memory_space=pltpu.VMEM)
IN_SMEM = pl.BlockSpec(memory_space=pltpu.SMEM)
IN_HBM = pl.BlockSpec(memory_space=pltpu.HBM)
IN_ANY = pl.BlockSpec(memory_space=pl.ANY)
LIMIT = pltpu.CompilerParams(vmem_limit_bytes=16 * 1024 * 1024)


def vmem(x):
    return pltpu.with_memory_space_constraint(x, pltpu.VMEM)


def hbm(x):
    return pltpu.with_memory_space_constraint(x, pltpu.HBM)


class Sizes:
    def __init__(self, deltas, anchors, new_query, n):
        self.n = n
        self.count, _, self.span, self.channels = deltas.shape
        self.rows = anchors.shape[2]
        self.repeat = self.span // self.rows
        self.steps = new_query.shape[1]
        self.heads = self.channels // HEAD_DIM
        self.q_local = new_query.shape[2] // HEAD_DIM
        self.mine = max(1, self.q_local // Q_PER_KV)
        self.rest = self.heads - self.mine
        self.group = self.q_local // self.mine
        self.wide = self.group * self.steps
        self.pages = self.span // PAGE
        self.page_rows = PAGE // self.repeat

    def anchor_at(self, which, parts):
        return (len(parts) * self.span + parts.index(which) * self.rows) * self.heads

    def side_at(self, parts):
        return len(parts) * self.heads * (self.span + self.rows)

    def message_rows(self, parts):
        return self.side_at(parts) + (TILE if 0 in parts else 0)

    def page_anchor_at(self):
        return 2 * self.heads * PAGE

    def page_side_at(self):
        return 2 * self.heads * (PAGE + self.page_rows)

    def page_message_rows(self):
        return self.page_side_at() + TILE

    def partner(self, k):
        return lax.axis_index("pool") ^ k


def request_for(size, k, route):
    index = jnp.int32(0)
    for j in range(size.count):
        index = jnp.where(route[j] == size.partner(k), jnp.int32(j), index)
    return index


def side_block(size, scale, length):
    row = lax.broadcasted_iota(jnp.int32, (TILE, HEAD_DIM), 0)
    scale = scale.astype(F32)
    out = jnp.where(row == 2 * size.heads, length.astype(F32), jnp.float32(0.0))
    for which in range(2):
        for h in range(size.heads):
            piece = scale[which:which + 1, h * HEAD_DIM:(h + 1) * HEAD_DIM]
            out = jnp.where(row == which * size.heads + h, piece, out)
    return out.astype(BF)


def pack_kernel(size, plan, more, after, route, lengths, deltas, anchors, scale, *rest):
    outs, (held, tables, block, sems) = rest[after:-4], rest[-4:]
    sub = lax.axis_index("sub")
    work = []
    for slot, (low, high, paged) in enumerate(plan):
        index = request_for(size, jnp.where(sub == 0, low, high), route)
        copies = []
        for which in range(2):
            for source, target, s in ((deltas, held, 0), (anchors, tables, 1)):
                copy = pltpu.make_async_copy(
                    source.at[index, which], target.at[2 * slot + which], sems.at[s, 2 * slot + which]
                )
                copy.start()
                copies.append(copy)
        whole, outs = outs[0], outs[1:]
        pages, outs = (outs[:size.pages], outs[size.pages:]) if paged else ((), outs)
        work.append((2 * slot, paged, index, copies, whole, pages))
    for k, out in zip(more, outs):
        out[...] = jnp.full(out.shape, lengths[request_for(size, k, route)], jnp.int32)
    for slot, paged, index, copies, whole, pages in work:
        side = side_block(size, scale[index], lengths[index])
        for copy in copies:
            copy.wait()

        def fill_whole(slot=slot, side=side, msg=whole):
            for which in range(2):
                for h in range(size.heads):
                    lanes = slice(h * HEAD_DIM, (h + 1) * HEAD_DIM)
                    at = (which * size.heads + h) * size.span
                    msg[at:at + size.span, :] = held[slot + which, :, lanes]
                    at = size.anchor_at(which, (0, 1)) + h * size.rows
                    msg[at:at + size.rows, :] = tables[slot + which, :, lanes]
            msg[size.side_at((0, 1)):size.side_at((0, 1)) + TILE, :] = side

        def fill_pages(slot=slot, side=side, pages=pages):
            for page, msg in enumerate(pages):
                for which in range(2):
                    table = tables[slot + which].astype(F32)
                    for h in range(size.heads):
                        lanes = slice(h * HEAD_DIM, (h + 1) * HEAD_DIM)
                        at = (which * size.heads + h) * PAGE
                        msg[at:at + PAGE, :] = held[slot + which, page * PAGE:(page + 1) * PAGE, lanes]
                        at = (which * size.heads + h) * size.page_rows
                        first = page * size.page_rows
                        block[at:at + size.page_rows, :] = table[first:first + size.page_rows, lanes]
                msg[size.page_anchor_at():size.page_side_at(), :] = block[...].astype(BF)
                msg[size.page_side_at():size.page_side_at() + TILE, :] = side

        if paged:
            pl.when(sub == 0)(fill_whole)
            pl.when(sub != 0)(fill_pages)
        else:
            fill_whole()


def pack(size, plan, more, after, route, lengths, deltas, anchors, scale):
    shapes = []
    for _, _, paged in plan:
        shapes.append(pltpu.VMEM((size.message_rows((0, 1)), HEAD_DIM), BF))
        if paged:
            shapes += [pltpu.VMEM((size.page_message_rows(), HEAD_DIM), BF)] * size.pages
    shapes += [pltpu.VMEM((8, HEAD_DIM), jnp.int32)] * len(more)
    slots = 2 * len(plan)
    outs = pl.pallas_call(
        functools.partial(pack_kernel, size, plan, more, len(after)),
        out_shape=shapes,
        in_specs=[IN_SMEM, IN_SMEM, IN_HBM, IN_HBM, IN_VMEM] + [IN_ANY] * len(after),
        out_specs=[IN_VMEM] * len(shapes),
        scratch_shapes=[
            pltpu.VMEM((slots, size.span, size.channels), BF),
            pltpu.VMEM((slots, size.rows, size.channels), BF),
            pltpu.VMEM((2 * size.heads * size.page_rows, HEAD_DIM), F32),
            pltpu.SemaphoreType.DMA((2, slots)),
        ],
        compiler_params=LIMIT,
        cost_estimate=pl.CostEstimate(
            flops=0, bytes_accessed=2 * slots * size.span * size.channels, transcendentals=0
        ),
    )(hbm(route), hbm(lengths), hbm(deltas), hbm(anchors), hbm(scale), *after)
    if not isinstance(outs, (list, tuple)):
        outs = [outs]
    got = []
    for _, _, paged in plan:
        whole, outs = outs[0], outs[1:]
        pages, outs = (outs[:size.pages], outs[size.pages:]) if paged else ((), outs)
        got.append((whole, pages))
    return got, outs


def levels_kernel(size, many, *refs):
    sub = lax.axis_index("sub")
    for sent, got, out in zip(refs[:many], refs[many:2 * many], refs[2 * many + 2:]):
        longer = jnp.max(jnp.maximum(sent[...], got[...]))
        pages = (longer + (PAGE - 1)) // PAGE - size.pages
        out[0] = jnp.where(sub == 0, 0, jnp.clip(pages, 0, size.pages))


def levels_of(size, sent, got, state):
    many = len(sent)
    out = pl.pallas_call(
        functools.partial(levels_kernel, size, many),
        in_specs=[IN_VMEM] * (2 * many) + [IN_HBM, IN_HBM],
        out_specs=[IN_SMEM] * many + [IN_HBM, IN_HBM],
        out_shape=[jax.ShapeDtypeStruct((1,), jnp.int32)] * many
        + [pltpu.HBM(x.shape, x.dtype) for x in state],
        input_output_aliases={2 * many: many, 2 * many + 1: many + 1},
        compiler_params=LIMIT,
    )(*[vmem(x) for x in (*sent, *got)], *state)
    return out[:many], tuple(out[many:])


def arrange_kernel(size, new_query, new_kv, query, fresh, wide, tall):
    sub = lax.axis_index("sub")
    rest = size.heads - size.mine
    tall[...] = jnp.zeros_like(tall)
    for r in range(size.count):
        for j in range(size.mine):
            for g in range(size.group):
                at = (j * size.group + g) * HEAD_DIM
                piece = new_query[r, :, at:at + HEAD_DIM].astype(F32)
                wide[g * size.steps:(g + 1) * size.steps, :] = piece
            query[r, j] = wide[...].astype(BF)
            for which in range(2):
                own, other = (
                    new_kv[r, which, :, h * HEAD_DIM:(h + 1) * HEAD_DIM].astype(F32) for h in (j, j + rest)
                )
                tall[:size.steps, :] = jnp.where(sub == 0, own, other)
                fresh[r, which, j] = tall[...].astype(BF)


def arrange(size, new_query, new_kv):
    return pl.pallas_call(
        functools.partial(arrange_kernel, size),
        in_specs=[IN_VMEM, IN_VMEM],
        out_specs=[IN_VMEM, IN_VMEM],
        out_shape=[
            pltpu.VMEM((size.count, size.mine, size.wide, HEAD_DIM), BF),
            pltpu.VMEM((size.count, 2, size.mine, TILE, HEAD_DIM), BF),
        ],
        scratch_shapes=[pltpu.VMEM((size.wide, HEAD_DIM), F32), pltpu.VMEM((TILE, HEAD_DIM), F32)],
        compiler_params=LIMIT,
    )(hbm(new_query), hbm(new_kv))


def row_copies(size, k, parts, cache, mine, theirs, sems):
    sub = lax.axis_index("sub")
    row = size.partner(k)
    copies = []
    for o, (out, first) in enumerate(((mine, sub * size.rest), (theirs, (1 - sub) * size.rest))):
        if o and not size.rest:
            break
        for p, which in enumerate(parts):
            for j in range(size.mine):
                lanes = pl.ds(pl.multiple_of((first + j) * HEAD_DIM, HEAD_DIM), HEAD_DIM)
                at = (p * size.mine + j) * size.span
                copies.append(pltpu.make_async_copy(
                    out.at[pl.ds(at, size.span)],
                    cache.at[row, which, :, lanes],
                    sems.at[o, p * size.mine + j],
                ))
    return copies


def rebuild_kernel(size, paged, chained, gated, low, *refs):
    high, refs = (refs[:size.pages + 1], refs[size.pages + 1:]) if paged else (refs[:1], refs[1:])
    if gated:
        refs[-1][0] = refs[0][0]
    mine, theirs, limit = refs[gated + 2 * chained + 2:][:3]
    sub = lax.axis_index("sub")

    def fill(upper):
        if upper and paged:
            *pages, lens = high
            at = size.page_side_at()
            side = pages[0][at:at + TILE, :].astype(F32)
            blocks = [x[size.page_anchor_at():at, :].astype(F32) for x in pages]
            length = lens[0:1, :].astype(F32)
        else:
            message = high[0] if upper else low
            at = size.side_at((0, 1))
            side = message[at:at + TILE, :].astype(F32)
            length = side[2 * size.heads:2 * size.heads + 1, :]
        limit[...] = jnp.broadcast_to(length, limit.shape)
        for o, out in enumerate((theirs, mine)):
            first = size.rest if (o == 0) != upper else 0
            for which in range(2):
                for j in range(size.mine):
                    h = which * size.heads + first + j
                    scale = side[h:h + 1, :]
                    to = (which * size.mine + j) * size.span
                    if not (upper and paged):
                        at = size.anchor_at(which, (0, 1)) + (first + j) * size.rows
                        table = message[at:at + size.rows, :].astype(F32)
                    for i in range(size.rows):
                        if upper and paged:
                            page, r = divmod(i, size.page_rows)
                            anchor = blocks[page][h * size.page_rows + r:h * size.page_rows + r + 1, :]
                            at = h * PAGE + r * size.repeat
                            delta = pages[page][at:at + size.repeat, :]
                        else:
                            anchor = table[i:i + 1, :]
                            at = h * size.span + i * size.repeat
                            delta = message[at:at + size.repeat, :]
                        value = anchor + scale * delta.astype(F32)
                        keep = float(int(upper) * size.span + i * size.repeat) < length
                        value = jnp.where(keep, value, jnp.float32(0.0)).astype(BF)
                        out[to + i * size.repeat:to + (i + 1) * size.repeat, :] = value

    pl.when(sub == 0)(functools.partial(fill, False))
    pl.when(sub != 0)(functools.partial(fill, True))


def rebuild(size, low, high, gate, state):
    args = [vmem(x) for x in (low, *high)]
    in_specs = [IN_VMEM] * len(args) + [IN_SMEM] * len(gate)
    args += list(gate)
    aliases = {}
    if state is not None:
        aliases = {len(args): 0, len(args) + 1: 1}
        args += list(state)
        in_specs += [IN_HBM, IN_HBM]
    given = (2 * size.mine * size.span, HEAD_DIM)
    out = pl.pallas_call(
        functools.partial(rebuild_kernel, size, len(high) > 1, state is not None, len(gate)),
        in_specs=in_specs,
        out_specs=[IN_HBM, IN_HBM, IN_VMEM, IN_VMEM, IN_VMEM] + [IN_SMEM] * len(gate),
        out_shape=[
            pltpu.HBM((size.count, 2, size.span, size.channels), BF),
            pltpu.HBM((size.count, size.steps, size.q_local * HEAD_DIM), BF),
            pltpu.VMEM(given, BF),
            pltpu.VMEM(given, BF),
            pltpu.VMEM((8, HEAD_DIM), F32),
        ] + [jax.ShapeDtypeStruct((1,), jnp.int32)] * len(gate),
        input_output_aliases=aliases,
        compiler_params=LIMIT,
        cost_estimate=pl.CostEstimate(
            flops=8 * size.span * size.channels,
            bytes_accessed=12 * size.span * size.channels,
            transcendentals=0,
        ),
    )(*args)
    return tuple(out[:2]), out[2:5], out[5:]


def weigh(size, j, q, new_key, key_mine, key_other, live_mine, live_other, causal):
    factor = 1.0 / math.sqrt(HEAD_DIM)
    s0 = lax.dot_general(q, key_mine, NT, preferred_element_type=F32) * factor
    s1 = lax.dot_general(q, key_other, NT, preferred_element_type=F32) * factor
    s2 = lax.dot_general(q, new_key, NT, preferred_element_type=F32) * factor
    s0 = jnp.where(live_mine, s0, jnp.float32(LOW))
    s1 = jnp.where(live_other, s1, jnp.float32(LOW))
    s2 = jnp.where(causal, s2, jnp.float32(LOW))
    top = jnp.maximum(
        jnp.max(jnp.maximum(s0, s1), axis=1, keepdims=True), jnp.max(s2, axis=1, keepdims=True)
    )
    w0 = jnp.where(live_mine, jnp.exp(s0 - top), jnp.float32(0.0))
    w1 = jnp.where(live_other, jnp.exp(s1 - top), jnp.float32(0.0))
    w2 = jnp.where(causal, jnp.exp(s2 - top), jnp.float32(0.0))
    total = jnp.sum(w0 + w1, axis=1, keepdims=True) + jnp.sum(w2, axis=1, keepdims=True)
    return w0.astype(BF), w1.astype(BF), w2.astype(BF), total


def masks(size, length, fresh):
    sub = lax.axis_index("sub")
    limit = length[0:1, 0:1]
    spot = lax.broadcasted_iota(jnp.int32, (1, size.span), 1)
    live_mine = (spot + sub * size.span).astype(F32) < limit
    live_other = (spot + (1 - sub) * size.span).astype(F32) < limit
    step = lax.broadcasted_iota(jnp.int32, (size.wide, fresh), 0) % size.steps
    token = lax.broadcasted_iota(jnp.int32, (size.wide, fresh), 1)
    return live_mine, live_other, (token <= step) & (token < size.steps)


def start_store(size, k, parts, cache, mine, theirs, sems):
    copies = row_copies(size, k, parts, cache, mine, theirs, sems)
    for copy in copies:
        copy.start()
    return copies


def store_heads(size, k, flat, made, attended, sem, copies):
    for j in range(size.mine):
        for g in range(size.group):
            at = (j * size.group + g) * HEAD_DIM
            made[:, at:at + HEAD_DIM] = flat[j, g * size.steps:(g + 1) * size.steps, :].astype(BF)
    copy = pltpu.make_async_copy(made, attended.at[size.partner(k)], sem)
    copy.start()
    for each in copies:
        each.wait()
    copy.wait()


def attend_kernel(size, k, after, query, new_kv, length, mine, other, theirs, *refs):
    cache, attended, made, flat, sem, sems = refs[after + 2:]
    row = size.partner(k)
    copies = start_store(size, k, (0, 1), cache, mine, theirs, sems)
    live_mine, live_other, causal = masks(size, length, new_kv.shape[3])
    for j in range(size.mine):
        keys = slice(j * size.span, (j + 1) * size.span)
        values = slice((size.mine + j) * size.span, (size.mine + j + 1) * size.span)
        w0, w1, w2, total = weigh(
            size, j, query[row, j], new_kv[row, 0, j], mine[keys, :], other[keys, :],
            live_mine, live_other, causal,
        )
        acc = jnp.dot(w0, mine[values, :], preferred_element_type=F32)
        acc = acc + jnp.dot(w1, other[values, :], preferred_element_type=F32)
        acc = acc + jnp.dot(w2, new_kv[row, 1, j], preferred_element_type=F32)
        flat[j] = acc / total
    store_heads(size, k, flat, made, attended, sem, copies)


def attend(size, k, query, fresh, length, mine, other, theirs, after, state):
    args = [vmem(x) for x in (query, fresh, length, mine, other, theirs)]
    in_specs = [IN_VMEM] * len(args) + [IN_ANY] * len(after) + [IN_HBM, IN_HBM]
    args += list(after)
    flops = 8 * size.mine * size.wide * size.span * HEAD_DIM
    return tuple(pl.pallas_call(
        functools.partial(attend_kernel, size, k, len(after)),
        in_specs=in_specs,
        out_specs=[IN_HBM, IN_HBM],
        out_shape=[pltpu.HBM(x.shape, x.dtype) for x in state],
        scratch_shapes=[
            pltpu.VMEM((size.steps, size.q_local * HEAD_DIM), BF),
            pltpu.VMEM((size.mine, size.wide, HEAD_DIM), F32),
            pltpu.SemaphoreType.DMA,
            pltpu.SemaphoreType.DMA((2, 2 * size.mine)),
        ],
        input_output_aliases={len(args): 0, len(args) + 1: 1},
        compiler_params=LIMIT,
        cost_estimate=pl.CostEstimate(
            flops=flops,
            bytes_accessed=8 * size.span * size.channels,
            transcendentals=2 * size.mine * size.wide * size.span,
        ),
    )(*args, *state))


def body(deltas, anchors, chan_scale, lengths, route, new_query, new_kv):
    n = lax.axis_size("pool")
    size = Sizes(deltas, anchors, new_query, n)
    raw = (route, lengths, deltas, anchors, chan_scale)
    others = list(range(2, n))
    lows = [1] + others[1:]

    def move(x, low=None, high=None):
        pairs = []
        for z in range(n):
            if low is not None:
                pairs.append((2 * z, 2 * (z ^ low)))
            if high is not None:
                pairs.append((2 * z + 1, 2 * (z ^ high) + 1))
        return lax.ppermute(x, ("pool", "sub"), pairs)

    def upper(level, pages, k):
        def branch(many):
            return lambda *xs: tuple(move(x, high=k) if i < many else x for i, x in enumerate(xs))
        return lax.switch(level.reshape(()), [branch(many) for many in range(size.pages + 1)], *pages)

    def swapped(x):
        return lax.ppermute(x, "sub", [(0, 1), (1, 0)])

    [(front, _)], _ = pack(size, [(2, 1, False)], [], (), *raw)
    mixed, sent = pack(
        size, [(low, k, True) for low, k in zip(lows, others)] + [(0, 0, False)], others, (), *raw
    )
    front = move(front, 2, 1)
    got = [move(x, high=k) for x, k in zip(sent, others)]
    whole = {low: move(x, low) for low, (x, _) in zip(lows, mixed)}
    whole[2] = front
    paged = {k: pages for k, (_, pages) in zip(others, mixed)}
    query, fresh = arrange(size, new_query, new_kv)

    own = mixed[-1][0]
    state, (mine, theirs, length), _ = rebuild(size, own, [own], (), None)
    state = attend(size, 0, query, fresh, length, mine, swapped(theirs), theirs, (), state)
    levels, state = levels_of(size, sent, got, state)
    levels = dict(zip(others, levels))
    arrived = dict(zip(others, got))
    held = []

    def take(k, high, gate, state):
        state, (mine, theirs, length), gate = rebuild(size, whole[k], high, gate, state)
        held.append((k, query, fresh, length, mine, swapped(theirs), theirs))
        return state, gate

    pages = upper(levels[2], paged[2], 2)
    state, _ = take(2, [*pages, arrived[2]], (), state)
    state, gate = take(1, [front], [levels[k] for k in others[1:2]], state)
    for at, k in enumerate(others[1:], 1):
        pages = upper(gate[0], paged[k], k)
        for each in held:
            state = attend(size, *each, pages[:1], state)
        held.clear()
        state, gate = take(k, [*pages, arrived[k]], [levels[j] for j in others[at + 1:at + 2]], state)
    for each in held:
        state = attend(size, *each, (), state)
    return state


def solution(mesh):
    placed = (
        P(("parts", "pool"), None, "sub", "tp"),
        P(("parts", "pool"), None, "sub", "tp"),
        P(("parts", "pool"), None, "tp"),
        P(("parts", "pool")),
        P(("parts", "pool")),
        P(("parts", "pool"), None, ("tp", "sub")),
        P(("parts", "pool"), None, None, "tp"),
    )
    return jax.shard_map(
        body,
        mesh=mesh,
        in_specs=placed,
        out_specs=(
            P(("parts", "pool"), None, "sub", "tp"),
            P(("parts", "pool"), None, ("tp", "sub")),
        ),
        check_vma=False,
    )
```

```python
import functools
import math

import jax
import jax.numpy as jnp
from jax import lax
from jax.experimental import pallas as pl
from jax.experimental.pallas import tpu as pltpu
from jax.sharding import PartitionSpec as P

HEAD_DIM = 128
Q_PER_KV = 8
TILE = 16
PAGE = 128
BF = jnp.bfloat16
F32 = jnp.float32
LOW = -1e30
NT = (((1,), (1,)), ((), ()))

IN_VMEM = pl.BlockSpec(memory_space=pltpu.VMEM)
IN_SMEM = pl.BlockSpec(memory_space=pltpu.SMEM)
IN_HBM = pl.BlockSpec(memory_space=pltpu.HBM)
LIMIT = pltpu.CompilerParams(vmem_limit_bytes=16 * 1024 * 1024)


def vmem(x):
    return pltpu.with_memory_space_constraint(x, pltpu.VMEM)


def hbm(x):
    return pltpu.with_memory_space_constraint(x, pltpu.HBM)


class Sizes:
    def __init__(self, deltas, anchors, new_query, n):
        self.n = n
        self.count, _, self.span, self.channels = deltas.shape
        self.rows = anchors.shape[2]
        self.repeat = self.span // self.rows
        self.steps = new_query.shape[1]
        self.heads = self.channels // HEAD_DIM
        self.q_local = new_query.shape[2] // HEAD_DIM
        self.mine = max(1, self.q_local // Q_PER_KV)
        self.rest = self.heads - self.mine
        self.group = self.q_local // self.mine
        self.wide = self.group * self.steps
        self.pages = self.span // PAGE
        self.page_rows = PAGE // self.repeat

    def anchor_at(self, which, parts):
        return (len(parts) * self.span + parts.index(which) * self.rows) * self.heads

    def side_at(self, parts):
        return len(parts) * self.heads * (self.span + self.rows)

    def message_rows(self, parts):
        return self.side_at(parts) + (TILE if 0 in parts else 0)

    def page_anchor_at(self):
        return 2 * self.heads * PAGE

    def page_side_at(self):
        return 2 * self.heads * (PAGE + self.page_rows)

    def page_message_rows(self, pages=1):
        return pages * (self.page_side_at() + TILE)

    def partner(self, k):
        return lax.axis_index("pool") ^ k


def request_for(size, k, route):
    index = jnp.int32(0)
    for j in range(size.count):
        index = jnp.where(route[j] == size.partner(k), jnp.int32(j), index)
    return index


def side_block(size, scale, length):
    row = lax.broadcasted_iota(jnp.int32, (TILE, HEAD_DIM), 0)
    scale = scale.astype(F32)
    out = jnp.where(row == 2 * size.heads, length.astype(F32), jnp.float32(0.0))
    for which in range(2):
        for h in range(size.heads):
            piece = scale[which:which + 1, h * HEAD_DIM:(h + 1) * HEAD_DIM]
            out = jnp.where(row == which * size.heads + h, piece, out)
    return out.astype(BF)


def pack_kernel(size, plan, more, route, lengths, deltas, anchors, scale, *rest):
    outs, (held, tables, block, sems) = rest[:-4], rest[-4:]
    sub = lax.axis_index("sub")
    work = []
    for slot, (low, high, kind) in enumerate(plan):
        index = request_for(size, jnp.where(sub == 0, low, high), route)
        copies = []
        for which in range(2):
            for source, target, s in ((deltas, held, 0), (anchors, tables, 1)):
                copy = pltpu.make_async_copy(
                    source.at[index, which], target.at[2 * slot + which], sems.at[s, 2 * slot + which]
                )
                copy.start()
                copies.append(copy)
        many = outputs_of(size, kind)
        work.append((2 * slot, kind, index, copies, outs[:many]))
        outs = outs[many:]
    for k, out in zip(more, outs):
        out[...] = jnp.full(out.shape, lengths[request_for(size, k, route)], jnp.int32)
    for slot, kind, index, copies, msgs in work:
        side = side_block(size, scale[index], lengths[index])
        for copy in copies:
            copy.wait()

        def fill_whole(msg, slot=slot, side=side):
            for which in range(2):
                for h in range(size.heads):
                    lanes = slice(h * HEAD_DIM, (h + 1) * HEAD_DIM)
                    at = (which * size.heads + h) * size.span
                    msg[at:at + size.span, :] = held[slot + which, :, lanes]
                    at = size.anchor_at(which, (0, 1)) + h * size.rows
                    msg[at:at + size.rows, :] = tables[slot + which, :, lanes]
            msg[size.side_at((0, 1)):size.side_at((0, 1)) + TILE, :] = side

        def fill_pages(slot=slot, side=side, msgs=msgs[1:]):
            for page in range(size.pages):
                base = page * size.page_message_rows()
                for which in range(2):
                    table = tables[slot + which].astype(F32)
                    for h in range(size.heads):
                        lanes = slice(h * HEAD_DIM, (h + 1) * HEAD_DIM)
                        at = base + (which * size.heads + h) * PAGE
                        for msg in msgs[page:]:
                            msg[at:at + PAGE, :] = held[slot + which, page * PAGE:(page + 1) * PAGE, lanes]
                        at = (which * size.heads + h) * size.page_rows
                        first = page * size.page_rows
                        block[at:at + size.page_rows, :] = table[first:first + size.page_rows, lanes]
                at, end = base + size.page_anchor_at(), base + size.page_side_at()
                for msg in msgs[page:]:
                    msg[at:end, :] = block[...].astype(BF)
                    msg[end:end + TILE, :] = side

        if kind == "own":
            fill_whole(msgs[0])
        else:
            pl.when(sub == 0)(functools.partial(fill_whole, msgs[0]))
            pl.when(sub != 0)(fill_pages if kind == "pages" else functools.partial(fill_whole, msgs[1]))


def outputs_of(size, kind):
    return {"own": 1, "front": 2, "pages": 1 + size.pages}[kind]


def pack(size, plan, more, route, lengths, deltas, anchors, scale):
    shapes = []
    for _, _, kind in plan:
        rows = [size.message_rows((0, 1))] * (1 if kind != "front" else 2)
        if kind == "pages":
            rows += [size.page_message_rows(p + 1) for p in range(size.pages)]
        shapes += [pltpu.VMEM((r, HEAD_DIM), BF) for r in rows]
    shapes += [pltpu.VMEM((8, HEAD_DIM), jnp.int32)] * len(more)
    slots = 2 * len(plan)
    outs = pl.pallas_call(
        functools.partial(pack_kernel, size, plan, more),
        out_shape=shapes,
        in_specs=[IN_SMEM, IN_SMEM, IN_HBM, IN_HBM, IN_VMEM],
        out_specs=[IN_VMEM] * len(shapes),
        scratch_shapes=[
            pltpu.VMEM((slots, size.span, size.channels), BF),
            pltpu.VMEM((slots, size.rows, size.channels), BF),
            pltpu.VMEM((2 * size.heads * size.page_rows, HEAD_DIM), F32),
            pltpu.SemaphoreType.DMA((2, slots)),
        ],
        compiler_params=LIMIT,
        cost_estimate=pl.CostEstimate(
            flops=0, bytes_accessed=2 * slots * size.span * size.channels, transcendentals=0
        ),
    )(hbm(route), hbm(lengths), hbm(deltas), hbm(anchors), hbm(scale))
    got = []
    for _, _, kind in plan:
        many = outputs_of(size, kind)
        got.append(outs[:many])
        outs = outs[many:]
    return got, outs


def levels_kernel(size, many, *refs):
    sub = lax.axis_index("sub")
    for sent, got, out in zip(refs[:many], refs[many:2 * many], refs[2 * many + 1:]):
        longer = jnp.max(jnp.maximum(sent[...], got[...]))
        pages = (longer + (PAGE - 1)) // PAGE - size.pages
        out[0] = jnp.where(sub == 0, 0, jnp.clip(pages, 0, size.pages))


def levels_of(size, sent, got, message):
    many = len(sent)
    out = pl.pallas_call(
        functools.partial(levels_kernel, size, many),
        in_specs=[IN_VMEM] * (2 * many + 1),
        out_specs=[IN_SMEM] * many + [IN_VMEM],
        out_shape=[jax.ShapeDtypeStruct((1,), jnp.int32)] * many + [pltpu.VMEM(message.shape, BF)],
        input_output_aliases={2 * many: many},
        compiler_params=LIMIT,
    )(*[vmem(x) for x in (*sent, *got, message)])
    return out[:many], out[many]


def arrange_kernel(size, new_query, new_kv, query, fresh, wide, tall):
    sub = lax.axis_index("sub")
    rest = size.heads - size.mine
    tall[...] = jnp.zeros_like(tall)
    for r in range(size.count):
        for j in range(size.mine):
            for g in range(size.group):
                at = (j * size.group + g) * HEAD_DIM
                piece = new_query[r, :, at:at + HEAD_DIM].astype(F32)
                wide[g * size.steps:(g + 1) * size.steps, :] = piece
            query[r, j] = wide[...].astype(BF)
            for which in range(2):
                own, other = (
                    new_kv[r, which, :, h * HEAD_DIM:(h + 1) * HEAD_DIM].astype(F32) for h in (j, j + rest)
                )
                tall[:size.steps, :] = jnp.where(sub == 0, own, other)
                fresh[r, which, j] = tall[...].astype(BF)


def arrange(size, new_query, new_kv):
    return pl.pallas_call(
        functools.partial(arrange_kernel, size),
        in_specs=[IN_VMEM, IN_VMEM],
        out_specs=[IN_VMEM, IN_VMEM],
        out_shape=[
            pltpu.VMEM((size.count, size.mine, size.wide, HEAD_DIM), BF),
            pltpu.VMEM((size.count, 2, size.mine, TILE, HEAD_DIM), BF),
        ],
        scratch_shapes=[pltpu.VMEM((size.wide, HEAD_DIM), F32), pltpu.VMEM((TILE, HEAD_DIM), F32)],
        compiler_params=LIMIT,
    )(hbm(new_query), hbm(new_kv))


def row_copies(size, k, parts, cache, mine, theirs, sems):
    sub = lax.axis_index("sub")
    row = size.partner(k)
    copies = []
    for o, (out, first) in enumerate(((mine, sub * size.rest), (theirs, (1 - sub) * size.rest))):
        if o and not size.rest:
            break
        for p, which in enumerate(parts):
            for j in range(size.mine):
                lanes = pl.ds(pl.multiple_of((first + j) * HEAD_DIM, HEAD_DIM), HEAD_DIM)
                at = (p * size.mine + j) * size.span
                copies.append(pltpu.make_async_copy(
                    out.at[pl.ds(at, size.span)],
                    cache.at[row, which, :, lanes],
                    sems.at[o, p * size.mine + j],
                ))
    return copies


def rebuild_kernel(size, paged, chained, gated, low, *refs):
    high, refs = refs[:1 + paged], refs[1 + paged:]
    mine, theirs, limit = refs[gated + 2 * chained + 2:][:3]
    sub = lax.axis_index("sub")

    def fill(upper):
        if upper and paged:
            pages, lens = high
            at = size.page_side_at()
            side = pages[at:at + TILE, :].astype(F32)
            bases = [p * size.page_message_rows() for p in range(size.pages)]
            blocks = [pages[x + size.page_anchor_at():x + at, :].astype(F32) for x in bases]
            length = lens[0:1, :].astype(F32)
        else:
            message = high[0] if upper else low
            at = size.side_at((0, 1))
            side = message[at:at + TILE, :].astype(F32)
            length = side[2 * size.heads:2 * size.heads + 1, :]
        limit[...] = jnp.broadcast_to(length, limit.shape)
        for o, out in enumerate((theirs, mine)):
            first = size.rest if (o == 0) != upper else 0
            for which in range(2):
                for j in range(size.mine):
                    h = which * size.heads + first + j
                    scale = side[h:h + 1, :]
                    to = (which * size.mine + j) * size.span
                    if not (upper and paged):
                        at = size.anchor_at(which, (0, 1)) + (first + j) * size.rows
                        table = message[at:at + size.rows, :].astype(F32)
                    for i in range(size.rows):
                        if upper and paged:
                            page, r = divmod(i, size.page_rows)
                            anchor = blocks[page][h * size.page_rows + r:h * size.page_rows + r + 1, :]
                            at = bases[page] + h * PAGE + r * size.repeat
                            delta = pages[at:at + size.repeat, :]
                        else:
                            anchor = table[i:i + 1, :]
                            at = h * size.span + i * size.repeat
                            delta = message[at:at + size.repeat, :]
                        value = anchor + scale * delta.astype(F32)
                        keep = float(int(upper) * size.span + i * size.repeat) < length
                        value = jnp.where(keep, value, jnp.float32(0.0)).astype(BF)
                        out[to + i * size.repeat:to + (i + 1) * size.repeat, :] = value

    pl.when(sub == 0)(functools.partial(fill, False))
    pl.when(sub != 0)(functools.partial(fill, True))


def rebuild(size, low, high, gate, state):
    args = [vmem(x) for x in (low, *high, *gate)]
    in_specs = [IN_VMEM] * len(args)
    aliases = {len(args) - 1: 5} if gate else {}
    if state is not None:
        aliases |= {len(args): 0, len(args) + 1: 1}
        args += list(state)
        in_specs += [IN_HBM, IN_HBM]
    given = (2 * size.mine * size.span, HEAD_DIM)
    out = pl.pallas_call(
        functools.partial(rebuild_kernel, size, len(high) > 1, state is not None, len(gate)),
        in_specs=in_specs,
        out_specs=[IN_HBM, IN_HBM, IN_VMEM, IN_VMEM, IN_VMEM] + [IN_VMEM] * len(gate),
        out_shape=[
            pltpu.HBM((size.count, 2, size.span, size.channels), BF),
            pltpu.HBM((size.count, size.steps, size.q_local * HEAD_DIM), BF),
            pltpu.VMEM(given, BF),
            pltpu.VMEM(given, BF),
            pltpu.VMEM((8, HEAD_DIM), F32),
        ] + [pltpu.VMEM(x.shape, BF) for x in gate],
        input_output_aliases=aliases,
        compiler_params=LIMIT,
        cost_estimate=pl.CostEstimate(
            flops=8 * size.span * size.channels,
            bytes_accessed=12 * size.span * size.channels,
            transcendentals=0,
        ),
    )(*args)
    return tuple(out[:2]), out[2:5], out[5:]


def weigh(size, j, q, new_key, key_mine, key_other, live_mine, live_other, causal):
    factor = 1.0 / math.sqrt(HEAD_DIM)
    s0 = lax.dot_general(q, key_mine, NT, preferred_element_type=F32) * factor
    s1 = lax.dot_general(q, key_other, NT, preferred_element_type=F32) * factor
    s2 = lax.dot_general(q, new_key, NT, preferred_element_type=F32) * factor
    s0 = jnp.where(live_mine, s0, jnp.float32(LOW))
    s1 = jnp.where(live_other, s1, jnp.float32(LOW))
    s2 = jnp.where(causal, s2, jnp.float32(LOW))
    top = jnp.maximum(
        jnp.max(jnp.maximum(s0, s1), axis=1, keepdims=True), jnp.max(s2, axis=1, keepdims=True)
    )
    w0 = jnp.where(live_mine, jnp.exp(s0 - top), jnp.float32(0.0))
    w1 = jnp.where(live_other, jnp.exp(s1 - top), jnp.float32(0.0))
    w2 = jnp.where(causal, jnp.exp(s2 - top), jnp.float32(0.0))
    total = jnp.sum(w0 + w1, axis=1, keepdims=True) + jnp.sum(w2, axis=1, keepdims=True)
    return w0.astype(BF), w1.astype(BF), w2.astype(BF), total


def masks(size, length, fresh):
    sub = lax.axis_index("sub")
    limit = length[0:1, 0:1]
    spot = lax.broadcasted_iota(jnp.int32, (1, size.span), 1)
    live_mine = (spot + sub * size.span).astype(F32) < limit
    live_other = (spot + (1 - sub) * size.span).astype(F32) < limit
    step = lax.broadcasted_iota(jnp.int32, (size.wide, fresh), 0) % size.steps
    token = lax.broadcasted_iota(jnp.int32, (size.wide, fresh), 1)
    return live_mine, live_other, (token <= step) & (token < size.steps)


def start_store(size, k, parts, cache, mine, theirs, sems):
    copies = row_copies(size, k, parts, cache, mine, theirs, sems)
    for copy in copies:
        copy.start()
    return copies


def store_heads(size, k, flat, made, attended, sem, copies):
    for j in range(size.mine):
        for g in range(size.group):
            at = (j * size.group + g) * HEAD_DIM
            made[:, at:at + HEAD_DIM] = flat[j, g * size.steps:(g + 1) * size.steps, :].astype(BF)
    copy = pltpu.make_async_copy(made, attended.at[size.partner(k)], sem)
    copy.start()
    for each in copies:
        each.wait()
    copy.wait()


def attend_kernel(size, k, after, gated, query, new_kv, length, mine, other, theirs, *refs):
    refs = refs[after + gated + 2:]
    cache, attended, (made, flat, sem, sems) = refs[0], refs[1], refs[-4:]
    row = size.partner(k)
    copies = start_store(size, k, (0, 1), cache, mine, theirs, sems)
    live_mine, live_other, causal = masks(size, length, new_kv.shape[3])
    for j in range(size.mine):
        keys = slice(j * size.span, (j + 1) * size.span)
        values = slice((size.mine + j) * size.span, (size.mine + j + 1) * size.span)
        w0, w1, w2, total = weigh(
            size, j, query[row, j], new_kv[row, 0, j], mine[keys, :], other[keys, :],
            live_mine, live_other, causal,
        )
        acc = jnp.dot(w0, mine[values, :], preferred_element_type=F32)
        acc = acc + jnp.dot(w1, other[values, :], preferred_element_type=F32)
        acc = acc + jnp.dot(w2, new_kv[row, 1, j], preferred_element_type=F32)
        flat[j] = acc / total
    store_heads(size, k, flat, made, attended, sem, copies)


def attend(size, k, query, fresh, length, mine, other, theirs, after, gate, state):
    args = [vmem(x) for x in (query, fresh, length, mine, other, theirs, *after, *gate)]
    in_specs = [IN_VMEM] * len(args) + [IN_HBM, IN_HBM]
    flops = 8 * size.mine * size.wide * size.span * HEAD_DIM
    aliases = {len(args): 0, len(args) + 1: 1} | ({len(args) - 1: 2} if gate else {})
    out = pl.pallas_call(
        functools.partial(attend_kernel, size, k, len(after), len(gate)),
        in_specs=in_specs,
        out_specs=[IN_HBM, IN_HBM] + [IN_VMEM] * len(gate),
        out_shape=[pltpu.HBM(x.shape, x.dtype) for x in state] + [pltpu.VMEM(x.shape, BF) for x in gate],
        scratch_shapes=[
            pltpu.VMEM((size.steps, size.q_local * HEAD_DIM), BF),
            pltpu.VMEM((size.mine, size.wide, HEAD_DIM), F32),
            pltpu.SemaphoreType.DMA,
            pltpu.SemaphoreType.DMA((2, 2 * size.mine)),
        ],
        input_output_aliases=aliases,
        compiler_params=LIMIT,
        cost_estimate=pl.CostEstimate(
            flops=flops,
            bytes_accessed=8 * size.span * size.channels,
            transcendentals=2 * size.mine * size.wide * size.span,
        ),
    )(*args, *state)
    return tuple(out[:2]), out[2:]


def body(deltas, anchors, chan_scale, lengths, route, new_query, new_kv):
    n = lax.axis_size("pool")
    size = Sizes(deltas, anchors, new_query, n)
    raw = (route, lengths, deltas, anchors, chan_scale)
    others = list(range(2, n))
    lows = [1] + others[1:]

    def move(x, low=None, high=None):
        pairs = []
        for z in range(n):
            if low is not None:
                pairs.append((2 * z, 2 * (z ^ low)))
            if high is not None:
                pairs.append((2 * z + 1, 2 * (z ^ high) + 1))
        return lax.ppermute(x, ("pool", "sub"), pairs)

    def upper(level, pages, k):
        def branch(many):
            def send(*xs):
                if many == 0:
                    return xs[-1]
                x = move(xs[many - 1], high=k)
                return x if many == size.pages else jnp.concatenate([x, xs[-1][x.shape[0]:]])
            return send
        return lax.switch(level.reshape(()), [branch(many) for many in range(size.pages + 1)], *pages)

    def swapped(x):
        return lax.ppermute(x, "sub", [(0, 1), (1, 0)])

    [(front, near)], sent = pack(size, [(2, 1, "front")], others, *raw)
    whole = {2: move(front, low=2)}
    got = [move(x, high=k) for x, k in zip(sent, others)]
    levels, near = levels_of(size, sent, got, near)
    near = move(near, high=1)
    plan = [(low, k, "pages") for low, k in zip(lows, others)] + [(0, 0, "own")]
    mixed, _ = pack(size, plan, [], *raw)
    whole.update({low: move(x[0], low=low) for low, x in zip(lows, mixed)})
    paged = {k: list(x[1:]) for k, x in zip(others, mixed)}
    levels, arrived = dict(zip(others, levels)), dict(zip(others, got))
    query, fresh = arrange(size, new_query, new_kv)

    def gate_of(k):
        return [paged[k][-1]] if k in paged else []

    def opened(k, gate):
        if gate:
            paged[k][-1] = gate[0]

    held = []

    def take(k, high, following, state):
        gate = gate_of(following)
        state, (mine, theirs, length), gate = rebuild(size, whole[k], high, gate, state)
        opened(following, gate)
        held.append((k, query, fresh, length, mine, swapped(theirs), theirs))
        return state

    whole[0] = mixed[-1][0]
    state = take(0, [whole[0]], None, None)
    state, gate = attend(size, *held.pop(), (), gate_of(2), state)
    opened(2, gate)
    pages = upper(levels[2], paged[2], 2)
    state = take(2, [pages, arrived[2]], None, state)
    state = take(1, [near], 3, state)
    for k in others[1:]:
        pages = upper(levels[k], paged[k], k)
        for each in held:
            state, _ = attend(size, *each, [pages], (), state)
        held.clear()
        state = take(k, [pages, arrived[k]], k + 1, state)
    for each in held:
        state, _ = attend(size, *each, (), (), state)
    return state


def solution(mesh):
    placed = (
        P(("parts", "pool"), None, "sub", "tp"),
        P(("parts", "pool"), None, "sub", "tp"),
        P(("parts", "pool"), None, "tp"),
        P(("parts", "pool")),
        P(("parts", "pool")),
        P(("parts", "pool"), None, ("tp", "sub")),
        P(("parts", "pool"), None, None, "tp"),
    )
    return jax.shard_map(
        body,
        mesh=mesh,
        in_specs=placed,
        out_specs=(
            P(("parts", "pool"), None, "sub", "tp"),
            P(("parts", "pool"), None, ("tp", "sub")),
        ),
        check_vma=False,
    )
```

```python
import functools
import math

import jax
import jax.numpy as jnp
from jax import lax
from jax.experimental import pallas as pl
from jax.experimental.pallas import tpu as pltpu
from jax.sharding import PartitionSpec as P

HEAD_DIM = 128
Q_PER_KV = 8
TILE = 16
PAGE = 128
BF = jnp.bfloat16
F32 = jnp.float32
LOW = -1e30
NT = (((1,), (1,)), ((), ()))

IN_VMEM = pl.BlockSpec(memory_space=pltpu.VMEM)
IN_SMEM = pl.BlockSpec(memory_space=pltpu.SMEM)
IN_HBM = pl.BlockSpec(memory_space=pltpu.HBM)
LIMIT = pltpu.CompilerParams(vmem_limit_bytes=16 * 1024 * 1024)


def vmem(x):
    return pltpu.with_memory_space_constraint(x, pltpu.VMEM)


def hbm(x):
    return pltpu.with_memory_space_constraint(x, pltpu.HBM)


class Sizes:
    def __init__(self, deltas, anchors, new_query, n):
        self.n = n
        self.count, _, self.span, self.channels = deltas.shape
        self.rows = anchors.shape[2]
        self.repeat = self.span // self.rows
        self.steps = new_query.shape[1]
        self.heads = self.channels // HEAD_DIM
        self.q_local = new_query.shape[2] // HEAD_DIM
        self.mine = max(1, self.q_local // Q_PER_KV)
        self.rest = self.heads - self.mine
        self.group = self.q_local // self.mine
        self.wide = self.group * self.steps
        self.pages = self.span // PAGE
        self.page_rows = PAGE // self.repeat

    def anchor_at(self, which, parts):
        return (len(parts) * self.span + parts.index(which) * self.rows) * self.heads

    def side_at(self, parts):
        return len(parts) * self.heads * (self.span + self.rows)

    def message_rows(self, parts):
        return self.side_at(parts) + (TILE if 0 in parts else 0)

    def page_anchor_at(self):
        return 2 * self.heads * PAGE

    def page_side_at(self):
        return 2 * self.heads * (PAGE + self.page_rows)

    def page_message_rows(self, pages=1):
        return pages * (self.page_side_at() + TILE)

    def partner(self, k):
        return lax.axis_index("pool") ^ k


def request_for(size, k, route):
    index = jnp.int32(0)
    for j in range(size.count):
        index = jnp.where(route[j] == size.partner(k), jnp.int32(j), index)
    return index


def side_block(size, scale, length):
    row = lax.broadcasted_iota(jnp.int32, (TILE, HEAD_DIM), 0)
    scale = scale.astype(F32)
    out = jnp.where(row == 2 * size.heads, length.astype(F32), jnp.float32(0.0))
    for which in range(2):
        for h in range(size.heads):
            piece = scale[which:which + 1, h * HEAD_DIM:(h + 1) * HEAD_DIM]
            out = jnp.where(row == which * size.heads + h, piece, out)
    return out.astype(BF)


def pack_kernel(size, plan, more, route, lengths, deltas, anchors, scale, *rest):
    outs, (held, tables, block, sems) = rest[:-4], rest[-4:]
    sub = lax.axis_index("sub")
    work = []
    for slot, (low, high, kind) in enumerate(plan):
        index = request_for(size, jnp.where(sub == 0, low, high), route)
        copies = []
        for which in range(2):
            for source, target, s in ((deltas, held, 0), (anchors, tables, 1)):
                copy = pltpu.make_async_copy(
                    source.at[index, which], target.at[2 * slot + which], sems.at[s, 2 * slot + which]
                )
                copy.start()
                copies.append(copy)
        many = outputs_of(size, kind)
        work.append((2 * slot, kind, index, copies, outs[:many]))
        outs = outs[many:]
    for k, out in zip(more, outs):
        out[...] = jnp.full(out.shape, lengths[request_for(size, k, route)], jnp.int32)
    for slot, kind, index, copies, msgs in work:
        side = side_block(size, scale[index], lengths[index])
        for copy in copies:
            copy.wait()

        def fill_whole(msg, slot=slot, side=side):
            for which in range(2):
                for h in range(size.heads):
                    lanes = slice(h * HEAD_DIM, (h + 1) * HEAD_DIM)
                    at = (which * size.heads + h) * size.span
                    msg[at:at + size.span, :] = held[slot + which, :, lanes]
                    at = size.anchor_at(which, (0, 1)) + h * size.rows
                    msg[at:at + size.rows, :] = tables[slot + which, :, lanes]
            msg[size.side_at((0, 1)):size.side_at((0, 1)) + TILE, :] = side

        def fill_pages(slot=slot, side=side, msgs=msgs[1:]):
            for page in range(size.pages):
                base = page * size.page_message_rows()
                for which in range(2):
                    table = tables[slot + which].astype(F32)
                    for h in range(size.heads):
                        lanes = slice(h * HEAD_DIM, (h + 1) * HEAD_DIM)
                        at = base + (which * size.heads + h) * PAGE
                        for msg in msgs[page:]:
                            msg[at:at + PAGE, :] = held[slot + which, page * PAGE:(page + 1) * PAGE, lanes]
                        at = (which * size.heads + h) * size.page_rows
                        first = page * size.page_rows
                        block[at:at + size.page_rows, :] = table[first:first + size.page_rows, lanes]
                at, end = base + size.page_anchor_at(), base + size.page_side_at()
                for msg in msgs[page:]:
                    msg[at:end, :] = block[...].astype(BF)
                    msg[end:end + TILE, :] = side

        if kind == "pages":
            pl.when(sub == 0)(functools.partial(fill_whole, msgs[0]))
            pl.when(sub != 0)(fill_pages)
        else:
            fill_whole(msgs[0])


def outputs_of(size, kind):
    return 1 + size.pages if kind == "pages" else 1


def pack(size, plan, more, route, lengths, deltas, anchors, scale):
    shapes = []
    for _, _, kind in plan:
        rows = [size.message_rows((0, 1))]
        if kind == "pages":
            rows += [size.page_message_rows(p + 1) for p in range(size.pages)]
        shapes += [pltpu.VMEM((r, HEAD_DIM), BF) for r in rows]
    shapes += [pltpu.VMEM((8, HEAD_DIM), jnp.int32)] * len(more)
    slots = 2 * len(plan)
    outs = pl.pallas_call(
        functools.partial(pack_kernel, size, plan, more),
        out_shape=shapes,
        in_specs=[IN_SMEM, IN_SMEM, IN_HBM, IN_HBM, IN_VMEM],
        out_specs=[IN_VMEM] * len(shapes),
        scratch_shapes=[
            pltpu.VMEM((slots, size.span, size.channels), BF),
            pltpu.VMEM((slots, size.rows, size.channels), BF),
            pltpu.VMEM((2 * size.heads * size.page_rows, HEAD_DIM), F32),
            pltpu.SemaphoreType.DMA((2, slots)),
        ],
        compiler_params=LIMIT,
        cost_estimate=pl.CostEstimate(
            flops=0, bytes_accessed=2 * slots * size.span * size.channels, transcendentals=0
        ),
    )(hbm(route), hbm(lengths), hbm(deltas), hbm(anchors), hbm(scale))
    outs = outs if isinstance(outs, (list, tuple)) else [outs]
    got = []
    for _, _, kind in plan:
        many = outputs_of(size, kind)
        got.append(outs[:many])
        outs = outs[many:]
    return got, outs


def levels_kernel(size, many, *refs):
    sub = lax.axis_index("sub")
    for sent, got, out in zip(refs[:many], refs[many:2 * many], refs[2 * many + 1:]):
        longer = jnp.max(jnp.maximum(sent[...], got[...]))
        pages = (longer + (PAGE - 1)) // PAGE - size.pages
        out[0] = jnp.where(sub == 0, 0, jnp.clip(pages, 0, size.pages))


def levels_of(size, sent, got, after):
    many = len(sent)
    return pl.pallas_call(
        functools.partial(levels_kernel, size, many),
        in_specs=[IN_VMEM] * (2 * many + 1),
        out_specs=[IN_SMEM] * many,
        out_shape=[jax.ShapeDtypeStruct((1,), jnp.int32)] * many,
        compiler_params=LIMIT,
    )(*[vmem(x) for x in (*sent, *got, after)])


def arrange_kernel(size, new_query, new_kv, query, fresh, wide, tall):
    sub = lax.axis_index("sub")
    rest = size.heads - size.mine
    tall[...] = jnp.zeros_like(tall)
    for r in range(size.count):
        for j in range(size.mine):
            for g in range(size.group):
                at = (j * size.group + g) * HEAD_DIM
                piece = new_query[r, :, at:at + HEAD_DIM].astype(F32)
                wide[g * size.steps:(g + 1) * size.steps, :] = piece
            query[r, j] = wide[...].astype(BF)
            for which in range(2):
                own, other = (
                    new_kv[r, which, :, h * HEAD_DIM:(h + 1) * HEAD_DIM].astype(F32) for h in (j, j + rest)
                )
                tall[:size.steps, :] = jnp.where(sub == 0, own, other)
                fresh[r, which, j] = tall[...].astype(BF)


def arrange(size, new_query, new_kv):
    return pl.pallas_call(
        functools.partial(arrange_kernel, size),
        in_specs=[IN_VMEM, IN_VMEM],
        out_specs=[IN_VMEM, IN_VMEM],
        out_shape=[
            pltpu.VMEM((size.count, size.mine, size.wide, HEAD_DIM), BF),
            pltpu.VMEM((size.count, 2, size.mine, TILE, HEAD_DIM), BF),
        ],
        scratch_shapes=[pltpu.VMEM((size.wide, HEAD_DIM), F32), pltpu.VMEM((TILE, HEAD_DIM), F32)],
        compiler_params=LIMIT,
    )(hbm(new_query), hbm(new_kv))


def row_copies(size, k, parts, cache, mine, theirs, sems):
    sub = lax.axis_index("sub")
    row = size.partner(k)
    copies = []
    for o, (out, first) in enumerate(((mine, sub * size.rest), (theirs, (1 - sub) * size.rest))):
        if o and not size.rest:
            break
        for p, which in enumerate(parts):
            for j in range(size.mine):
                lanes = pl.ds(pl.multiple_of((first + j) * HEAD_DIM, HEAD_DIM), HEAD_DIM)
                at = (p * size.mine + j) * size.span
                copies.append(pltpu.make_async_copy(
                    out.at[pl.ds(at, size.span)],
                    cache.at[row, which, :, lanes],
                    sems.at[o, p * size.mine + j],
                ))
    return copies


def rebuild_kernel(size, paged, chained, gated, low, *refs):
    high, refs = refs[:1 + paged], refs[1 + paged:]
    mine, theirs, limit = refs[gated + 2 * chained + 2:][:3]
    sub = lax.axis_index("sub")

    def fill(upper):
        if upper and paged:
            pages, lens = high
            at = size.page_side_at()
            side = pages[at:at + TILE, :].astype(F32)
            bases = [p * size.page_message_rows() for p in range(size.pages)]
            blocks = [pages[x + size.page_anchor_at():x + at, :].astype(F32) for x in bases]
            length = lens[0:1, :].astype(F32)
        else:
            message = high[0] if upper else low
            at = size.side_at((0, 1))
            side = message[at:at + TILE, :].astype(F32)
            length = side[2 * size.heads:2 * size.heads + 1, :]
        limit[...] = jnp.broadcast_to(length, limit.shape)
        for o, out in enumerate((theirs, mine)):
            first = size.rest if (o == 0) != upper else 0
            for which in range(2):
                for j in range(size.mine):
                    h = which * size.heads + first + j
                    scale = side[h:h + 1, :]
                    to = (which * size.mine + j) * size.span
                    if not (upper and paged):
                        at = size.anchor_at(which, (0, 1)) + (first + j) * size.rows
                        table = message[at:at + size.rows, :].astype(F32)
                    for i in range(size.rows):
                        if upper and paged:
                            page, r = divmod(i, size.page_rows)
                            anchor = blocks[page][h * size.page_rows + r:h * size.page_rows + r + 1, :]
                            at = bases[page] + h * PAGE + r * size.repeat
                            delta = pages[at:at + size.repeat, :]
                        else:
                            anchor = table[i:i + 1, :]
                            at = h * size.span + i * size.repeat
                            delta = message[at:at + size.repeat, :]
                        value = anchor + scale * delta.astype(F32)
                        keep = float(int(upper) * size.span + i * size.repeat) < length
                        value = jnp.where(keep, value, jnp.float32(0.0)).astype(BF)
                        out[to + i * size.repeat:to + (i + 1) * size.repeat, :] = value

    pl.when(sub == 0)(functools.partial(fill, False))
    pl.when(sub != 0)(functools.partial(fill, True))


def rebuild(size, low, high, gate, state):
    args = [vmem(x) for x in (low, *high, *gate)]
    in_specs = [IN_VMEM] * len(args)
    aliases = {len(args) - 1: 5} if gate else {}
    if state is not None:
        aliases |= {len(args): 0, len(args) + 1: 1}
        args += list(state)
        in_specs += [IN_HBM, IN_HBM]
    given = (2 * size.mine * size.span, HEAD_DIM)
    out = pl.pallas_call(
        functools.partial(rebuild_kernel, size, len(high) > 1, state is not None, len(gate)),
        in_specs=in_specs,
        out_specs=[IN_HBM, IN_HBM, IN_VMEM, IN_VMEM, IN_VMEM] + [IN_VMEM] * len(gate),
        out_shape=[
            pltpu.HBM((size.count, 2, size.span, size.channels), BF),
            pltpu.HBM((size.count, size.steps, size.q_local * HEAD_DIM), BF),
            pltpu.VMEM(given, BF),
            pltpu.VMEM(given, BF),
            pltpu.VMEM((8, HEAD_DIM), F32),
        ] + [pltpu.VMEM(x.shape, BF) for x in gate],
        input_output_aliases=aliases,
        compiler_params=LIMIT,
        cost_estimate=pl.CostEstimate(
            flops=8 * size.span * size.channels,
            bytes_accessed=12 * size.span * size.channels,
            transcendentals=0,
        ),
    )(*args)
    return tuple(out[:2]), out[2:5], out[5:]


def weigh(size, j, q, new_key, key_mine, key_other, live_mine, live_other, causal):
    factor = 1.0 / math.sqrt(HEAD_DIM)
    s0 = lax.dot_general(q, key_mine, NT, preferred_element_type=F32) * factor
    s1 = lax.dot_general(q, key_other, NT, preferred_element_type=F32) * factor
    s2 = lax.dot_general(q, new_key, NT, preferred_element_type=F32) * factor
    s0 = jnp.where(live_mine, s0, jnp.float32(LOW))
    s1 = jnp.where(live_other, s1, jnp.float32(LOW))
    s2 = jnp.where(causal, s2, jnp.float32(LOW))
    top = jnp.maximum(
        jnp.max(jnp.maximum(s0, s1), axis=1, keepdims=True), jnp.max(s2, axis=1, keepdims=True)
    )
    w0 = jnp.where(live_mine, jnp.exp(s0 - top), jnp.float32(0.0))
    w1 = jnp.where(live_other, jnp.exp(s1 - top), jnp.float32(0.0))
    w2 = jnp.where(causal, jnp.exp(s2 - top), jnp.float32(0.0))
    total = jnp.sum(w0 + w1, axis=1, keepdims=True) + jnp.sum(w2, axis=1, keepdims=True)
    return w0.astype(BF), w1.astype(BF), w2.astype(BF), total


def masks(size, length, fresh):
    sub = lax.axis_index("sub")
    limit = length[0:1, 0:1]
    spot = lax.broadcasted_iota(jnp.int32, (1, size.span), 1)
    live_mine = (spot + sub * size.span).astype(F32) < limit
    live_other = (spot + (1 - sub) * size.span).astype(F32) < limit
    step = lax.broadcasted_iota(jnp.int32, (size.wide, fresh), 0) % size.steps
    token = lax.broadcasted_iota(jnp.int32, (size.wide, fresh), 1)
    return live_mine, live_other, (token <= step) & (token < size.steps)


def start_store(size, k, parts, cache, mine, theirs, sems):
    copies = row_copies(size, k, parts, cache, mine, theirs, sems)
    for copy in copies:
        copy.start()
    return copies


def store_heads(size, k, flat, made, attended, sem, copies):
    for j in range(size.mine):
        for g in range(size.group):
            at = (j * size.group + g) * HEAD_DIM
            made[:, at:at + HEAD_DIM] = flat[j, g * size.steps:(g + 1) * size.steps, :].astype(BF)
    copy = pltpu.make_async_copy(made, attended.at[size.partner(k)], sem)
    copy.start()
    for each in copies:
        each.wait()
    copy.wait()


def attend_kernel(size, k, after, gated, query, new_kv, length, mine, other, theirs, *refs):
    refs = refs[after + gated + 2:]
    cache, attended, (made, flat, sem, sems) = refs[0], refs[1], refs[-4:]
    row = size.partner(k)
    copies = start_store(size, k, (0, 1), cache, mine, theirs, sems)
    live_mine, live_other, causal = masks(size, length, new_kv.shape[3])
    for j in range(size.mine):
        keys = slice(j * size.span, (j + 1) * size.span)
        values = slice((size.mine + j) * size.span, (size.mine + j + 1) * size.span)
        w0, w1, w2, total = weigh(
            size, j, query[row, j], new_kv[row, 0, j], mine[keys, :], other[keys, :],
            live_mine, live_other, causal,
        )
        acc = jnp.dot(w0, mine[values, :], preferred_element_type=F32)
        acc = acc + jnp.dot(w1, other[values, :], preferred_element_type=F32)
        acc = acc + jnp.dot(w2, new_kv[row, 1, j], preferred_element_type=F32)
        flat[j] = acc / total
    store_heads(size, k, flat, made, attended, sem, copies)


def attend(size, k, query, fresh, length, mine, other, theirs, after, gate, state):
    args = [vmem(x) for x in (query, fresh, length, mine, other, theirs, *after, *gate)]
    in_specs = [IN_VMEM] * len(args) + [IN_HBM, IN_HBM]
    flops = 8 * size.mine * size.wide * size.span * HEAD_DIM
    aliases = {len(args): 0, len(args) + 1: 1} | ({len(args) - 1: 2} if gate else {})
    out = pl.pallas_call(
        functools.partial(attend_kernel, size, k, len(after), len(gate)),
        in_specs=in_specs,
        out_specs=[IN_HBM, IN_HBM] + [IN_VMEM] * len(gate),
        out_shape=[pltpu.HBM(x.shape, x.dtype) for x in state] + [pltpu.VMEM(x.shape, BF) for x in gate],
        scratch_shapes=[
            pltpu.VMEM((size.steps, size.q_local * HEAD_DIM), BF),
            pltpu.VMEM((size.mine, size.wide, HEAD_DIM), F32),
            pltpu.SemaphoreType.DMA,
            pltpu.SemaphoreType.DMA((2, 2 * size.mine)),
        ],
        input_output_aliases=aliases,
        compiler_params=LIMIT,
        cost_estimate=pl.CostEstimate(
            flops=flops,
            bytes_accessed=8 * size.span * size.channels,
            transcendentals=2 * size.mine * size.wide * size.span,
        ),
    )(*args, *state)
    return tuple(out[:2]), out[2:]


def body(deltas, anchors, chan_scale, lengths, route, new_query, new_kv):
    n = lax.axis_size("pool")
    size = Sizes(deltas, anchors, new_query, n)
    raw = (route, lengths, deltas, anchors, chan_scale)
    others = list(range(2, n))
    lows = [1] + others[1:]

    def move(x, low=None, high=None):
        pairs = []
        for z in range(n):
            if low is not None:
                pairs.append((2 * z, 2 * (z ^ low)))
            if high is not None:
                pairs.append((2 * z + 1, 2 * (z ^ high) + 1))
        return lax.ppermute(x, ("pool", "sub"), pairs)

    def upper(level, pages, k):
        def branch(many):
            def send(*xs):
                if many == 0:
                    return xs[-1]
                x = move(xs[many - 1], high=k)
                return x if many == size.pages else jnp.concatenate([x, xs[-1][x.shape[0]:]])
            return send
        return lax.switch(level.reshape(()), [branch(many) for many in range(size.pages + 1)], *pages)

    def swapped(x):
        return lax.ppermute(x, "sub", [(0, 1), (1, 0)])

    [(front,)], _ = pack(size, [(2, 1, "whole")], [], *raw)
    plan = [(low, k, "pages") for low, k in zip(lows, others)] + [(0, 0, "whole")]
    mixed, sent = pack(size, plan, others, *raw)
    front = move(front, 2, 1)
    got = [move(x, high=k) for x, k in zip(sent, others)]
    whole = {low: move(x[0], low=low) for low, x in zip(lows, mixed)}
    whole.update({2: front, 0: mixed[-1][0]})
    paged = {k: list(x[1:]) for k, x in zip(others, mixed)}
    query, fresh = arrange(size, new_query, new_kv)
    levels, arrived = dict(zip(others, levels_of(size, sent, got, fresh))), dict(zip(others, got))

    def gate_of(k):
        return [paged[k][-1]] if k in paged else []

    def opened(k, gate):
        if gate:
            paged[k][-1] = gate[0]

    held = []

    def take(k, high, following, state):
        gate = gate_of(following)
        state, (mine, theirs, length), gate = rebuild(size, whole[k], high, gate, state)
        opened(following, gate)
        held.append((k, query, fresh, length, mine, swapped(theirs), theirs))
        return state

    pages = upper(levels[2], paged[2], 2)
    state = take(2, [pages, arrived[2]], None, None)
    state = take(1, [front], None, state)
    state = take(0, [whole[0]], 3, state)
    for k in others[1:]:
        pages = upper(levels[k], paged[k], k)
        for each in held[::-1]:
            state, _ = attend(size, *each, [pages], (), state)
        held.clear()
        state = take(k, [pages, arrived[k]], k + 1, state)
    for each in held:
        state, _ = attend(size, *each, (), (), state)
    return state


def solution(mesh):
    placed = (
        P(("parts", "pool"), None, "sub", "tp"),
        P(("parts", "pool"), None, "sub", "tp"),
        P(("parts", "pool"), None, "tp"),
        P(("parts", "pool")),
        P(("parts", "pool")),
        P(("parts", "pool"), None, ("tp", "sub")),
        P(("parts", "pool"), None, None, "tp"),
    )
    return jax.shard_map(
        body,
        mesh=mesh,
        in_specs=placed,
        out_specs=(
            P(("parts", "pool"), None, "sub", "tp"),
            P(("parts", "pool"), None, ("tp", "sub")),
        ),
        check_vma=False,
    )
```

```python
import functools
import math

import jax
import jax.numpy as jnp
from jax import lax
from jax.experimental import pallas as pl
from jax.experimental.pallas import tpu as pltpu
from jax.sharding import PartitionSpec as P

HEAD_DIM = 128
Q_PER_KV = 8
TILE = 16
BF = jnp.bfloat16
F32 = jnp.float32
LOW = -1e30
NT = (((1,), (1,)), ((), ()))

IN_VMEM = pl.BlockSpec(memory_space=pltpu.VMEM)
IN_SMEM = pl.BlockSpec(memory_space=pltpu.SMEM)
IN_HBM = pl.BlockSpec(memory_space=pltpu.HBM)
LIMIT = pltpu.CompilerParams(vmem_limit_bytes=16 * 1024 * 1024)


def vmem(x):
    return pltpu.with_memory_space_constraint(x, pltpu.VMEM)


def hbm(x):
    return pltpu.with_memory_space_constraint(x, pltpu.HBM)


def far(n, k):
    return tuple(z ^ k for z in range(n))


def pick(values, at):
    out = jnp.int32(values[0])
    for i, value in enumerate(values[1:], 1):
        out = jnp.where(at == i, jnp.int32(value), out)
    return out


class Sizes:
    def __init__(self, deltas, anchors, new_query, n):
        self.n = n
        self.count, _, self.span, self.channels = deltas.shape
        self.rows = anchors.shape[2]
        self.repeat = self.span // self.rows
        self.steps = new_query.shape[1]
        self.heads = self.channels // HEAD_DIM
        self.q_local = new_query.shape[2] // HEAD_DIM
        self.mine = max(1, self.q_local // Q_PER_KV)
        self.group = self.q_local // self.mine
        self.wide = self.group * self.steps

    def anchor_at(self, which, parts):
        return (len(parts) * self.span + parts.index(which) * self.rows) * self.heads

    def side_at(self, parts):
        return len(parts) * self.heads * (self.span + self.rows)

    def message_rows(self, parts):
        return self.side_at(parts) + (TILE if 0 in parts else 0)

    def source_row(self, k):
        return pick(far(self.n, k), lax.axis_index("pool"))


def side_block(size, scale, length):
    row = lax.broadcasted_iota(jnp.int32, (TILE, HEAD_DIM), 0)
    scale = scale.astype(F32)
    out = jnp.where(row == 2 * size.heads, length.astype(F32), jnp.float32(0.0))
    for which in range(2):
        for h in range(size.heads):
            piece = scale[which:which + 1, h * HEAD_DIM:(h + 1) * HEAD_DIM]
            out = jnp.where(row == which * size.heads + h, piece, out)
    return out.astype(BF)


def pack_kernel(size, plan, route, lengths, deltas, anchors, scale, *rest):
    outs, (held, tables, sems) = rest[:-3], rest[-3:]
    z = lax.axis_index("pool")
    work = []
    for m, (k, parts) in enumerate(plan):
        dest = pick(far(size.n, k), z)
        index = jnp.int32(0)
        for j in range(size.count):
            index = jnp.where(route[j] == dest, jnp.int32(j), index)
        for which in parts:
            slot = len(work)
            copies = (
                pltpu.make_async_copy(deltas.at[index, which], held.at[slot], sems.at[0, slot]),
                pltpu.make_async_copy(anchors.at[index, which], tables.at[slot], sems.at[1, slot]),
            )
            for copy in copies:
                copy.start()
            work.append((outs[m], parts, which, slot, copies))
        if 0 in parts:
            outs[m][pl.ds(size.side_at(parts), TILE), :] = side_block(size, scale[index], lengths[index])
    for msg, parts, which, slot, copies in work:
        for copy in copies:
            copy.wait()
        for h in range(size.heads):
            lanes = slice(h * HEAD_DIM, (h + 1) * HEAD_DIM)
            at = (parts.index(which) * size.heads + h) * size.span
            msg[at:at + size.span, :] = held[slot, :, lanes]
            at = size.anchor_at(which, parts) + h * size.rows
            msg[at:at + size.rows, :] = tables[slot, :, lanes]


def pack(size, plan, route, lengths, deltas, anchors, scale):
    shapes = [pltpu.VMEM((size.message_rows(parts), HEAD_DIM), BF) for _, parts in plan]
    slots = sum(len(parts) for _, parts in plan)
    return pl.pallas_call(
        functools.partial(pack_kernel, size, plan),
        out_shape=shapes,
        in_specs=[IN_SMEM, IN_SMEM, IN_HBM, IN_HBM, IN_VMEM],
        out_specs=[IN_VMEM] * len(shapes),
        scratch_shapes=[
            pltpu.VMEM((slots, size.span, size.channels), BF),
            pltpu.VMEM((slots, size.rows, size.channels), BF),
            pltpu.SemaphoreType.DMA((2, slots)),
        ],
        compiler_params=LIMIT,
        cost_estimate=pl.CostEstimate(
            flops=0, bytes_accessed=2 * slots * size.span * size.channels, transcendentals=0
        ),
    )(hbm(route), hbm(lengths), hbm(deltas), hbm(anchors), hbm(scale))


def arrange_kernel(size, new_query, new_kv, query, fresh, wide, tall):
    sub = lax.axis_index("sub")
    rest = size.heads - size.mine
    tall[...] = jnp.zeros_like(tall)
    for r in range(size.count):
        for j in range(size.mine):
            for g in range(size.group):
                at = (j * size.group + g) * HEAD_DIM
                piece = new_query[r, :, at:at + HEAD_DIM].astype(F32)
                wide[g * size.steps:(g + 1) * size.steps, :] = piece
            query[r, j] = wide[...].astype(BF)
            for which in range(2):
                own, other = (
                    new_kv[r, which, :, h * HEAD_DIM:(h + 1) * HEAD_DIM].astype(F32) for h in (j, j + rest)
                )
                tall[:size.steps, :] = jnp.where(sub == 0, own, other)
                fresh[r, which, j] = tall[...].astype(BF)


def arrange(size, new_query, new_kv):
    return pl.pallas_call(
        functools.partial(arrange_kernel, size),
        in_specs=[IN_VMEM, IN_VMEM],
        out_specs=[IN_VMEM, IN_VMEM],
        out_shape=[
            pltpu.VMEM((size.count, size.mine, size.wide, HEAD_DIM), BF),
            pltpu.VMEM((size.count, 2, size.mine, TILE, HEAD_DIM), BF),
        ],
        scratch_shapes=[pltpu.VMEM((size.wide, HEAD_DIM), F32), pltpu.VMEM((TILE, HEAD_DIM), F32)],
        compiler_params=LIMIT,
    )(hbm(new_query), hbm(new_kv))


def row_copies(size, k, parts, cache, mine, theirs, sems):
    sub = lax.axis_index("sub")
    row = size.source_row(k)
    rest = size.heads - size.mine
    copies = []
    for o, (out, first) in enumerate(((mine, sub * rest), (theirs, (1 - sub) * rest))):
        if o and not rest:
            break
        for p, which in enumerate(parts):
            for j in range(size.mine):
                lanes = pl.ds(pl.multiple_of((first + j) * HEAD_DIM, HEAD_DIM), HEAD_DIM)
                at = (p * size.mine + j) * size.span
                copies.append(pltpu.make_async_copy(
                    out.at[pl.ds(at, size.span)],
                    cache.at[row, which, :, lanes],
                    sems.at[o, p * size.mine + j],
                ))
    return copies


def rebuild_heads(size, parts, message, tables, mine, theirs):
    sub = lax.axis_index("sub")
    rest = size.heads - size.mine
    side_at = size.side_at(parts if 0 in parts else (0,))
    side = tables[side_at:side_at + TILE, :].astype(F32)
    length = side[2 * size.heads:2 * size.heads + 1, :]
    base = sub * size.span
    for o, out in enumerate((theirs, mine)):
        first = (1 - sub) * rest if o == 0 else sub * rest
        other = sub == 0 if o == 0 else sub != 0
        for p, which in enumerate(parts):
            for j in range(size.mine):
                h = which * size.heads + j
                scale = jnp.where(other, side[h + rest:h + rest + 1, :], side[h:h + 1, :])
                table = pl.multiple_of(
                    size.anchor_at(which, parts) + (first + j) * size.rows, TILE
                )
                anchor = message[pl.ds(table, size.rows), :].astype(F32)
                source = (p * size.heads + first + j) * size.span
                to = (p * size.mine + j) * size.span
                for i in range(size.rows):
                    at = pl.multiple_of(source + i * size.repeat, TILE)
                    value = anchor[i:i + 1, :] + scale * message[pl.ds(at, size.repeat), :].astype(F32)
                    keep = (base + i * size.repeat).astype(F32) < length
                    value = jnp.where(keep, value, jnp.float32(0.0)).astype(BF)
                    out[to + i * size.repeat:to + (i + 1) * size.repeat, :] = value


def rebuild_kernel(size, parts, chained, message, *refs):
    _, _, mine, theirs = refs[2 * chained:]
    rebuild_heads(size, parts, message, message, mine, theirs)


def rebuild(size, parts, message, state):
    args = [vmem(message)]
    in_specs = [IN_VMEM] * len(args)
    aliases = {}
    if state is not None:
        aliases = {len(args): 0, len(args) + 1: 1}
        args += list(state)
        in_specs += [IN_HBM, IN_HBM]
    given = (len(parts) * size.mine * size.span, HEAD_DIM)
    out = pl.pallas_call(
        functools.partial(rebuild_kernel, size, parts, state is not None),
        in_specs=in_specs,
        out_specs=[IN_HBM, IN_HBM, IN_VMEM, IN_VMEM],
        out_shape=[
            pltpu.HBM((size.count, 2, size.span, size.channels), BF),
            pltpu.HBM((size.count, size.steps, size.q_local * HEAD_DIM), BF),
            pltpu.VMEM(given, BF),
            pltpu.VMEM(given, BF),
        ],
        input_output_aliases=aliases,
        compiler_params=LIMIT,
        cost_estimate=pl.CostEstimate(
            flops=4 * len(parts) * size.span * size.channels,
            bytes_accessed=6 * len(parts) * size.span * size.channels,
            transcendentals=0,
        ),
    )(*args)
    return tuple(out[:2]), out[2], out[3]


def weigh(size, j, q, new_key, key_mine, key_other, live_mine, live_other, causal):
    factor = 1.0 / math.sqrt(HEAD_DIM)
    s0 = lax.dot_general(q, key_mine, NT, preferred_element_type=F32) * factor
    s1 = lax.dot_general(q, key_other, NT, preferred_element_type=F32) * factor
    s2 = lax.dot_general(q, new_key, NT, preferred_element_type=F32) * factor
    s0 = jnp.where(live_mine, s0, jnp.float32(LOW))
    s1 = jnp.where(live_other, s1, jnp.float32(LOW))
    s2 = jnp.where(causal, s2, jnp.float32(LOW))
    top = jnp.maximum(
        jnp.max(jnp.maximum(s0, s1), axis=1, keepdims=True), jnp.max(s2, axis=1, keepdims=True)
    )
    w0 = jnp.where(live_mine, jnp.exp(s0 - top), jnp.float32(0.0))
    w1 = jnp.where(live_other, jnp.exp(s1 - top), jnp.float32(0.0))
    w2 = jnp.where(causal, jnp.exp(s2 - top), jnp.float32(0.0))
    total = jnp.sum(w0 + w1, axis=1, keepdims=True) + jnp.sum(w2, axis=1, keepdims=True)
    return w0.astype(BF), w1.astype(BF), w2.astype(BF), total


def masks(size, tables, parts, fresh):
    sub = lax.axis_index("sub")
    at = size.side_at(parts)
    side = tables[at:at + TILE, :].astype(F32)
    length = side[2 * size.heads:2 * size.heads + 1, 0:1]
    spot = lax.broadcasted_iota(jnp.int32, (1, size.span), 1)
    live_mine = (spot + sub * size.span).astype(F32) < length
    live_other = (spot + (1 - sub) * size.span).astype(F32) < length
    step = lax.broadcasted_iota(jnp.int32, (size.wide, fresh), 0) % size.steps
    token = lax.broadcasted_iota(jnp.int32, (size.wide, fresh), 1)
    return live_mine, live_other, (token <= step) & (token < size.steps)


def start_store(size, k, parts, cache, mine, theirs, sems):
    copies = row_copies(size, k, parts, cache, mine, theirs, sems)
    for copy in copies:
        copy.start()
    return copies


def store_heads(size, k, flat, made, attended, sem, copies):
    for j in range(size.mine):
        for g in range(size.group):
            at = (j * size.group + g) * HEAD_DIM
            made[:, at:at + HEAD_DIM] = flat[j, g * size.steps:(g + 1) * size.steps, :].astype(BF)
    copy = pltpu.make_async_copy(made, attended.at[size.source_row(k)], sem)
    copy.start()
    for each in copies:
        each.wait()
    copy.wait()


def attend_kernel(size, k, query, new_kv, tables, mine, other, theirs, *refs):
    cache, attended, made, flat, sem, sems = refs[2:]
    row = size.source_row(k)
    copies = start_store(size, k, (0, 1), cache, mine, theirs, sems)
    live_mine, live_other, causal = masks(size, tables, (0, 1), new_kv.shape[3])
    for j in range(size.mine):
        keys = slice(j * size.span, (j + 1) * size.span)
        values = slice((size.mine + j) * size.span, (size.mine + j + 1) * size.span)
        w0, w1, w2, total = weigh(
            size, j, query[row, j], new_kv[row, 0, j], mine[keys, :], other[keys, :],
            live_mine, live_other, causal,
        )
        acc = jnp.dot(w0, mine[values, :], preferred_element_type=F32)
        acc = acc + jnp.dot(w1, other[values, :], preferred_element_type=F32)
        acc = acc + jnp.dot(w2, new_kv[row, 1, j], preferred_element_type=F32)
        flat[j] = acc / total
    store_heads(size, k, flat, made, attended, sem, copies)


def weights_kernel(size, k, query, new_kv, tables, mine, other, theirs, *refs):
    cache, _, weights, lent, share, totals, sems = refs[2:]
    row = size.source_row(k)
    copies = start_store(size, k, (0,), cache, mine, theirs, sems)
    live_mine, live_other, causal = masks(size, tables, (0,), new_kv.shape[3])
    for j in range(size.mine):
        keys = slice(j * size.span, (j + 1) * size.span)
        w0, w1, w2, total = weigh(
            size, j, query[row, j], new_kv[row, 0, j], mine[keys, :], other[keys, :],
            live_mine, live_other, causal,
        )
        weights[j] = w0
        lent[j] = w1
        share[j] = jnp.dot(w2, new_kv[row, 1, j], preferred_element_type=F32)
        totals[j] = jnp.broadcast_to(total, totals.shape[1:])
    for copy in copies:
        copy.wait()


def values_kernel(size, weights, share, lent, message, tables, *refs):
    _, _, mine, theirs, kept, given = refs[2:]
    rebuild_heads(size, (1,), message, tables, mine, theirs)
    for j in range(size.mine):
        values = slice(j * size.span, (j + 1) * size.span)
        kept[j] = share[j] + jnp.dot(weights[j], mine[values, :], preferred_element_type=F32)
        given[j] = jnp.dot(lent[j], theirs[values, :], preferred_element_type=F32)


def store_kernel(size, k, mine, theirs, *refs):
    cache, _, sems = refs[2:]
    for copy in start_store(size, k, (1,), cache, mine, theirs, sems):
        copy.wait()


def finish_kernel(size, k, kept, got, totals, *refs):
    _, attended, made, flat, sem = refs[2:]
    for j in range(size.mine):
        flat[j] = (kept[j] + got[j]) / totals[j]
    store_heads(size, k, flat, made, attended, sem, ())


def chained_call(size, kernel, args, state, shapes, scratch, flops):
    args = [vmem(x) for x in args]
    many = len(args)
    out = pl.pallas_call(
        kernel,
        in_specs=[IN_VMEM] * many + [IN_HBM, IN_HBM],
        out_specs=[IN_HBM, IN_HBM] + [IN_VMEM] * len(shapes),
        out_shape=[pltpu.HBM(x.shape, x.dtype) for x in state] + shapes,
        scratch_shapes=scratch,
        input_output_aliases={many: 0, many + 1: 1},
        compiler_params=LIMIT,
        cost_estimate=pl.CostEstimate(
            flops=flops,
            bytes_accessed=8 * size.span * size.channels,
            transcendentals=2 * size.mine * size.wide * size.span,
        ),
    )(*args, *state)
    return tuple(out[:2]), out[2:]


def body(deltas, anchors, chan_scale, lengths, route, new_query, new_kv):
    n = lax.axis_size("pool")
    size = Sizes(deltas, anchors, new_query, n)
    both = (0, 1)
    order = [2, 1] + list(range(3, n))
    last = order[-1]
    plan = [(k, both) for k in order[:-1]] + [(last, (0,)), (last, (1,)), (0, both)]
    query, fresh = arrange(size, new_query, new_kv)
    message = {}
    for part in (plan[:1], plan[1:]):
        for (k, parts), msg in zip(part, pack(size, part, route, lengths, deltas, anchors, chan_scale)):
            if k:
                msg = lax.ppermute(msg, "pool", list(enumerate(far(n, k))))
            message[k, parts] = msg

    def swapped(x):
        return lax.ppermute(x, "sub", [(0, 1), (1, 0)])

    flops = 8 * size.mine * size.wide * size.span * HEAD_DIM
    rows = [
        pltpu.VMEM((size.steps, size.q_local * HEAD_DIM), BF),
        pltpu.VMEM((size.mine, size.wide, HEAD_DIM), F32),
        pltpu.SemaphoreType.DMA,
    ]
    sems = pltpu.SemaphoreType.DMA((2, 2 * size.mine))
    wide = pltpu.VMEM((size.mine, size.wide, HEAD_DIM), F32)

    def attend(k, mine, other, theirs, state):
        state, _ = chained_call(
            size, functools.partial(attend_kernel, size, k),
            (query, fresh, message[k, both], mine, other, theirs), state, [], rows + [sems], flops,
        )
        return state

    def take(k, parts, state):
        state, mine, theirs = rebuild(size, parts, message[k, parts], state)
        return state, mine, swapped(theirs), theirs

    state, held = None, []
    for k in [0] + order[:-1]:
        state, *each = take(k, both, state)
        held.append((k, *each))
        if k:
            state = attend(*held.pop(0), state)
    state = attend(*held.pop(0), state)
    state, *keys = take(last, (0,), state)
    half = pltpu.VMEM((size.mine, size.wide, size.span), BF)
    state, (weights, lent, share, totals) = chained_call(
        size, functools.partial(weights_kernel, size, last),
        (query, fresh, message[last, (0,)], *keys), state, [half, half, wide, wide], [sems], flops // 2,
    )
    given = pltpu.VMEM((size.mine * size.span, HEAD_DIM), BF)
    state, (mine, theirs, kept, given) = chained_call(
        size, functools.partial(values_kernel, size),
        (weights, share, swapped(lent), message[last, (1,)], message[last, (0,)]), state,
        [given, given, wide, wide], [], flops // 2,
    )
    got = swapped(given)
    state, _ = chained_call(
        size, functools.partial(store_kernel, size, last), (mine, theirs), state, [], [sems], 0
    )
    state, _ = chained_call(
        size, functools.partial(finish_kernel, size, last), (kept, got, totals), state, [], rows, 0
    )
    return state


def solution(mesh):
    placed = (
        P(("parts", "pool"), None, "sub", "tp"),
        P(("parts", "pool"), None, "sub", "tp"),
        P(("parts", "pool"), None, "tp"),
        P(("parts", "pool")),
        P(("parts", "pool")),
        P(("parts", "pool"), None, ("tp", "sub")),
        P(("parts", "pool"), None, None, "tp"),
    )
    return jax.shard_map(
        body,
        mesh=mesh,
        in_specs=placed,
        out_specs=(
            P(("parts", "pool"), None, "sub", "tp"),
            P(("parts", "pool"), None, ("tp", "sub")),
        ),
        check_vma=False,
    )
```

```python
import functools
import math

import jax
import jax.numpy as jnp
from jax import lax
from jax.experimental import pallas as pl
from jax.experimental.pallas import tpu as pltpu
from jax.sharding import PartitionSpec as P

HEAD_DIM = 128
Q_PER_KV = 8
TILE = 16
BF = jnp.bfloat16
F32 = jnp.float32
LOW = -1e30
NT = (((1,), (1,)), ((), ()))

IN_VMEM = pl.BlockSpec(memory_space=pltpu.VMEM)
IN_SMEM = pl.BlockSpec(memory_space=pltpu.SMEM)
IN_HBM = pl.BlockSpec(memory_space=pltpu.HBM)
LIMIT = pltpu.CompilerParams(vmem_limit_bytes=16 * 1024 * 1024)


def vmem(x):
    return pltpu.with_memory_space_constraint(x, pltpu.VMEM)


def hbm(x):
    return pltpu.with_memory_space_constraint(x, pltpu.HBM)


def far(n, k):
    return tuple(z ^ k for z in range(n))


def pick(values, at):
    out = jnp.int32(values[0])
    for i, value in enumerate(values[1:], 1):
        out = jnp.where(at == i, jnp.int32(value), out)
    return out


class Sizes:
    def __init__(self, deltas, anchors, new_query, n):
        self.n = n
        self.count, _, self.span, self.channels = deltas.shape
        self.rows = anchors.shape[2]
        self.repeat = self.span // self.rows
        self.steps = new_query.shape[1]
        self.heads = self.channels // HEAD_DIM
        self.q_local = new_query.shape[2] // HEAD_DIM
        self.mine = max(1, self.q_local // Q_PER_KV)
        self.group = self.q_local // self.mine
        self.wide = self.group * self.steps

    def anchor_at(self, which, parts):
        return (len(parts) * self.span + parts.index(which) * self.rows) * self.heads

    def side_at(self, parts):
        return len(parts) * self.heads * (self.span + self.rows)

    def message_rows(self, parts):
        return self.side_at(parts) + (TILE if 0 in parts else 0)

    def source_row(self, k):
        return pick(far(self.n, k), lax.axis_index("pool"))


def side_block(size, scale, length):
    row = lax.broadcasted_iota(jnp.int32, (TILE, HEAD_DIM), 0)
    scale = scale.astype(F32)
    out = jnp.where(row == 2 * size.heads, length.astype(F32), jnp.float32(0.0))
    for which in range(2):
        for h in range(size.heads):
            piece = scale[which:which + 1, h * HEAD_DIM:(h + 1) * HEAD_DIM]
            out = jnp.where(row == which * size.heads + h, piece, out)
    return out.astype(BF)


def pack_kernel(size, plan, route, lengths, deltas, anchors, scale, *rest):
    outs, (held, tables, sems) = rest[:-3], rest[-3:]
    z = lax.axis_index("pool")
    work = []
    for m, (k, parts) in enumerate(plan):
        dest = pick(far(size.n, k), z)
        index = jnp.int32(0)
        for j in range(size.count):
            index = jnp.where(route[j] == dest, jnp.int32(j), index)
        for which in parts:
            slot = len(work)
            copies = (
                pltpu.make_async_copy(deltas.at[index, which], held.at[slot], sems.at[0, slot]),
                pltpu.make_async_copy(anchors.at[index, which], tables.at[slot], sems.at[1, slot]),
            )
            for copy in copies:
                copy.start()
            work.append((outs[m], parts, which, slot, copies))
        if 0 in parts:
            outs[m][pl.ds(size.side_at(parts), TILE), :] = side_block(size, scale[index], lengths[index])
    for msg, parts, which, slot, copies in work:
        for copy in copies:
            copy.wait()
        for h in range(size.heads):
            lanes = slice(h * HEAD_DIM, (h + 1) * HEAD_DIM)
            at = (parts.index(which) * size.heads + h) * size.span
            msg[at:at + size.span, :] = held[slot, :, lanes]
            at = size.anchor_at(which, parts) + h * size.rows
            msg[at:at + size.rows, :] = tables[slot, :, lanes]


def pack(size, plan, route, lengths, deltas, anchors, scale):
    shapes = [pltpu.VMEM((size.message_rows(parts), HEAD_DIM), BF) for _, parts in plan]
    slots = sum(len(parts) for _, parts in plan)
    return pl.pallas_call(
        functools.partial(pack_kernel, size, plan),
        out_shape=shapes,
        in_specs=[IN_SMEM, IN_SMEM, IN_HBM, IN_HBM, IN_VMEM],
        out_specs=[IN_VMEM] * len(shapes),
        scratch_shapes=[
            pltpu.VMEM((slots, size.span, size.channels), BF),
            pltpu.VMEM((slots, size.rows, size.channels), BF),
            pltpu.SemaphoreType.DMA((2, slots)),
        ],
        compiler_params=LIMIT,
        cost_estimate=pl.CostEstimate(
            flops=0, bytes_accessed=2 * slots * size.span * size.channels, transcendentals=0
        ),
    )(hbm(route), hbm(lengths), hbm(deltas), hbm(anchors), hbm(scale))


def arrange_kernel(size, new_query, new_kv, query, fresh, wide, tall):
    sub = lax.axis_index("sub")
    rest = size.heads - size.mine
    tall[...] = jnp.zeros_like(tall)
    for r in range(size.count):
        for j in range(size.mine):
            for g in range(size.group):
                at = (j * size.group + g) * HEAD_DIM
                piece = new_query[r, :, at:at + HEAD_DIM].astype(F32)
                wide[g * size.steps:(g + 1) * size.steps, :] = piece
            query[r, j] = wide[...].astype(BF)
            for which in range(2):
                own, other = (
                    new_kv[r, which, :, h * HEAD_DIM:(h + 1) * HEAD_DIM].astype(F32) for h in (j, j + rest)
                )
                tall[:size.steps, :] = jnp.where(sub == 0, own, other)
                fresh[r, which, j] = tall[...].astype(BF)


def arrange(size, new_query, new_kv):
    return pl.pallas_call(
        functools.partial(arrange_kernel, size),
        in_specs=[IN_VMEM, IN_VMEM],
        out_specs=[IN_VMEM, IN_VMEM],
        out_shape=[
            pltpu.VMEM((size.count, size.mine, size.wide, HEAD_DIM), BF),
            pltpu.VMEM((size.count, 2, size.mine, TILE, HEAD_DIM), BF),
        ],
        scratch_shapes=[pltpu.VMEM((size.wide, HEAD_DIM), F32), pltpu.VMEM((TILE, HEAD_DIM), F32)],
        compiler_params=LIMIT,
    )(hbm(new_query), hbm(new_kv))


def row_copies(size, k, parts, cache, mine, theirs, sems, base=0):
    sub = lax.axis_index("sub")
    row = size.source_row(k)
    rest = size.heads - size.mine
    copies = []
    for o, (out, first) in enumerate(((mine, sub * rest), (theirs, (1 - sub) * rest))):
        if o and not rest:
            break
        for p, which in enumerate(parts):
            for j in range(size.mine):
                lanes = pl.ds(pl.multiple_of((first + j) * HEAD_DIM, HEAD_DIM), HEAD_DIM)
                at = (p * size.mine + j) * size.span
                copies.append(pltpu.make_async_copy(
                    out.at[pl.ds(at, size.span)],
                    cache.at[row, which, :, lanes],
                    sems.at[o, base + p * size.mine + j],
                ))
    return copies


def rebuild_heads(size, parts, message, tables, mine, theirs):
    sub = lax.axis_index("sub")
    rest = size.heads - size.mine
    side_at = size.side_at(parts if 0 in parts else (0,))
    side = tables[side_at:side_at + TILE, :].astype(F32)
    length = side[2 * size.heads:2 * size.heads + 1, :]
    base = sub * size.span
    for o, out in enumerate((theirs, mine)):
        first = (1 - sub) * rest if o == 0 else sub * rest
        other = sub == 0 if o == 0 else sub != 0
        for p, which in enumerate(parts):
            for j in range(size.mine):
                h = which * size.heads + j
                scale = jnp.where(other, side[h + rest:h + rest + 1, :], side[h:h + 1, :])
                table = pl.multiple_of(
                    size.anchor_at(which, parts) + (first + j) * size.rows, TILE
                )
                anchor = message[pl.ds(table, size.rows), :].astype(F32)
                source = (p * size.heads + first + j) * size.span
                to = (p * size.mine + j) * size.span
                for i in range(size.rows):
                    at = pl.multiple_of(source + i * size.repeat, TILE)
                    value = anchor[i:i + 1, :] + scale * message[pl.ds(at, size.repeat), :].astype(F32)
                    keep = (base + i * size.repeat).astype(F32) < length
                    value = jnp.where(keep, value, jnp.float32(0.0)).astype(BF)
                    out[to + i * size.repeat:to + (i + 1) * size.repeat, :] = value


def rebuild_kernel(size, parts, skip, message, tables, *refs):
    mine, theirs = refs[skip + 2:skip + 4]
    rebuild_heads(size, parts, message, tables, mine, theirs)


def rebuild(size, parts, message, tables, state, gate):
    args = [vmem(x) for x in (message, tables, *gate)]
    aliases = {2 + i: 4 + i for i in range(len(gate))}
    in_specs = [IN_VMEM] * len(args)
    if state is not None:
        aliases |= {len(args): 0, len(args) + 1: 1}
        args += list(state)
        in_specs += [IN_HBM, IN_HBM]
    given = (len(parts) * size.mine * size.span, HEAD_DIM)
    out = pl.pallas_call(
        functools.partial(rebuild_kernel, size, parts, len(args) - 2),
        in_specs=in_specs,
        out_specs=[IN_HBM, IN_HBM] + [IN_VMEM] * (2 + len(gate)),
        out_shape=[
            pltpu.HBM((size.count, 2, size.span, size.channels), BF),
            pltpu.HBM((size.count, size.steps, size.q_local * HEAD_DIM), BF),
            pltpu.VMEM(given, BF),
            pltpu.VMEM(given, BF),
        ] + [pltpu.VMEM(x.shape, BF) for x in gate],
        input_output_aliases=aliases,
        compiler_params=LIMIT,
        cost_estimate=pl.CostEstimate(
            flops=4 * len(parts) * size.span * size.channels,
            bytes_accessed=6 * len(parts) * size.span * size.channels,
            transcendentals=0,
        ),
    )(*args)
    return tuple(out[:2]), out[2], out[3], out[4:]


def weigh(size, j, q, new_key, key_mine, key_other, live_mine, live_other, causal):
    factor = 1.0 / math.sqrt(HEAD_DIM)
    s0 = lax.dot_general(q, key_mine, NT, preferred_element_type=F32) * factor
    s1 = lax.dot_general(q, key_other, NT, preferred_element_type=F32) * factor
    s2 = lax.dot_general(q, new_key, NT, preferred_element_type=F32) * factor
    s0 = jnp.where(live_mine, s0, jnp.float32(LOW))
    s1 = jnp.where(live_other, s1, jnp.float32(LOW))
    s2 = jnp.where(causal, s2, jnp.float32(LOW))
    top = jnp.maximum(
        jnp.max(jnp.maximum(s0, s1), axis=1, keepdims=True), jnp.max(s2, axis=1, keepdims=True)
    )
    w0 = jnp.where(live_mine, jnp.exp(s0 - top), jnp.float32(0.0))
    w1 = jnp.where(live_other, jnp.exp(s1 - top), jnp.float32(0.0))
    w2 = jnp.where(causal, jnp.exp(s2 - top), jnp.float32(0.0))
    total = jnp.sum(w0 + w1, axis=1, keepdims=True) + jnp.sum(w2, axis=1, keepdims=True)
    return w0.astype(BF), w1.astype(BF), w2.astype(BF), total


def masks(size, tables, parts, fresh):
    sub = lax.axis_index("sub")
    at = size.side_at(parts)
    side = tables[at:at + TILE, :].astype(F32)
    length = side[2 * size.heads:2 * size.heads + 1, 0:1]
    spot = lax.broadcasted_iota(jnp.int32, (1, size.span), 1)
    live_mine = (spot + sub * size.span).astype(F32) < length
    live_other = (spot + (1 - sub) * size.span).astype(F32) < length
    step = lax.broadcasted_iota(jnp.int32, (size.wide, fresh), 0) % size.steps
    token = lax.broadcasted_iota(jnp.int32, (size.wide, fresh), 1)
    return live_mine, live_other, (token <= step) & (token < size.steps)


def start_store(size, k, parts, cache, mine, theirs, sems, base=0):
    copies = row_copies(size, k, parts, cache, mine, theirs, sems, base)
    for copy in copies:
        copy.start()
    return copies


def store_heads(size, k, flat, made, attended, sem, copies):
    for j in range(size.mine):
        for g in range(size.group):
            at = (j * size.group + g) * HEAD_DIM
            made[:, at:at + HEAD_DIM] = flat[j, g * size.steps:(g + 1) * size.steps, :].astype(BF)
    copy = pltpu.make_async_copy(made, attended.at[size.source_row(k)], sem)
    copy.start()
    for each in copies:
        each.wait()
    copy.wait()


def attend_kernel(size, k, parts, query, new_kv, tables, mine, other, theirs, *refs):
    own, rest, away = (mine, other, theirs) if len(parts) == 2 else refs[:3]
    shift = size.mine if len(parts) == 2 else 0
    cache, attended, made, flat, sem, sems = refs[-6:]
    row = size.source_row(k)
    copies = start_store(size, k, parts, cache, mine, theirs, sems)
    if len(parts) == 1:
        copies += start_store(size, k, (1,), cache, own, away, sems, size.mine)
    live_mine, live_other, causal = masks(size, tables, parts, new_kv.shape[3])
    for j in range(size.mine):
        keys = slice(j * size.span, (j + 1) * size.span)
        values = slice((shift + j) * size.span, (shift + j + 1) * size.span)
        w0, w1, w2, total = weigh(
            size, j, query[row, j], new_kv[row, 0, j], mine[keys, :], other[keys, :],
            live_mine, live_other, causal,
        )
        acc = jnp.dot(w0, own[values, :], preferred_element_type=F32)
        acc = acc + jnp.dot(w1, rest[values, :], preferred_element_type=F32)
        acc = acc + jnp.dot(w2, new_kv[row, 1, j], preferred_element_type=F32)
        flat[j] = acc / total
    store_heads(size, k, flat, made, attended, sem, copies)


def weights_kernel(size, k, query, new_kv, tables, mine, other, theirs, *refs):
    cache, _, weights, lent, share, totals, sems = refs[2:]
    row = size.source_row(k)
    copies = start_store(size, k, (0,), cache, mine, theirs, sems)
    live_mine, live_other, causal = masks(size, tables, (0,), new_kv.shape[3])
    for j in range(size.mine):
        keys = slice(j * size.span, (j + 1) * size.span)
        w0, w1, w2, total = weigh(
            size, j, query[row, j], new_kv[row, 0, j], mine[keys, :], other[keys, :],
            live_mine, live_other, causal,
        )
        weights[j] = w0
        lent[j] = w1
        share[j] = jnp.dot(w2, new_kv[row, 1, j], preferred_element_type=F32)
        totals[j] = jnp.broadcast_to(total, totals.shape[1:])
    for copy in copies:
        copy.wait()


def values_kernel(size, weights, share, lent, message, tables, *refs):
    _, _, mine, theirs, kept, given = refs[2:]
    rebuild_heads(size, (1,), message, tables, mine, theirs)
    for j in range(size.mine):
        values = slice(j * size.span, (j + 1) * size.span)
        kept[j] = share[j] + jnp.dot(weights[j], mine[values, :], preferred_element_type=F32)
        given[j] = jnp.dot(lent[j], theirs[values, :], preferred_element_type=F32)


def store_kernel(size, k, mine, theirs, *refs):
    cache, _, sems = refs[2:]
    for copy in start_store(size, k, (1,), cache, mine, theirs, sems):
        copy.wait()


def finish_kernel(size, k, kept, got, totals, *refs):
    _, attended, made, flat, sem = refs[2:]
    for j in range(size.mine):
        flat[j] = (kept[j] + got[j]) / totals[j]
    store_heads(size, k, flat, made, attended, sem, ())


def chained_call(size, kernel, args, state, shapes, scratch, flops):
    args = [vmem(x) for x in args]
    many = len(args)
    out = pl.pallas_call(
        kernel,
        in_specs=[IN_VMEM] * many + [IN_HBM, IN_HBM],
        out_specs=[IN_HBM, IN_HBM] + [IN_VMEM] * len(shapes),
        out_shape=[pltpu.HBM(x.shape, x.dtype) for x in state] + shapes,
        scratch_shapes=scratch,
        input_output_aliases={many: 0, many + 1: 1},
        compiler_params=LIMIT,
        cost_estimate=pl.CostEstimate(
            flops=flops,
            bytes_accessed=8 * size.span * size.channels,
            transcendentals=2 * size.mine * size.wide * size.span,
        ),
    )(*args, *state)
    return tuple(out[:2]), out[2:]


def body(deltas, anchors, chan_scale, lengths, route, new_query, new_kv):
    n = lax.axis_size("pool")
    size = Sizes(deltas, anchors, new_query, n)
    both = (0, 1)
    order = [2, 1] + list(range(3, n))
    last = order[-1]
    halves = [(k, (p,)) for k in order[1:-1] for p in both]
    plan = [(order[0], both), (last, (0,))] + halves + [(last, (1,)), (0, both)]
    query, fresh = arrange(size, new_query, new_kv)
    message, packed = {}, {}

    def send(k, parts):
        message[k, parts] = lax.ppermute(packed[k, parts], "pool", list(enumerate(far(n, k))))

    for part in (plan[:1], plan[1:]):
        for (k, parts), msg in zip(part, pack(size, part, route, lengths, deltas, anchors, chan_scale)):
            packed[k, parts] = msg
            if k and (k, parts) not in halves:
                send(k, parts)

    def swapped(x):
        return lax.ppermute(x, "sub", [(0, 1), (1, 0)])

    flops = 8 * size.mine * size.wide * size.span * HEAD_DIM
    rows = [
        pltpu.VMEM((size.steps, size.q_local * HEAD_DIM), BF),
        pltpu.VMEM((size.mine, size.wide, HEAD_DIM), F32),
        pltpu.SemaphoreType.DMA,
    ]
    sems = pltpu.SemaphoreType.DMA((2, 2 * size.mine))
    wide = pltpu.VMEM((size.mine, size.wide, HEAD_DIM), F32)

    def attend(k, parts, arrays, state):
        tables = (message if k else packed)[k, parts]
        state, _ = chained_call(
            size, functools.partial(attend_kernel, size, k, parts),
            (query, fresh, tables, *arrays), state, [], rows + [sems], flops,
        )
        return state

    def take(k, parts, state, gate=()):
        msg, tables = (
            (message if k else packed)[k, p] for p in (parts, parts if 0 in parts else (0,))
        )
        state, mine, theirs, gate = rebuild(size, parts, msg, tables, state, gate)
        return state, mine, swapped(theirs), theirs, gate

    state, *own, _ = take(0, both, None)
    state = attend(0, both, own, state)
    state, *first, gate = take(order[0], both, state, [packed[x] for x in halves])
    for (k, parts), msg in zip(halves, gate):
        packed[k, parts] = msg
        send(k, parts)
    state, *keys, _ = take(last, (0,), state)
    state = attend(order[0], both, first, state)
    half = pltpu.VMEM((size.mine, size.wide, size.span), BF)
    state, (weights, lent, share, totals) = chained_call(
        size, functools.partial(weights_kernel, size, last),
        (query, fresh, message[last, (0,)], *keys), state, [half, half, wide, wide], [sems], flops // 2,
    )
    for k in order[1:-1]:
        state, *each, _ = take(k, (0,), state)
        state, *more, _ = take(k, (1,), state)
        state = attend(k, (0,), (*each, *more), state)
    given = pltpu.VMEM((size.mine * size.span, HEAD_DIM), BF)
    state, (mine, theirs, kept, given) = chained_call(
        size, functools.partial(values_kernel, size),
        (weights, share, swapped(lent), message[last, (1,)], message[last, (0,)]), state,
        [given, given, wide, wide], [], flops // 2,
    )
    got = swapped(given)
    state, _ = chained_call(
        size, functools.partial(store_kernel, size, last), (mine, theirs), state, [], [sems], 0
    )
    state, _ = chained_call(
        size, functools.partial(finish_kernel, size, last), (kept, got, totals), state, [], rows, 0
    )
    return state


def solution(mesh):
    placed = (
        P(("parts", "pool"), None, "sub", "tp"),
        P(("parts", "pool"), None, "sub", "tp"),
        P(("parts", "pool"), None, "tp"),
        P(("parts", "pool")),
        P(("parts", "pool")),
        P(("parts", "pool"), None, ("tp", "sub")),
        P(("parts", "pool"), None, None, "tp"),
    )
    return jax.shard_map(
        body,
        mesh=mesh,
        in_specs=placed,
        out_specs=(
            P(("parts", "pool"), None, "sub", "tp"),
            P(("parts", "pool"), None, ("tp", "sub")),
        ),
        check_vma=False,
    )
```

```python
import functools
import math

import jax
import jax.numpy as jnp
from jax import lax
from jax.experimental import pallas as pl
from jax.experimental.pallas import tpu as pltpu
from jax.sharding import PartitionSpec as P

HEAD_DIM = 128
Q_PER_KV = 8
TILE = 16
BF = jnp.bfloat16
F32 = jnp.float32
LOW = -1e30
NT = (((1,), (1,)), ((), ()))

IN_VMEM = pl.BlockSpec(memory_space=pltpu.VMEM)
IN_SMEM = pl.BlockSpec(memory_space=pltpu.SMEM)
IN_HBM = pl.BlockSpec(memory_space=pltpu.HBM)
LIMIT = pltpu.CompilerParams(vmem_limit_bytes=16 * 1024 * 1024)


def vmem(x):
    return pltpu.with_memory_space_constraint(x, pltpu.VMEM)


def hbm(x):
    return pltpu.with_memory_space_constraint(x, pltpu.HBM)


def far(n, k):
    return tuple(z ^ k for z in range(n))


def pick(values, at):
    out = jnp.int32(values[0])
    for i, value in enumerate(values[1:], 1):
        out = jnp.where(at == i, jnp.int32(value), out)
    return out


class Sizes:
    def __init__(self, deltas, anchors, new_query, n):
        self.n = n
        self.count, _, self.span, self.channels = deltas.shape
        self.rows = anchors.shape[2]
        self.repeat = self.span // self.rows
        self.steps = new_query.shape[1]
        self.heads = self.channels // HEAD_DIM
        self.q_local = new_query.shape[2] // HEAD_DIM
        self.mine = max(1, self.q_local // Q_PER_KV)
        self.group = self.q_local // self.mine
        self.wide = self.group * self.steps

    def anchor_at(self, which, parts):
        return (len(parts) * self.span + parts.index(which) * self.rows) * self.heads

    def side_at(self, parts):
        return len(parts) * self.heads * (self.span + self.rows)

    def message_rows(self, parts):
        return self.side_at(parts) + (TILE if 0 in parts else 0)

    def source_row(self, k):
        return pick(far(self.n, k), lax.axis_index("pool"))


def side_block(size, scale, length):
    row = lax.broadcasted_iota(jnp.int32, (TILE, HEAD_DIM), 0)
    scale = scale.astype(F32)
    out = jnp.where(row == 2 * size.heads, length.astype(F32), jnp.float32(0.0))
    for which in range(2):
        for h in range(size.heads):
            piece = scale[which:which + 1, h * HEAD_DIM:(h + 1) * HEAD_DIM]
            out = jnp.where(row == which * size.heads + h, piece, out)
    return out.astype(BF)


def pack_kernel(size, plan, route, lengths, deltas, anchors, scale, *rest):
    outs, (held, tables, sems) = rest[:-3], rest[-3:]
    z = lax.axis_index("pool")
    work = []
    for m, (k, parts) in enumerate(plan):
        dest = pick(far(size.n, k), z)
        index = jnp.int32(0)
        for j in range(size.count):
            index = jnp.where(route[j] == dest, jnp.int32(j), index)
        for which in parts:
            slot = len(work)
            copies = (
                pltpu.make_async_copy(deltas.at[index, which], held.at[slot], sems.at[0, slot]),
                pltpu.make_async_copy(anchors.at[index, which], tables.at[slot], sems.at[1, slot]),
            )
            for copy in copies:
                copy.start()
            work.append((outs[m], parts, which, slot, copies))
        if 0 in parts:
            outs[m][pl.ds(size.side_at(parts), TILE), :] = side_block(size, scale[index], lengths[index])
    for msg, parts, which, slot, copies in work:
        for copy in copies:
            copy.wait()
        for h in range(size.heads):
            lanes = slice(h * HEAD_DIM, (h + 1) * HEAD_DIM)
            at = (parts.index(which) * size.heads + h) * size.span
            msg[at:at + size.span, :] = held[slot, :, lanes]
            at = size.anchor_at(which, parts) + h * size.rows
            msg[at:at + size.rows, :] = tables[slot, :, lanes]


def pack(size, plan, route, lengths, deltas, anchors, scale):
    shapes = [pltpu.VMEM((size.message_rows(parts), HEAD_DIM), BF) for _, parts in plan]
    slots = sum(len(parts) for _, parts in plan)
    return pl.pallas_call(
        functools.partial(pack_kernel, size, plan),
        out_shape=shapes,
        in_specs=[IN_SMEM, IN_SMEM, IN_HBM, IN_HBM, IN_VMEM],
        out_specs=[IN_VMEM] * len(shapes),
        scratch_shapes=[
            pltpu.VMEM((slots, size.span, size.channels), BF),
            pltpu.VMEM((slots, size.rows, size.channels), BF),
            pltpu.SemaphoreType.DMA((2, slots)),
        ],
        compiler_params=LIMIT,
        cost_estimate=pl.CostEstimate(
            flops=0, bytes_accessed=2 * slots * size.span * size.channels, transcendentals=0
        ),
    )(hbm(route), hbm(lengths), hbm(deltas), hbm(anchors), hbm(scale))


def arrange_kernel(size, new_query, new_kv, query, fresh, wide, tall):
    sub = lax.axis_index("sub")
    rest = size.heads - size.mine
    tall[...] = jnp.zeros_like(tall)
    for r in range(size.count):
        for j in range(size.mine):
            for g in range(size.group):
                at = (j * size.group + g) * HEAD_DIM
                piece = new_query[r, :, at:at + HEAD_DIM].astype(F32)
                wide[g * size.steps:(g + 1) * size.steps, :] = piece
            query[r, j] = wide[...].astype(BF)
            for which in range(2):
                own, other = (
                    new_kv[r, which, :, h * HEAD_DIM:(h + 1) * HEAD_DIM].astype(F32) for h in (j, j + rest)
                )
                tall[:size.steps, :] = jnp.where(sub == 0, own, other)
                fresh[r, which, j] = tall[...].astype(BF)


def arrange(size, new_query, new_kv):
    return pl.pallas_call(
        functools.partial(arrange_kernel, size),
        in_specs=[IN_VMEM, IN_VMEM],
        out_specs=[IN_VMEM, IN_VMEM],
        out_shape=[
            pltpu.VMEM((size.count, size.mine, size.wide, HEAD_DIM), BF),
            pltpu.VMEM((size.count, 2, size.mine, TILE, HEAD_DIM), BF),
        ],
        scratch_shapes=[pltpu.VMEM((size.wide, HEAD_DIM), F32), pltpu.VMEM((TILE, HEAD_DIM), F32)],
        compiler_params=LIMIT,
    )(hbm(new_query), hbm(new_kv))


def row_copies(size, k, parts, cache, mine, theirs, sems, base=0):
    sub = lax.axis_index("sub")
    row = size.source_row(k)
    rest = size.heads - size.mine
    copies = []
    for o, (out, first) in enumerate(((mine, sub * rest), (theirs, (1 - sub) * rest))):
        if o and not rest:
            break
        for p, which in enumerate(parts):
            for j in range(size.mine):
                lanes = pl.ds(pl.multiple_of((first + j) * HEAD_DIM, HEAD_DIM), HEAD_DIM)
                at = (p * size.mine + j) * size.span
                copies.append(pltpu.make_async_copy(
                    out.at[pl.ds(at, size.span)],
                    cache.at[row, which, :, lanes],
                    sems.at[o, base + p * size.mine + j],
                ))
    return copies


def rebuild_heads(size, parts, message, tables, mine, theirs):
    sub = lax.axis_index("sub")
    rest = size.heads - size.mine
    side_at = size.side_at(parts if 0 in parts else (0,))
    side = tables[side_at:side_at + TILE, :].astype(F32)
    length = side[2 * size.heads:2 * size.heads + 1, :]
    base = sub * size.span
    for o, out in enumerate((theirs, mine)):
        first = (1 - sub) * rest if o == 0 else sub * rest
        other = sub == 0 if o == 0 else sub != 0
        for p, which in enumerate(parts):
            for j in range(size.mine):
                h = which * size.heads + j
                scale = jnp.where(other, side[h + rest:h + rest + 1, :], side[h:h + 1, :])
                table = pl.multiple_of(
                    size.anchor_at(which, parts) + (first + j) * size.rows, TILE
                )
                anchor = message[pl.ds(table, size.rows), :].astype(F32)
                source = (p * size.heads + first + j) * size.span
                to = (p * size.mine + j) * size.span
                for i in range(size.rows):
                    at = pl.multiple_of(source + i * size.repeat, TILE)
                    value = anchor[i:i + 1, :] + scale * message[pl.ds(at, size.repeat), :].astype(F32)
                    keep = (base + i * size.repeat).astype(F32) < length
                    value = jnp.where(keep, value, jnp.float32(0.0)).astype(BF)
                    out[to + i * size.repeat:to + (i + 1) * size.repeat, :] = value


def rebuild_kernel(size, parts, skip, message, tables, *refs):
    mine, theirs = refs[skip + 2:skip + 4]
    rebuild_heads(size, parts, message, tables, mine, theirs)


def rebuild(size, parts, message, tables, state, gate):
    args = [vmem(x) for x in (message, tables, *gate)]
    aliases = {2 + i: 4 + i for i in range(len(gate))}
    in_specs = [IN_VMEM] * len(args)
    if state is not None:
        aliases |= {len(args): 0, len(args) + 1: 1}
        args += list(state)
        in_specs += [IN_HBM, IN_HBM]
    given = (len(parts) * size.mine * size.span, HEAD_DIM)
    out = pl.pallas_call(
        functools.partial(rebuild_kernel, size, parts, len(args) - 2),
        in_specs=in_specs,
        out_specs=[IN_HBM, IN_HBM] + [IN_VMEM] * (2 + len(gate)),
        out_shape=[
            pltpu.HBM((size.count, 2, size.span, size.channels), BF),
            pltpu.HBM((size.count, size.steps, size.q_local * HEAD_DIM), BF),
            pltpu.VMEM(given, BF),
            pltpu.VMEM(given, BF),
        ] + [pltpu.VMEM(x.shape, BF) for x in gate],
        input_output_aliases=aliases,
        compiler_params=LIMIT,
        cost_estimate=pl.CostEstimate(
            flops=4 * len(parts) * size.span * size.channels,
            bytes_accessed=6 * len(parts) * size.span * size.channels,
            transcendentals=0,
        ),
    )(*args)
    return tuple(out[:2]), out[2], out[3], out[4:]


def weigh(size, j, q, new_key, key_mine, key_other, live_mine, live_other, causal):
    factor = 1.0 / math.sqrt(HEAD_DIM)
    s0 = lax.dot_general(q, key_mine, NT, preferred_element_type=F32) * factor
    s1 = lax.dot_general(q, key_other, NT, preferred_element_type=F32) * factor
    s2 = lax.dot_general(q, new_key, NT, preferred_element_type=F32) * factor
    s0 = jnp.where(live_mine, s0, jnp.float32(LOW))
    s1 = jnp.where(live_other, s1, jnp.float32(LOW))
    s2 = jnp.where(causal, s2, jnp.float32(LOW))
    top = jnp.maximum(
        jnp.max(jnp.maximum(s0, s1), axis=1, keepdims=True), jnp.max(s2, axis=1, keepdims=True)
    )
    w0 = jnp.where(live_mine, jnp.exp(s0 - top), jnp.float32(0.0))
    w1 = jnp.where(live_other, jnp.exp(s1 - top), jnp.float32(0.0))
    w2 = jnp.where(causal, jnp.exp(s2 - top), jnp.float32(0.0))
    total = jnp.sum(w0 + w1, axis=1, keepdims=True) + jnp.sum(w2, axis=1, keepdims=True)
    return w0.astype(BF), w1.astype(BF), w2.astype(BF), total


def masks(size, tables, parts, fresh):
    sub = lax.axis_index("sub")
    at = size.side_at(parts)
    side = tables[at:at + TILE, :].astype(F32)
    length = side[2 * size.heads:2 * size.heads + 1, 0:1]
    spot = lax.broadcasted_iota(jnp.int32, (1, size.span), 1)
    live_mine = (spot + sub * size.span).astype(F32) < length
    live_other = (spot + (1 - sub) * size.span).astype(F32) < length
    step = lax.broadcasted_iota(jnp.int32, (size.wide, fresh), 0) % size.steps
    token = lax.broadcasted_iota(jnp.int32, (size.wide, fresh), 1)
    return live_mine, live_other, (token <= step) & (token < size.steps)


def start_store(size, k, parts, cache, mine, theirs, sems, base=0):
    copies = row_copies(size, k, parts, cache, mine, theirs, sems, base)
    for copy in copies:
        copy.start()
    return copies


def store_heads(size, k, flat, made, attended, sem, copies):
    for j in range(size.mine):
        for g in range(size.group):
            at = (j * size.group + g) * HEAD_DIM
            made[:, at:at + HEAD_DIM] = flat[j, g * size.steps:(g + 1) * size.steps, :].astype(BF)
    copy = pltpu.make_async_copy(made, attended.at[size.source_row(k)], sem)
    copy.start()
    for each in copies:
        each.wait()
    copy.wait()


def attend_kernel(size, k, parts, query, new_kv, tables, mine, other, theirs, *refs):
    own, rest, away = (mine, other, theirs) if len(parts) == 2 else refs[:3]
    shift = size.mine if len(parts) == 2 else 0
    cache, attended, made, flat, sem, sems = refs[-6:]
    row = size.source_row(k)
    copies = start_store(size, k, parts, cache, mine, theirs, sems)
    if len(parts) == 1:
        copies += start_store(size, k, (1,), cache, own, away, sems, size.mine)
    live_mine, live_other, causal = masks(size, tables, parts, new_kv.shape[3])
    for j in range(size.mine):
        keys = slice(j * size.span, (j + 1) * size.span)
        values = slice((shift + j) * size.span, (shift + j + 1) * size.span)
        w0, w1, w2, total = weigh(
            size, j, query[row, j], new_kv[row, 0, j], mine[keys, :], other[keys, :],
            live_mine, live_other, causal,
        )
        acc = jnp.dot(w0, own[values, :], preferred_element_type=F32)
        acc = acc + jnp.dot(w1, rest[values, :], preferred_element_type=F32)
        acc = acc + jnp.dot(w2, new_kv[row, 1, j], preferred_element_type=F32)
        flat[j] = acc / total
    store_heads(size, k, flat, made, attended, sem, copies)


def weights_kernel(size, k, query, new_kv, tables, mine, other, theirs, *refs):
    cache, _, weights, lent, share, totals, sems = refs[2:]
    row = size.source_row(k)
    copies = start_store(size, k, (0,), cache, mine, theirs, sems)
    live_mine, live_other, causal = masks(size, tables, (0,), new_kv.shape[3])
    for j in range(size.mine):
        keys = slice(j * size.span, (j + 1) * size.span)
        w0, w1, w2, total = weigh(
            size, j, query[row, j], new_kv[row, 0, j], mine[keys, :], other[keys, :],
            live_mine, live_other, causal,
        )
        weights[j] = w0
        lent[j] = w1
        share[j] = jnp.dot(w2, new_kv[row, 1, j], preferred_element_type=F32)
        totals[j] = jnp.broadcast_to(total, totals.shape[1:])
    for copy in copies:
        copy.wait()


def values_kernel(size, weights, share, lent, message, tables, *refs):
    _, _, mine, theirs, kept, given = refs[2:]
    rebuild_heads(size, (1,), message, tables, mine, theirs)
    for j in range(size.mine):
        values = slice(j * size.span, (j + 1) * size.span)
        kept[j] = share[j] + jnp.dot(weights[j], mine[values, :], preferred_element_type=F32)
        given[j] = jnp.dot(lent[j], theirs[values, :], preferred_element_type=F32)


def store_kernel(size, k, mine, theirs, *refs):
    cache, _, sems = refs[2:]
    for copy in start_store(size, k, (1,), cache, mine, theirs, sems):
        copy.wait()


def finish_kernel(size, k, kept, got, totals, *refs):
    _, attended, made, flat, sem = refs[2:]
    for j in range(size.mine):
        flat[j] = (kept[j] + got[j]) / totals[j]
    store_heads(size, k, flat, made, attended, sem, ())


def chained_call(size, kernel, args, state, shapes, scratch, flops):
    args = [vmem(x) for x in args]
    many = len(args)
    out = pl.pallas_call(
        kernel,
        in_specs=[IN_VMEM] * many + [IN_HBM, IN_HBM],
        out_specs=[IN_HBM, IN_HBM] + [IN_VMEM] * len(shapes),
        out_shape=[pltpu.HBM(x.shape, x.dtype) for x in state] + shapes,
        scratch_shapes=scratch,
        input_output_aliases={many: 0, many + 1: 1},
        compiler_params=LIMIT,
        cost_estimate=pl.CostEstimate(
            flops=flops,
            bytes_accessed=8 * size.span * size.channels,
            transcendentals=2 * size.mine * size.wide * size.span,
        ),
    )(*args, *state)
    return tuple(out[:2]), out[2:]


def body(deltas, anchors, chan_scale, lengths, route, new_query, new_kv):
    n = lax.axis_size("pool")
    size = Sizes(deltas, anchors, new_query, n)
    both = (0, 1)
    order = [2, 1] + list(range(3, n))
    last = order[-1]
    nears = order[1:-1]
    plan = [(order[0], both)] + [(k, (0,)) for k in nears] + [(last, (0,))]
    plan += [(k, (1,)) for k in nears] + [(last, (1,)), (0, both)]
    query, fresh = arrange(size, new_query, new_kv)
    message, packed = {}, {}

    def send(k, parts):
        message[k, parts] = lax.ppermute(packed[k, parts], "pool", list(enumerate(far(n, k))))

    for part in (plan[:1], plan[1:]):
        for (k, parts), msg in zip(part, pack(size, part, route, lengths, deltas, anchors, chan_scale)):
            packed[k, parts] = msg
            if k:
                send(k, parts)

    def swapped(x):
        return lax.ppermute(x, "sub", [(0, 1), (1, 0)])

    flops = 8 * size.mine * size.wide * size.span * HEAD_DIM
    rows = [
        pltpu.VMEM((size.steps, size.q_local * HEAD_DIM), BF),
        pltpu.VMEM((size.mine, size.wide, HEAD_DIM), F32),
        pltpu.SemaphoreType.DMA,
    ]
    sems = pltpu.SemaphoreType.DMA((2, 2 * size.mine))
    wide = pltpu.VMEM((size.mine, size.wide, HEAD_DIM), F32)

    def attend(k, parts, arrays, state):
        tables = (message if k else packed)[k, parts]
        state, _ = chained_call(
            size, functools.partial(attend_kernel, size, k, parts),
            (query, fresh, tables, *arrays), state, [], rows + [sems], flops,
        )
        return state

    def take(k, parts, state, gate=()):
        msg, tables = (
            (message if k else packed)[k, p] for p in (parts, parts if 0 in parts else (0,))
        )
        state, mine, theirs, gate = rebuild(size, parts, msg, tables, state, gate)
        return state, mine, swapped(theirs), theirs, gate

    state, *own, _ = take(0, both, None)
    state, *first, _ = take(order[0], both, state)
    state = attend(0, both, own, state)
    near = {}
    for k in nears:
        state, *near[k], _ = take(k, (0,), state)
    state, *keys, _ = take(last, (0,), state)
    state = attend(order[0], both, first, state)
    for k in nears:
        state, *more, _ = take(k, (1,), state)
        near[k] += more
    half = pltpu.VMEM((size.mine, size.wide, size.span), BF)
    state, (weights, lent, share, totals) = chained_call(
        size, functools.partial(weights_kernel, size, last),
        (query, fresh, message[last, (0,)], *keys), state, [half, half, wide, wide], [sems], flops // 2,
    )
    for k in nears:
        state = attend(k, (0,), near[k], state)
    given = pltpu.VMEM((size.mine * size.span, HEAD_DIM), BF)
    state, (mine, theirs, kept, given) = chained_call(
        size, functools.partial(values_kernel, size),
        (weights, share, swapped(lent), message[last, (1,)], message[last, (0,)]), state,
        [given, given, wide, wide], [], flops // 2,
    )
    got = swapped(given)
    state, _ = chained_call(
        size, functools.partial(store_kernel, size, last), (mine, theirs), state, [], [sems], 0
    )
    state, _ = chained_call(
        size, functools.partial(finish_kernel, size, last), (kept, got, totals), state, [], rows, 0
    )
    return state


def solution(mesh):
    placed = (
        P(("parts", "pool"), None, "sub", "tp"),
        P(("parts", "pool"), None, "sub", "tp"),
        P(("parts", "pool"), None, "tp"),
        P(("parts", "pool")),
        P(("parts", "pool")),
        P(("parts", "pool"), None, ("tp", "sub")),
        P(("parts", "pool"), None, None, "tp"),
    )
    return jax.shard_map(
        body,
        mesh=mesh,
        in_specs=placed,
        out_specs=(
            P(("parts", "pool"), None, "sub", "tp"),
            P(("parts", "pool"), None, ("tp", "sub")),
        ),
        check_vma=False,
    )
```

```python
import functools
import math

import jax
import jax.numpy as jnp
from jax import lax
from jax.experimental import pallas as pl
from jax.experimental.pallas import tpu as pltpu
from jax.sharding import PartitionSpec as P

HEAD_DIM = 128
Q_PER_KV = 8
TILE = 16
BF = jnp.bfloat16
F32 = jnp.float32
LOW = -1e30
NT = (((1,), (1,)), ((), ()))

IN_VMEM = pl.BlockSpec(memory_space=pltpu.VMEM)
IN_SMEM = pl.BlockSpec(memory_space=pltpu.SMEM)
IN_HBM = pl.BlockSpec(memory_space=pltpu.HBM)
LIMIT = pltpu.CompilerParams(vmem_limit_bytes=16 * 1024 * 1024)


def vmem(x):
    return pltpu.with_memory_space_constraint(x, pltpu.VMEM)


def hbm(x):
    return pltpu.with_memory_space_constraint(x, pltpu.HBM)


def far(n, k):
    return tuple(z ^ k for z in range(n))


def pick(values, at):
    out = jnp.int32(values[0])
    for i, value in enumerate(values[1:], 1):
        out = jnp.where(at == i, jnp.int32(value), out)
    return out


class Sizes:
    def __init__(self, deltas, anchors, new_query, n):
        self.n = n
        self.count, _, self.span, self.channels = deltas.shape
        self.rows = anchors.shape[2]
        self.repeat = self.span // self.rows
        self.steps = new_query.shape[1]
        self.heads = self.channels // HEAD_DIM
        self.q_local = new_query.shape[2] // HEAD_DIM
        self.mine = max(1, self.q_local // Q_PER_KV)
        self.group = self.q_local // self.mine
        self.wide = self.group * self.steps
        self.rest = self.heads - self.mine

    def anchor_at(self, which, parts):
        return (len(parts) * self.span + parts.index(which) * self.rows) * self.heads

    def side_at(self, parts):
        return len(parts) * self.heads * (self.span + self.rows)

    def message_rows(self, parts):
        return self.side_at(parts) + (TILE if 0 in parts else 0)

    def halved(self, parts):
        return parts == (1,) and self.rest > 0

    def half_rows(self):
        return self.mine * (self.span + self.rows)

    def source_row(self, k):
        return pick(far(self.n, k), lax.axis_index("pool"))


def side_block(size, scale, length):
    row = lax.broadcasted_iota(jnp.int32, (TILE, HEAD_DIM), 0)
    scale = scale.astype(F32)
    out = jnp.where(row == 2 * size.heads, length.astype(F32), jnp.float32(0.0))
    for which in range(2):
        for h in range(size.heads):
            piece = scale[which:which + 1, h * HEAD_DIM:(h + 1) * HEAD_DIM]
            out = jnp.where(row == which * size.heads + h, piece, out)
    return out.astype(BF)


def pack_kernel(size, plan, route, lengths, deltas, anchors, scale, *rest):
    outs, (held, tables, sems) = rest[:-3], rest[-3:]
    z = lax.axis_index("pool")
    sub = lax.axis_index("sub")
    outs, work = list(outs), []
    for k, parts in plan:
        msgs = [outs.pop(0) for _ in range(1 + size.halved(parts))]
        dest = pick(far(size.n, k), z)
        index = jnp.int32(0)
        for j in range(size.count):
            index = jnp.where(route[j] == dest, jnp.int32(j), index)
        for which in parts:
            slot = len(work)
            copies = (
                pltpu.make_async_copy(deltas.at[index, which], held.at[slot], sems.at[0, slot]),
                pltpu.make_async_copy(anchors.at[index, which], tables.at[slot], sems.at[1, slot]),
            )
            for copy in copies:
                copy.start()
            work.append((msgs, parts, which, slot, copies))
        if 0 in parts:
            side = side_block(size, scale[index], lengths[index])
            msgs[0][pl.ds(size.side_at(parts), TILE), :] = side
    for msgs, parts, which, slot, copies in work:
        for copy in copies:
            copy.wait()

        def fill(upper, msgs=msgs, parts=parts, which=which, slot=slot):
            for h in range(size.heads):
                lanes = slice(h * HEAD_DIM, (h + 1) * HEAD_DIM)
                if len(msgs) == 2:
                    own = (h >= size.rest) == upper
                    j, msg = h % size.mine, msgs[int(own)]
                    at, table = j * size.span, size.mine * size.span + j * size.rows
                else:
                    msg = msgs[0]
                    at = (parts.index(which) * size.heads + h) * size.span
                    table = size.anchor_at(which, parts) + h * size.rows
                msg[at:at + size.span, :] = held[slot, :, lanes]
                msg[table:table + size.rows, :] = tables[slot, :, lanes]

        if len(msgs) == 2:
            pl.when(sub == 0)(functools.partial(fill, False))
            pl.when(sub != 0)(functools.partial(fill, True))
        else:
            fill(False)


def pack(size, plan, route, lengths, deltas, anchors, scale):
    shapes = []
    for _, parts in plan:
        rows = [size.half_rows()] * 2 if size.halved(parts) else [size.message_rows(parts)]
        shapes += [pltpu.VMEM((r, HEAD_DIM), BF) for r in rows]
    slots = sum(len(parts) for _, parts in plan)
    return pl.pallas_call(
        functools.partial(pack_kernel, size, plan),
        out_shape=shapes,
        in_specs=[IN_SMEM, IN_SMEM, IN_HBM, IN_HBM, IN_VMEM],
        out_specs=[IN_VMEM] * len(shapes),
        scratch_shapes=[
            pltpu.VMEM((slots, size.span, size.channels), BF),
            pltpu.VMEM((slots, size.rows, size.channels), BF),
            pltpu.SemaphoreType.DMA((2, slots)),
        ],
        compiler_params=LIMIT,
        cost_estimate=pl.CostEstimate(
            flops=0, bytes_accessed=2 * slots * size.span * size.channels, transcendentals=0
        ),
    )(hbm(route), hbm(lengths), hbm(deltas), hbm(anchors), hbm(scale))


def arrange_kernel(size, new_query, new_kv, query, fresh, wide, tall):
    sub = lax.axis_index("sub")
    rest = size.heads - size.mine
    tall[...] = jnp.zeros_like(tall)
    for r in range(size.count):
        for j in range(size.mine):
            for g in range(size.group):
                at = (j * size.group + g) * HEAD_DIM
                piece = new_query[r, :, at:at + HEAD_DIM].astype(F32)
                wide[g * size.steps:(g + 1) * size.steps, :] = piece
            query[r, j] = wide[...].astype(BF)
            for which in range(2):
                own, other = (
                    new_kv[r, which, :, h * HEAD_DIM:(h + 1) * HEAD_DIM].astype(F32) for h in (j, j + rest)
                )
                tall[:size.steps, :] = jnp.where(sub == 0, own, other)
                fresh[r, which, j] = tall[...].astype(BF)


def arrange(size, new_query, new_kv):
    return pl.pallas_call(
        functools.partial(arrange_kernel, size),
        in_specs=[IN_VMEM, IN_VMEM],
        out_specs=[IN_VMEM, IN_VMEM],
        out_shape=[
            pltpu.VMEM((size.count, size.mine, size.wide, HEAD_DIM), BF),
            pltpu.VMEM((size.count, 2, size.mine, TILE, HEAD_DIM), BF),
        ],
        scratch_shapes=[pltpu.VMEM((size.wide, HEAD_DIM), F32), pltpu.VMEM((TILE, HEAD_DIM), F32)],
        compiler_params=LIMIT,
    )(hbm(new_query), hbm(new_kv))


def side_copies(size, k, parts, cache, out, own, sems, base=0):
    sub = lax.axis_index("sub")
    row = size.source_row(k)
    first = (sub if own else 1 - sub) * size.rest
    copies = []
    for p, which in enumerate(parts):
        for j in range(size.mine):
            lanes = pl.ds(pl.multiple_of((first + j) * HEAD_DIM, HEAD_DIM), HEAD_DIM)
            at = p * size.mine + j
            source = out[at] if isinstance(out, tuple) else out.at[pl.ds(at * size.span, size.span)]
            copies.append(
                pltpu.make_async_copy(source, cache.at[row, which, :, lanes], sems.at[base, at])
            )
    return copies


def row_copies(size, k, parts, cache, mine, theirs, sems):
    copies = side_copies(size, k, parts, cache, mine, True, sems)
    if size.rest:
        copies += side_copies(size, k, parts, cache, theirs, False, sems, 1)
    return copies


def rebuild_half(size, message, tables, out, own):
    sub = lax.axis_index("sub")
    side_at = size.side_at((0,))
    side = tables[side_at:side_at + TILE, :].astype(F32)
    length = side[2 * size.heads:2 * size.heads + 1, :]
    base = sub * size.span
    last = sub != 0 if own else sub == 0
    for j in range(size.mine):
        h = size.heads + j
        scale = jnp.where(last, side[h + size.rest:h + size.rest + 1, :], side[h:h + 1, :])
        table = size.mine * size.span + j * size.rows
        anchor = message[table:table + size.rows, :].astype(F32)
        for i in range(size.rows):
            part = slice(j * size.span + i * size.repeat, j * size.span + (i + 1) * size.repeat)
            value = anchor[i:i + 1, :] + scale * message[part, :].astype(F32)
            keep = (base + i * size.repeat).astype(F32) < length
            out[part, :] = jnp.where(keep, value, jnp.float32(0.0)).astype(BF)


def rebuild_heads(size, parts, message, tables, mine, theirs):
    sub = lax.axis_index("sub")
    rest = size.heads - size.mine
    side_at = size.side_at(parts if 0 in parts else (0,))
    side = tables[side_at:side_at + TILE, :].astype(F32)
    length = side[2 * size.heads:2 * size.heads + 1, :]
    base = sub * size.span
    for o, out in enumerate((theirs, mine)):
        first = (1 - sub) * rest if o == 0 else sub * rest
        other = sub == 0 if o == 0 else sub != 0
        for p, which in enumerate(parts):
            for j in range(size.mine):
                h = which * size.heads + j
                scale = jnp.where(other, side[h + rest:h + rest + 1, :], side[h:h + 1, :])
                table = pl.multiple_of(
                    size.anchor_at(which, parts) + (first + j) * size.rows, TILE
                )
                anchor = message[pl.ds(table, size.rows), :].astype(F32)
                source = (p * size.heads + first + j) * size.span
                to = (p * size.mine + j) * size.span
                target = out
                if isinstance(out, tuple):
                    target, to = out[p * size.mine + j], 0
                for i in range(size.rows):
                    at = pl.multiple_of(source + i * size.repeat, TILE)
                    value = anchor[i:i + 1, :] + scale * message[pl.ds(at, size.repeat), :].astype(F32)
                    keep = (base + i * size.repeat).astype(F32) < length
                    value = jnp.where(keep, value, jnp.float32(0.0)).astype(BF)
                    target[to + i * size.repeat:to + (i + 1) * size.repeat, :] = value


def rebuild_kernel(size, parts, chained, split, message, *refs):
    mine, *theirs = refs[2 * chained + 2:]
    rebuild_heads(size, parts, message, message, mine, tuple(theirs) if split else theirs[0])


def rebuild(size, parts, message, state, split=False):
    args = [vmem(message)]
    in_specs = [IN_VMEM]
    aliases = {}
    if state is not None:
        aliases = {1: 0, 2: 1}
        args += list(state)
        in_specs += [IN_HBM, IN_HBM]
    given = (len(parts) * size.mine * size.span, HEAD_DIM)
    many, one = (size.mine, (size.span, HEAD_DIM)) if split else (1, given)
    out = pl.pallas_call(
        functools.partial(rebuild_kernel, size, parts, state is not None, split),
        in_specs=in_specs,
        out_specs=[IN_HBM, IN_HBM, IN_VMEM] + [IN_VMEM] * many,
        out_shape=[
            pltpu.HBM((size.count, 2, size.span, size.channels), BF),
            pltpu.HBM((size.count, size.steps, size.q_local * HEAD_DIM), BF),
            pltpu.VMEM(given, BF),
        ] + [pltpu.VMEM(one, BF)] * many,
        input_output_aliases=aliases,
        compiler_params=LIMIT,
        cost_estimate=pl.CostEstimate(
            flops=4 * len(parts) * size.span * size.channels,
            bytes_accessed=6 * len(parts) * size.span * size.channels,
            transcendentals=0,
        ),
    )(*args)
    return tuple(out[:2]), out[2], (tuple(out[3:]) if split else out[3])


def weigh(size, j, q, new_key, key_mine, key_other, live_mine, live_other, causal):
    factor = 1.0 / math.sqrt(HEAD_DIM)
    s0 = lax.dot_general(q, key_mine, NT, preferred_element_type=F32) * factor
    s1 = lax.dot_general(q, key_other, NT, preferred_element_type=F32) * factor
    s2 = lax.dot_general(q, new_key, NT, preferred_element_type=F32) * factor
    s0 = jnp.where(live_mine, s0, jnp.float32(LOW))
    s1 = jnp.where(live_other, s1, jnp.float32(LOW))
    s2 = jnp.where(causal, s2, jnp.float32(LOW))
    top = jnp.maximum(
        jnp.max(jnp.maximum(s0, s1), axis=1, keepdims=True), jnp.max(s2, axis=1, keepdims=True)
    )
    w0 = jnp.where(live_mine, jnp.exp(s0 - top), jnp.float32(0.0))
    w1 = jnp.where(live_other, jnp.exp(s1 - top), jnp.float32(0.0))
    w2 = jnp.where(causal, jnp.exp(s2 - top), jnp.float32(0.0))
    total = jnp.sum(w0 + w1, axis=1, keepdims=True) + jnp.sum(w2, axis=1, keepdims=True)
    return w0.astype(BF), w1.astype(BF), w2.astype(BF), total


def masks(size, tables, parts, fresh):
    sub = lax.axis_index("sub")
    at = size.side_at(parts)
    side = tables[at:at + TILE, :].astype(F32)
    length = side[2 * size.heads:2 * size.heads + 1, 0:1]
    spot = lax.broadcasted_iota(jnp.int32, (1, size.span), 1)
    live_mine = (spot + sub * size.span).astype(F32) < length
    live_other = (spot + (1 - sub) * size.span).astype(F32) < length
    step = lax.broadcasted_iota(jnp.int32, (size.wide, fresh), 0) % size.steps
    token = lax.broadcasted_iota(jnp.int32, (size.wide, fresh), 1)
    return live_mine, live_other, (token <= step) & (token < size.steps)


def start_store(size, k, parts, cache, mine, theirs, sems):
    copies = row_copies(size, k, parts, cache, mine, theirs, sems)
    for copy in copies:
        copy.start()
    return copies


def store_heads(size, k, flat, made, attended, sem, copies):
    for j in range(size.mine):
        for g in range(size.group):
            at = (j * size.group + g) * HEAD_DIM
            made[:, at:at + HEAD_DIM] = flat[j, g * size.steps:(g + 1) * size.steps, :].astype(BF)
    copy = pltpu.make_async_copy(made, attended.at[size.source_row(k)], sem)
    copy.start()
    for each in copies:
        each.wait()
    copy.wait()


def attend_kernel(size, k, query, new_kv, tables, mine, other, theirs, *refs):
    cache, attended, made, flat, sem, sems = refs[2:]
    row = size.source_row(k)
    copies = start_store(size, k, (0, 1), cache, mine, theirs, sems)
    live_mine, live_other, causal = masks(size, tables, (0, 1), new_kv.shape[3])
    for j in range(size.mine):
        keys = slice(j * size.span, (j + 1) * size.span)
        values = slice((size.mine + j) * size.span, (size.mine + j + 1) * size.span)
        w0, w1, w2, total = weigh(
            size, j, query[row, j], new_kv[row, 0, j], mine[keys, :], other[keys, :],
            live_mine, live_other, causal,
        )
        acc = jnp.dot(w0, mine[values, :], preferred_element_type=F32)
        acc = acc + jnp.dot(w1, other[values, :], preferred_element_type=F32)
        acc = acc + jnp.dot(w2, new_kv[row, 1, j], preferred_element_type=F32)
        flat[j] = acc / total
    store_heads(size, k, flat, made, attended, sem, copies)


def weights_kernel(size, k, split, query, new_kv, tables, mine, *refs):
    many = size.mine if split else 1
    other, theirs, refs = refs[:many], refs[many:2 * many], refs[2 * many:]
    theirs = theirs if split else theirs[0]
    cache, _, weights, lent, share, totals, sems = refs[2:]
    row = size.source_row(k)
    copies = start_store(size, k, (0,), cache, mine, theirs, sems)
    live_mine, live_other, causal = masks(size, tables, (0,), new_kv.shape[3])
    for j in range(size.mine):
        keys = slice(j * size.span, (j + 1) * size.span)
        w0, w1, w2, total = weigh(
            size, j, query[row, j], new_kv[row, 0, j], mine[keys, :],
            other[j][...] if split else other[0][keys, :],
            live_mine, live_other, causal,
        )
        weights[j] = w0
        lent[j] = w1
        share[j] = jnp.dot(w2, new_kv[row, 1, j], preferred_element_type=F32)
        totals[j] = jnp.broadcast_to(total, totals.shape[1:])
    for copy in copies:
        copy.wait()


def lend_kernel(size, lent, message, tables, *refs):
    _, _, theirs, given = refs[2:]
    rebuild_half(size, message, tables, theirs, False)
    for j in range(size.mine):
        values = slice(j * size.span, (j + 1) * size.span)
        given[j] = jnp.dot(lent[j], theirs[values, :], preferred_element_type=F32)


def lent_store_kernel(size, k, theirs, *refs):
    cache, _, sems = refs[2:]
    copies = side_copies(size, k, (1,), cache, theirs, False, sems)
    for copy in copies:
        copy.start()
    for copy in copies:
        copy.wait()


def last_kernel(size, k, weights, share, totals, got, message, tables, *refs):
    cache, attended, mine, made, flat, sem, sems = refs[2:]
    rebuild_half(size, message, tables, mine, True)
    copies = side_copies(size, k, (1,), cache, mine, True, sems)
    for copy in copies:
        copy.start()
    for j in range(size.mine):
        values = slice(j * size.span, (j + 1) * size.span)
        acc = share[j] + jnp.dot(weights[j], mine[values, :], preferred_element_type=F32)
        flat[j] = (acc + got[j]) / totals[j]
    store_heads(size, k, flat, made, attended, sem, copies)


def values_kernel(size, weights, share, lent, message, tables, *refs):
    _, _, mine, theirs, kept, given = refs[2:]
    rebuild_heads(size, (1,), message, tables, mine, theirs)
    for j in range(size.mine):
        values = slice(j * size.span, (j + 1) * size.span)
        kept[j] = share[j] + jnp.dot(weights[j], mine[values, :], preferred_element_type=F32)
        given[j] = jnp.dot(lent[j], theirs[values, :], preferred_element_type=F32)


def store_kernel(size, k, mine, theirs, *refs):
    cache, _, sems = refs[2:]
    for copy in start_store(size, k, (1,), cache, mine, theirs, sems):
        copy.wait()


def finish_kernel(size, k, kept, got, totals, *refs):
    _, attended, made, flat, sem = refs[2:]
    for j in range(size.mine):
        flat[j] = (kept[j] + got[j]) / totals[j]
    store_heads(size, k, flat, made, attended, sem, ())


def chained_call(size, kernel, args, state, shapes, scratch, flops):
    args = [vmem(x) for x in args]
    many = len(args)
    out = pl.pallas_call(
        kernel,
        in_specs=[IN_VMEM] * many + [IN_HBM, IN_HBM],
        out_specs=[IN_HBM, IN_HBM] + [IN_VMEM] * len(shapes),
        out_shape=[pltpu.HBM(x.shape, x.dtype) for x in state] + shapes,
        scratch_shapes=scratch,
        input_output_aliases={many: 0, many + 1: 1},
        compiler_params=LIMIT,
        cost_estimate=pl.CostEstimate(
            flops=flops,
            bytes_accessed=8 * size.span * size.channels,
            transcendentals=2 * size.mine * size.wide * size.span,
        ),
    )(*args, *state)
    return tuple(out[:2]), out[2:]


def body(deltas, anchors, chan_scale, lengths, route, new_query, new_kv):
    n = lax.axis_size("pool")
    size = Sizes(deltas, anchors, new_query, n)
    both = (0, 1)
    order = [2, 1] + list(range(3, n))
    last = order[-1]
    plan = [(k, both) for k in order[:-1]] + [(last, (0,)), (last, (1,)), (0, both)]
    query, fresh = arrange(size, new_query, new_kv)
    message = {}
    for part in (plan[:1], plan[1:]):
        msgs = list(pack(size, part, route, lengths, deltas, anchors, chan_scale))
        for k, parts in part:
            for half in range(1 + size.halved(parts)):
                msg = msgs.pop(0)
                if k:
                    msg = lax.ppermute(msg, "pool", list(enumerate(far(n, k))))
                message[(k, parts, half) if size.halved(parts) else (k, parts)] = msg

    def swapped(x):
        return lax.ppermute(x, "sub", [(0, 1), (1, 0)])

    flops = 8 * size.mine * size.wide * size.span * HEAD_DIM
    rows = [
        pltpu.VMEM((size.steps, size.q_local * HEAD_DIM), BF),
        pltpu.VMEM((size.mine, size.wide, HEAD_DIM), F32),
        pltpu.SemaphoreType.DMA,
    ]
    sems = pltpu.SemaphoreType.DMA((2, 2 * size.mine))
    wide = pltpu.VMEM((size.mine, size.wide, HEAD_DIM), F32)

    def attend(k, mine, other, theirs, state):
        state, _ = chained_call(
            size, functools.partial(attend_kernel, size, k),
            (query, fresh, message[k, both], mine, other, theirs), state, [], rows + [sems], flops,
        )
        return state

    def take(k, parts, state):
        state, mine, theirs = rebuild(size, parts, message[k, parts], state)
        return state, mine, swapped(theirs), theirs

    state, held = None, []
    for k in [0] + order[:-1]:
        state, *each = take(k, both, state)
        held.append((k, *each))
        if k:
            state = attend(*held.pop(0), state)
    state = attend(*held.pop(0), state)
    split = size.rest > 0
    tables = message[last, (0,)]
    state, mine, theirs = rebuild(size, (0,), tables, state, split)
    theirs = theirs if split else (theirs,)
    half = pltpu.VMEM((size.mine, size.wide, size.span), BF)
    state, (weights, lent, share, totals) = chained_call(
        size, functools.partial(weights_kernel, size, last, split),
        (query, fresh, tables, mine, *[swapped(x) for x in theirs], *theirs), state,
        [half, half, wide, wide], [sems], flops // 2,
    )
    given = pltpu.VMEM((size.mine * size.span, HEAD_DIM), BF)
    if split:
        state, (theirs, sums) = chained_call(
            size, functools.partial(lend_kernel, size),
            (swapped(lent), message[last, (1,), 0], tables), state, [given, wide], [], flops // 4,
        )
        got = swapped(sums)
        state, _ = chained_call(
            size, functools.partial(lent_store_kernel, size, last), (theirs,), state, [], [sems], 0
        )
        state, _ = chained_call(
            size, functools.partial(last_kernel, size, last),
            (weights, share, totals, got, message[last, (1,), 1], tables), state,
            [], [given] + rows + [sems], flops // 4,
        )
        return state
    state, (mine, theirs, kept, sums) = chained_call(
        size, functools.partial(values_kernel, size),
        (weights, share, swapped(lent), message[last, (1,)], tables), state,
        [given, given, wide, wide], [], flops // 2,
    )
    got = swapped(sums)
    state, _ = chained_call(
        size, functools.partial(store_kernel, size, last), (mine, theirs), state, [], [sems], 0
    )
    state, _ = chained_call(
        size, functools.partial(finish_kernel, size, last), (kept, got, totals), state, [], rows, 0
    )
    return state


def solution(mesh):
    placed = (
        P(("parts", "pool"), None, "sub", "tp"),
        P(("parts", "pool"), None, "sub", "tp"),
        P(("parts", "pool"), None, "tp"),
        P(("parts", "pool")),
        P(("parts", "pool")),
        P(("parts", "pool"), None, ("tp", "sub")),
        P(("parts", "pool"), None, None, "tp"),
    )
    return jax.shard_map(
        body,
        mesh=mesh,
        in_specs=placed,
        out_specs=(
            P(("parts", "pool"), None, "sub", "tp"),
            P(("parts", "pool"), None, ("tp", "sub")),
        ),
        check_vma=False,
    )
```

```python
import functools
import math

import jax
import jax.numpy as jnp
from jax import lax
from jax.experimental import pallas as pl
from jax.experimental.pallas import tpu as pltpu
from jax.sharding import PartitionSpec as P

HEAD_DIM = 128
Q_PER_KV = 8
TILE = 16
BF = jnp.bfloat16
F32 = jnp.float32
LOW = -1e30
NT = (((1,), (1,)), ((), ()))

IN_VMEM = pl.BlockSpec(memory_space=pltpu.VMEM)
IN_SMEM = pl.BlockSpec(memory_space=pltpu.SMEM)
IN_HBM = pl.BlockSpec(memory_space=pltpu.HBM)
LIMIT = pltpu.CompilerParams(vmem_limit_bytes=16 * 1024 * 1024)


def vmem(x):
    return pltpu.with_memory_space_constraint(x, pltpu.VMEM)


def hbm(x):
    return pltpu.with_memory_space_constraint(x, pltpu.HBM)


def far(n, k):
    ring = (0, 2, 1, 3) if n == 4 else tuple(range(n))
    return tuple(ring[(ring.index(z) + k) % n] for z in range(n))


def pick(values, at):
    out = jnp.int32(values[0])
    for i, value in enumerate(values[1:], 1):
        out = jnp.where(at == i, jnp.int32(value), out)
    return out


class Sizes:
    def __init__(self, deltas, anchors, new_query, n):
        self.n = n
        self.count, _, self.span, self.channels = deltas.shape
        self.rows = anchors.shape[2]
        self.repeat = self.span // self.rows
        self.steps = new_query.shape[1]
        self.heads = self.channels // HEAD_DIM
        self.q_local = new_query.shape[2] // HEAD_DIM
        self.mine = max(1, self.q_local // Q_PER_KV)
        self.group = self.q_local // self.mine
        self.wide = self.group * self.steps
        self.rest = self.heads - self.mine

    def anchor_at(self, which, parts):
        return (len(parts) * self.span + parts.index(which) * self.rows) * self.heads

    def side_at(self, parts):
        return len(parts) * self.heads * (self.span + self.rows)

    def message_rows(self, parts):
        return self.side_at(parts) + (TILE if 0 in parts else 0)

    def halved(self, parts):
        return parts == (1,) and self.rest > 0

    def half_rows(self):
        return self.mine * (self.span + self.rows)

    def source_row(self, k):
        return pick(far(self.n, self.n - k), lax.axis_index("pool"))


def side_block(size, scale, length):
    row = lax.broadcasted_iota(jnp.int32, (TILE, HEAD_DIM), 0)
    scale = scale.astype(F32)
    out = jnp.where(row == 2 * size.heads, length.astype(F32), jnp.float32(0.0))
    for which in range(2):
        for h in range(size.heads):
            piece = scale[which:which + 1, h * HEAD_DIM:(h + 1) * HEAD_DIM]
            out = jnp.where(row == which * size.heads + h, piece, out)
    return out.astype(BF)


def pack_kernel(size, plan, route, lengths, deltas, anchors, scale, *rest):
    outs, (held, tables, sems) = rest[:-3], rest[-3:]
    z = lax.axis_index("pool")
    sub = lax.axis_index("sub")
    outs, work = list(outs), []
    for k, parts in plan:
        msgs = [outs.pop(0) for _ in range(1 + size.halved(parts))]
        dest = pick(far(size.n, k), z)
        index = jnp.int32(0)
        for j in range(size.count):
            index = jnp.where(route[j] == dest, jnp.int32(j), index)
        for which in parts:
            slot = len(work)
            copies = (
                pltpu.make_async_copy(deltas.at[index, which], held.at[slot], sems.at[0, slot]),
                pltpu.make_async_copy(anchors.at[index, which], tables.at[slot], sems.at[1, slot]),
            )
            for copy in copies:
                copy.start()
            work.append((msgs, parts, which, slot, copies))
        if 0 in parts:
            side = side_block(size, scale[index], lengths[index])
            msgs[0][pl.ds(size.side_at(parts), TILE), :] = side
    for msgs, parts, which, slot, copies in work:
        for copy in copies:
            copy.wait()

        def fill(upper, msgs=msgs, parts=parts, which=which, slot=slot):
            for h in range(size.heads):
                lanes = slice(h * HEAD_DIM, (h + 1) * HEAD_DIM)
                if len(msgs) == 2:
                    own = (h >= size.rest) == upper
                    j, msg = h % size.mine, msgs[int(own)]
                    at, table = j * size.span, size.mine * size.span + j * size.rows
                else:
                    msg = msgs[0]
                    at = (parts.index(which) * size.heads + h) * size.span
                    table = size.anchor_at(which, parts) + h * size.rows
                msg[at:at + size.span, :] = held[slot, :, lanes]
                msg[table:table + size.rows, :] = tables[slot, :, lanes]

        if len(msgs) == 2:
            pl.when(sub == 0)(functools.partial(fill, False))
            pl.when(sub != 0)(functools.partial(fill, True))
        else:
            fill(False)


def pack(size, plan, route, lengths, deltas, anchors, scale):
    shapes = []
    for _, parts in plan:
        rows = [size.half_rows()] * 2 if size.halved(parts) else [size.message_rows(parts)]
        shapes += [pltpu.VMEM((r, HEAD_DIM), BF) for r in rows]
    slots = sum(len(parts) for _, parts in plan)
    return pl.pallas_call(
        functools.partial(pack_kernel, size, plan),
        out_shape=shapes,
        in_specs=[IN_SMEM, IN_SMEM, IN_HBM, IN_HBM, IN_VMEM],
        out_specs=[IN_VMEM] * len(shapes),
        scratch_shapes=[
            pltpu.VMEM((slots, size.span, size.channels), BF),
            pltpu.VMEM((slots, size.rows, size.channels), BF),
            pltpu.SemaphoreType.DMA((2, slots)),
        ],
        compiler_params=LIMIT,
        cost_estimate=pl.CostEstimate(
            flops=0, bytes_accessed=2 * slots * size.span * size.channels, transcendentals=0
        ),
    )(hbm(route), hbm(lengths), hbm(deltas), hbm(anchors), hbm(scale))


def arrange_kernel(size, new_query, new_kv, query, fresh, wide, tall):
    sub = lax.axis_index("sub")
    rest = size.heads - size.mine
    tall[...] = jnp.zeros_like(tall)
    for r in range(size.count):
        for j in range(size.mine):
            for g in range(size.group):
                at = (j * size.group + g) * HEAD_DIM
                piece = new_query[r, :, at:at + HEAD_DIM].astype(F32)
                wide[g * size.steps:(g + 1) * size.steps, :] = piece
            query[r, j] = wide[...].astype(BF)
            for which in range(2):
                own, other = (
                    new_kv[r, which, :, h * HEAD_DIM:(h + 1) * HEAD_DIM].astype(F32) for h in (j, j + rest)
                )
                tall[:size.steps, :] = jnp.where(sub == 0, own, other)
                fresh[r, which, j] = tall[...].astype(BF)


def arrange(size, new_query, new_kv):
    return pl.pallas_call(
        functools.partial(arrange_kernel, size),
        in_specs=[IN_VMEM, IN_VMEM],
        out_specs=[IN_VMEM, IN_VMEM],
        out_shape=[
            pltpu.VMEM((size.count, size.mine, size.wide, HEAD_DIM), BF),
            pltpu.VMEM((size.count, 2, size.mine, TILE, HEAD_DIM), BF),
        ],
        scratch_shapes=[pltpu.VMEM((size.wide, HEAD_DIM), F32), pltpu.VMEM((TILE, HEAD_DIM), F32)],
        compiler_params=LIMIT,
    )(hbm(new_query), hbm(new_kv))


def side_copies(size, k, parts, cache, out, own, sems, base=0):
    sub = lax.axis_index("sub")
    row = size.source_row(k)
    first = (sub if own else 1 - sub) * size.rest
    copies = []
    for p, which in enumerate(parts):
        for j in range(size.mine):
            lanes = pl.ds(pl.multiple_of((first + j) * HEAD_DIM, HEAD_DIM), HEAD_DIM)
            at = p * size.mine + j
            source = out[at] if isinstance(out, tuple) else out.at[pl.ds(at * size.span, size.span)]
            copies.append(
                pltpu.make_async_copy(source, cache.at[row, which, :, lanes], sems.at[base, at])
            )
    return copies


def row_copies(size, k, parts, cache, mine, theirs, sems):
    copies = side_copies(size, k, parts, cache, mine, True, sems)
    if size.rest:
        copies += side_copies(size, k, parts, cache, theirs, False, sems, 1)
    return copies


def rebuild_half(size, message, tables, out, own):
    sub = lax.axis_index("sub")
    side_at = size.side_at((0,))
    side = tables[side_at:side_at + TILE, :].astype(F32)
    length = side[2 * size.heads:2 * size.heads + 1, :]
    base = sub * size.span
    last = sub != 0 if own else sub == 0
    for j in range(size.mine):
        h = size.heads + j
        scale = jnp.where(last, side[h + size.rest:h + size.rest + 1, :], side[h:h + 1, :])
        table = size.mine * size.span + j * size.rows
        anchor = message[table:table + size.rows, :].astype(F32)
        for i in range(size.rows):
            part = slice(j * size.span + i * size.repeat, j * size.span + (i + 1) * size.repeat)
            value = anchor[i:i + 1, :] + scale * message[part, :].astype(F32)
            keep = (base + i * size.repeat).astype(F32) < length
            out[part, :] = jnp.where(keep, value, jnp.float32(0.0)).astype(BF)


def rebuild_heads(size, parts, message, tables, mine, theirs):
    sub = lax.axis_index("sub")
    rest = size.heads - size.mine
    side_at = size.side_at(parts if 0 in parts else (0,))
    side = tables[side_at:side_at + TILE, :].astype(F32)
    length = side[2 * size.heads:2 * size.heads + 1, :]
    base = sub * size.span
    for o, out in enumerate((theirs, mine)):
        first = (1 - sub) * rest if o == 0 else sub * rest
        other = sub == 0 if o == 0 else sub != 0
        for p, which in enumerate(parts):
            for j in range(size.mine):
                h = which * size.heads + j
                scale = jnp.where(other, side[h + rest:h + rest + 1, :], side[h:h + 1, :])
                table = pl.multiple_of(
                    size.anchor_at(which, parts) + (first + j) * size.rows, TILE
                )
                anchor = message[pl.ds(table, size.rows), :].astype(F32)
                source = (p * size.heads + first + j) * size.span
                to = (p * size.mine + j) * size.span
                target = out
                if isinstance(out, tuple):
                    target, to = out[p * size.mine + j], 0
                for i in range(size.rows):
                    at = pl.multiple_of(source + i * size.repeat, TILE)
                    value = anchor[i:i + 1, :] + scale * message[pl.ds(at, size.repeat), :].astype(F32)
                    keep = (base + i * size.repeat).astype(F32) < length
                    value = jnp.where(keep, value, jnp.float32(0.0)).astype(BF)
                    target[to + i * size.repeat:to + (i + 1) * size.repeat, :] = value


def rebuild_kernel(size, parts, chained, split, message, *refs):
    mine, *theirs = refs[2 * chained + 2:]
    rebuild_heads(size, parts, message, message, mine, tuple(theirs) if split else theirs[0])


def rebuild(size, parts, message, state, split=False):
    args = [vmem(message)]
    in_specs = [IN_VMEM]
    aliases = {}
    if state is not None:
        aliases = {1: 0, 2: 1}
        args += list(state)
        in_specs += [IN_HBM, IN_HBM]
    given = (len(parts) * size.mine * size.span, HEAD_DIM)
    many, one = (size.mine, (size.span, HEAD_DIM)) if split else (1, given)
    out = pl.pallas_call(
        functools.partial(rebuild_kernel, size, parts, state is not None, split),
        in_specs=in_specs,
        out_specs=[IN_HBM, IN_HBM, IN_VMEM] + [IN_VMEM] * many,
        out_shape=[
            pltpu.HBM((size.count, 2, size.span, size.channels), BF),
            pltpu.HBM((size.count, size.steps, size.q_local * HEAD_DIM), BF),
            pltpu.VMEM(given, BF),
        ] + [pltpu.VMEM(one, BF)] * many,
        input_output_aliases=aliases,
        compiler_params=LIMIT,
        cost_estimate=pl.CostEstimate(
            flops=4 * len(parts) * size.span * size.channels,
            bytes_accessed=6 * len(parts) * size.span * size.channels,
            transcendentals=0,
        ),
    )(*args)
    return tuple(out[:2]), out[2], (tuple(out[3:]) if split else out[3])


def weigh(size, j, q, new_key, key_mine, key_other, live_mine, live_other, causal):
    factor = 1.0 / math.sqrt(HEAD_DIM)
    s0 = lax.dot_general(q, key_mine, NT, preferred_element_type=F32) * factor
    s1 = lax.dot_general(q, key_other, NT, preferred_element_type=F32) * factor
    s2 = lax.dot_general(q, new_key, NT, preferred_element_type=F32) * factor
    s0 = jnp.where(live_mine, s0, jnp.float32(LOW))
    s1 = jnp.where(live_other, s1, jnp.float32(LOW))
    s2 = jnp.where(causal, s2, jnp.float32(LOW))
    top = jnp.maximum(
        jnp.max(jnp.maximum(s0, s1), axis=1, keepdims=True), jnp.max(s2, axis=1, keepdims=True)
    )
    w0 = jnp.where(live_mine, jnp.exp(s0 - top), jnp.float32(0.0))
    w1 = jnp.where(live_other, jnp.exp(s1 - top), jnp.float32(0.0))
    w2 = jnp.where(causal, jnp.exp(s2 - top), jnp.float32(0.0))
    total = jnp.sum(w0 + w1, axis=1, keepdims=True) + jnp.sum(w2, axis=1, keepdims=True)
    return w0.astype(BF), w1.astype(BF), w2.astype(BF), total


def masks(size, tables, parts, fresh):
    sub = lax.axis_index("sub")
    at = size.side_at(parts)
    side = tables[at:at + TILE, :].astype(F32)
    length = side[2 * size.heads:2 * size.heads + 1, 0:1]
    spot = lax.broadcasted_iota(jnp.int32, (1, size.span), 1)
    live_mine = (spot + sub * size.span).astype(F32) < length
    live_other = (spot + (1 - sub) * size.span).astype(F32) < length
    step = lax.broadcasted_iota(jnp.int32, (size.wide, fresh), 0) % size.steps
    token = lax.broadcasted_iota(jnp.int32, (size.wide, fresh), 1)
    return live_mine, live_other, (token <= step) & (token < size.steps)


def start_store(size, k, parts, cache, mine, theirs, sems):
    copies = row_copies(size, k, parts, cache, mine, theirs, sems)
    for copy in copies:
        copy.start()
    return copies


def store_heads(size, k, flat, made, attended, sem, copies):
    for j in range(size.mine):
        for g in range(size.group):
            at = (j * size.group + g) * HEAD_DIM
            made[:, at:at + HEAD_DIM] = flat[j, g * size.steps:(g + 1) * size.steps, :].astype(BF)
    copy = pltpu.make_async_copy(made, attended.at[size.source_row(k)], sem)
    copy.start()
    for each in copies:
        each.wait()
    copy.wait()


def attend_kernel(size, k, query, new_kv, tables, mine, other, theirs, *refs):
    cache, attended, made, flat, sem, sems = refs[2:]
    row = size.source_row(k)
    copies = start_store(size, k, (0, 1), cache, mine, theirs, sems)
    live_mine, live_other, causal = masks(size, tables, (0, 1), new_kv.shape[3])
    for j in range(size.mine):
        keys = slice(j * size.span, (j + 1) * size.span)
        values = slice((size.mine + j) * size.span, (size.mine + j + 1) * size.span)
        w0, w1, w2, total = weigh(
            size, j, query[row, j], new_kv[row, 0, j], mine[keys, :], other[keys, :],
            live_mine, live_other, causal,
        )
        acc = jnp.dot(w0, mine[values, :], preferred_element_type=F32)
        acc = acc + jnp.dot(w1, other[values, :], preferred_element_type=F32)
        acc = acc + jnp.dot(w2, new_kv[row, 1, j], preferred_element_type=F32)
        flat[j] = acc / total
    store_heads(size, k, flat, made, attended, sem, copies)


def weights_kernel(size, k, split, query, new_kv, tables, mine, *refs):
    many = size.mine if split else 1
    other, theirs, refs = refs[:many], refs[many:2 * many], refs[2 * many:]
    theirs = theirs if split else theirs[0]
    cache, _, weights, lent, share, totals, sems = refs[2:]
    row = size.source_row(k)
    copies = start_store(size, k, (0,), cache, mine, theirs, sems)
    live_mine, live_other, causal = masks(size, tables, (0,), new_kv.shape[3])
    for j in range(size.mine):
        keys = slice(j * size.span, (j + 1) * size.span)
        w0, w1, w2, total = weigh(
            size, j, query[row, j], new_kv[row, 0, j], mine[keys, :],
            other[j][...] if split else other[0][keys, :],
            live_mine, live_other, causal,
        )
        weights[j] = w0
        lent[j] = w1
        share[j] = jnp.dot(w2, new_kv[row, 1, j], preferred_element_type=F32)
        totals[j] = jnp.broadcast_to(total, totals.shape[1:])
    for copy in copies:
        copy.wait()


def lend_kernel(size, lent, message, tables, *refs):
    _, _, theirs, given = refs[2:]
    rebuild_half(size, message, tables, theirs, False)
    for j in range(size.mine):
        values = slice(j * size.span, (j + 1) * size.span)
        given[j] = jnp.dot(lent[j], theirs[values, :], preferred_element_type=F32)


def lent_store_kernel(size, k, theirs, *refs):
    cache, _, sems = refs[2:]
    copies = side_copies(size, k, (1,), cache, theirs, False, sems)
    for copy in copies:
        copy.start()
    for copy in copies:
        copy.wait()


def last_kernel(size, k, weights, share, totals, got, message, tables, *refs):
    cache, attended, mine, made, flat, sem, sems = refs[2:]
    rebuild_half(size, message, tables, mine, True)
    copies = side_copies(size, k, (1,), cache, mine, True, sems)
    for copy in copies:
        copy.start()
    for j in range(size.mine):
        values = slice(j * size.span, (j + 1) * size.span)
        acc = share[j] + jnp.dot(weights[j], mine[values, :], preferred_element_type=F32)
        flat[j] = (acc + got[j]) / totals[j]
    store_heads(size, k, flat, made, attended, sem, copies)


def values_kernel(size, weights, share, lent, message, tables, *refs):
    _, _, mine, theirs, kept, given = refs[2:]
    rebuild_heads(size, (1,), message, tables, mine, theirs)
    for j in range(size.mine):
        values = slice(j * size.span, (j + 1) * size.span)
        kept[j] = share[j] + jnp.dot(weights[j], mine[values, :], preferred_element_type=F32)
        given[j] = jnp.dot(lent[j], theirs[values, :], preferred_element_type=F32)


def store_kernel(size, k, mine, theirs, *refs):
    cache, _, sems = refs[2:]
    for copy in start_store(size, k, (1,), cache, mine, theirs, sems):
        copy.wait()


def finish_kernel(size, k, kept, got, totals, *refs):
    _, attended, made, flat, sem = refs[2:]
    for j in range(size.mine):
        flat[j] = (kept[j] + got[j]) / totals[j]
    store_heads(size, k, flat, made, attended, sem, ())


def chained_call(size, kernel, args, state, shapes, scratch, flops):
    args = [vmem(x) for x in args]
    many = len(args)
    out = pl.pallas_call(
        kernel,
        in_specs=[IN_VMEM] * many + [IN_HBM, IN_HBM],
        out_specs=[IN_HBM, IN_HBM] + [IN_VMEM] * len(shapes),
        out_shape=[pltpu.HBM(x.shape, x.dtype) for x in state] + shapes,
        scratch_shapes=scratch,
        input_output_aliases={many: 0, many + 1: 1},
        compiler_params=LIMIT,
        cost_estimate=pl.CostEstimate(
            flops=flops,
            bytes_accessed=8 * size.span * size.channels,
            transcendentals=2 * size.mine * size.wide * size.span,
        ),
    )(*args, *state)
    return tuple(out[:2]), out[2:]


def body(deltas, anchors, chan_scale, lengths, route, new_query, new_kv):
    n = lax.axis_size("pool")
    size = Sizes(deltas, anchors, new_query, n)
    both = (0, 1)
    order = list(range(n - 1, 0, -1))
    last = order[-1]
    plan = [(k, both) for k in order[:-1]] + [(last, (0,)), (last, (1,)), (0, both)]
    query, fresh = arrange(size, new_query, new_kv)
    message = {}
    for part in (plan[:1], plan[1:]):
        msgs = list(pack(size, part, route, lengths, deltas, anchors, chan_scale))
        for k, parts in part:
            for half in range(1 + size.halved(parts)):
                msg = msgs.pop(0)
                if k:
                    msg = lax.ppermute(msg, "pool", list(enumerate(far(n, k))))
                message[(k, parts, half) if size.halved(parts) else (k, parts)] = msg

    def swapped(x):
        return lax.ppermute(x, "sub", [(0, 1), (1, 0)])

    flops = 8 * size.mine * size.wide * size.span * HEAD_DIM
    rows = [
        pltpu.VMEM((size.steps, size.q_local * HEAD_DIM), BF),
        pltpu.VMEM((size.mine, size.wide, HEAD_DIM), F32),
        pltpu.SemaphoreType.DMA,
    ]
    sems = pltpu.SemaphoreType.DMA((2, 2 * size.mine))
    wide = pltpu.VMEM((size.mine, size.wide, HEAD_DIM), F32)

    def attend(k, mine, other, theirs, state):
        state, _ = chained_call(
            size, functools.partial(attend_kernel, size, k),
            (query, fresh, message[k, both], mine, other, theirs), state, [], rows + [sems], flops,
        )
        return state

    def take(k, parts, state):
        state, mine, theirs = rebuild(size, parts, message[k, parts], state)
        return state, mine, swapped(theirs), theirs

    state, held = None, []
    for k in [0] + order[:-1]:
        state, *each = take(k, both, state)
        held.append((k, *each))
        if k:
            state = attend(*held.pop(0), state)
    state = attend(*held.pop(0), state)
    split = size.rest > 0
    tables = message[last, (0,)]
    state, mine, theirs = rebuild(size, (0,), tables, state, split)
    theirs = theirs if split else (theirs,)
    half = pltpu.VMEM((size.mine, size.wide, size.span), BF)
    state, (weights, lent, share, totals) = chained_call(
        size, functools.partial(weights_kernel, size, last, split),
        (query, fresh, tables, mine, *[swapped(x) for x in theirs], *theirs), state,
        [half, half, wide, wide], [sems], flops // 2,
    )
    given = pltpu.VMEM((size.mine * size.span, HEAD_DIM), BF)
    if split:
        state, (theirs, sums) = chained_call(
            size, functools.partial(lend_kernel, size),
            (swapped(lent), message[last, (1,), 0], tables), state, [given, wide], [], flops // 4,
        )
        got = swapped(sums)
        state, _ = chained_call(
            size, functools.partial(lent_store_kernel, size, last), (theirs,), state, [], [sems], 0
        )
        state, _ = chained_call(
            size, functools.partial(last_kernel, size, last),
            (weights, share, totals, got, message[last, (1,), 1], tables), state,
            [], [given] + rows + [sems], flops // 4,
        )
        return state
    state, (mine, theirs, kept, sums) = chained_call(
        size, functools.partial(values_kernel, size),
        (weights, share, swapped(lent), message[last, (1,)], tables), state,
        [given, given, wide, wide], [], flops // 2,
    )
    got = swapped(sums)
    state, _ = chained_call(
        size, functools.partial(store_kernel, size, last), (mine, theirs), state, [], [sems], 0
    )
    state, _ = chained_call(
        size, functools.partial(finish_kernel, size, last), (kept, got, totals), state, [], rows, 0
    )
    return state


def solution(mesh):
    placed = (
        P(("parts", "pool"), None, "sub", "tp"),
        P(("parts", "pool"), None, "sub", "tp"),
        P(("parts", "pool"), None, "tp"),
        P(("parts", "pool")),
        P(("parts", "pool")),
        P(("parts", "pool"), None, ("tp", "sub")),
        P(("parts", "pool"), None, None, "tp"),
    )
    return jax.shard_map(
        body,
        mesh=mesh,
        in_specs=placed,
        out_specs=(
            P(("parts", "pool"), None, "sub", "tp"),
            P(("parts", "pool"), None, ("tp", "sub")),
        ),
        check_vma=False,
    )
```

```python
import functools
import math

import jax
import jax.numpy as jnp
from jax import lax
from jax.experimental import pallas as pl
from jax.experimental.pallas import tpu as pltpu
from jax.sharding import PartitionSpec as P

HEAD_DIM = 128
Q_PER_KV = 8
TILE = 16
BF = jnp.bfloat16
F32 = jnp.float32
LOW = -1e30
NT = (((1,), (1,)), ((), ()))

IN_VMEM = pl.BlockSpec(memory_space=pltpu.VMEM)
IN_SMEM = pl.BlockSpec(memory_space=pltpu.SMEM)
IN_HBM = pl.BlockSpec(memory_space=pltpu.HBM)
LIMIT = pltpu.CompilerParams(vmem_limit_bytes=16 * 1024 * 1024)


def vmem(x):
    return pltpu.with_memory_space_constraint(x, pltpu.VMEM)


def hbm(x):
    return pltpu.with_memory_space_constraint(x, pltpu.HBM)


def far(n, k):
    ring = (0, 2, 1, 3) if n == 4 else tuple(range(n))
    return tuple(ring[(ring.index(z) + k) % n] for z in range(n))


def pick(values, at):
    out = jnp.int32(values[0])
    for i, value in enumerate(values[1:], 1):
        out = jnp.where(at == i, jnp.int32(value), out)
    return out


class Sizes:
    def __init__(self, deltas, anchors, new_query, n):
        self.n = n
        self.count, _, self.span, self.channels = deltas.shape
        self.rows = anchors.shape[2]
        self.repeat = self.span // self.rows
        self.steps = new_query.shape[1]
        self.heads = self.channels // HEAD_DIM
        self.q_local = new_query.shape[2] // HEAD_DIM
        self.mine = max(1, self.q_local // Q_PER_KV)
        self.group = self.q_local // self.mine
        self.wide = self.group * self.steps
        self.rest = self.heads - self.mine
        self.last = 1

    def anchor_at(self, which, parts):
        return (len(parts) * self.span + parts.index(which) * self.rows) * self.heads

    def side_at(self, parts):
        return len(parts) * self.heads * (self.span + self.rows)

    def message_rows(self, parts):
        return self.side_at(parts) + (TILE if 0 in parts else 0)

    def halved(self, k, parts):
        return k == self.last and parts == (1,) and self.rest > 0

    def half_rows(self):
        return self.mine * (self.span + self.rows)

    def source_row(self, k):
        return pick(far(self.n, self.n - k), lax.axis_index("pool"))


def side_block(size, scale, length):
    row = lax.broadcasted_iota(jnp.int32, (TILE, HEAD_DIM), 0)
    scale = scale.astype(F32)
    out = jnp.where(row == 2 * size.heads, length.astype(F32), jnp.float32(0.0))
    for which in range(2):
        for h in range(size.heads):
            piece = scale[which:which + 1, h * HEAD_DIM:(h + 1) * HEAD_DIM]
            out = jnp.where(row == which * size.heads + h, piece, out)
    return out.astype(BF)


def pack_kernel(size, plan, route, lengths, deltas, anchors, scale, *rest):
    outs, (held, tables, sems) = rest[:-3], rest[-3:]
    z = lax.axis_index("pool")
    sub = lax.axis_index("sub")
    outs, work = list(outs), []
    for k, parts in plan:
        msgs = [outs.pop(0) for _ in range(1 + size.halved(k, parts))]
        dest = pick(far(size.n, k), z)
        index = jnp.int32(0)
        for j in range(size.count):
            index = jnp.where(route[j] == dest, jnp.int32(j), index)
        for which in parts:
            slot = len(work)
            copies = (
                pltpu.make_async_copy(deltas.at[index, which], held.at[slot], sems.at[0, slot]),
                pltpu.make_async_copy(anchors.at[index, which], tables.at[slot], sems.at[1, slot]),
            )
            for copy in copies:
                copy.start()
            work.append((msgs, parts, which, slot, copies))
        if 0 in parts:
            side = side_block(size, scale[index], lengths[index])
            msgs[0][pl.ds(size.side_at(parts), TILE), :] = side
    for msgs, parts, which, slot, copies in work:
        for copy in copies:
            copy.wait()

        def fill(upper, msgs=msgs, parts=parts, which=which, slot=slot):
            for h in range(size.heads):
                lanes = slice(h * HEAD_DIM, (h + 1) * HEAD_DIM)
                if len(msgs) == 2:
                    own = (h >= size.rest) == upper
                    j, msg = h % size.mine, msgs[int(own)]
                    at, table = j * size.span, size.mine * size.span + j * size.rows
                else:
                    msg = msgs[0]
                    at = (parts.index(which) * size.heads + h) * size.span
                    table = size.anchor_at(which, parts) + h * size.rows
                msg[at:at + size.span, :] = held[slot, :, lanes]
                msg[table:table + size.rows, :] = tables[slot, :, lanes]

        if len(msgs) == 2:
            pl.when(sub == 0)(functools.partial(fill, False))
            pl.when(sub != 0)(functools.partial(fill, True))
        else:
            fill(False)


def pack(size, plan, route, lengths, deltas, anchors, scale):
    shapes = []
    for k, parts in plan:
        rows = [size.half_rows()] * 2 if size.halved(k, parts) else [size.message_rows(parts)]
        shapes += [pltpu.VMEM((r, HEAD_DIM), BF) for r in rows]
    slots = sum(len(parts) for _, parts in plan)
    return pl.pallas_call(
        functools.partial(pack_kernel, size, plan),
        out_shape=shapes,
        in_specs=[IN_SMEM, IN_SMEM, IN_HBM, IN_HBM, IN_VMEM],
        out_specs=[IN_VMEM] * len(shapes),
        scratch_shapes=[
            pltpu.VMEM((slots, size.span, size.channels), BF),
            pltpu.VMEM((slots, size.rows, size.channels), BF),
            pltpu.SemaphoreType.DMA((2, slots)),
        ],
        compiler_params=LIMIT,
        cost_estimate=pl.CostEstimate(
            flops=0, bytes_accessed=2 * slots * size.span * size.channels, transcendentals=0
        ),
    )(hbm(route), hbm(lengths), hbm(deltas), hbm(anchors), hbm(scale))


def arrange_kernel(size, new_query, new_kv, query, fresh, wide, tall):
    sub = lax.axis_index("sub")
    rest = size.heads - size.mine
    tall[...] = jnp.zeros_like(tall)
    for r in range(size.count):
        for j in range(size.mine):
            for g in range(size.group):
                at = (j * size.group + g) * HEAD_DIM
                piece = new_query[r, :, at:at + HEAD_DIM].astype(F32)
                wide[g * size.steps:(g + 1) * size.steps, :] = piece
            query[r, j] = wide[...].astype(BF)
            for which in range(2):
                own, other = (
                    new_kv[r, which, :, h * HEAD_DIM:(h + 1) * HEAD_DIM].astype(F32) for h in (j, j + rest)
                )
                tall[:size.steps, :] = jnp.where(sub == 0, own, other)
                fresh[r, which, j] = tall[...].astype(BF)


def arrange(size, new_query, new_kv):
    return pl.pallas_call(
        functools.partial(arrange_kernel, size),
        in_specs=[IN_VMEM, IN_VMEM],
        out_specs=[IN_VMEM, IN_VMEM],
        out_shape=[
            pltpu.VMEM((size.count, size.mine, size.wide, HEAD_DIM), BF),
            pltpu.VMEM((size.count, 2, size.mine, TILE, HEAD_DIM), BF),
        ],
        scratch_shapes=[pltpu.VMEM((size.wide, HEAD_DIM), F32), pltpu.VMEM((TILE, HEAD_DIM), F32)],
        compiler_params=LIMIT,
    )(hbm(new_query), hbm(new_kv))


def side_copies(size, k, parts, cache, out, own, sems, base=0):
    sub = lax.axis_index("sub")
    row = size.source_row(k)
    first = (sub if own else 1 - sub) * size.rest
    copies = []
    for p, which in enumerate(parts):
        for j in range(size.mine):
            lanes = pl.ds(pl.multiple_of((first + j) * HEAD_DIM, HEAD_DIM), HEAD_DIM)
            at = p * size.mine + j
            source = out[at] if isinstance(out, tuple) else out.at[pl.ds(at * size.span, size.span)]
            copies.append(
                pltpu.make_async_copy(source, cache.at[row, which, :, lanes], sems.at[base, at])
            )
    return copies


def row_copies(size, k, parts, cache, mine, theirs, sems):
    copies = side_copies(size, k, parts, cache, mine, True, sems)
    if size.rest:
        copies += side_copies(size, k, parts, cache, theirs, False, sems, 1)
    return copies


def rebuild_half(size, message, tables, out, own):
    sub = lax.axis_index("sub")
    side_at = size.side_at((0,))
    side = tables[side_at:side_at + TILE, :].astype(F32)
    length = side[2 * size.heads:2 * size.heads + 1, :]
    base = sub * size.span
    last = sub != 0 if own else sub == 0
    for j in range(size.mine):
        h = size.heads + j
        scale = jnp.where(last, side[h + size.rest:h + size.rest + 1, :], side[h:h + 1, :])
        table = size.mine * size.span + j * size.rows
        anchor = message[table:table + size.rows, :].astype(F32)
        for i in range(size.rows):
            part = slice(j * size.span + i * size.repeat, j * size.span + (i + 1) * size.repeat)
            value = anchor[i:i + 1, :] + scale * message[part, :].astype(F32)
            keep = (base + i * size.repeat).astype(F32) < length
            out[part, :] = jnp.where(keep, value, jnp.float32(0.0)).astype(BF)


def rebuild_heads(size, parts, message, tables, mine, theirs):
    sub = lax.axis_index("sub")
    rest = size.heads - size.mine
    side_at = size.side_at(parts if 0 in parts else (0,))
    side = tables[side_at:side_at + TILE, :].astype(F32)
    length = side[2 * size.heads:2 * size.heads + 1, :]
    base = sub * size.span
    for o, out in enumerate((theirs, mine)):
        first = (1 - sub) * rest if o == 0 else sub * rest
        other = sub == 0 if o == 0 else sub != 0
        for p, which in enumerate(parts):
            for j in range(size.mine):
                h = which * size.heads + j
                scale = jnp.where(other, side[h + rest:h + rest + 1, :], side[h:h + 1, :])
                table = pl.multiple_of(
                    size.anchor_at(which, parts) + (first + j) * size.rows, TILE
                )
                anchor = message[pl.ds(table, size.rows), :].astype(F32)
                source = (p * size.heads + first + j) * size.span
                to = (p * size.mine + j) * size.span
                target = out
                if isinstance(out, tuple):
                    target, to = out[p * size.mine + j], 0
                for i in range(size.rows):
                    at = pl.multiple_of(source + i * size.repeat, TILE)
                    value = anchor[i:i + 1, :] + scale * message[pl.ds(at, size.repeat), :].astype(F32)
                    keep = (base + i * size.repeat).astype(F32) < length
                    value = jnp.where(keep, value, jnp.float32(0.0)).astype(BF)
                    target[to + i * size.repeat:to + (i + 1) * size.repeat, :] = value


def rebuild_kernel(size, parts, chained, split, pair, message, *refs):
    mine, *theirs = refs[pair + 2 * chained + 2:]
    if pair:
        half = size.mine * size.span
        for which, source in enumerate((message, refs[0])):
            rows = pl.ds(which * half, half)
            rebuild_heads(size, (which,), source, message, mine.at[rows], theirs[0].at[rows])
    else:
        rebuild_heads(size, parts, message, message, mine, tuple(theirs) if split else theirs[0])


def rebuild(size, parts, messages, state, split=False):
    args = [vmem(x) for x in messages]
    in_specs = [IN_VMEM] * len(args)
    aliases = {}
    if state is not None:
        aliases = {len(args): 0, len(args) + 1: 1}
        args += list(state)
        in_specs += [IN_HBM, IN_HBM]
    given = (len(parts) * size.mine * size.span, HEAD_DIM)
    many, one = (size.mine, (size.span, HEAD_DIM)) if split else (1, given)
    out = pl.pallas_call(
        functools.partial(rebuild_kernel, size, parts, state is not None, split, len(messages) - 1),
        in_specs=in_specs,
        out_specs=[IN_HBM, IN_HBM, IN_VMEM] + [IN_VMEM] * many,
        out_shape=[
            pltpu.HBM((size.count, 2, size.span, size.channels), BF),
            pltpu.HBM((size.count, size.steps, size.q_local * HEAD_DIM), BF),
            pltpu.VMEM(given, BF),
        ] + [pltpu.VMEM(one, BF)] * many,
        input_output_aliases=aliases,
        compiler_params=LIMIT,
        cost_estimate=pl.CostEstimate(
            flops=4 * len(parts) * size.span * size.channels,
            bytes_accessed=6 * len(parts) * size.span * size.channels,
            transcendentals=0,
        ),
    )(*args)
    return tuple(out[:2]), out[2], (tuple(out[3:]) if split else out[3])


def weigh(size, j, q, new_key, key_mine, key_other, live_mine, live_other, causal):
    factor = 1.0 / math.sqrt(HEAD_DIM)
    s0 = lax.dot_general(q, key_mine, NT, preferred_element_type=F32) * factor
    s1 = lax.dot_general(q, key_other, NT, preferred_element_type=F32) * factor
    s2 = lax.dot_general(q, new_key, NT, preferred_element_type=F32) * factor
    s0 = jnp.where(live_mine, s0, jnp.float32(LOW))
    s1 = jnp.where(live_other, s1, jnp.float32(LOW))
    s2 = jnp.where(causal, s2, jnp.float32(LOW))
    top = jnp.maximum(
        jnp.max(jnp.maximum(s0, s1), axis=1, keepdims=True), jnp.max(s2, axis=1, keepdims=True)
    )
    w0 = jnp.where(live_mine, jnp.exp(s0 - top), jnp.float32(0.0))
    w1 = jnp.where(live_other, jnp.exp(s1 - top), jnp.float32(0.0))
    w2 = jnp.where(causal, jnp.exp(s2 - top), jnp.float32(0.0))
    total = jnp.sum(w0 + w1, axis=1, keepdims=True) + jnp.sum(w2, axis=1, keepdims=True)
    return w0.astype(BF), w1.astype(BF), w2.astype(BF), total


def masks(size, tables, parts, fresh):
    sub = lax.axis_index("sub")
    at = size.side_at(parts)
    side = tables[at:at + TILE, :].astype(F32)
    length = side[2 * size.heads:2 * size.heads + 1, 0:1]
    spot = lax.broadcasted_iota(jnp.int32, (1, size.span), 1)
    live_mine = (spot + sub * size.span).astype(F32) < length
    live_other = (spot + (1 - sub) * size.span).astype(F32) < length
    step = lax.broadcasted_iota(jnp.int32, (size.wide, fresh), 0) % size.steps
    token = lax.broadcasted_iota(jnp.int32, (size.wide, fresh), 1)
    return live_mine, live_other, (token <= step) & (token < size.steps)


def start_store(size, k, parts, cache, mine, theirs, sems):
    copies = row_copies(size, k, parts, cache, mine, theirs, sems)
    for copy in copies:
        copy.start()
    return copies


def store_heads(size, k, flat, made, attended, sem, copies):
    for j in range(size.mine):
        for g in range(size.group):
            at = (j * size.group + g) * HEAD_DIM
            made[:, at:at + HEAD_DIM] = flat[j, g * size.steps:(g + 1) * size.steps, :].astype(BF)
    copy = pltpu.make_async_copy(made, attended.at[size.source_row(k)], sem)
    copy.start()
    for each in copies:
        each.wait()
    copy.wait()


def attend_kernel(size, k, parts, query, new_kv, tables, mine, other, theirs, *refs):
    cache, attended, made, flat, sem, sems = refs[2:]
    row = size.source_row(k)
    copies = start_store(size, k, (0, 1), cache, mine, theirs, sems)
    live_mine, live_other, causal = masks(size, tables, parts, new_kv.shape[3])
    for j in range(size.mine):
        keys = slice(j * size.span, (j + 1) * size.span)
        values = slice((size.mine + j) * size.span, (size.mine + j + 1) * size.span)
        w0, w1, w2, total = weigh(
            size, j, query[row, j], new_kv[row, 0, j], mine[keys, :], other[keys, :],
            live_mine, live_other, causal,
        )
        acc = jnp.dot(w0, mine[values, :], preferred_element_type=F32)
        acc = acc + jnp.dot(w1, other[values, :], preferred_element_type=F32)
        acc = acc + jnp.dot(w2, new_kv[row, 1, j], preferred_element_type=F32)
        flat[j] = acc / total
    store_heads(size, k, flat, made, attended, sem, copies)


def weights_kernel(size, k, split, query, new_kv, tables, mine, *refs):
    many = size.mine if split else 1
    other, theirs, refs = refs[:many], refs[many:2 * many], refs[2 * many:]
    theirs = theirs if split else theirs[0]
    cache, _, weights, lent, share, totals, sems = refs[2:]
    row = size.source_row(k)
    copies = start_store(size, k, (0,), cache, mine, theirs, sems)
    live_mine, live_other, causal = masks(size, tables, (0,), new_kv.shape[3])
    for j in range(size.mine):
        keys = slice(j * size.span, (j + 1) * size.span)
        w0, w1, w2, total = weigh(
            size, j, query[row, j], new_kv[row, 0, j], mine[keys, :],
            other[j][...] if split else other[0][keys, :],
            live_mine, live_other, causal,
        )
        weights[j] = w0
        lent[j] = w1
        share[j] = jnp.dot(w2, new_kv[row, 1, j], preferred_element_type=F32)
        totals[j] = jnp.broadcast_to(total, totals.shape[1:])
    for copy in copies:
        copy.wait()


def lend_kernel(size, lent, message, tables, *refs):
    _, _, theirs, given = refs[2:]
    rebuild_half(size, message, tables, theirs, False)
    for j in range(size.mine):
        values = slice(j * size.span, (j + 1) * size.span)
        given[j] = jnp.dot(lent[j], theirs[values, :], preferred_element_type=F32)


def lent_store_kernel(size, k, theirs, *refs):
    cache, _, sems = refs[2:]
    copies = side_copies(size, k, (1,), cache, theirs, False, sems)
    for copy in copies:
        copy.start()
    for copy in copies:
        copy.wait()


def last_kernel(size, k, weights, share, totals, got, message, tables, *refs):
    cache, attended, mine, made, flat, sem, sems = refs[2:]
    rebuild_half(size, message, tables, mine, True)
    copies = side_copies(size, k, (1,), cache, mine, True, sems)
    for copy in copies:
        copy.start()
    for j in range(size.mine):
        values = slice(j * size.span, (j + 1) * size.span)
        acc = share[j] + jnp.dot(weights[j], mine[values, :], preferred_element_type=F32)
        flat[j] = (acc + got[j]) / totals[j]
    store_heads(size, k, flat, made, attended, sem, copies)


def values_kernel(size, weights, share, lent, message, tables, *refs):
    _, _, mine, theirs, kept, given = refs[2:]
    rebuild_heads(size, (1,), message, tables, mine, theirs)
    for j in range(size.mine):
        values = slice(j * size.span, (j + 1) * size.span)
        kept[j] = share[j] + jnp.dot(weights[j], mine[values, :], preferred_element_type=F32)
        given[j] = jnp.dot(lent[j], theirs[values, :], preferred_element_type=F32)


def store_kernel(size, k, mine, theirs, *refs):
    cache, _, sems = refs[2:]
    for copy in start_store(size, k, (1,), cache, mine, theirs, sems):
        copy.wait()


def finish_kernel(size, k, kept, got, totals, *refs):
    _, attended, made, flat, sem = refs[2:]
    for j in range(size.mine):
        flat[j] = (kept[j] + got[j]) / totals[j]
    store_heads(size, k, flat, made, attended, sem, ())


def chained_call(size, kernel, args, state, shapes, scratch, flops):
    args = [vmem(x) for x in args]
    many = len(args)
    out = pl.pallas_call(
        kernel,
        in_specs=[IN_VMEM] * many + [IN_HBM, IN_HBM],
        out_specs=[IN_HBM, IN_HBM] + [IN_VMEM] * len(shapes),
        out_shape=[pltpu.HBM(x.shape, x.dtype) for x in state] + shapes,
        scratch_shapes=scratch,
        input_output_aliases={many: 0, many + 1: 1},
        compiler_params=LIMIT,
        cost_estimate=pl.CostEstimate(
            flops=flops,
            bytes_accessed=8 * size.span * size.channels,
            transcendentals=2 * size.mine * size.wide * size.span,
        ),
    )(*args, *state)
    return tuple(out[:2]), out[2:]


def body(deltas, anchors, chan_scale, lengths, route, new_query, new_kv):
    n = lax.axis_size("pool")
    size = Sizes(deltas, anchors, new_query, n)
    both = (0, 1)
    order = list(range(n - 1, 0, -1))
    last = order[-1]
    plan = [(order[0], (1,)), (order[0], (0,))]
    plan += [(k, (p,)) for k in order[1:] for p in both] + [(0, both)]
    query, fresh = arrange(size, new_query, new_kv)
    message = {}
    for part in (plan[:1], plan[1:]):
        msgs = list(pack(size, part, route, lengths, deltas, anchors, chan_scale))
        for k, parts in part:
            for half in range(1 + size.halved(k, parts)):
                msg = msgs.pop(0)
                if k:
                    msg = lax.ppermute(msg, "pool", list(enumerate(far(n, k))))
                message[(k, parts, half) if size.halved(k, parts) else (k, parts)] = msg

    def swapped(x):
        return lax.ppermute(x, "sub", [(0, 1), (1, 0)])

    flops = 8 * size.mine * size.wide * size.span * HEAD_DIM
    rows = [
        pltpu.VMEM((size.steps, size.q_local * HEAD_DIM), BF),
        pltpu.VMEM((size.mine, size.wide, HEAD_DIM), F32),
        pltpu.SemaphoreType.DMA,
    ]
    sems = pltpu.SemaphoreType.DMA((2, 2 * size.mine))
    wide = pltpu.VMEM((size.mine, size.wide, HEAD_DIM), F32)

    def attend(k, mine, other, theirs, state):
        state, _ = chained_call(
            size, functools.partial(attend_kernel, size, k, both if (k, both) in message else (0,)),
            (query, fresh, messages_of(k)[0], mine, other, theirs), state, [], rows + [sems], flops,
        )
        return state

    def messages_of(k):
        return [message[k, p] for p in ([both] if (k, both) in message else [(0,), (1,)])]

    def take(k, parts, state):
        state, mine, theirs = rebuild(size, parts, messages_of(k), state)
        return state, mine, swapped(theirs), theirs

    state, held = None, []
    for k in [0] + order[:-1]:
        state, *each = take(k, both, state)
        held.append((k, *each))
        if k:
            state = attend(*held.pop(0), state)
    state = attend(*held.pop(0), state)
    split = size.rest > 0
    tables = message[last, (0,)]
    state, mine, theirs = rebuild(size, (0,), [tables], state, split)
    theirs = theirs if split else (theirs,)
    half = pltpu.VMEM((size.mine, size.wide, size.span), BF)
    state, (weights, lent, share, totals) = chained_call(
        size, functools.partial(weights_kernel, size, last, split),
        (query, fresh, tables, mine, *[swapped(x) for x in theirs], *theirs), state,
        [half, half, wide, wide], [sems], flops // 2,
    )
    given = pltpu.VMEM((size.mine * size.span, HEAD_DIM), BF)
    if split:
        state, (theirs, sums) = chained_call(
            size, functools.partial(lend_kernel, size),
            (swapped(lent), message[last, (1,), 0], tables), state, [given, wide], [], flops // 4,
        )
        got = swapped(sums)
        state, _ = chained_call(
            size, functools.partial(lent_store_kernel, size, last), (theirs,), state, [], [sems], 0
        )
        state, _ = chained_call(
            size, functools.partial(last_kernel, size, last),
            (weights, share, totals, got, message[last, (1,), 1], tables), state,
            [], [given] + rows + [sems], flops // 4,
        )
        return state
    state, (mine, theirs, kept, sums) = chained_call(
        size, functools.partial(values_kernel, size),
        (weights, share, swapped(lent), message[last, (1,)], tables), state,
        [given, given, wide, wide], [], flops // 2,
    )
    got = swapped(sums)
    state, _ = chained_call(
        size, functools.partial(store_kernel, size, last), (mine, theirs), state, [], [sems], 0
    )
    state, _ = chained_call(
        size, functools.partial(finish_kernel, size, last), (kept, got, totals), state, [], rows, 0
    )
    return state


def solution(mesh):
    placed = (
        P(("parts", "pool"), None, "sub", "tp"),
        P(("parts", "pool"), None, "sub", "tp"),
        P(("parts", "pool"), None, "tp"),
        P(("parts", "pool")),
        P(("parts", "pool")),
        P(("parts", "pool"), None, ("tp", "sub")),
        P(("parts", "pool"), None, None, "tp"),
    )
    return jax.shard_map(
        body,
        mesh=mesh,
        in_specs=placed,
        out_specs=(
            P(("parts", "pool"), None, "sub", "tp"),
            P(("parts", "pool"), None, ("tp", "sub")),
        ),
        check_vma=False,
    )
```

```python
import functools
import math

import jax
import jax.numpy as jnp
from jax import lax
from jax.experimental import pallas as pl
from jax.experimental.pallas import tpu as pltpu
from jax.sharding import PartitionSpec as P

HEAD_DIM = 128
Q_PER_KV = 8
TILE = 16
BF = jnp.bfloat16
F32 = jnp.float32
LOW = -1e30
NT = (((1,), (1,)), ((), ()))

IN_VMEM = pl.BlockSpec(memory_space=pltpu.VMEM)
IN_SMEM = pl.BlockSpec(memory_space=pltpu.SMEM)
IN_HBM = pl.BlockSpec(memory_space=pltpu.HBM)
LIMIT = pltpu.CompilerParams(vmem_limit_bytes=16 * 1024 * 1024)


def vmem(x):
    return pltpu.with_memory_space_constraint(x, pltpu.VMEM)


def hbm(x):
    return pltpu.with_memory_space_constraint(x, pltpu.HBM)


def far(n, k):
    ring = (0, 2, 1, 3) if n == 4 else tuple(range(n))
    return tuple(ring[(ring.index(z) + k) % n] for z in range(n))


def pick(values, at):
    out = jnp.int32(values[0])
    for i, value in enumerate(values[1:], 1):
        out = jnp.where(at == i, jnp.int32(value), out)
    return out


class Sizes:
    def __init__(self, deltas, anchors, new_query, n):
        self.n = n
        self.count, _, self.span, self.channels = deltas.shape
        self.rows = anchors.shape[2]
        self.repeat = self.span // self.rows
        self.steps = new_query.shape[1]
        self.heads = self.channels // HEAD_DIM
        self.q_local = new_query.shape[2] // HEAD_DIM
        self.mine = max(1, self.q_local // Q_PER_KV)
        self.group = self.q_local // self.mine
        self.wide = self.group * self.steps
        self.rest = self.heads - self.mine
        self.last = 1

    def anchor_at(self, which, parts):
        return (len(parts) * self.span + parts.index(which) * self.rows) * self.heads

    def side_at(self, parts):
        return len(parts) * self.heads * (self.span + self.rows)

    def message_rows(self, parts):
        return self.side_at(parts) + (TILE if 0 in parts else 0)

    def halved(self, k, parts):
        return k == self.last and parts == (1,) and self.rest > 0

    def half_rows(self):
        return self.mine * (self.span + self.rows)

    def source_row(self, k):
        return pick(far(self.n, self.n - k), lax.axis_index("pool"))


def side_block(size, scale, length):
    row = lax.broadcasted_iota(jnp.int32, (TILE, HEAD_DIM), 0)
    scale = scale.astype(F32)
    out = jnp.where(row == 2 * size.heads, length.astype(F32), jnp.float32(0.0))
    for which in range(2):
        for h in range(size.heads):
            piece = scale[which:which + 1, h * HEAD_DIM:(h + 1) * HEAD_DIM]
            out = jnp.where(row == which * size.heads + h, piece, out)
    return out.astype(BF)


def pack_kernel(size, plan, route, lengths, deltas, anchors, scale, *rest):
    outs, (held, tables, sems) = rest[:-3], rest[-3:]
    z = lax.axis_index("pool")
    sub = lax.axis_index("sub")
    outs, work = list(outs), []
    for k, parts in plan:
        msgs = [outs.pop(0) for _ in range(1 + size.halved(k, parts))]
        dest = pick(far(size.n, k), z)
        index = jnp.int32(0)
        for j in range(size.count):
            index = jnp.where(route[j] == dest, jnp.int32(j), index)
        for which in parts:
            slot = len(work)
            copies = (
                pltpu.make_async_copy(deltas.at[index, which], held.at[slot], sems.at[0, slot]),
                pltpu.make_async_copy(anchors.at[index, which], tables.at[slot], sems.at[1, slot]),
            )
            for copy in copies:
                copy.start()
            work.append((msgs, parts, which, slot, copies))
        if 0 in parts:
            side = side_block(size, scale[index], lengths[index])
            msgs[0][pl.ds(size.side_at(parts), TILE), :] = side
    for msgs, parts, which, slot, copies in work:
        for copy in copies:
            copy.wait()

        def fill(upper, msgs=msgs, parts=parts, which=which, slot=slot):
            for h in range(size.heads):
                lanes = slice(h * HEAD_DIM, (h + 1) * HEAD_DIM)
                if len(msgs) == 2:
                    own = (h >= size.rest) == upper
                    j, msg = h % size.mine, msgs[int(own)]
                    at, table = j * size.span, size.mine * size.span + j * size.rows
                else:
                    msg = msgs[0]
                    at = (parts.index(which) * size.heads + h) * size.span
                    table = size.anchor_at(which, parts) + h * size.rows
                msg[at:at + size.span, :] = held[slot, :, lanes]
                msg[table:table + size.rows, :] = tables[slot, :, lanes]

        if len(msgs) == 2:
            pl.when(sub == 0)(functools.partial(fill, False))
            pl.when(sub != 0)(functools.partial(fill, True))
        else:
            fill(False)


def pack(size, plan, route, lengths, deltas, anchors, scale):
    shapes = []
    for k, parts in plan:
        rows = [size.half_rows()] * 2 if size.halved(k, parts) else [size.message_rows(parts)]
        shapes += [pltpu.VMEM((r, HEAD_DIM), BF) for r in rows]
    slots = sum(len(parts) for _, parts in plan)
    return pl.pallas_call(
        functools.partial(pack_kernel, size, plan),
        out_shape=shapes,
        in_specs=[IN_SMEM, IN_SMEM, IN_HBM, IN_HBM, IN_VMEM],
        out_specs=[IN_VMEM] * len(shapes),
        scratch_shapes=[
            pltpu.VMEM((slots, size.span, size.channels), BF),
            pltpu.VMEM((slots, size.rows, size.channels), BF),
            pltpu.SemaphoreType.DMA((2, slots)),
        ],
        compiler_params=LIMIT,
        cost_estimate=pl.CostEstimate(
            flops=0, bytes_accessed=2 * slots * size.span * size.channels, transcendentals=0
        ),
    )(hbm(route), hbm(lengths), hbm(deltas), hbm(anchors), hbm(scale))


def arrange_kernel(size, new_query, new_kv, query, fresh, wide, tall):
    sub = lax.axis_index("sub")
    rest = size.heads - size.mine
    tall[...] = jnp.zeros_like(tall)
    for r in range(size.count):
        for j in range(size.mine):
            for g in range(size.group):
                at = (j * size.group + g) * HEAD_DIM
                piece = new_query[r, :, at:at + HEAD_DIM].astype(F32)
                wide[g * size.steps:(g + 1) * size.steps, :] = piece
            query[r, j] = wide[...].astype(BF)
            for which in range(2):
                own, other = (
                    new_kv[r, which, :, h * HEAD_DIM:(h + 1) * HEAD_DIM].astype(F32) for h in (j, j + rest)
                )
                tall[:size.steps, :] = jnp.where(sub == 0, own, other)
                fresh[r, which, j] = tall[...].astype(BF)


def arrange(size, new_query, new_kv):
    return pl.pallas_call(
        functools.partial(arrange_kernel, size),
        in_specs=[IN_VMEM, IN_VMEM],
        out_specs=[IN_VMEM, IN_VMEM],
        out_shape=[
            pltpu.VMEM((size.count, size.mine, size.wide, HEAD_DIM), BF),
            pltpu.VMEM((size.count, 2, size.mine, TILE, HEAD_DIM), BF),
        ],
        scratch_shapes=[pltpu.VMEM((size.wide, HEAD_DIM), F32), pltpu.VMEM((TILE, HEAD_DIM), F32)],
        compiler_params=LIMIT,
    )(hbm(new_query), hbm(new_kv))


def side_copies(size, k, parts, cache, out, own, sems, base=0):
    sub = lax.axis_index("sub")
    row = size.source_row(k)
    first = (sub if own else 1 - sub) * size.rest
    copies = []
    for p, which in enumerate(parts):
        for j in range(size.mine):
            lanes = pl.ds(pl.multiple_of((first + j) * HEAD_DIM, HEAD_DIM), HEAD_DIM)
            at = p * size.mine + j
            source = out[at] if isinstance(out, tuple) else out.at[pl.ds(at * size.span, size.span)]
            copies.append(
                pltpu.make_async_copy(source, cache.at[row, which, :, lanes], sems.at[base, at])
            )
    return copies


def row_copies(size, k, parts, cache, mine, theirs, sems):
    copies = side_copies(size, k, parts, cache, mine, True, sems)
    if size.rest:
        copies += side_copies(size, k, parts, cache, theirs, False, sems, 1)
    return copies


def rebuild_half(size, message, tables, out, own):
    sub = lax.axis_index("sub")
    side_at = size.side_at((0,))
    side = tables[side_at:side_at + TILE, :].astype(F32)
    length = side[2 * size.heads:2 * size.heads + 1, :]
    base = sub * size.span
    last = sub != 0 if own else sub == 0
    for j in range(size.mine):
        h = size.heads + j
        scale = jnp.where(last, side[h + size.rest:h + size.rest + 1, :], side[h:h + 1, :])
        table = size.mine * size.span + j * size.rows
        anchor = message[table:table + size.rows, :].astype(F32)
        for i in range(size.rows):
            part = slice(j * size.span + i * size.repeat, j * size.span + (i + 1) * size.repeat)
            value = anchor[i:i + 1, :] + scale * message[part, :].astype(F32)
            keep = (base + i * size.repeat).astype(F32) < length
            out[part, :] = jnp.where(keep, value, jnp.float32(0.0)).astype(BF)


def rebuild_heads(size, parts, message, tables, mine, theirs):
    sub = lax.axis_index("sub")
    rest = size.heads - size.mine
    side_at = size.side_at(parts if 0 in parts else (0,))
    side = tables[side_at:side_at + TILE, :].astype(F32)
    length = side[2 * size.heads:2 * size.heads + 1, :]
    base = sub * size.span
    for o, out in enumerate((theirs, mine)):
        first = (1 - sub) * rest if o == 0 else sub * rest
        other = sub == 0 if o == 0 else sub != 0
        for p, which in enumerate(parts):
            for j in range(size.mine):
                h = which * size.heads + j
                scale = jnp.where(other, side[h + rest:h + rest + 1, :], side[h:h + 1, :])
                table = pl.multiple_of(
                    size.anchor_at(which, parts) + (first + j) * size.rows, TILE
                )
                anchor = message[pl.ds(table, size.rows), :].astype(F32)
                source = (p * size.heads + first + j) * size.span
                to = (p * size.mine + j) * size.span
                target = out
                if isinstance(out, tuple):
                    target, to = out[p * size.mine + j], 0
                for i in range(size.rows):
                    at = pl.multiple_of(source + i * size.repeat, TILE)
                    value = anchor[i:i + 1, :] + scale * message[pl.ds(at, size.repeat), :].astype(F32)
                    keep = (base + i * size.repeat).astype(F32) < length
                    value = jnp.where(keep, value, jnp.float32(0.0)).astype(BF)
                    target[to + i * size.repeat:to + (i + 1) * size.repeat, :] = value


def rebuild_kernel(size, parts, chained, split, pair, message, *refs):
    mine, *theirs = refs[pair + 2 * chained + 2:]
    if pair:
        half = size.mine * size.span
        for which, source in enumerate((message, refs[0])):
            rows = pl.ds(which * half, half)
            rebuild_heads(size, (which,), source, message, mine.at[rows], theirs[0].at[rows])
    else:
        rebuild_heads(size, parts, message, message, mine, tuple(theirs) if split else theirs[0])


def rebuild(size, parts, messages, state, split=False):
    args = [vmem(x) for x in messages]
    in_specs = [IN_VMEM] * len(args)
    aliases = {}
    if state is not None:
        aliases = {len(args): 0, len(args) + 1: 1}
        args += list(state)
        in_specs += [IN_HBM, IN_HBM]
    given = (len(parts) * size.mine * size.span, HEAD_DIM)
    many, one = (size.mine, (size.span, HEAD_DIM)) if split else (1, given)
    out = pl.pallas_call(
        functools.partial(rebuild_kernel, size, parts, state is not None, split, len(messages) - 1),
        in_specs=in_specs,
        out_specs=[IN_HBM, IN_HBM, IN_VMEM] + [IN_VMEM] * many,
        out_shape=[
            pltpu.HBM((size.count, 2, size.span, size.channels), BF),
            pltpu.HBM((size.count, size.steps, size.q_local * HEAD_DIM), BF),
            pltpu.VMEM(given, BF),
        ] + [pltpu.VMEM(one, BF)] * many,
        input_output_aliases=aliases,
        compiler_params=LIMIT,
        cost_estimate=pl.CostEstimate(
            flops=4 * len(parts) * size.span * size.channels,
            bytes_accessed=6 * len(parts) * size.span * size.channels,
            transcendentals=0,
        ),
    )(*args)
    return tuple(out[:2]), out[2], (tuple(out[3:]) if split else out[3])


def weigh(size, j, q, new_key, key_mine, key_other, live_mine, live_other, causal):
    factor = 1.0 / math.sqrt(HEAD_DIM)
    s0 = lax.dot_general(q, key_mine, NT, preferred_element_type=F32) * factor
    s1 = lax.dot_general(q, key_other, NT, preferred_element_type=F32) * factor
    s2 = lax.dot_general(q, new_key, NT, preferred_element_type=F32) * factor
    s0 = jnp.where(live_mine, s0, jnp.float32(LOW))
    s1 = jnp.where(live_other, s1, jnp.float32(LOW))
    s2 = jnp.where(causal, s2, jnp.float32(LOW))
    top = jnp.maximum(
        jnp.max(jnp.maximum(s0, s1), axis=1, keepdims=True), jnp.max(s2, axis=1, keepdims=True)
    )
    w0 = jnp.where(live_mine, jnp.exp(s0 - top), jnp.float32(0.0))
    w1 = jnp.where(live_other, jnp.exp(s1 - top), jnp.float32(0.0))
    w2 = jnp.where(causal, jnp.exp(s2 - top), jnp.float32(0.0))
    total = jnp.sum(w0 + w1, axis=1, keepdims=True) + jnp.sum(w2, axis=1, keepdims=True)
    return w0.astype(BF), w1.astype(BF), w2.astype(BF), total


def masks(size, tables, parts, fresh):
    sub = lax.axis_index("sub")
    at = size.side_at(parts)
    side = tables[at:at + TILE, :].astype(F32)
    length = side[2 * size.heads:2 * size.heads + 1, 0:1]
    spot = lax.broadcasted_iota(jnp.int32, (1, size.span), 1)
    live_mine = (spot + sub * size.span).astype(F32) < length
    live_other = (spot + (1 - sub) * size.span).astype(F32) < length
    step = lax.broadcasted_iota(jnp.int32, (size.wide, fresh), 0) % size.steps
    token = lax.broadcasted_iota(jnp.int32, (size.wide, fresh), 1)
    return live_mine, live_other, (token <= step) & (token < size.steps)


def start_store(size, k, parts, cache, mine, theirs, sems):
    copies = row_copies(size, k, parts, cache, mine, theirs, sems)
    for copy in copies:
        copy.start()
    return copies


def store_heads(size, k, flat, made, attended, sem, copies):
    for j in range(size.mine):
        for g in range(size.group):
            at = (j * size.group + g) * HEAD_DIM
            made[:, at:at + HEAD_DIM] = flat[j, g * size.steps:(g + 1) * size.steps, :].astype(BF)
    copy = pltpu.make_async_copy(made, attended.at[size.source_row(k)], sem)
    copy.start()
    for each in copies:
        each.wait()
    copy.wait()


def attend_kernel(size, k, parts, query, new_kv, tables, mine, other, theirs, *refs):
    cache, attended, made, flat, sem, sems = refs[2:]
    row = size.source_row(k)
    copies = start_store(size, k, (0, 1), cache, mine, theirs, sems)
    live_mine, live_other, causal = masks(size, tables, parts, new_kv.shape[3])
    for j in range(size.mine):
        keys = slice(j * size.span, (j + 1) * size.span)
        values = slice((size.mine + j) * size.span, (size.mine + j + 1) * size.span)
        w0, w1, w2, total = weigh(
            size, j, query[row, j], new_kv[row, 0, j], mine[keys, :], other[keys, :],
            live_mine, live_other, causal,
        )
        acc = jnp.dot(w0, mine[values, :], preferred_element_type=F32)
        acc = acc + jnp.dot(w1, other[values, :], preferred_element_type=F32)
        acc = acc + jnp.dot(w2, new_kv[row, 1, j], preferred_element_type=F32)
        flat[j] = acc / total
    store_heads(size, k, flat, made, attended, sem, copies)


def weights_kernel(size, k, split, query, new_kv, tables, mine, *refs):
    many = size.mine if split else 1
    other, refs = refs[:many], refs[many:]
    _, _, weights, lent, share, totals = refs[2:]
    row = size.source_row(k)
    live_mine, live_other, causal = masks(size, tables, (0,), new_kv.shape[3])
    for j in range(size.mine):
        keys = slice(j * size.span, (j + 1) * size.span)
        w0, w1, w2, total = weigh(
            size, j, query[row, j], new_kv[row, 0, j], mine[keys, :],
            other[j][...] if split else other[0][keys, :],
            live_mine, live_other, causal,
        )
        weights[j] = w0
        lent[j] = w1
        share[j] = jnp.dot(w2, new_kv[row, 1, j], preferred_element_type=F32)
        totals[j] = jnp.broadcast_to(total, totals.shape[1:])


def lend_kernel(size, lent, message, tables, *refs):
    _, _, theirs, given = refs[2:]
    rebuild_half(size, message, tables, theirs, False)
    for j in range(size.mine):
        values = slice(j * size.span, (j + 1) * size.span)
        given[j] = jnp.dot(lent[j], theirs[values, :], preferred_element_type=F32)


def lent_store_kernel(size, k, theirs, mine, *refs):
    keys, refs = tuple(refs[:size.mine]), refs[size.mine:]
    cache, _, sems, more = refs[2:]
    copies = side_copies(size, k, (1,), cache, theirs, False, sems)
    copies += row_copies(size, k, (0,), cache, mine, keys, more)
    for copy in copies:
        copy.start()
    for copy in copies:
        copy.wait()


def last_kernel(size, k, weights, share, totals, got, message, tables, *refs):
    cache, attended, mine, made, flat, sem, sems = refs[2:]
    rebuild_half(size, message, tables, mine, True)
    copies = side_copies(size, k, (1,), cache, mine, True, sems)
    for copy in copies:
        copy.start()
    for j in range(size.mine):
        values = slice(j * size.span, (j + 1) * size.span)
        acc = share[j] + jnp.dot(weights[j], mine[values, :], preferred_element_type=F32)
        flat[j] = (acc + got[j]) / totals[j]
    store_heads(size, k, flat, made, attended, sem, copies)


def values_kernel(size, weights, share, lent, message, tables, *refs):
    _, _, mine, theirs, kept, given = refs[2:]
    rebuild_heads(size, (1,), message, tables, mine, theirs)
    for j in range(size.mine):
        values = slice(j * size.span, (j + 1) * size.span)
        kept[j] = share[j] + jnp.dot(weights[j], mine[values, :], preferred_element_type=F32)
        given[j] = jnp.dot(lent[j], theirs[values, :], preferred_element_type=F32)


def store_kernel(size, k, mine, theirs, key_mine, key_theirs, *refs):
    cache, _, sems, more = refs[2:]
    copies = start_store(size, k, (1,), cache, mine, theirs, sems)
    copies += start_store(size, k, (0,), cache, key_mine, key_theirs, more)
    for copy in copies:
        copy.wait()


def finish_kernel(size, k, kept, got, totals, *refs):
    _, attended, made, flat, sem = refs[2:]
    for j in range(size.mine):
        flat[j] = (kept[j] + got[j]) / totals[j]
    store_heads(size, k, flat, made, attended, sem, ())


def chained_call(size, kernel, args, state, shapes, scratch, flops):
    args = [vmem(x) for x in args]
    many = len(args)
    out = pl.pallas_call(
        kernel,
        in_specs=[IN_VMEM] * many + [IN_HBM, IN_HBM],
        out_specs=[IN_HBM, IN_HBM] + [IN_VMEM] * len(shapes),
        out_shape=[pltpu.HBM(x.shape, x.dtype) for x in state] + shapes,
        scratch_shapes=scratch,
        input_output_aliases={many: 0, many + 1: 1},
        compiler_params=LIMIT,
        cost_estimate=pl.CostEstimate(
            flops=flops,
            bytes_accessed=8 * size.span * size.channels,
            transcendentals=2 * size.mine * size.wide * size.span,
        ),
    )(*args, *state)
    return tuple(out[:2]), out[2:]


def body(deltas, anchors, chan_scale, lengths, route, new_query, new_kv):
    n = lax.axis_size("pool")
    size = Sizes(deltas, anchors, new_query, n)
    both = (0, 1)
    order = list(range(n - 1, 0, -1))
    last = order[-1]
    plan = [(order[0], (1,)), (order[0], (0,))]
    plan += [(k, (p,)) for k in order[1:] for p in both] + [(0, both)]
    query, fresh = arrange(size, new_query, new_kv)
    message = {}
    for part in (plan[:1], plan[1:]):
        msgs = list(pack(size, part, route, lengths, deltas, anchors, chan_scale))
        for k, parts in part:
            for half in range(1 + size.halved(k, parts)):
                msg = msgs.pop(0)
                if k:
                    msg = lax.ppermute(msg, "pool", list(enumerate(far(n, k))))
                message[(k, parts, half) if size.halved(k, parts) else (k, parts)] = msg

    def swapped(x):
        return lax.ppermute(x, "sub", [(0, 1), (1, 0)])

    flops = 8 * size.mine * size.wide * size.span * HEAD_DIM
    rows = [
        pltpu.VMEM((size.steps, size.q_local * HEAD_DIM), BF),
        pltpu.VMEM((size.mine, size.wide, HEAD_DIM), F32),
        pltpu.SemaphoreType.DMA,
    ]
    sems = pltpu.SemaphoreType.DMA((2, 2 * size.mine))
    wide = pltpu.VMEM((size.mine, size.wide, HEAD_DIM), F32)

    def attend(k, mine, other, theirs, state):
        state, _ = chained_call(
            size, functools.partial(attend_kernel, size, k, both if (k, both) in message else (0,)),
            (query, fresh, messages_of(k)[0], mine, other, theirs), state, [], rows + [sems], flops,
        )
        return state

    def messages_of(k):
        return [message[k, p] for p in ([both] if (k, both) in message else [(0,), (1,)])]

    def take(k, parts, state):
        state, mine, theirs = rebuild(size, parts, messages_of(k), state)
        return state, mine, swapped(theirs), theirs

    state, held = None, []
    for k in [0] + order[:-1]:
        state, *each = take(k, both, state)
        held.append((k, *each))
        if k:
            state = attend(*held.pop(0), state)
    state = attend(*held.pop(0), state)
    split = size.rest > 0
    tables = message[last, (0,)]
    state, key_mine, theirs = rebuild(size, (0,), [tables], state, split)
    keys = theirs if split else (theirs,)
    half = pltpu.VMEM((size.mine, size.wide, size.span), BF)
    state, (weights, lent, share, totals) = chained_call(
        size, functools.partial(weights_kernel, size, last, split),
        (query, fresh, tables, key_mine, *[swapped(x) for x in keys]), state,
        [half, half, wide, wide], [], flops // 2,
    )
    given = pltpu.VMEM((size.mine * size.span, HEAD_DIM), BF)
    if split:
        state, (theirs, sums) = chained_call(
            size, functools.partial(lend_kernel, size),
            (swapped(lent), message[last, (1,), 0], tables), state, [given, wide], [], flops // 4,
        )
        got = swapped(sums)
        state, _ = chained_call(
            size, functools.partial(lent_store_kernel, size, last), (theirs, key_mine, *keys), state,
            [], [sems, sems], 0,
        )
        state, _ = chained_call(
            size, functools.partial(last_kernel, size, last),
            (weights, share, totals, got, message[last, (1,), 1], tables), state,
            [], [given] + rows + [sems], flops // 4,
        )
        return state
    state, (mine, theirs, kept, sums) = chained_call(
        size, functools.partial(values_kernel, size),
        (weights, share, swapped(lent), message[last, (1,)], tables), state,
        [given, given, wide, wide], [], flops // 2,
    )
    got = swapped(sums)
    state, _ = chained_call(
        size, functools.partial(store_kernel, size, last), (mine, theirs, key_mine, *keys), state,
        [], [sems, sems], 0,
    )
    state, _ = chained_call(
        size, functools.partial(finish_kernel, size, last), (kept, got, totals), state, [], rows, 0
    )
    return state


def solution(mesh):
    placed = (
        P(("parts", "pool"), None, "sub", "tp"),
        P(("parts", "pool"), None, "sub", "tp"),
        P(("parts", "pool"), None, "tp"),
        P(("parts", "pool")),
        P(("parts", "pool")),
        P(("parts", "pool"), None, ("tp", "sub")),
        P(("parts", "pool"), None, None, "tp"),
    )
    return jax.shard_map(
        body,
        mesh=mesh,
        in_specs=placed,
        out_specs=(
            P(("parts", "pool"), None, "sub", "tp"),
            P(("parts", "pool"), None, ("tp", "sub")),
        ),
        check_vma=False,
    )
```

```python
import functools
import math

import jax
import jax.numpy as jnp
from jax import lax
from jax.experimental import pallas as pl
from jax.experimental.pallas import tpu as pltpu
from jax.sharding import PartitionSpec as P

HEAD_DIM = 128
Q_PER_KV = 8
TILE = 16
BF = jnp.bfloat16
F32 = jnp.float32
LOW = -1e30
NT = (((1,), (1,)), ((), ()))

IN_VMEM = pl.BlockSpec(memory_space=pltpu.VMEM)
IN_SMEM = pl.BlockSpec(memory_space=pltpu.SMEM)
IN_HBM = pl.BlockSpec(memory_space=pltpu.HBM)
LIMIT = pltpu.CompilerParams(vmem_limit_bytes=16 * 1024 * 1024)


def vmem(x):
    return pltpu.with_memory_space_constraint(x, pltpu.VMEM)


def hbm(x):
    return pltpu.with_memory_space_constraint(x, pltpu.HBM)


def far(n, k):
    ring = (0, 2, 1, 3) if n == 4 else tuple(range(n))
    return tuple(ring[(ring.index(z) + k) % n] for z in range(n))


def pick(values, at):
    out = jnp.int32(values[0])
    for i, value in enumerate(values[1:], 1):
        out = jnp.where(at == i, jnp.int32(value), out)
    return out


class Sizes:
    def __init__(self, deltas, anchors, new_query, n):
        self.n = n
        self.count, _, self.span, self.channels = deltas.shape
        self.rows = anchors.shape[2]
        self.repeat = self.span // self.rows
        self.steps = new_query.shape[1]
        self.heads = self.channels // HEAD_DIM
        self.q_local = new_query.shape[2] // HEAD_DIM
        self.mine = max(1, self.q_local // Q_PER_KV)
        self.group = self.q_local // self.mine
        self.wide = self.group * self.steps
        self.rest = self.heads - self.mine
        self.last = 1

    def anchor_at(self, which, parts):
        return (len(parts) * self.span + parts.index(which) * self.rows) * self.heads

    def side_at(self, parts):
        return len(parts) * self.heads * (self.span + self.rows)

    def message_rows(self, parts):
        return self.side_at(parts) + (TILE if 0 in parts else 0)

    def halved(self, k, parts):
        return k == self.last and parts == (1,) and self.rest > 0

    def half_rows(self):
        return self.mine * (self.span + self.rows)

    def source_row(self, k):
        return pick(far(self.n, self.n - k), lax.axis_index("pool"))


def side_block(size, scale, length):
    row = lax.broadcasted_iota(jnp.int32, (TILE, HEAD_DIM), 0)
    scale = scale.astype(F32)
    out = jnp.where(row == 2 * size.heads, length.astype(F32), jnp.float32(0.0))
    for which in range(2):
        for h in range(size.heads):
            piece = scale[which:which + 1, h * HEAD_DIM:(h + 1) * HEAD_DIM]
            out = jnp.where(row == which * size.heads + h, piece, out)
    return out.astype(BF)


def pack_kernel(size, plan, route, lengths, deltas, anchors, scale, *rest):
    outs, (held, tables, sems) = rest[:-3], rest[-3:]
    z = lax.axis_index("pool")
    sub = lax.axis_index("sub")
    outs, work = list(outs), []
    for k, parts in plan:
        msgs = [outs.pop(0) for _ in range(1 + size.halved(k, parts))]
        dest = pick(far(size.n, k), z)
        index = jnp.int32(0)
        for j in range(size.count):
            index = jnp.where(route[j] == dest, jnp.int32(j), index)
        for which in parts:
            slot = len(work)
            copies = (
                pltpu.make_async_copy(deltas.at[index, which], held.at[slot], sems.at[0, slot]),
                pltpu.make_async_copy(anchors.at[index, which], tables.at[slot], sems.at[1, slot]),
            )
            for copy in copies:
                copy.start()
            work.append((msgs, parts, which, slot, copies))
        if 0 in parts:
            side = side_block(size, scale[index], lengths[index])
            msgs[0][pl.ds(size.side_at(parts), TILE), :] = side
    for msgs, parts, which, slot, copies in work:
        for copy in copies:
            copy.wait()

        def fill(upper, msgs=msgs, parts=parts, which=which, slot=slot):
            for h in range(size.heads):
                lanes = slice(h * HEAD_DIM, (h + 1) * HEAD_DIM)
                if len(msgs) == 2:
                    own = (h >= size.rest) == upper
                    j, msg = h % size.mine, msgs[int(own)]
                    at, table = j * size.span, size.mine * size.span + j * size.rows
                else:
                    msg = msgs[0]
                    at = (parts.index(which) * size.heads + h) * size.span
                    table = size.anchor_at(which, parts) + h * size.rows
                msg[at:at + size.span, :] = held[slot, :, lanes]
                msg[table:table + size.rows, :] = tables[slot, :, lanes]

        if len(msgs) == 2:
            pl.when(sub == 0)(functools.partial(fill, False))
            pl.when(sub != 0)(functools.partial(fill, True))
        else:
            fill(False)


def pack(size, plan, route, lengths, deltas, anchors, scale):
    shapes = []
    for k, parts in plan:
        rows = [size.half_rows()] * 2 if size.halved(k, parts) else [size.message_rows(parts)]
        shapes += [pltpu.VMEM((r, HEAD_DIM), BF) for r in rows]
    slots = sum(len(parts) for _, parts in plan)
    return pl.pallas_call(
        functools.partial(pack_kernel, size, plan),
        out_shape=shapes,
        in_specs=[IN_SMEM, IN_SMEM, IN_HBM, IN_HBM, IN_VMEM],
        out_specs=[IN_VMEM] * len(shapes),
        scratch_shapes=[
            pltpu.VMEM((slots, size.span, size.channels), BF),
            pltpu.VMEM((slots, size.rows, size.channels), BF),
            pltpu.SemaphoreType.DMA((2, slots)),
        ],
        compiler_params=LIMIT,
        cost_estimate=pl.CostEstimate(
            flops=0, bytes_accessed=2 * slots * size.span * size.channels, transcendentals=0
        ),
    )(hbm(route), hbm(lengths), hbm(deltas), hbm(anchors), hbm(scale))


def arrange_kernel(size, new_query, new_kv, query, fresh, wide, tall):
    sub = lax.axis_index("sub")
    rest = size.heads - size.mine
    tall[...] = jnp.zeros_like(tall)
    for r in range(size.count):
        for j in range(size.mine):
            for g in range(size.group):
                at = (j * size.group + g) * HEAD_DIM
                piece = new_query[r, :, at:at + HEAD_DIM].astype(F32)
                wide[g * size.steps:(g + 1) * size.steps, :] = piece
            query[r, j] = wide[...].astype(BF)
            for which in range(2):
                own, other = (
                    new_kv[r, which, :, h * HEAD_DIM:(h + 1) * HEAD_DIM].astype(F32) for h in (j, j + rest)
                )
                tall[:size.steps, :] = jnp.where(sub == 0, own, other)
                fresh[r, which, j] = tall[...].astype(BF)


def arrange(size, new_query, new_kv):
    return pl.pallas_call(
        functools.partial(arrange_kernel, size),
        in_specs=[IN_VMEM, IN_VMEM],
        out_specs=[IN_VMEM, IN_VMEM],
        out_shape=[
            pltpu.VMEM((size.count, size.mine, size.wide, HEAD_DIM), BF),
            pltpu.VMEM((size.count, 2, size.mine, TILE, HEAD_DIM), BF),
        ],
        scratch_shapes=[pltpu.VMEM((size.wide, HEAD_DIM), F32), pltpu.VMEM((TILE, HEAD_DIM), F32)],
        compiler_params=LIMIT,
    )(hbm(new_query), hbm(new_kv))


def side_copies(size, k, parts, cache, out, own, sems, base=0):
    sub = lax.axis_index("sub")
    row = size.source_row(k)
    first = (sub if own else 1 - sub) * size.rest
    copies = []
    for p, which in enumerate(parts):
        for j in range(size.mine):
            lanes = pl.ds(pl.multiple_of((first + j) * HEAD_DIM, HEAD_DIM), HEAD_DIM)
            at = p * size.mine + j
            source = out[at] if isinstance(out, tuple) else out.at[pl.ds(at * size.span, size.span)]
            copies.append(
                pltpu.make_async_copy(source, cache.at[row, which, :, lanes], sems.at[base, at])
            )
    return copies


def row_copies(size, k, parts, cache, mine, theirs, sems):
    copies = side_copies(size, k, parts, cache, mine, True, sems)
    if size.rest:
        copies += side_copies(size, k, parts, cache, theirs, False, sems, 1)
    return copies


def rebuild_half(size, message, tables, out, own):
    sub = lax.axis_index("sub")
    side_at = size.side_at((0,))
    side = tables[side_at:side_at + TILE, :].astype(F32)
    length = side[2 * size.heads:2 * size.heads + 1, :]
    base = sub * size.span
    last = sub != 0 if own else sub == 0
    for j in range(size.mine):
        h = size.heads + j
        scale = jnp.where(last, side[h + size.rest:h + size.rest + 1, :], side[h:h + 1, :])
        table = size.mine * size.span + j * size.rows
        anchor = message[table:table + size.rows, :].astype(F32)
        for i in range(size.rows):
            part = slice(j * size.span + i * size.repeat, j * size.span + (i + 1) * size.repeat)
            value = anchor[i:i + 1, :] + scale * message[part, :].astype(F32)
            keep = (base + i * size.repeat).astype(F32) < length
            out[j][i * size.repeat:(i + 1) * size.repeat, :] = jnp.where(
                keep, value, jnp.float32(0.0)
            ).astype(BF)


def rebuild_heads(size, parts, message, tables, mine, theirs):
    sub = lax.axis_index("sub")
    rest = size.heads - size.mine
    side_at = size.side_at(parts if 0 in parts else (0,))
    side = tables[side_at:side_at + TILE, :].astype(F32)
    length = side[2 * size.heads:2 * size.heads + 1, :]
    base = sub * size.span
    for o, out in enumerate((theirs, mine)):
        first = (1 - sub) * rest if o == 0 else sub * rest
        other = sub == 0 if o == 0 else sub != 0
        for p, which in enumerate(parts):
            for j in range(size.mine):
                h = which * size.heads + j
                scale = jnp.where(other, side[h + rest:h + rest + 1, :], side[h:h + 1, :])
                table = pl.multiple_of(
                    size.anchor_at(which, parts) + (first + j) * size.rows, TILE
                )
                anchor = message[pl.ds(table, size.rows), :].astype(F32)
                source = (p * size.heads + first + j) * size.span
                to = (p * size.mine + j) * size.span
                target = out
                if isinstance(out, tuple):
                    target, to = out[p * size.mine + j], 0
                for i in range(size.rows):
                    at = pl.multiple_of(source + i * size.repeat, TILE)
                    value = anchor[i:i + 1, :] + scale * message[pl.ds(at, size.repeat), :].astype(F32)
                    keep = (base + i * size.repeat).astype(F32) < length
                    value = jnp.where(keep, value, jnp.float32(0.0)).astype(BF)
                    target[to + i * size.repeat:to + (i + 1) * size.repeat, :] = value


def rebuild_kernel(size, parts, chained, split, pair, message, *refs):
    mine, *theirs = refs[pair + 2 * chained + 2:]
    if pair:
        half = size.mine * size.span
        for which, source in enumerate((message, refs[0])):
            rows = pl.ds(which * half, half)
            rebuild_heads(size, (which,), source, message, mine.at[rows], theirs[0].at[rows])
    else:
        rebuild_heads(size, parts, message, message, mine, tuple(theirs) if split else theirs[0])


def rebuild(size, parts, messages, state, split=False):
    args = [vmem(x) for x in messages]
    in_specs = [IN_VMEM] * len(args)
    aliases = {}
    if state is not None:
        aliases = {len(args): 0, len(args) + 1: 1}
        args += list(state)
        in_specs += [IN_HBM, IN_HBM]
    given = (len(parts) * size.mine * size.span, HEAD_DIM)
    many, one = (size.mine, (size.span, HEAD_DIM)) if split else (1, given)
    out = pl.pallas_call(
        functools.partial(rebuild_kernel, size, parts, state is not None, split, len(messages) - 1),
        in_specs=in_specs,
        out_specs=[IN_HBM, IN_HBM, IN_VMEM] + [IN_VMEM] * many,
        out_shape=[
            pltpu.HBM((size.count, 2, size.span, size.channels), BF),
            pltpu.HBM((size.count, size.steps, size.q_local * HEAD_DIM), BF),
            pltpu.VMEM(given, BF),
        ] + [pltpu.VMEM(one, BF)] * many,
        input_output_aliases=aliases,
        compiler_params=LIMIT,
        cost_estimate=pl.CostEstimate(
            flops=4 * len(parts) * size.span * size.channels,
            bytes_accessed=6 * len(parts) * size.span * size.channels,
            transcendentals=0,
        ),
    )(*args)
    return tuple(out[:2]), out[2], (tuple(out[3:]) if split else out[3])


def weigh(size, j, q, new_key, key_mine, key_other, live_mine, live_other, causal):
    factor = 1.0 / math.sqrt(HEAD_DIM)
    s0 = lax.dot_general(q, key_mine, NT, preferred_element_type=F32) * factor
    s1 = lax.dot_general(q, key_other, NT, preferred_element_type=F32) * factor
    s2 = lax.dot_general(q, new_key, NT, preferred_element_type=F32) * factor
    s0 = jnp.where(live_mine, s0, jnp.float32(LOW))
    s1 = jnp.where(live_other, s1, jnp.float32(LOW))
    s2 = jnp.where(causal, s2, jnp.float32(LOW))
    top = jnp.maximum(
        jnp.max(jnp.maximum(s0, s1), axis=1, keepdims=True), jnp.max(s2, axis=1, keepdims=True)
    )
    w0 = jnp.where(live_mine, jnp.exp(s0 - top), jnp.float32(0.0))
    w1 = jnp.where(live_other, jnp.exp(s1 - top), jnp.float32(0.0))
    w2 = jnp.where(causal, jnp.exp(s2 - top), jnp.float32(0.0))
    total = jnp.sum(w0 + w1, axis=1, keepdims=True) + jnp.sum(w2, axis=1, keepdims=True)
    return w0.astype(BF), w1.astype(BF), w2.astype(BF), total


def masks(size, tables, parts, fresh):
    sub = lax.axis_index("sub")
    at = size.side_at(parts)
    side = tables[at:at + TILE, :].astype(F32)
    length = side[2 * size.heads:2 * size.heads + 1, 0:1]
    spot = lax.broadcasted_iota(jnp.int32, (1, size.span), 1)
    live_mine = (spot + sub * size.span).astype(F32) < length
    live_other = (spot + (1 - sub) * size.span).astype(F32) < length
    step = lax.broadcasted_iota(jnp.int32, (size.wide, fresh), 0) % size.steps
    token = lax.broadcasted_iota(jnp.int32, (size.wide, fresh), 1)
    return live_mine, live_other, (token <= step) & (token < size.steps)


def start_store(size, k, parts, cache, mine, theirs, sems):
    copies = row_copies(size, k, parts, cache, mine, theirs, sems)
    for copy in copies:
        copy.start()
    return copies


def store_heads(size, k, flat, made, attended, sem, copies):
    for j in range(size.mine):
        for g in range(size.group):
            at = (j * size.group + g) * HEAD_DIM
            made[:, at:at + HEAD_DIM] = flat[j, g * size.steps:(g + 1) * size.steps, :].astype(BF)
    copy = pltpu.make_async_copy(made, attended.at[size.source_row(k)], sem)
    copy.start()
    for each in copies:
        each.wait()
    copy.wait()


def attend_kernel(size, k, parts, query, new_kv, tables, mine, other, theirs, *refs):
    cache, attended, made, flat, sem, sems = refs[2:]
    row = size.source_row(k)
    copies = start_store(size, k, (0, 1), cache, mine, theirs, sems)
    live_mine, live_other, causal = masks(size, tables, parts, new_kv.shape[3])
    for j in range(size.mine):
        keys = slice(j * size.span, (j + 1) * size.span)
        values = slice((size.mine + j) * size.span, (size.mine + j + 1) * size.span)
        w0, w1, w2, total = weigh(
            size, j, query[row, j], new_kv[row, 0, j], mine[keys, :], other[keys, :],
            live_mine, live_other, causal,
        )
        acc = jnp.dot(w0, mine[values, :], preferred_element_type=F32)
        acc = acc + jnp.dot(w1, other[values, :], preferred_element_type=F32)
        acc = acc + jnp.dot(w2, new_kv[row, 1, j], preferred_element_type=F32)
        flat[j] = acc / total
    store_heads(size, k, flat, made, attended, sem, copies)


def weights_kernel(size, k, split, query, new_kv, tables, mine, *refs):
    many = size.mine if split else 1
    other, refs = refs[:many], refs[many:]
    _, _, weights, lent, share, totals = refs[2:]
    row = size.source_row(k)
    live_mine, live_other, causal = masks(size, tables, (0,), new_kv.shape[3])
    for j in range(size.mine):
        keys = slice(j * size.span, (j + 1) * size.span)
        w0, w1, w2, total = weigh(
            size, j, query[row, j], new_kv[row, 0, j], mine[keys, :],
            other[j][...] if split else other[0][keys, :],
            live_mine, live_other, causal,
        )
        weights[j] = w0
        lent[j] = w1
        share[j] = jnp.dot(w2, new_kv[row, 1, j], preferred_element_type=F32)
        totals[j] = jnp.broadcast_to(total, totals.shape[1:])


def theirs_kernel(size, message, tables, *refs):
    rebuild_half(size, message, tables, refs[4:], False)


def lent_store_kernel(size, k, mine, *refs):
    many = size.mine
    theirs, keys, refs = tuple(refs[:many]), tuple(refs[many:2 * many]), refs[2 * many:]
    cache, _, sems, more = refs[2:]
    copies = side_copies(size, k, (1,), cache, theirs, False, sems)
    copies += row_copies(size, k, (0,), cache, mine, keys, more)
    for copy in copies:
        copy.start()
    for copy in copies:
        copy.wait()


def last_kernel(size, k, weights, lent, share, totals, message, tables, *refs):
    others, refs = refs[:size.mine], refs[size.mine + 2:]
    cache, attended, *rest = refs
    mine, (made, flat, sem, sems) = tuple(rest[:size.mine]), rest[size.mine:]
    rebuild_half(size, message, tables, mine, True)
    copies = side_copies(size, k, (1,), cache, mine, True, sems)
    for copy in copies:
        copy.start()
    for j in range(size.mine):
        acc = share[j] + jnp.dot(weights[j], mine[j][...], preferred_element_type=F32)
        acc = acc + jnp.dot(lent[j], others[j][...], preferred_element_type=F32)
        flat[j] = acc / totals[j]
    store_heads(size, k, flat, made, attended, sem, copies)


def values_kernel(size, weights, share, lent, message, tables, *refs):
    _, _, mine, theirs, kept, given = refs[2:]
    rebuild_heads(size, (1,), message, tables, mine, theirs)
    for j in range(size.mine):
        values = slice(j * size.span, (j + 1) * size.span)
        kept[j] = share[j] + jnp.dot(weights[j], mine[values, :], preferred_element_type=F32)
        given[j] = jnp.dot(lent[j], theirs[values, :], preferred_element_type=F32)


def store_kernel(size, k, mine, theirs, key_mine, key_theirs, *refs):
    cache, _, sems, more = refs[2:]
    copies = start_store(size, k, (1,), cache, mine, theirs, sems)
    copies += start_store(size, k, (0,), cache, key_mine, key_theirs, more)
    for copy in copies:
        copy.wait()


def finish_kernel(size, k, kept, got, totals, *refs):
    _, attended, made, flat, sem = refs[2:]
    for j in range(size.mine):
        flat[j] = (kept[j] + got[j]) / totals[j]
    store_heads(size, k, flat, made, attended, sem, ())


def chained_call(size, kernel, args, state, shapes, scratch, flops):
    args = [vmem(x) for x in args]
    many = len(args)
    out = pl.pallas_call(
        kernel,
        in_specs=[IN_VMEM] * many + [IN_HBM, IN_HBM],
        out_specs=[IN_HBM, IN_HBM] + [IN_VMEM] * len(shapes),
        out_shape=[pltpu.HBM(x.shape, x.dtype) for x in state] + shapes,
        scratch_shapes=scratch,
        input_output_aliases={many: 0, many + 1: 1},
        compiler_params=LIMIT,
        cost_estimate=pl.CostEstimate(
            flops=flops,
            bytes_accessed=8 * size.span * size.channels,
            transcendentals=2 * size.mine * size.wide * size.span,
        ),
    )(*args, *state)
    return tuple(out[:2]), out[2:]


def body(deltas, anchors, chan_scale, lengths, route, new_query, new_kv):
    n = lax.axis_size("pool")
    size = Sizes(deltas, anchors, new_query, n)
    both = (0, 1)
    order = list(range(n - 1, 0, -1))
    last = order[-1]
    plan = [(order[0], (1,)), (order[0], (0,))]
    plan += [(k, (p,)) for k in order[1:] for p in both] + [(0, both)]
    query, fresh = arrange(size, new_query, new_kv)
    message = {}
    for part in (plan[:1], plan[1:]):
        msgs = list(pack(size, part, route, lengths, deltas, anchors, chan_scale))
        for k, parts in part:
            for half in range(1 + size.halved(k, parts)):
                msg = msgs.pop(0)
                if k:
                    msg = lax.ppermute(msg, "pool", list(enumerate(far(n, k))))
                message[(k, parts, half) if size.halved(k, parts) else (k, parts)] = msg

    def swapped(x):
        return lax.ppermute(x, "sub", [(0, 1), (1, 0)])

    flops = 8 * size.mine * size.wide * size.span * HEAD_DIM
    rows = [
        pltpu.VMEM((size.steps, size.q_local * HEAD_DIM), BF),
        pltpu.VMEM((size.mine, size.wide, HEAD_DIM), F32),
        pltpu.SemaphoreType.DMA,
    ]
    sems = pltpu.SemaphoreType.DMA((2, 2 * size.mine))
    wide = pltpu.VMEM((size.mine, size.wide, HEAD_DIM), F32)

    def attend(k, mine, other, theirs, state):
        state, _ = chained_call(
            size, functools.partial(attend_kernel, size, k, both if (k, both) in message else (0,)),
            (query, fresh, messages_of(k)[0], mine, other, theirs), state, [], rows + [sems], flops,
        )
        return state

    def messages_of(k):
        return [message[k, p] for p in ([both] if (k, both) in message else [(0,), (1,)])]

    def take(k, parts, state):
        state, mine, theirs = rebuild(size, parts, messages_of(k), state)
        return state, mine, swapped(theirs), theirs

    state, held = None, []
    for k in [0] + order[:-1]:
        state, *each = take(k, both, state)
        held.append((k, *each))
        if k:
            state = attend(*held.pop(0), state)
    state = attend(*held.pop(0), state)
    split = size.rest > 0
    tables = message[last, (0,)]
    state, key_mine, theirs = rebuild(size, (0,), [tables], state, split)
    keys = theirs if split else (theirs,)
    half = pltpu.VMEM((size.mine, size.wide, size.span), BF)
    state, (weights, lent, share, totals) = chained_call(
        size, functools.partial(weights_kernel, size, last, split),
        (query, fresh, tables, key_mine, *[swapped(x) for x in keys]), state,
        [half, half, wide, wide], [], flops // 2,
    )
    given = pltpu.VMEM((size.mine * size.span, HEAD_DIM), BF)
    if split:
        head = pltpu.VMEM((size.span, HEAD_DIM), BF)
        state, theirs = chained_call(
            size, functools.partial(theirs_kernel, size), (message[last, (1,), 0], tables), state,
            [head] * size.mine, [], flops // 8,
        )
        others = [swapped(x) for x in theirs]
        state, _ = chained_call(
            size, functools.partial(lent_store_kernel, size, last), (key_mine, *theirs, *keys), state,
            [], [sems, sems], 0,
        )
        state, _ = chained_call(
            size, functools.partial(last_kernel, size, last),
            (weights, lent, share, totals, message[last, (1,), 1], tables, *others), state,
            [], [head] * size.mine + rows + [sems], flops // 4,
        )
        return state
    state, (mine, theirs, kept, sums) = chained_call(
        size, functools.partial(values_kernel, size),
        (weights, share, swapped(lent), message[last, (1,)], tables), state,
        [given, given, wide, wide], [], flops // 2,
    )
    got = swapped(sums)
    state, _ = chained_call(
        size, functools.partial(store_kernel, size, last), (mine, theirs, key_mine, *keys), state,
        [], [sems, sems], 0,
    )
    state, _ = chained_call(
        size, functools.partial(finish_kernel, size, last), (kept, got, totals), state, [], rows, 0
    )
    return state


def solution(mesh):
    placed = (
        P(("parts", "pool"), None, "sub", "tp"),
        P(("parts", "pool"), None, "sub", "tp"),
        P(("parts", "pool"), None, "tp"),
        P(("parts", "pool")),
        P(("parts", "pool")),
        P(("parts", "pool"), None, ("tp", "sub")),
        P(("parts", "pool"), None, None, "tp"),
    )
    return jax.shard_map(
        body,
        mesh=mesh,
        in_specs=placed,
        out_specs=(
            P(("parts", "pool"), None, "sub", "tp"),
            P(("parts", "pool"), None, ("tp", "sub")),
        ),
        check_vma=False,
    )
```

```python
import functools
import math

import jax
import jax.numpy as jnp
from jax import lax
from jax.experimental import pallas as pl
from jax.experimental.pallas import tpu as pltpu
from jax.sharding import PartitionSpec as P

HEAD_DIM = 128
Q_PER_KV = 8
TILE = 16
BF = jnp.bfloat16
F32 = jnp.float32
LOW = -1e30
NT = (((1,), (1,)), ((), ()))

IN_VMEM = pl.BlockSpec(memory_space=pltpu.VMEM)
IN_SMEM = pl.BlockSpec(memory_space=pltpu.SMEM)
IN_HBM = pl.BlockSpec(memory_space=pltpu.HBM)
LIMIT = pltpu.CompilerParams(vmem_limit_bytes=16 * 1024 * 1024)


def vmem(x):
    return pltpu.with_memory_space_constraint(x, pltpu.VMEM)


def hbm(x):
    return pltpu.with_memory_space_constraint(x, pltpu.HBM)


def far(n, k):
    ring = (0, 2, 1, 3) if n == 4 else tuple(range(n))
    return tuple(ring[(ring.index(z) + k) % n] for z in range(n))


def pick(values, at):
    out = jnp.int32(values[0])
    for i, value in enumerate(values[1:], 1):
        out = jnp.where(at == i, jnp.int32(value), out)
    return out


class Sizes:
    def __init__(self, deltas, anchors, new_query, n):
        self.n = n
        self.count, _, self.span, self.channels = deltas.shape
        self.rows = anchors.shape[2]
        self.repeat = self.span // self.rows
        self.steps = new_query.shape[1]
        self.heads = self.channels // HEAD_DIM
        self.q_local = new_query.shape[2] // HEAD_DIM
        self.mine = max(1, self.q_local // Q_PER_KV)
        self.group = self.q_local // self.mine
        self.wide = self.group * self.steps
        self.rest = self.heads - self.mine
        self.last = 1

    def anchor_at(self, which, parts):
        return (len(parts) * self.span + parts.index(which) * self.rows) * self.heads

    def side_at(self, parts):
        return len(parts) * self.heads * (self.span + self.rows)

    def message_rows(self, parts):
        return self.side_at(parts) + (TILE if 0 in parts else 0)

    def halved(self, k, parts):
        return k == self.last and parts == (1,) and self.rest > 0

    def half_rows(self):
        return self.mine * (self.span + self.rows)

    def source_row(self, k):
        return pick(far(self.n, self.n - k), lax.axis_index("pool"))


def side_block(size, scale, length):
    row = lax.broadcasted_iota(jnp.int32, (TILE, HEAD_DIM), 0)
    scale = scale.astype(F32)
    out = jnp.where(row == 2 * size.heads, length.astype(F32), jnp.float32(0.0))
    for which in range(2):
        for h in range(size.heads):
            piece = scale[which:which + 1, h * HEAD_DIM:(h + 1) * HEAD_DIM]
            out = jnp.where(row == which * size.heads + h, piece, out)
    return out.astype(BF)


def pack_kernel(size, plan, route, lengths, deltas, anchors, scale, *rest):
    outs, (held, tables, sems) = rest[:-3], rest[-3:]
    z = lax.axis_index("pool")
    sub = lax.axis_index("sub")
    outs, work = list(outs), []
    for k, parts in plan:
        msgs = [outs.pop(0) for _ in range(1 + size.halved(k, parts))]
        dest = pick(far(size.n, k), z)
        index = jnp.int32(0)
        for j in range(size.count):
            index = jnp.where(route[j] == dest, jnp.int32(j), index)
        for which in parts:
            slot = len(work)
            copies = (
                pltpu.make_async_copy(deltas.at[index, which], held.at[slot], sems.at[0, slot]),
                pltpu.make_async_copy(anchors.at[index, which], tables.at[slot], sems.at[1, slot]),
            )
            for copy in copies:
                copy.start()
            work.append((msgs, parts, which, slot, copies))
        if 0 in parts:
            side = side_block(size, scale[index], lengths[index])
            msgs[0][pl.ds(size.side_at(parts), TILE), :] = side
    for msgs, parts, which, slot, copies in work:
        for copy in copies:
            copy.wait()

        def fill(upper, msgs=msgs, parts=parts, which=which, slot=slot):
            for h in range(size.heads):
                lanes = slice(h * HEAD_DIM, (h + 1) * HEAD_DIM)
                if len(msgs) == 2:
                    own = (h >= size.rest) == upper
                    j, msg = h % size.mine, msgs[int(own)]
                    at, table = j * size.span, size.mine * size.span + j * size.rows
                else:
                    msg = msgs[0]
                    at = (parts.index(which) * size.heads + h) * size.span
                    table = size.anchor_at(which, parts) + h * size.rows
                msg[at:at + size.span, :] = held[slot, :, lanes]
                msg[table:table + size.rows, :] = tables[slot, :, lanes]

        if len(msgs) == 2:
            pl.when(sub == 0)(functools.partial(fill, False))
            pl.when(sub != 0)(functools.partial(fill, True))
        else:
            fill(False)


def pack(size, plan, route, lengths, deltas, anchors, scale):
    shapes = []
    for k, parts in plan:
        rows = [size.half_rows()] * 2 if size.halved(k, parts) else [size.message_rows(parts)]
        shapes += [pltpu.VMEM((r, HEAD_DIM), BF) for r in rows]
    slots = sum(len(parts) for _, parts in plan)
    return pl.pallas_call(
        functools.partial(pack_kernel, size, plan),
        out_shape=shapes,
        in_specs=[IN_SMEM, IN_SMEM, IN_HBM, IN_HBM, IN_VMEM],
        out_specs=[IN_VMEM] * len(shapes),
        scratch_shapes=[
            pltpu.VMEM((slots, size.span, size.channels), BF),
            pltpu.VMEM((slots, size.rows, size.channels), BF),
            pltpu.SemaphoreType.DMA((2, slots)),
        ],
        compiler_params=LIMIT,
        cost_estimate=pl.CostEstimate(
            flops=0, bytes_accessed=2 * slots * size.span * size.channels, transcendentals=0
        ),
    )(hbm(route), hbm(lengths), hbm(deltas), hbm(anchors), hbm(scale))


def arrange_kernel(size, new_query, new_kv, query, fresh, wide, tall):
    sub = lax.axis_index("sub")
    rest = size.heads - size.mine
    tall[...] = jnp.zeros_like(tall)
    for r in range(size.count):
        for j in range(size.mine):
            for g in range(size.group):
                at = (j * size.group + g) * HEAD_DIM
                piece = new_query[r, :, at:at + HEAD_DIM].astype(F32)
                wide[g * size.steps:(g + 1) * size.steps, :] = piece
            query[r, j] = wide[...].astype(BF)
            for which in range(2):
                own, other = (
                    new_kv[r, which, :, h * HEAD_DIM:(h + 1) * HEAD_DIM].astype(F32) for h in (j, j + rest)
                )
                tall[:size.steps, :] = jnp.where(sub == 0, own, other)
                fresh[r, which, j] = tall[...].astype(BF)


def arrange(size, new_query, new_kv):
    return pl.pallas_call(
        functools.partial(arrange_kernel, size),
        in_specs=[IN_VMEM, IN_VMEM],
        out_specs=[IN_VMEM, IN_VMEM],
        out_shape=[
            pltpu.VMEM((size.count, size.mine, size.wide, HEAD_DIM), BF),
            pltpu.VMEM((size.count, 2, size.mine, TILE, HEAD_DIM), BF),
        ],
        scratch_shapes=[pltpu.VMEM((size.wide, HEAD_DIM), F32), pltpu.VMEM((TILE, HEAD_DIM), F32)],
        compiler_params=LIMIT,
    )(hbm(new_query), hbm(new_kv))


def side_copies(size, k, parts, cache, out, own, sems, base=0):
    sub = lax.axis_index("sub")
    row = size.source_row(k)
    first = (sub if own else 1 - sub) * size.rest
    copies = []
    for p, which in enumerate(parts):
        for j in range(size.mine):
            lanes = pl.ds(pl.multiple_of((first + j) * HEAD_DIM, HEAD_DIM), HEAD_DIM)
            at = p * size.mine + j
            source = out[at] if isinstance(out, tuple) else out.at[pl.ds(at * size.span, size.span)]
            copies.append(
                pltpu.make_async_copy(source, cache.at[row, which, :, lanes], sems.at[base, at])
            )
    return copies


def row_copies(size, k, parts, cache, mine, theirs, sems):
    copies = side_copies(size, k, parts, cache, mine, True, sems)
    if size.rest:
        copies += side_copies(size, k, parts, cache, theirs, False, sems, 1)
    return copies


def rebuild_half(size, message, tables, out, own):
    sub = lax.axis_index("sub")
    side_at = size.side_at((0,))
    side = tables[side_at:side_at + TILE, :].astype(F32)
    length = side[2 * size.heads:2 * size.heads + 1, :]
    base = sub * size.span
    last = sub != 0 if own else sub == 0
    for j in range(size.mine):
        h = size.heads + j
        scale = jnp.where(last, side[h + size.rest:h + size.rest + 1, :], side[h:h + 1, :])
        table = size.mine * size.span + j * size.rows
        anchor = message[table:table + size.rows, :].astype(F32)
        for i in range(size.rows):
            part = slice(j * size.span + i * size.repeat, j * size.span + (i + 1) * size.repeat)
            value = anchor[i:i + 1, :] + scale * message[part, :].astype(F32)
            keep = (base + i * size.repeat).astype(F32) < length
            out[j][i * size.repeat:(i + 1) * size.repeat, :] = jnp.where(
                keep, value, jnp.float32(0.0)
            ).astype(BF)


def rebuild_heads(size, parts, message, tables, mine, theirs):
    sub = lax.axis_index("sub")
    rest = size.heads - size.mine
    side_at = size.side_at(parts if 0 in parts else (0,))
    side = tables[side_at:side_at + TILE, :].astype(F32)
    length = side[2 * size.heads:2 * size.heads + 1, :]
    base = sub * size.span
    for o, out in enumerate((theirs, mine)):
        first = (1 - sub) * rest if o == 0 else sub * rest
        other = sub == 0 if o == 0 else sub != 0
        for p, which in enumerate(parts):
            for j in range(size.mine):
                h = which * size.heads + j
                scale = jnp.where(other, side[h + rest:h + rest + 1, :], side[h:h + 1, :])
                table = pl.multiple_of(
                    size.anchor_at(which, parts) + (first + j) * size.rows, TILE
                )
                anchor = message[pl.ds(table, size.rows), :].astype(F32)
                source = (p * size.heads + first + j) * size.span
                to = (p * size.mine + j) * size.span
                target = out
                if isinstance(out, tuple):
                    target, to = out[p * size.mine + j], 0
                for i in range(size.rows):
                    at = pl.multiple_of(source + i * size.repeat, TILE)
                    value = anchor[i:i + 1, :] + scale * message[pl.ds(at, size.repeat), :].astype(F32)
                    keep = (base + i * size.repeat).astype(F32) < length
                    value = jnp.where(keep, value, jnp.float32(0.0)).astype(BF)
                    target[to + i * size.repeat:to + (i + 1) * size.repeat, :] = value


def rebuild_kernel(size, parts, chained, split, pair, message, *refs):
    mine, *theirs = refs[pair + 2 * chained + 2:]
    if pair:
        half = size.mine * size.span
        for which, source in enumerate((message, refs[0])):
            rows = pl.ds(which * half, half)
            rebuild_heads(size, (which,), source, message, mine.at[rows], theirs[0].at[rows])
    else:
        rebuild_heads(size, parts, message, message, mine, tuple(theirs) if split else theirs[0])


def rebuild(size, parts, messages, state, split=False):
    args = [vmem(x) for x in messages]
    in_specs = [IN_VMEM] * len(args)
    aliases = {}
    if state is not None:
        aliases = {len(args): 0, len(args) + 1: 1}
        args += list(state)
        in_specs += [IN_HBM, IN_HBM]
    given = (len(parts) * size.mine * size.span, HEAD_DIM)
    many, one = (size.mine, (size.span, HEAD_DIM)) if split else (1, given)
    out = pl.pallas_call(
        functools.partial(rebuild_kernel, size, parts, state is not None, split, len(messages) - 1),
        in_specs=in_specs,
        out_specs=[IN_HBM, IN_HBM, IN_VMEM] + [IN_VMEM] * many,
        out_shape=[
            pltpu.HBM((size.count, 2, size.span, size.channels), BF),
            pltpu.HBM((size.count, size.steps, size.q_local * HEAD_DIM), BF),
            pltpu.VMEM(given, BF),
        ] + [pltpu.VMEM(one, BF)] * many,
        input_output_aliases=aliases,
        compiler_params=LIMIT,
        cost_estimate=pl.CostEstimate(
            flops=4 * len(parts) * size.span * size.channels,
            bytes_accessed=6 * len(parts) * size.span * size.channels,
            transcendentals=0,
        ),
    )(*args)
    return tuple(out[:2]), out[2], (tuple(out[3:]) if split else out[3])


def weigh(size, j, q, new_key, key_mine, key_other, live_mine, live_other, causal):
    factor = 1.0 / math.sqrt(HEAD_DIM)
    s0 = lax.dot_general(q, key_mine, NT, preferred_element_type=F32) * factor
    s1 = lax.dot_general(q, key_other, NT, preferred_element_type=F32) * factor
    s2 = lax.dot_general(q, new_key, NT, preferred_element_type=F32) * factor
    s0 = jnp.where(live_mine, s0, jnp.float32(LOW))
    s1 = jnp.where(live_other, s1, jnp.float32(LOW))
    s2 = jnp.where(causal, s2, jnp.float32(LOW))
    top = jnp.maximum(
        jnp.max(jnp.maximum(s0, s1), axis=1, keepdims=True), jnp.max(s2, axis=1, keepdims=True)
    )
    w0 = jnp.where(live_mine, jnp.exp(s0 - top), jnp.float32(0.0))
    w1 = jnp.where(live_other, jnp.exp(s1 - top), jnp.float32(0.0))
    w2 = jnp.where(causal, jnp.exp(s2 - top), jnp.float32(0.0))
    total = jnp.sum(w0 + w1, axis=1, keepdims=True) + jnp.sum(w2, axis=1, keepdims=True)
    return w0.astype(BF), w1.astype(BF), w2.astype(BF), total


def masks(size, tables, parts, fresh):
    sub = lax.axis_index("sub")
    at = size.side_at(parts)
    side = tables[at:at + TILE, :].astype(F32)
    length = side[2 * size.heads:2 * size.heads + 1, 0:1]
    spot = lax.broadcasted_iota(jnp.int32, (1, size.span), 1)
    live_mine = (spot + sub * size.span).astype(F32) < length
    live_other = (spot + (1 - sub) * size.span).astype(F32) < length
    step = lax.broadcasted_iota(jnp.int32, (size.wide, fresh), 0) % size.steps
    token = lax.broadcasted_iota(jnp.int32, (size.wide, fresh), 1)
    return live_mine, live_other, (token <= step) & (token < size.steps)


def start_store(size, k, parts, cache, mine, theirs, sems):
    copies = row_copies(size, k, parts, cache, mine, theirs, sems)
    for copy in copies:
        copy.start()
    return copies


def store_heads(size, k, flat, made, attended, sem, copies):
    for j in range(size.mine):
        for g in range(size.group):
            at = (j * size.group + g) * HEAD_DIM
            made[:, at:at + HEAD_DIM] = flat[j, g * size.steps:(g + 1) * size.steps, :].astype(BF)
    copy = pltpu.make_async_copy(made, attended.at[size.source_row(k)], sem)
    copy.start()
    for each in copies:
        each.wait()
    copy.wait()


def attend_kernel(size, k, parts, query, new_kv, tables, mine, other, theirs, *refs):
    cache, attended, made, flat, sem, sems = refs[2:]
    row = size.source_row(k)
    copies = start_store(size, k, (0, 1), cache, mine, theirs, sems)
    live_mine, live_other, causal = masks(size, tables, parts, new_kv.shape[3])
    for j in range(size.mine):
        keys = slice(j * size.span, (j + 1) * size.span)
        values = slice((size.mine + j) * size.span, (size.mine + j + 1) * size.span)
        w0, w1, w2, total = weigh(
            size, j, query[row, j], new_kv[row, 0, j], mine[keys, :], other[keys, :],
            live_mine, live_other, causal,
        )
        acc = jnp.dot(w0, mine[values, :], preferred_element_type=F32)
        acc = acc + jnp.dot(w1, other[values, :], preferred_element_type=F32)
        acc = acc + jnp.dot(w2, new_kv[row, 1, j], preferred_element_type=F32)
        flat[j] = acc / total
    store_heads(size, k, flat, made, attended, sem, copies)


def weights_kernel(size, k, split, query, new_kv, tables, mine, *refs):
    many = size.mine if split else 1
    other, refs = refs[:many], refs[many:]
    _, _, weights, lent, share, totals = refs[2:]
    row = size.source_row(k)
    live_mine, live_other, causal = masks(size, tables, (0,), new_kv.shape[3])
    for j in range(size.mine):
        keys = slice(j * size.span, (j + 1) * size.span)
        w0, w1, w2, total = weigh(
            size, j, query[row, j], new_kv[row, 0, j], mine[keys, :],
            other[j][...] if split else other[0][keys, :],
            live_mine, live_other, causal,
        )
        weights[j] = w0
        lent[j] = w1
        share[j] = jnp.dot(w2, new_kv[row, 1, j], preferred_element_type=F32)
        totals[j] = jnp.broadcast_to(total, totals.shape[1:])


def theirs_kernel(size, message, tables, *refs):
    rebuild_half(size, message, tables, refs[4:], False)


def lent_store_kernel(size, k, mine, *refs):
    many = size.mine
    theirs, keys, refs = tuple(refs[:many]), tuple(refs[many:2 * many]), refs[2 * many:]
    cache, _, sems, more = refs[2:]
    copies = side_copies(size, k, (1,), cache, theirs, False, sems)
    copies += row_copies(size, k, (0,), cache, mine, keys, more)
    for copy in copies:
        copy.start()
    for copy in copies:
        copy.wait()


def last_kernel(size, k, weights, lent, share, totals, message, tables, *refs):
    others, refs = refs[:size.mine], refs[size.mine + 2:]
    cache, attended, *rest = refs
    mine, (made, flat, sem, sems) = tuple(rest[:size.mine]), rest[size.mine:]
    rebuild_half(size, message, tables, mine, True)
    copies = side_copies(size, k, (1,), cache, mine, True, sems)
    for copy in copies:
        copy.start()
    for j in range(size.mine):
        acc = share[j] + jnp.dot(weights[j], mine[j][...], preferred_element_type=F32)
        acc = acc + jnp.dot(lent[j], others[j][...], preferred_element_type=F32)
        flat[j] = acc / totals[j]
    store_heads(size, k, flat, made, attended, sem, copies)


def values_kernel(size, weights, share, lent, message, tables, *refs):
    _, _, mine, theirs, kept, given = refs[2:]
    rebuild_heads(size, (1,), message, tables, mine, theirs)
    for j in range(size.mine):
        values = slice(j * size.span, (j + 1) * size.span)
        kept[j] = share[j] + jnp.dot(weights[j], mine[values, :], preferred_element_type=F32)
        given[j] = jnp.dot(lent[j], theirs[values, :], preferred_element_type=F32)


def store_kernel(size, k, mine, theirs, key_mine, key_theirs, *refs):
    cache, _, sems, more = refs[2:]
    copies = start_store(size, k, (1,), cache, mine, theirs, sems)
    copies += start_store(size, k, (0,), cache, key_mine, key_theirs, more)
    for copy in copies:
        copy.wait()


def finish_kernel(size, k, kept, got, totals, *refs):
    _, attended, made, flat, sem = refs[2:]
    for j in range(size.mine):
        flat[j] = (kept[j] + got[j]) / totals[j]
    store_heads(size, k, flat, made, attended, sem, ())


def chained_call(size, kernel, args, state, shapes, scratch, flops):
    args = [vmem(x) for x in args]
    many = len(args)
    out = pl.pallas_call(
        kernel,
        in_specs=[IN_VMEM] * many + [IN_HBM, IN_HBM],
        out_specs=[IN_HBM, IN_HBM] + [IN_VMEM] * len(shapes),
        out_shape=[pltpu.HBM(x.shape, x.dtype) for x in state] + shapes,
        scratch_shapes=scratch,
        input_output_aliases={many: 0, many + 1: 1},
        compiler_params=LIMIT,
        cost_estimate=pl.CostEstimate(
            flops=flops,
            bytes_accessed=8 * size.span * size.channels,
            transcendentals=2 * size.mine * size.wide * size.span,
        ),
    )(*args, *state)
    return tuple(out[:2]), out[2:]


def body(deltas, anchors, chan_scale, lengths, route, new_query, new_kv):
    n = lax.axis_size("pool")
    size = Sizes(deltas, anchors, new_query, n)
    both = (0, 1)
    order = list(range(n - 1, 0, -1))
    last = order[-1]
    plan = [(order[0], (1,)), (order[0], (0,))]
    plan += [(k, (p,)) for k in order[1:] for p in both] + [(0, both)]
    query, fresh = arrange(size, new_query, new_kv)
    message = {}
    for part in (plan[:1], plan[1:]):
        msgs = list(pack(size, part, route, lengths, deltas, anchors, chan_scale))
        for k, parts in part:
            for half in range(1 + size.halved(k, parts)):
                msg = msgs.pop(0)
                if k:
                    msg = lax.ppermute(msg, "pool", list(enumerate(far(n, k))))
                message[(k, parts, half) if size.halved(k, parts) else (k, parts)] = msg

    def swapped(x):
        return lax.ppermute(x, "sub", [(0, 1), (1, 0)])

    flops = 8 * size.mine * size.wide * size.span * HEAD_DIM
    rows = [
        pltpu.VMEM((size.steps, size.q_local * HEAD_DIM), BF),
        pltpu.VMEM((size.mine, size.wide, HEAD_DIM), F32),
        pltpu.SemaphoreType.DMA,
    ]
    sems = pltpu.SemaphoreType.DMA((2, 2 * size.mine))
    wide = pltpu.VMEM((size.mine, size.wide, HEAD_DIM), F32)

    def attend(k, mine, other, theirs, state):
        state, _ = chained_call(
            size, functools.partial(attend_kernel, size, k, both if (k, both) in message else (0,)),
            (query, fresh, messages_of(k)[0], mine, other, theirs), state, [], rows + [sems], flops,
        )
        return state

    def messages_of(k):
        return [message[k, p] for p in ([both] if (k, both) in message else [(0,), (1,)])]

    def take(k, parts, state):
        state, mine, theirs = rebuild(size, parts, messages_of(k), state)
        return state, mine, swapped(theirs), theirs

    state, held = None, []
    for k in [0] + order[:-1]:
        state, *each = take(k, both, state)
        held.append((k, *each))
        if k:
            state = attend(*held.pop(0), state)
    state = attend(*held.pop(0), state)
    split = size.rest > 0
    tables = message[last, (0,)]
    state, key_mine, theirs = rebuild(size, (0,), [tables], state, split)
    keys = theirs if split else (theirs,)
    key_others = [swapped(x) for x in keys]
    if split:
        head = pltpu.VMEM((size.span, HEAD_DIM), BF)
        state, theirs = chained_call(
            size, functools.partial(theirs_kernel, size), (message[last, (1,), 0], tables), state,
            [head] * size.mine, [], flops // 8,
        )
        others = [swapped(x) for x in theirs]
    half = pltpu.VMEM((size.mine, size.wide, size.span), BF)
    state, (weights, lent, share, totals) = chained_call(
        size, functools.partial(weights_kernel, size, last, split),
        (query, fresh, tables, key_mine, *key_others), state,
        [half, half, wide, wide], [], flops // 2,
    )
    given = pltpu.VMEM((size.mine * size.span, HEAD_DIM), BF)
    if split:
        state, _ = chained_call(
            size, functools.partial(lent_store_kernel, size, last), (key_mine, *theirs, *keys), state,
            [], [sems, sems], 0,
        )
        state, _ = chained_call(
            size, functools.partial(last_kernel, size, last),
            (weights, lent, share, totals, message[last, (1,), 1], tables, *others), state,
            [], [head] * size.mine + rows + [sems], flops // 4,
        )
        return state
    state, (mine, theirs, kept, sums) = chained_call(
        size, functools.partial(values_kernel, size),
        (weights, share, swapped(lent), message[last, (1,)], tables), state,
        [given, given, wide, wide], [], flops // 2,
    )
    got = swapped(sums)
    state, _ = chained_call(
        size, functools.partial(store_kernel, size, last), (mine, theirs, key_mine, *keys), state,
        [], [sems, sems], 0,
    )
    state, _ = chained_call(
        size, functools.partial(finish_kernel, size, last), (kept, got, totals), state, [], rows, 0
    )
    return state


def solution(mesh):
    placed = (
        P(("parts", "pool"), None, "sub", "tp"),
        P(("parts", "pool"), None, "sub", "tp"),
        P(("parts", "pool"), None, "tp"),
        P(("parts", "pool")),
        P(("parts", "pool")),
        P(("parts", "pool"), None, ("tp", "sub")),
        P(("parts", "pool"), None, None, "tp"),
    )
    return jax.shard_map(
        body,
        mesh=mesh,
        in_specs=placed,
        out_specs=(
            P(("parts", "pool"), None, "sub", "tp"),
            P(("parts", "pool"), None, ("tp", "sub")),
        ),
        check_vma=False,
    )
```

```python
import functools
import math

import jax
import jax.numpy as jnp
from jax import lax
from jax.experimental import pallas as pl
from jax.experimental.pallas import tpu as pltpu
from jax.sharding import PartitionSpec as P

HEAD_DIM = 128
Q_PER_KV = 8
TILE = 16
BF = jnp.bfloat16
F32 = jnp.float32
LOW = -1e30
NT = (((1,), (1,)), ((), ()))

IN_VMEM = pl.BlockSpec(memory_space=pltpu.VMEM)
IN_SMEM = pl.BlockSpec(memory_space=pltpu.SMEM)
IN_HBM = pl.BlockSpec(memory_space=pltpu.HBM)
LIMIT = pltpu.CompilerParams(vmem_limit_bytes=16 * 1024 * 1024)


def vmem(x):
    return pltpu.with_memory_space_constraint(x, pltpu.VMEM)


def hbm(x):
    return pltpu.with_memory_space_constraint(x, pltpu.HBM)


def far(n, k):
    ring = (0, 2, 1, 3) if n == 4 else tuple(range(n))
    return tuple(ring[(ring.index(z) + k) % n] for z in range(n))


def pick(values, at):
    out = jnp.int32(values[0])
    for i, value in enumerate(values[1:], 1):
        out = jnp.where(at == i, jnp.int32(value), out)
    return out


class Sizes:
    def __init__(self, deltas, anchors, new_query, n):
        self.n = n
        self.count, _, self.span, self.channels = deltas.shape
        self.rows = anchors.shape[2]
        self.repeat = self.span // self.rows
        self.steps = new_query.shape[1]
        self.heads = self.channels // HEAD_DIM
        self.q_local = new_query.shape[2] // HEAD_DIM
        self.mine = max(1, self.q_local // Q_PER_KV)
        self.group = self.q_local // self.mine
        self.wide = self.group * self.steps
        self.rest = self.heads - self.mine
        self.last = 1

    def anchor_at(self, which, parts):
        return (len(parts) * self.span + parts.index(which) * self.rows) * self.heads

    def side_at(self, parts):
        return len(parts) * self.heads * (self.span + self.rows)

    def message_rows(self, parts):
        return self.side_at(parts) + (TILE if 0 in parts else 0)

    def halved(self, k, parts):
        return k == self.last and parts == (1,) and self.rest > 0

    def half_rows(self):
        return self.mine * (self.span + self.rows)

    def source_row(self, k):
        return pick(far(self.n, self.n - k), lax.axis_index("pool"))


def side_block(size, scale, length):
    row = lax.broadcasted_iota(jnp.int32, (TILE, HEAD_DIM), 0)
    scale = scale.astype(F32)
    out = jnp.where(row == 2 * size.heads, length.astype(F32), jnp.float32(0.0))
    for which in range(2):
        for h in range(size.heads):
            piece = scale[which:which + 1, h * HEAD_DIM:(h + 1) * HEAD_DIM]
            out = jnp.where(row == which * size.heads + h, piece, out)
    return out.astype(BF)


def pack_kernel(size, plan, route, lengths, deltas, anchors, scale, *rest):
    outs, (held, tables, sems) = rest[:-3], rest[-3:]
    z = lax.axis_index("pool")
    sub = lax.axis_index("sub")
    outs, work = list(outs), []
    for k, parts in plan:
        msgs = [outs.pop(0) for _ in range(1 + size.halved(k, parts))]
        dest = pick(far(size.n, k), z)
        index = jnp.int32(0)
        for j in range(size.count):
            index = jnp.where(route[j] == dest, jnp.int32(j), index)
        for which in parts:
            slot = len(work)
            copies = (
                pltpu.make_async_copy(deltas.at[index, which], held.at[slot], sems.at[0, slot]),
                pltpu.make_async_copy(anchors.at[index, which], tables.at[slot], sems.at[1, slot]),
            )
            for copy in copies:
                copy.start()
            work.append((msgs, parts, which, slot, copies))
        if 0 in parts:
            side = side_block(size, scale[index], lengths[index])
            msgs[0][pl.ds(size.side_at(parts), TILE), :] = side
    for msgs, parts, which, slot, copies in work:
        for copy in copies:
            copy.wait()

        def fill(upper, msgs=msgs, parts=parts, which=which, slot=slot):
            for h in range(size.heads):
                lanes = slice(h * HEAD_DIM, (h + 1) * HEAD_DIM)
                if len(msgs) == 2:
                    own = (h >= size.rest) == upper
                    j, msg = h % size.mine, msgs[int(own)]
                    at, table = j * size.span, size.mine * size.span + j * size.rows
                else:
                    msg = msgs[0]
                    at = (parts.index(which) * size.heads + h) * size.span
                    table = size.anchor_at(which, parts) + h * size.rows
                msg[at:at + size.span, :] = held[slot, :, lanes]
                msg[table:table + size.rows, :] = tables[slot, :, lanes]

        if len(msgs) == 2:
            pl.when(sub == 0)(functools.partial(fill, False))
            pl.when(sub != 0)(functools.partial(fill, True))
        else:
            fill(False)


def pack(size, plan, route, lengths, deltas, anchors, scale):
    shapes = []
    for k, parts in plan:
        rows = [size.half_rows()] * 2 if size.halved(k, parts) else [size.message_rows(parts)]
        shapes += [pltpu.VMEM((r, HEAD_DIM), BF) for r in rows]
    slots = sum(len(parts) for _, parts in plan)
    return pl.pallas_call(
        functools.partial(pack_kernel, size, plan),
        out_shape=shapes,
        in_specs=[IN_SMEM, IN_SMEM, IN_HBM, IN_HBM, IN_VMEM],
        out_specs=[IN_VMEM] * len(shapes),
        scratch_shapes=[
            pltpu.VMEM((slots, size.span, size.channels), BF),
            pltpu.VMEM((slots, size.rows, size.channels), BF),
            pltpu.SemaphoreType.DMA((2, slots)),
        ],
        compiler_params=LIMIT,
        cost_estimate=pl.CostEstimate(
            flops=0, bytes_accessed=2 * slots * size.span * size.channels, transcendentals=0
        ),
    )(hbm(route), hbm(lengths), hbm(deltas), hbm(anchors), hbm(scale))


def arrange_kernel(size, new_query, new_kv, query, fresh, wide, tall):
    sub = lax.axis_index("sub")
    rest = size.heads - size.mine
    tall[...] = jnp.zeros_like(tall)
    for r in range(size.count):
        for j in range(size.mine):
            for g in range(size.group):
                at = (j * size.group + g) * HEAD_DIM
                piece = new_query[r, :, at:at + HEAD_DIM].astype(F32)
                wide[g * size.steps:(g + 1) * size.steps, :] = piece
            query[r, j] = wide[...].astype(BF)
            for which in range(2):
                own, other = (
                    new_kv[r, which, :, h * HEAD_DIM:(h + 1) * HEAD_DIM].astype(F32) for h in (j, j + rest)
                )
                tall[:size.steps, :] = jnp.where(sub == 0, own, other)
                fresh[r, which, j] = tall[...].astype(BF)


def arrange(size, new_query, new_kv):
    return pl.pallas_call(
        functools.partial(arrange_kernel, size),
        in_specs=[IN_VMEM, IN_VMEM],
        out_specs=[IN_VMEM, IN_VMEM],
        out_shape=[
            pltpu.VMEM((size.count, size.mine, size.wide, HEAD_DIM), BF),
            pltpu.VMEM((size.count, 2, size.mine, TILE, HEAD_DIM), BF),
        ],
        scratch_shapes=[pltpu.VMEM((size.wide, HEAD_DIM), F32), pltpu.VMEM((TILE, HEAD_DIM), F32)],
        compiler_params=LIMIT,
    )(hbm(new_query), hbm(new_kv))


def side_copies(size, k, parts, cache, out, own, sems, base=0):
    sub = lax.axis_index("sub")
    row = size.source_row(k)
    first = (sub if own else 1 - sub) * size.rest
    copies = []
    for p, which in enumerate(parts):
        for j in range(size.mine):
            lanes = pl.ds(pl.multiple_of((first + j) * HEAD_DIM, HEAD_DIM), HEAD_DIM)
            at = p * size.mine + j
            source = out[at] if isinstance(out, tuple) else out.at[pl.ds(at * size.span, size.span)]
            copies.append(
                pltpu.make_async_copy(source, cache.at[row, which, :, lanes], sems.at[base, at])
            )
    return copies


def row_copies(size, k, parts, cache, mine, theirs, sems):
    copies = side_copies(size, k, parts, cache, mine, True, sems)
    if size.rest:
        copies += side_copies(size, k, parts, cache, theirs, False, sems, 1)
    return copies


def rebuild_half(size, message, tables, out, own):
    sub = lax.axis_index("sub")
    side_at = size.side_at((0,))
    side = tables[side_at:side_at + TILE, :].astype(F32)
    length = side[2 * size.heads:2 * size.heads + 1, :]
    base = sub * size.span
    last = sub != 0 if own else sub == 0
    for j in range(size.mine):
        h = size.heads + j
        scale = jnp.where(last, side[h + size.rest:h + size.rest + 1, :], side[h:h + 1, :])
        table = size.mine * size.span + j * size.rows
        anchor = message[table:table + size.rows, :].astype(F32)
        for i in range(size.rows):
            part = slice(j * size.span + i * size.repeat, j * size.span + (i + 1) * size.repeat)
            value = anchor[i:i + 1, :] + scale * message[part, :].astype(F32)
            keep = (base + i * size.repeat).astype(F32) < length
            out[j][i * size.repeat:(i + 1) * size.repeat, :] = jnp.where(
                keep, value, jnp.float32(0.0)
            ).astype(BF)


def rebuild_heads(size, parts, message, tables, mine, theirs):
    sub = lax.axis_index("sub")
    rest = size.heads - size.mine
    side_at = size.side_at(parts if 0 in parts else (0,))
    side = tables[side_at:side_at + TILE, :].astype(F32)
    length = side[2 * size.heads:2 * size.heads + 1, :]
    base = sub * size.span
    for o, out in enumerate((theirs, mine)):
        first = (1 - sub) * rest if o == 0 else sub * rest
        other = sub == 0 if o == 0 else sub != 0
        for p, which in enumerate(parts):
            for j in range(size.mine):
                h = which * size.heads + j
                scale = jnp.where(other, side[h + rest:h + rest + 1, :], side[h:h + 1, :])
                table = pl.multiple_of(
                    size.anchor_at(which, parts) + (first + j) * size.rows, TILE
                )
                anchor = message[pl.ds(table, size.rows), :].astype(F32)
                source = (p * size.heads + first + j) * size.span
                to = (p * size.mine + j) * size.span
                target = out
                if isinstance(out, tuple):
                    target, to = out[p * size.mine + j], 0
                for i in range(size.rows):
                    at = pl.multiple_of(source + i * size.repeat, TILE)
                    value = anchor[i:i + 1, :] + scale * message[pl.ds(at, size.repeat), :].astype(F32)
                    keep = (base + i * size.repeat).astype(F32) < length
                    value = jnp.where(keep, value, jnp.float32(0.0)).astype(BF)
                    target[to + i * size.repeat:to + (i + 1) * size.repeat, :] = value


def rebuild_kernel(size, parts, chained, split, pair, message, *refs):
    mine, *theirs = refs[pair + 2 * chained + 2:]
    if pair:
        half = size.mine * size.span
        for which, source in enumerate((message, refs[0])):
            rows = pl.ds(which * half, half)
            rebuild_heads(size, (which,), source, message, mine.at[rows], theirs[0].at[rows])
    else:
        rebuild_heads(size, parts, message, message, mine, tuple(theirs) if split else theirs[0])


def rebuild(size, parts, messages, state, split=False):
    args = [vmem(x) for x in messages]
    in_specs = [IN_VMEM] * len(args)
    aliases = {}
    if state is not None:
        aliases = {len(args): 0, len(args) + 1: 1}
        args += list(state)
        in_specs += [IN_HBM, IN_HBM]
    given = (len(parts) * size.mine * size.span, HEAD_DIM)
    many, one = (size.mine, (size.span, HEAD_DIM)) if split else (1, given)
    out = pl.pallas_call(
        functools.partial(rebuild_kernel, size, parts, state is not None, split, len(messages) - 1),
        in_specs=in_specs,
        out_specs=[IN_HBM, IN_HBM, IN_VMEM] + [IN_VMEM] * many,
        out_shape=[
            pltpu.HBM((size.count, 2, size.span, size.channels), BF),
            pltpu.HBM((size.count, size.steps, size.q_local * HEAD_DIM), BF),
            pltpu.VMEM(given, BF),
        ] + [pltpu.VMEM(one, BF)] * many,
        input_output_aliases=aliases,
        compiler_params=LIMIT,
        cost_estimate=pl.CostEstimate(
            flops=4 * len(parts) * size.span * size.channels,
            bytes_accessed=6 * len(parts) * size.span * size.channels,
            transcendentals=0,
        ),
    )(*args)
    return tuple(out[:2]), out[2], (tuple(out[3:]) if split else out[3])


def weigh(size, j, q, new_key, key_mine, key_other, live_mine, live_other, causal):
    factor = 1.0 / math.sqrt(HEAD_DIM)
    s0 = lax.dot_general(q, key_mine, NT, preferred_element_type=F32) * factor
    s1 = lax.dot_general(q, key_other, NT, preferred_element_type=F32) * factor
    s2 = lax.dot_general(q, new_key, NT, preferred_element_type=F32) * factor
    s0 = jnp.where(live_mine, s0, jnp.float32(LOW))
    s1 = jnp.where(live_other, s1, jnp.float32(LOW))
    s2 = jnp.where(causal, s2, jnp.float32(LOW))
    top = jnp.maximum(
        jnp.max(jnp.maximum(s0, s1), axis=1, keepdims=True), jnp.max(s2, axis=1, keepdims=True)
    )
    w0 = jnp.where(live_mine, jnp.exp(s0 - top), jnp.float32(0.0))
    w1 = jnp.where(live_other, jnp.exp(s1 - top), jnp.float32(0.0))
    w2 = jnp.where(causal, jnp.exp(s2 - top), jnp.float32(0.0))
    total = jnp.sum(w0 + w1, axis=1, keepdims=True) + jnp.sum(w2, axis=1, keepdims=True)
    return w0.astype(BF), w1.astype(BF), w2.astype(BF), total


def masks(size, tables, parts, fresh):
    sub = lax.axis_index("sub")
    at = size.side_at(parts)
    side = tables[at:at + TILE, :].astype(F32)
    length = side[2 * size.heads:2 * size.heads + 1, 0:1]
    spot = lax.broadcasted_iota(jnp.int32, (1, size.span), 1)
    live_mine = (spot + sub * size.span).astype(F32) < length
    live_other = (spot + (1 - sub) * size.span).astype(F32) < length
    step = lax.broadcasted_iota(jnp.int32, (size.wide, fresh), 0) % size.steps
    token = lax.broadcasted_iota(jnp.int32, (size.wide, fresh), 1)
    return live_mine, live_other, (token <= step) & (token < size.steps)


def start_store(size, k, parts, cache, mine, theirs, sems):
    copies = row_copies(size, k, parts, cache, mine, theirs, sems)
    for copy in copies:
        copy.start()
    return copies


def store_heads(size, k, flat, made, attended, sem, copies):
    for j in range(size.mine):
        for g in range(size.group):
            at = (j * size.group + g) * HEAD_DIM
            made[:, at:at + HEAD_DIM] = flat[j, g * size.steps:(g + 1) * size.steps, :].astype(BF)
    copy = pltpu.make_async_copy(made, attended.at[size.source_row(k)], sem)
    copy.start()
    for each in copies:
        each.wait()
    copy.wait()


def attend_kernel(size, k, parts, query, new_kv, tables, mine, other, theirs, *refs):
    cache, attended, made, flat, sem, sems = refs[2:]
    row = size.source_row(k)
    copies = start_store(size, k, (0, 1), cache, mine, theirs, sems)
    live_mine, live_other, causal = masks(size, tables, parts, new_kv.shape[3])
    for j in range(size.mine):
        keys = slice(j * size.span, (j + 1) * size.span)
        values = slice((size.mine + j) * size.span, (size.mine + j + 1) * size.span)
        w0, w1, w2, total = weigh(
            size, j, query[row, j], new_kv[row, 0, j], mine[keys, :], other[keys, :],
            live_mine, live_other, causal,
        )
        acc = jnp.dot(w0, mine[values, :], preferred_element_type=F32)
        acc = acc + jnp.dot(w1, other[values, :], preferred_element_type=F32)
        acc = acc + jnp.dot(w2, new_kv[row, 1, j], preferred_element_type=F32)
        flat[j] = acc / total
    store_heads(size, k, flat, made, attended, sem, copies)


def weights_kernel(size, k, split, query, new_kv, tables, mine, *refs):
    many = size.mine if split else 1
    other, refs = refs[:many], refs[many:]
    _, _, weights, lent, share, totals = refs[2:]
    row = size.source_row(k)
    live_mine, live_other, causal = masks(size, tables, (0,), new_kv.shape[3])
    for j in range(size.mine):
        keys = slice(j * size.span, (j + 1) * size.span)
        w0, w1, w2, total = weigh(
            size, j, query[row, j], new_kv[row, 0, j], mine[keys, :],
            other[j][...] if split else other[0][keys, :],
            live_mine, live_other, causal,
        )
        weights[j] = w0
        lent[j] = w1
        share[j] = jnp.dot(w2, new_kv[row, 1, j], preferred_element_type=F32)
        totals[j] = jnp.broadcast_to(total, totals.shape[1:])


def theirs_kernel(size, message, tables, *refs):
    rebuild_half(size, message, tables, refs[4:], False)


def lent_store_kernel(size, k, mine, *refs):
    many = size.mine
    theirs, keys, refs = tuple(refs[:many]), tuple(refs[many:2 * many]), refs[2 * many:]
    cache, _, sems, more = refs[2:]
    copies = side_copies(size, k, (1,), cache, theirs, False, sems)
    copies += row_copies(size, k, (0,), cache, mine, keys, more)
    for copy in copies:
        copy.start()
    for copy in copies:
        copy.wait()


def last_kernel(size, k, weights, lent, share, totals, message, tables, *refs):
    others, refs = refs[:size.mine], refs[size.mine + 2:]
    cache, attended, *rest = refs
    mine, (made, flat, sem, sems) = tuple(rest[:size.mine]), rest[size.mine:]
    rebuild_half(size, message, tables, mine, True)
    copies = side_copies(size, k, (1,), cache, mine, True, sems)
    for copy in copies:
        copy.start()
    for j in range(size.mine):
        acc = share[j] + jnp.dot(weights[j], mine[j][...], preferred_element_type=F32)
        acc = acc + jnp.dot(lent[j], others[j][...], preferred_element_type=F32)
        flat[j] = acc / totals[j]
    store_heads(size, k, flat, made, attended, sem, copies)


def values_kernel(size, weights, share, lent, message, tables, *refs):
    _, _, mine, theirs, kept, given = refs[2:]
    rebuild_heads(size, (1,), message, tables, mine, theirs)
    for j in range(size.mine):
        values = slice(j * size.span, (j + 1) * size.span)
        kept[j] = share[j] + jnp.dot(weights[j], mine[values, :], preferred_element_type=F32)
        given[j] = jnp.dot(lent[j], theirs[values, :], preferred_element_type=F32)


def store_kernel(size, k, mine, theirs, key_mine, key_theirs, *refs):
    cache, _, sems, more = refs[2:]
    copies = start_store(size, k, (1,), cache, mine, theirs, sems)
    copies += start_store(size, k, (0,), cache, key_mine, key_theirs, more)
    for copy in copies:
        copy.wait()


def finish_kernel(size, k, kept, got, totals, *refs):
    _, attended, made, flat, sem = refs[2:]
    for j in range(size.mine):
        flat[j] = (kept[j] + got[j]) / totals[j]
    store_heads(size, k, flat, made, attended, sem, ())


def chained_call(size, kernel, args, state, shapes, scratch, flops):
    args = [vmem(x) for x in args]
    many = len(args)
    out = pl.pallas_call(
        kernel,
        in_specs=[IN_VMEM] * many + [IN_HBM, IN_HBM],
        out_specs=[IN_HBM, IN_HBM] + [IN_VMEM] * len(shapes),
        out_shape=[pltpu.HBM(x.shape, x.dtype) for x in state] + shapes,
        scratch_shapes=scratch,
        input_output_aliases={many: 0, many + 1: 1},
        compiler_params=LIMIT,
        cost_estimate=pl.CostEstimate(
            flops=flops,
            bytes_accessed=8 * size.span * size.channels,
            transcendentals=2 * size.mine * size.wide * size.span,
        ),
    )(*args, *state)
    return tuple(out[:2]), out[2:]


def body(deltas, anchors, chan_scale, lengths, route, new_query, new_kv):
    n = lax.axis_size("pool")
    size = Sizes(deltas, anchors, new_query, n)
    both = (0, 1)
    order = list(range(n - 1, 0, -1))
    last = order[-1]
    plan = [(order[0], (1,)), (order[0], (0,))]
    plan += [(k, (p,)) for k in order[1:] for p in both] + [(0, both)]
    query, fresh = arrange(size, new_query, new_kv)
    message = {}
    for part in (plan[:1], plan[1:]):
        msgs = list(pack(size, part, route, lengths, deltas, anchors, chan_scale))
        for k, parts in part:
            for half in range(1 + size.halved(k, parts)):
                msg = msgs.pop(0)
                if k:
                    msg = lax.ppermute(msg, "pool", list(enumerate(far(n, k))))
                message[(k, parts, half) if size.halved(k, parts) else (k, parts)] = msg

    def swapped(x):
        return lax.ppermute(x, "sub", [(0, 1), (1, 0)])

    flops = 8 * size.mine * size.wide * size.span * HEAD_DIM
    rows = [
        pltpu.VMEM((size.steps, size.q_local * HEAD_DIM), BF),
        pltpu.VMEM((size.mine, size.wide, HEAD_DIM), F32),
        pltpu.SemaphoreType.DMA,
    ]
    sems = pltpu.SemaphoreType.DMA((2, 2 * size.mine))
    wide = pltpu.VMEM((size.mine, size.wide, HEAD_DIM), F32)

    def attend(k, mine, other, theirs, state):
        state, _ = chained_call(
            size, functools.partial(attend_kernel, size, k, both if (k, both) in message else (0,)),
            (query, fresh, messages_of(k)[0], mine, other, theirs), state, [], rows + [sems], flops,
        )
        return state

    def messages_of(k):
        return [message[k, p] for p in ([both] if (k, both) in message else [(0,), (1,)])]

    def take(k, parts, state):
        state, mine, theirs = rebuild(size, parts, messages_of(k), state)
        return state, mine, swapped(theirs), theirs

    state, held = None, []
    for k in [order[0], 0] + order[1:-1]:
        state, *each = take(k, both, state)
        held.append((k, *each))
        if len(held) > 1:
            state = attend(*held.pop(0), state)
    state = attend(*held.pop(0), state)
    split = size.rest > 0
    tables = message[last, (0,)]
    state, key_mine, theirs = rebuild(size, (0,), [tables], state, split)
    keys = theirs if split else (theirs,)
    half = pltpu.VMEM((size.mine, size.wide, size.span), BF)
    state, (weights, lent, share, totals) = chained_call(
        size, functools.partial(weights_kernel, size, last, split),
        (query, fresh, tables, key_mine, *[swapped(x) for x in keys]), state,
        [half, half, wide, wide], [], flops // 2,
    )
    given = pltpu.VMEM((size.mine * size.span, HEAD_DIM), BF)
    if split:
        head = pltpu.VMEM((size.span, HEAD_DIM), BF)
        state, theirs = chained_call(
            size, functools.partial(theirs_kernel, size), (message[last, (1,), 0], tables), state,
            [head] * size.mine, [], flops // 8,
        )
        others = [swapped(x) for x in theirs]
        state, _ = chained_call(
            size, functools.partial(lent_store_kernel, size, last), (key_mine, *theirs, *keys), state,
            [], [sems, sems], 0,
        )
        state, _ = chained_call(
            size, functools.partial(last_kernel, size, last),
            (weights, lent, share, totals, message[last, (1,), 1], tables, *others), state,
            [], [head] * size.mine + rows + [sems], flops // 4,
        )
        return state
    state, (mine, theirs, kept, sums) = chained_call(
        size, functools.partial(values_kernel, size),
        (weights, share, swapped(lent), message[last, (1,)], tables), state,
        [given, given, wide, wide], [], flops // 2,
    )
    got = swapped(sums)
    state, _ = chained_call(
        size, functools.partial(store_kernel, size, last), (mine, theirs, key_mine, *keys), state,
        [], [sems, sems], 0,
    )
    state, _ = chained_call(
        size, functools.partial(finish_kernel, size, last), (kept, got, totals), state, [], rows, 0
    )
    return state


def solution(mesh):
    placed = (
        P(("parts", "pool"), None, "sub", "tp"),
        P(("parts", "pool"), None, "sub", "tp"),
        P(("parts", "pool"), None, "tp"),
        P(("parts", "pool")),
        P(("parts", "pool")),
        P(("parts", "pool"), None, ("tp", "sub")),
        P(("parts", "pool"), None, None, "tp"),
    )
    return jax.shard_map(
        body,
        mesh=mesh,
        in_specs=placed,
        out_specs=(
            P(("parts", "pool"), None, "sub", "tp"),
            P(("parts", "pool"), None, ("tp", "sub")),
        ),
        check_vma=False,
    )
```
